32 devices in a mesh: branch: 4 (over y, x), dp: 8 (over z, core).
Axes of the slice: x: 2, y: 2, z: 4, core: 2. Of those that a mesh axis runs over, the one named last changes fastest.
Arguments:
- tokens: bfloat16 [16384, 768], P('dp'), may hold values from -6 to 6
- cotangent: bfloat16 [16384, 768], P('dp'), may hold values from -6 to 6
- gain_before: float32 [768], replicated, may hold values from 0.1 to 1.9
- gain_middle: float32 [768], replicated, may hold values from 0.1 to 1.9
- router_vector: float32 [768], replicated, may hold values from -0.21875 to 0.21875
- local_heads: bfloat16 [768, 3, 512], P(None, None, 'branch'), may hold values from -0.3125 to 0.3125
- local_merge: bfloat16 [512, 768], P('branch'), may hold values from -0.5 to 0.5
- routed_heads: bfloat16 [768, 3, 768], P(None, None, 'branch'), may hold values from -0.3125 to 0.3125
- routed_merge: bfloat16 [768, 768], P('branch'), may hold values from -1.75 to 1.75
- local_expand: bfloat16 [768, 2, 1024], P(None, None, 'branch'), may hold values from -0.21875 to 0.21875
- local_reduce: bfloat16 [1024, 768], P('branch'), may hold values from -0.1875 to 0.1875
- routed_expand: bfloat16 [768, 2, 4096], P(None, None, 'branch'), may hold values from -0.21875 to 0.21875
- routed_reduce: bfloat16 [4096, 768], P('branch'), may hold values from -0.1875 to 0.1875
- routed_slots: int32 [4096], P('dp'), may hold values from 0 to 2047, as said below
- routed_counts: int32 [8], replicated, may hold values from 0 to 512, as said below
Outputs:
- layer_output: float32 [16384, 768], P('dp')
- tokens_delta: float32 [16384, 768], P('dp')
- delta_gain_before: float32 [768], replicated
- delta_gain_middle: float32 [768], replicated
- delta_router: float32 [768], replicated
- delta_local_heads: float32 [768, 3, 512], P(None, None, 'branch')
- delta_local_merge: float32 [512, 768], P('branch')
- delta_routed_heads: float32 [768, 3, 768], P(None, None, 'branch')
- delta_routed_merge: float32 [768, 768], P('branch')
- delta_local_expand: float32 [768, 2, 1024], P(None, None, 'branch')
- delta_local_reduce: float32 [1024, 768], P('branch')
- delta_routed_expand: float32 [768, 2, 4096], P(None, None, 'branch')
- delta_routed_reduce: float32 [4096, 768], P('branch')
The draws below stay inside these ranges and needn't reach their ends.
Inputs may be any that keep to these rules, and one draw needn't show every extreme that they name: `routed_counts`: entry e counts the routed tokens among the 2048 tokens of block e; blocks 2k and 2k + 1 together hold exactly 512; at least one entry equals 512. `routed_slots`: the 512 entries of block e begin with the positions, within its 2048 tokens, of its routed tokens in increasing order, as many as routed_counts[e]; the other entries are 0 and unused.
All inputs are finite; a program needn't handle non-finite values.
Results may differ from the reference program's by a relative error of at most 0.02.
The reference program's roundings to bfloat16 on the way count: a program that leaves them out, or rounds other values in their place, can miss the bound.
Values may be sent and summed in bfloat16 or wider, within the bound.
A program may use at most 384 MiB of HBM per device.

```python
import jax
import jax.numpy as jnp
from jax import lax

D = 768
HL = 8
HH = 12
DH = 64
FL = 1024
FH = 4096
WIN = 128
TOK_DEV = 2048
TOKENS = 16384
ROUTED = 2048
CAP = 512
N_DP = 8


def routing_plan(key):
    base_key = jax.random.fold_in(key, 7)
    even_share = TOK_DEV // 8
    pair_count = N_DP // 2
    moves = jax.random.randint(jax.random.fold_in(base_key, 2), (pair_count,), 0, even_share + 1)
    full_pair = jax.random.randint(jax.random.fold_in(base_key, 4), (), 0, pair_count)
    moves = moves.at[full_pair].set(even_share)
    signs = jax.random.randint(jax.random.fold_in(base_key, 5), (pair_count,), 0, 2) * 2 - 1
    shifted = moves * signs
    counts = jnp.stack([even_share + shifted, even_share - shifted], 1).reshape(-1).astype(jnp.int32)
    device_keys = jax.random.split(jax.random.fold_in(base_key, 3), N_DP)
    position_draws = jax.vmap(lambda device_key: jax.random.permutation(device_key, TOK_DEV))(device_keys)[:, :CAP]
    live_slots = jnp.arange(CAP)[None, :] < counts[:, None]
    chosen = jnp.sort(jnp.where(live_slots, position_draws, TOK_DEV), axis=1)
    slot_table = jnp.where(chosen == TOK_DEV, 0, chosen)
    return (counts, slot_table.reshape(-1).astype(jnp.int32))


def draw_routed_counts(key, part):
    return routing_plan(key)[0]


def draw_routed_slots(key, part):
    return routing_plan(key)[1]


def level_of(key, shape, cuts, low, largest):
    def one(position, shards_of):
        heights = jax.random.uniform(jax.random.fold_in(jax.random.fold_in(key, 6), position), (shards_of,), jnp.float32, low / len(cuts), largest / len(cuts))
        return jnp.repeat(jnp.exp(heights), shape[position] // shards_of).reshape((-1,) + (1,) * (len(shape) - position - 1))

    factor_of = one(*cuts[0])
    for cut in cuts[1:]:
        factor_of = factor_of * one(*cut)
    return factor_of


def gaussian(own_key, dims, scale, most, pieces=(), kind=jnp.bfloat16):
    array = scale * jax.random.normal(own_key, dims, jnp.float32)
    if pieces:
        array = array * level_of(own_key, dims, pieces, -0.22, 0.18)
    return jnp.clip(array, -most, most).astype(kind)


def setup_inputs(seed: int = 0) -> dict:
    key_of = jax.random.split(jax.random.key(seed), 16)
    return {
        "tokens": gaussian(key_of[0], (TOKENS, D), 1.0, 6.0, ((0, 8),)),
        "cotangent": gaussian(key_of[1], (TOKENS, D), 1.0, 6.0, ((0, 8),)),
        "gain_before": jnp.clip(1.0 + 0.18 * jax.random.normal(key_of[2], (D,), jnp.float32), 0.1, 1.9),
        "gain_middle": jnp.clip(1.0 + 0.18 * jax.random.normal(key_of[3], (D,), jnp.float32), 0.1, 1.9),
        "router_vector": gaussian(key_of[4], (D,), D ** -0.5, 0.21875, (), jnp.float32),
        "local_heads": gaussian(key_of[5], (D, 3, HL * DH), (D // 2) ** -0.5, 0.3125, ((2, 4),)),
        "local_merge": gaussian(key_of[6], (HL * DH, D), (HL * DH // 4) ** -0.5, 0.5, ((0, 4),)),
        "routed_heads": gaussian(key_of[7], (D, 3, HH * DH), (D // 2) ** -0.5, 0.3125, ((2, 4),)),
        "routed_merge": gaussian(key_of[8], (HH * DH, D), (HH * DH // 64) ** -0.5, 1.75, ((0, 4),)),
        "local_expand": gaussian(key_of[9], (D, 2, FL), D ** -0.5, 0.21875, ((2, 4),)),
        "local_reduce": gaussian(key_of[10], (FL, D), FL ** -0.5, 0.1875, ((0, 4),)),
        "routed_expand": gaussian(key_of[11], (D, 2, FH), D ** -0.5, 0.21875, ((2, 4),)),
        "routed_reduce": gaussian(key_of[12], (FH, D), (FH // 4) ** -0.5, 0.1875, ((0, 4),)),
        "routed_slots": draw_routed_slots(jax.random.fold_in(key_of[15], 71), 0),
        "routed_counts": draw_routed_counts(jax.random.fold_in(key_of[15], 71), 0),
    }


EPSILON = 1e-06
NEGATIVE = -1e+30
HIGHEST_PRECISION = lax.Precision.HIGHEST

@jax.custom_vjp
def low(v):
    return lax.optimization_barrier(v.astype(jnp.bfloat16)).astype(jnp.float32)

@jax.custom_vjp
def low_back(v):
    return v

def low_keep(v):
    return (low(v), None)

def low_pass(kept, grad):
    return (grad,)

def back_keep(v):
    return (v, None)

def back_low(kept, grad):
    return (low(grad),)
low.defvjp(low_keep, low_pass)
low_back.defvjp(back_keep, back_low)

def norm_rows(values, gain_vector):
    return values * lax.rsqrt(lax.optimization_barrier(jnp.mean(values * values, axis=-1, keepdims=True)) + EPSILON) * gain_vector

def split_heads(values):
    return values.reshape(values.shape[0], -1, DH)

def local_attention(query_heads, key_heads, value_heads):
    length = query_heads.shape[0]
    block_rows = 512
    border = jnp.zeros((WIN, key_heads.shape[1], DH), jnp.float32)
    keys_padded = jnp.concatenate([border, key_heads, border], 0)
    values_padded = jnp.concatenate([border, value_heads, border], 0)

    def one_block(block_index):
        block_start = block_index * block_rows
        query_block = lax.dynamic_slice_in_dim(query_heads, block_start, block_rows, 0)
        key_block = lax.dynamic_slice_in_dim(keys_padded, block_start, block_rows + 2 * WIN, 0)
        value_block = lax.dynamic_slice_in_dim(values_padded, block_start, block_rows + 2 * WIN, 0)
        query_place = block_start + jnp.arange(block_rows, dtype=jnp.int32)
        key_place = block_start - WIN + jnp.arange(block_rows + 2 * WIN, dtype=jnp.int32)
        allowed = (jnp.abs(query_place[:, None] - key_place[None, :]) <= WIN) & (key_place[None, :] >= 0) & (key_place[None, :] < length)
        scores = low_back(jnp.einsum('qhe,khe->hqk', query_block, key_block, precision=HIGHEST_PRECISION) * DH ** (-0.5))
        scores = jnp.where(allowed[None], scores, NEGATIVE)
        weights = low(jax.nn.softmax(scores, axis=-1))
        return low(low_back(jnp.einsum('hqk,khe->qhe', weights, value_block, precision=HIGHEST_PRECISION)))
    blocks = lax.map(jax.checkpoint(one_block), jnp.arange(length // block_rows, dtype=jnp.int32))
    return blocks.reshape(length, -1)

def routed_attention(query_heads, key_heads, value_heads):
    length = query_heads.shape[0]
    block_rows = min(512, length)

    def one_block(block_index):
        query_block = lax.dynamic_slice_in_dim(query_heads, block_index * block_rows, block_rows, 0)
        scores = low_back(jnp.einsum('qhe,khe->hqk', query_block, key_heads, precision=HIGHEST_PRECISION) * DH ** (-0.5))
        weights = low(jax.nn.softmax(scores, axis=-1))
        return low(low_back(jnp.einsum('hqk,khe->qhe', weights, value_heads, precision=HIGHEST_PRECISION)))
    blocks = lax.map(jax.checkpoint(one_block), jnp.arange(length // block_rows, dtype=jnp.int32))
    return blocks.reshape(length, -1)

def routed_index(routed_slots, routed_counts):
    slot_table = routed_slots.reshape(N_DP, CAP)
    starts = (jnp.cumsum(routed_counts) - routed_counts).astype(jnp.int32)
    slot_ids = jnp.arange(CAP, dtype=jnp.int32)
    slot_ranks = starts[:, None] + slot_ids[None, :]
    live_slots = slot_ids[None, :] < routed_counts[:, None]
    targets = jnp.where(live_slots, slot_ranks, ROUTED).reshape(-1).astype(jnp.int32)
    places = (slot_table + (jnp.arange(N_DP, dtype=jnp.int32) * TOK_DEV)[:, None]).reshape(-1).astype(jnp.int32)
    return jnp.zeros((ROUTED,), jnp.int32).at[targets].set(places, mode='drop')

def feed_forward(normed, expand):
    gate_pair = low_back(jnp.einsum('td,dcf->tcf', normed, expand, precision=HIGHEST_PRECISION))
    return low(jax.nn.gelu(gate_pair[:, 0], approximate=True) * gate_pair[:, 1])

def layer_forward(tokens, gain_before, gain_middle, router_vector, local_heads, local_merge, routed_heads, routed_merge, local_expand, local_reduce, routed_expand, routed_reduce, index_rows):
    first_normed = low(norm_rows(tokens, gain_before))
    local_proj = low(low_back(jnp.einsum('td,dcf->tcf', first_normed, local_heads, precision=HIGHEST_PRECISION)))
    local_context = local_attention(split_heads(local_proj[:, 0]), split_heads(local_proj[:, 1]), split_heads(local_proj[:, 2]))
    local_attn = low_back(jnp.dot(local_context, local_merge, precision=HIGHEST_PRECISION))
    picked_first = first_normed[index_rows]
    gate_value = jax.nn.sigmoid(jnp.dot(picked_first, router_vector, precision=HIGHEST_PRECISION))
    routed_proj = low(low_back(jnp.einsum('td,dcf->tcf', picked_first, routed_heads, precision=HIGHEST_PRECISION)))
    routed_context = routed_attention(split_heads(routed_proj[:, 0]), split_heads(routed_proj[:, 1]), split_heads(routed_proj[:, 2]))
    routed_attn = low_back(jnp.dot(routed_context, routed_merge, precision=HIGHEST_PRECISION))
    middle = tokens + local_attn + jnp.zeros_like(tokens).at[index_rows].add(gate_value[:, None] * routed_attn)
    second_normed = low(norm_rows(middle, gain_middle))
    local_ff = low_back(jnp.dot(feed_forward(second_normed, local_expand), local_reduce, precision=HIGHEST_PRECISION))
    routed_ff = low_back(jnp.dot(feed_forward(second_normed[index_rows], routed_expand), routed_reduce, precision=HIGHEST_PRECISION))
    return middle + local_ff + jnp.zeros_like(middle).at[index_rows].add(gate_value[:, None] * routed_ff)

def reference(tokens, cotangent, gain_before, gain_middle, router_vector, local_heads, local_merge, routed_heads, routed_merge, local_expand, local_reduce, routed_expand, routed_reduce, routed_slots, routed_counts):
    index_rows = routed_index(routed_slots, routed_counts)
    floats = [value.astype(jnp.float32) for value in (tokens, gain_before, gain_middle, router_vector, local_heads, local_merge, routed_heads, routed_merge, local_expand, local_reduce, routed_expand, routed_reduce)]

    def forward_only(*values):
        return layer_forward(*values, index_rows)
    output_rows, pull_back = jax.vjp(forward_only, *floats)
    grads = pull_back(cotangent.astype(jnp.float32))
    return (output_rows, grads[0], grads[1], grads[2], grads[3], grads[4], grads[5], grads[6], grads[7], grads[8], grads[9], grads[10], grads[11])
```

```python
import jax
import jax.numpy as jnp
from jax import lax
from jax.sharding import Mesh
from jax.sharding import PartitionSpec as P

DH = 64
WIN = 128
EPSILON = 1e-06
NEGATIVE = -1e30
HIGHEST = lax.Precision.HIGHEST
F32 = jnp.float32
BF16 = jnp.bfloat16
SCALE = DH ** (-0.5)
DP = ("zz", "core")
GROUP = ("branch", "core")


def mm(a, b, ca, cb):
    return lax.dot_general(a, b, (((ca,), (cb,)), ((), ())), preferred_element_type=F32)


def norm_parts(values):
    r = lax.rsqrt(jnp.mean(values * values, axis=-1, keepdims=True) + EPSILON)
    return r, values * r


def norm_back(dn, xh, r, gain):
    g = dn * gain
    return r * (g - xh * jnp.mean(g * xh, axis=-1, keepdims=True))


def gelu_parts(u):
    c = 0.7978845608028654
    t = jnp.tanh(c * (u + 0.044715 * u * u * u))
    g = 0.5 * u * (1.0 + t)
    dg = 0.5 * (1.0 + t) + 0.5 * u * (1.0 - t * t) * c * (1.0 + 3 * 0.044715 * u * u)
    return g, dg


def feed(n, seed, w_gate, w_up, w_down):
    u = mm(n, w_gate, 1, 0)
    v = mm(n, w_up, 1, 0)
    g, dg = gelu_parts(u)
    hidden = (g * v).astype(BF16)
    out = mm(hidden, w_down, 1, 0)
    dh = mm(seed, w_down, 1, 1)
    du = (dh * v * dg).astype(BF16)
    dv = (dh * g).astype(BF16)
    dn = mm(du, w_gate, 1, 1) + mm(dv, w_up, 1, 1)
    dwg = mm(n, du, 0, 0)
    dwu = mm(n, dv, 0, 0)
    dwd = mm(hidden, seed, 0, 0)
    return out, dn, dwg, dwu, dwd


def windows(x, count):
    return jnp.stack([x[i * WIN : (i + 3) * WIN] for i in range(count)], 0)


def local_scores(q4, kw, allowed):
    s = jnp.einsum("nqhe,nkhe->nhqk", q4, kw, preferred_element_type=F32) * SCALE
    return jnp.where(allowed[:, None], s, NEGATIVE)


def per_device(
    tokens,
    cotangent,
    gain_before,
    gain_middle,
    router_vector,
    local_heads,
    local_merge,
    routed_heads,
    routed_merge,
    local_expand,
    local_reduce,
    routed_expand,
    routed_reduce,
    routed_slots,
    routed_counts,
):
    nb = lax.axis_size("branch")
    nz = lax.axis_size("zz")
    ndp = 2 * nz
    b = lax.axis_index("branch")
    z = lax.axis_index("zz")
    core = lax.axis_index("core")
    d = 2 * z + core
    rows, D = tokens.shape
    own = rows // nb
    cap = routed_slots.shape[0]
    half = cap // 2
    hl = local_heads.shape[2]
    fl = local_expand.shape[2]
    fh = routed_expand.shape[2] // 2
    rw = routed_heads.shape[2]
    heads_l = nb * hl // DH
    heads_r = rw // DH
    blocks = own // WIN

    lh = lax.all_gather(local_heads.transpose(1, 0, 2), "branch")
    lm = lax.all_gather(local_merge, "branch", axis=0, tiled=True)
    le = lax.all_gather(local_expand.transpose(1, 0, 2), "branch")
    lr = lax.all_gather(local_reduce, "branch", axis=0, tiled=True)
    lh3 = lh.transpose(1, 2, 0, 3).reshape(3, D, nb * hl)
    le2 = le.transpose(1, 2, 0, 3).reshape(2, D, nb * fl)

    n_own = routed_counts[d]
    offset = jnp.where(core == 0, 0, cap - n_own)
    ranks = jnp.arange(cap, dtype=jnp.int32)
    live = (ranks >= offset) & (ranks < offset + n_own)
    rolled = jnp.take(routed_slots, jnp.mod(ranks - offset, cap), axis=0)
    ids = jnp.where(live, rolled, -1)
    pick = (ids[:, None] == jnp.arange(rows, dtype=jnp.int32)[None, :]).astype(BF16)
    pick_own = lax.dynamic_slice(pick, (0, b * own), (cap, own))
    mask_own = (jnp.sum(pick_own.astype(F32), 0) > 0.5)[:, None]

    pair_rows = mm(pick, jnp.concatenate([tokens, cotangent], 1), 1, 0).astype(BF16)
    pair_rows = lax.psum(pair_rows, "core").astype(F32)
    tok_r, cot_r = pair_rows[:, :D], pair_rows[:, D:]
    r1r, xh1r = norm_parts(tok_r)
    first_r = (xh1r * gain_before).astype(BF16)
    gate = jax.nn.sigmoid(jnp.dot(first_r.astype(F32), router_vector, precision=HIGHEST))[:, None]
    first_half = lax.dynamic_slice(first_r, (core * half, 0), (half, D))
    gate_half = lax.dynamic_slice(gate, (core * half, 0), (half, 1))
    proj_r = jnp.einsum("rd,dcf->rcf", first_half, routed_heads, preferred_element_type=F32).astype(BF16)
    kv = lax.all_gather(
        jnp.concatenate([proj_r[:, 1], proj_r[:, 2]], 1), DP, axis=0, tiled=True
    )

    perm_up = [(i, i + 1) for i in range(ndp - 1)]
    perm_down = [(i + 1, i) for i in range(ndp - 1)]
    before = lax.ppermute(tokens[rows - WIN :], DP, perm_up)
    after = lax.ppermute(tokens[:WIN], DP, perm_down)
    wide = jnp.concatenate([before, tokens, after], 0)
    wide_own = lax.dynamic_slice(wide, (b * own, 0), (own + 2 * WIN, D)).astype(F32)
    cot_own = lax.dynamic_slice(cotangent, (b * own, 0), (own, D))
    r1w, xh1w = norm_parts(wide_own)
    first_w = (xh1w * gain_before).astype(BF16)
    first_own = first_w[WIN : WIN + own]
    tok_own, r1, xh1 = (v[WIN : WIN + own] for v in (wide_own, r1w, xh1w))

    q = mm(first_own, lh3[0], 1, 0).astype(BF16)
    k = mm(first_w, lh3[1], 1, 0).astype(BF16)
    v = mm(first_w, lh3[2], 1, 0).astype(BF16)
    q4 = q.reshape(blocks, WIN, heads_l, DH)
    kw = windows(k.reshape(-1, heads_l, DH), blocks)
    vw = windows(v.reshape(-1, heads_l, DH), blocks)
    qpos = jnp.arange(WIN, dtype=jnp.int32)
    kpos = jnp.arange(3 * WIN, dtype=jnp.int32)
    near = jnp.abs(qpos[:, None] + WIN - kpos[None, :]) <= WIN
    first_key = d * rows + b * own - WIN + jnp.arange(blocks, dtype=jnp.int32)[:, None] * WIN + kpos[None, :]
    inside = (first_key >= 0) & (first_key < ndp * rows)
    allowed = near[None] & inside[:, None, :]
    s = local_scores(q4, kw, allowed)
    peak = jnp.max(s, -1, keepdims=True)
    w = jnp.exp(s - peak)
    tot = jnp.sum(w, -1, keepdims=True)
    lse_l = peak + jnp.log(tot)
    probs = (w / tot).astype(BF16)
    ctx_l = jnp.einsum("nhqk,nkhe->nqhe", probs, vw, preferred_element_type=F32).astype(BF16)
    ctx_l = ctx_l.reshape(own, heads_l * DH)
    local_attn = mm(ctx_l, lm, 1, 0)

    qr = proj_r[:, 0].reshape(half, heads_r, DH)
    kr = kv[:, :rw].reshape(-1, heads_r, DH)
    vr = kv[:, rw:].reshape(-1, heads_r, DH)
    sr = jnp.einsum("qhe,khe->hqk", qr, kr, preferred_element_type=F32) * SCALE
    peak_r = jnp.max(sr, -1, keepdims=True)
    wr = jnp.exp(sr - peak_r)
    tot_r = jnp.sum(wr, -1, keepdims=True)
    lse_r = peak_r + jnp.log(tot_r)
    ctx_r = jnp.einsum("hqk,khe->qhe", (wr / tot_r).astype(BF16), vr, preferred_element_type=F32)
    ctx_r = ctx_r.astype(BF16).reshape(half, rw)
    attn_r = mm(ctx_r, routed_merge, 1, 0)

    def at_half(x):
        return lax.dynamic_update_slice(jnp.zeros((cap, x.shape[1]), x.dtype), x, (core * half, 0))

    part = mm(pick_own, local_attn.astype(BF16), 1, 0) + at_half(gate_half * attn_r)
    mixed_r = lax.psum(part.astype(BF16), GROUP)
    mixed_own = jnp.where(mask_own, mm(pick_own, mixed_r, 0, 0), local_attn)
    middle_own = tok_own + mixed_own
    middle_r = tok_r + mixed_r.astype(F32)
    r2, xh2 = norm_parts(middle_own)
    second_own = (xh2 * gain_middle).astype(BF16)
    r2r, xh2r = norm_parts(middle_r)
    second_r = (xh2r * gain_middle).astype(BF16)

    ff_l, dn_l, d_lg, d_lu, d_ld = feed(second_own, cot_own, le2[0], le2[1], lr)
    re_half = lax.dynamic_slice(routed_expand, (0, 0, core * fh), (D, 2, fh))
    rr_half = lax.dynamic_slice(routed_reduce, (core * fh, 0), (fh, D))
    seed_r = (gate * cot_r).astype(BF16)
    ff_r, dn_r, d_rg, d_ru, d_rd = feed(second_r, seed_r, re_half[:, 0], re_half[:, 1], rr_half)
    gate_feed = jnp.sum(cot_r * ff_r, -1, keepdims=True)

    both = jnp.concatenate(
        [ff_r.astype(BF16), (dn_r + mm(pick_own, dn_l.astype(BF16), 1, 0)).astype(BF16)], 1
    )
    both = lax.psum(both, GROUP)
    ffr_sum, dn2_r = both[:, :D].astype(F32), both[:, D:]
    layer_own = (
        middle_own + ff_l + mm(pick_own, (gate * ffr_sum).astype(BF16), 0, 0)
    ).astype(BF16)
    layer_output = lax.all_gather(layer_own, "branch", axis=0, tiled=True).astype(F32)

    dn2_own = jnp.where(mask_own, mm(pick_own, dn2_r, 0, 0), dn_l)
    gm_own = cot_own.astype(F32) + norm_back(dn2_own, xh2, r2, gain_middle)
    gm_r = cot_r + norm_back(dn2_r.astype(F32), xh2r, r2r, gain_middle)
    delta_gain_middle = jnp.sum(dn2_own * xh2, 0)

    gm_low = gm_own.astype(BF16)
    dctx = mm(gm_low, lm, 1, 1).astype(BF16)
    d_lm = mm(ctx_l, gm_low, 0, 0)
    do4 = dctx.reshape(blocks, WIN, heads_l, DH)
    p = jnp.exp(local_scores(q4, kw, allowed) - lse_l)
    dp_ = jnp.einsum("nqhe,nkhe->nhqk", do4, vw, preferred_element_type=F32)
    inner = jnp.sum(p * dp_, -1, keepdims=True)
    ds = (p * (dp_ - inner)).astype(BF16)
    dq = jnp.einsum("nhqk,nkhe->nqhe", ds, kw, preferred_element_type=F32) * SCALE
    dkw = jnp.einsum("nhqk,nqhe->nkhe", ds, q4, preferred_element_type=F32) * SCALE
    dvw = jnp.einsum("nhqk,nqhe->nkhe", p.astype(BF16), do4, preferred_element_type=F32)
    dkv = jnp.concatenate(
        [dkw.reshape(blocks, 3 * WIN, -1), dvw.reshape(blocks, 3 * WIN, -1)], 2
    )
    ext = jnp.zeros((own + 2 * WIN, dkv.shape[2]), F32)
    for i in range(blocks):
        ext = ext.at[i * WIN : (i + 3) * WIN].add(dkv[i])
    total_dev = nb * ndp
    place = [(i % nb) * ndp + i // nb for i in range(total_dev)]
    up = [(place[i], place[i + 1]) for i in range(total_dev - 1)]
    down = [(place[i + 1], place[i]) for i in range(total_dev - 1)]
    everyone = ("branch",) + DP
    from_prev = lax.ppermute(ext[own + WIN :].astype(BF16), everyone, up).astype(F32)
    from_next = lax.ppermute(ext[:WIN].astype(BF16), everyone, down).astype(F32)
    dkv_own = ext[WIN : WIN + own].at[:WIN].add(from_prev).at[own - WIN :].add(from_next)
    dkv_own = dkv_own.astype(BF16)
    wl = heads_l * DH
    dq_own = dq.reshape(own, wl).astype(BF16)
    dk_own, dv_own = dkv_own[:, :wl], dkv_own[:, wl:]
    gf_l = mm(dq_own, lh3[0], 1, 1) + mm(dk_own, lh3[1], 1, 1) + mm(dv_own, lh3[2], 1, 1)
    d_lh = jnp.stack([mm(first_own, x, 0, 0) for x in (dq_own, dk_own, dv_own)], 0)

    gm_half = lax.dynamic_slice(gm_r, (core * half, 0), (half, D))
    seed_a = (gate_half * gm_half).astype(BF16)
    dctx_r = mm(seed_a, routed_merge, 1, 1).astype(BF16).reshape(half, heads_r, DH)
    d_rm = mm(ctx_r, seed_a, 0, 0)
    gate_attn = jnp.sum(gm_half * attn_r, -1, keepdims=True)
    pr = jnp.exp(sr - lse_r)
    dpr = jnp.einsum("qhe,khe->hqk", dctx_r, vr, preferred_element_type=F32)
    inner_r = jnp.sum(pr * dpr, -1, keepdims=True)
    dsr = (pr * (dpr - inner_r)).astype(BF16)
    dqr = jnp.einsum("hqk,khe->qhe", dsr, kr, preferred_element_type=F32) * SCALE
    dkr = jnp.einsum("hqk,qhe->khe", dsr, qr, preferred_element_type=F32) * SCALE
    dvr = jnp.einsum("hqk,qhe->khe", pr.astype(BF16), dctx_r, preferred_element_type=F32)
    dkvr = jnp.concatenate([dkr.reshape(-1, rw), dvr.reshape(-1, rw)], 1).astype(BF16)
    dkvr = lax.psum_scatter(dkvr, DP, scatter_dimension=0, tiled=True)
    triple = jnp.stack([dqr.reshape(half, rw).astype(BF16), dkvr[:, :rw], dkvr[:, rw:]], 1)
    picked = jnp.einsum("rcf,dcf->rd", triple, routed_heads, preferred_element_type=F32)
    d_rh = jnp.einsum("rd,rcf->dcf", first_half, triple, preferred_element_type=F32)
    d_logit = (at_half(gate_attn) + gate_feed) * gate * (1.0 - gate)
    router_part = jnp.sum(d_logit * first_r.astype(F32), 0)

    part3 = at_half(picked) + d_logit * router_vector[None, :] + mm(pick_own, gf_l.astype(BF16), 1, 0)
    gf_r = lax.psum(part3.astype(BF16), GROUP)
    gf_own = jnp.where(mask_own, mm(pick_own, gf_r, 0, 0), gf_l)
    td_own = (gm_own + norm_back(gf_own, xh1, r1, gain_before)).astype(BF16)
    delta_gain_before = jnp.sum(gf_own * xh1, 0)
    tokens_delta = lax.all_gather(td_own, "branch", axis=0, tiled=True).astype(F32)

    vectors = lax.psum(
        jnp.stack([delta_gain_before, delta_gain_middle, router_part]).astype(F32),
        ("branch",) + DP,
    )

    def over_branch(x, dim):
        return lax.psum_scatter(x.astype(BF16), "branch", scatter_dimension=dim, tiled=True)

    g_le = lax.psum(over_branch(jnp.stack([d_lg, d_lu], 0), 2), DP)
    g_lr = lax.psum(over_branch(d_ld, 0), DP)
    g_lh = lax.psum(over_branch(d_lh, 2), DP)
    g_lm = lax.psum(over_branch(d_lm, 0), DP)
    g_re = lax.all_gather(
        lax.psum(jnp.stack([d_rg, d_ru], 0).astype(BF16), "zz"), "core", axis=2, tiled=True
    )
    g_rr = lax.all_gather(lax.psum(d_rd.astype(BF16), "zz"), "core", axis=0, tiled=True)
    g_rh = lax.psum(d_rh.astype(BF16), DP)
    g_rm = lax.psum(d_rm.astype(BF16), DP)
    return (
        layer_output,
        tokens_delta,
        vectors[0],
        vectors[1],
        vectors[2],
        g_lh.transpose(1, 0, 2).astype(F32),
        g_lm.astype(F32),
        g_rh.astype(F32),
        g_rm.astype(F32),
        g_le.transpose(1, 0, 2).astype(F32),
        g_lr.astype(F32),
        g_re.transpose(1, 0, 2).astype(F32),
        g_rr.astype(F32),
    )


def solution(mesh):
    nb = mesh.shape["branch"]
    fine = Mesh(mesh.devices.reshape(nb, -1, 2), ("branch", "zz", "core"))
    rows = P(DP, None)
    cols = P(None, None, "branch")
    deep = P("branch", None)
    return jax.shard_map(
        per_device,
        mesh=fine,
        in_specs=(
            rows, rows, P(), P(), P(), cols, deep, cols, deep, cols, deep, cols, deep, P(DP), P(),
        ),
        out_specs=(
            rows, rows, P(), P(), P(), cols, deep, cols, deep, cols, deep, cols, deep,
        ),
        check_vma=False,
    )
```

```python
import functools

import jax
import jax.numpy as jnp
from jax import lax
from jax.experimental import pallas as pl
from jax.experimental.pallas import tpu as pltpu
from jax.sharding import Mesh
from jax.sharding import PartitionSpec as P

DH = 64
WIN = 128
EPSILON = 1e-06
NEGATIVE = -1e30
HIGHEST = lax.Precision.HIGHEST
F32 = jnp.float32
BF16 = jnp.bfloat16
SCALE = DH ** (-0.5)
DP = ("zz", "core")
GROUP = ("branch", "core")


def mm(a, b, ca, cb):
    return lax.dot_general(a, b, (((ca,), (cb,)), ((), ())), preferred_element_type=F32)


def norm_parts(values):
    r = lax.rsqrt(jnp.mean(values * values, axis=-1, keepdims=True) + EPSILON)
    return r, values * r


def norm_back(dn, xh, r, gain):
    g = dn * gain
    return r * (g - xh * jnp.mean(g * xh, axis=-1, keepdims=True))


def gelu_parts(u):
    c = 0.7978845608028654
    t = jnp.tanh(c * (u + 0.044715 * u * u * u))
    g = 0.5 * u * (1.0 + t)
    dg = 0.5 * (1.0 + t) + 0.5 * u * (1.0 - t * t) * c * (1.0 + 3 * 0.044715 * u * u)
    return g, dg


def feed(n, seed, w_gate, w_up, w_down):
    u = mm(n, w_gate, 1, 0)
    v = mm(n, w_up, 1, 0)
    g, dg = gelu_parts(u)
    hidden = (g * v).astype(BF16)
    out = mm(hidden, w_down, 1, 0)
    dh = mm(seed, w_down, 1, 1)
    du = (dh * v * dg).astype(BF16)
    dv = (dh * g).astype(BF16)
    dn = mm(du, w_gate, 1, 1) + mm(dv, w_up, 1, 1)
    dwg = mm(n, du, 0, 0)
    dwu = mm(n, dv, 0, 0)
    dwd = mm(hidden, seed, 0, 0)
    return out, dn, dwg, dwu, dwd


def windows(x, count):
    return jnp.stack([x[i * WIN : (i + 3) * WIN] for i in range(count)], 0)


def local_scores(q4, kw, allowed):
    s = jnp.einsum("nqhe,nkhe->nhqk", q4, kw, preferred_element_type=F32) * SCALE
    return jnp.where(allowed[:, None], s, NEGATIVE)


MESH = pl.DeviceIdType.MESH


def remote(src, dst, send, recv, device):
    return pltpu.make_async_remote_copy(
        src_ref=src, dst_ref=dst, send_sem=send, recv_sem=recv, device_id=device, device_id_type=MESH
    )


def greet(devices):
    barrier = pltpu.get_barrier_semaphore()
    for device in devices:
        pl.semaphore_signal(barrier, inc=1, device_id=device, device_id_type=MESH)
    pl.semaphore_wait(barrier, len(devices))


def here():
    return lax.axis_index("branch"), lax.axis_index("zz"), lax.axis_index("core")


def others(me, count):
    return [lax.rem(me + k, count) for k in range(1, count)]


def band(start, size):
    return pl.ds(pl.multiple_of(start, size), size)


def group_sum_kernel(nb, x, o, sib, part, came, sib_s, sib_r, rs_s, rs_r, ag_s, ag_r, fw_s, fw_r):
    b, z, c = here()
    half = x.shape[0] // 2
    ch = half // nb
    twin = (b, z, 1 - c)
    peers = others(b, nb)

    def rows(core, j):
        return band(core * half + j * ch, ch)

    greet([twin] + [(j, z, c) for j in peers])
    order = peers + [b]
    to_twin = [remote(x.at[rows(1 - c, j)], sib.at[j], sib_s.at[j], sib_r.at[j], twin) for j in order]
    for copy in to_twin:
        copy.start()
    sends = []
    for j, copy in zip(peers, to_twin):
        copy.wait_recv()
        part[j] = (x[rows(c, j)].astype(F32) + sib[j].astype(F32)).astype(BF16)
        send = remote(part.at[j], came.at[b], rs_s.at[j], rs_r.at[b], (j, z, c))
        send.start()
        sends.append(send)
    to_twin[-1].wait_recv()
    total = x[rows(c, b)].astype(F32) + sib[b].astype(F32)
    for j in peers:
        remote(part.at[j], came.at[j], rs_s.at[j], rs_r.at[j], (j, z, c)).wait_recv()
        total = total + came[j].astype(F32)
    mine = o.at[rows(c, b)]
    mine[...] = total.astype(BF16)
    for j in peers:
        send = remote(mine, mine, ag_s.at[j], ag_r.at[b], (j, z, c))
        send.start()
        sends.append(send)
    send = remote(mine, mine, fw_s.at[b], fw_r.at[b], twin)
    send.start()
    sends.append(send)
    for j in peers:
        piece = o.at[rows(c, j)]
        remote(piece, piece, ag_s.at[j], ag_r.at[j], (j, z, c)).wait_recv()
        send = remote(piece, piece, fw_s.at[j], fw_r.at[j], twin)
        send.start()
        sends.append(send)
    for j in order:
        piece = o.at[rows(1 - c, j)]
        remote(piece, piece, fw_s.at[j], fw_r.at[j], twin).wait_recv()
    for copy in to_twin + sends:
        copy.wait_send()


def group_sum(x, nb, cid):
    rows, width = x.shape
    ch = rows // 2 // nb
    dma = pltpu.SemaphoreType.DMA((nb,))
    return pl.pallas_call(
        functools.partial(group_sum_kernel, nb),
        out_shape=jax.ShapeDtypeStruct(x.shape, BF16),
        in_specs=[pl.BlockSpec(memory_space=pltpu.VMEM)],
        out_specs=pl.BlockSpec(memory_space=pltpu.VMEM),
        scratch_shapes=[pltpu.VMEM((nb, ch, width), BF16)] * 3 + [dma] * 8,
        compiler_params=pltpu.CompilerParams(
            collective_id=cid, has_side_effects=True, vmem_limit_bytes=40 << 20
        ),
    )(x)


def block_sum_kernel(nz, x, o, sib, part, came, sib_s, sib_r, rs_s, rs_r):
    b, z, c = here()
    ch = o.shape[0]
    twin = (b, z, 1 - c)
    peers = others(z, nz)

    def rows(core, j):
        return band((2 * j + core) * ch, ch)

    greet([twin] + [(b, j, c) for j in peers])
    order = peers + [z]
    to_twin = [remote(x.at[rows(1 - c, j)], sib.at[j], sib_s.at[j], sib_r.at[j], twin) for j in order]
    for copy in to_twin:
        copy.start()
    sends = []
    for j, copy in zip(peers, to_twin):
        copy.wait_recv()
        part[j] = (x[rows(c, j)].astype(F32) + sib[j].astype(F32)).astype(BF16)
        send = remote(part.at[j], came.at[z], rs_s.at[j], rs_r.at[z], (b, j, c))
        send.start()
        sends.append(send)
    to_twin[-1].wait_recv()
    total = x[rows(c, z)].astype(F32) + sib[z].astype(F32)
    for j in peers:
        remote(part.at[j], came.at[j], rs_s.at[j], rs_r.at[j], (b, j, c)).wait_recv()
        total = total + came[j].astype(F32)
    o[...] = total.astype(BF16)
    for copy in to_twin + sends:
        copy.wait_send()


def block_sum(x, nz, cid):
    rows, width = x.shape
    ch = rows // (2 * nz)
    dma = pltpu.SemaphoreType.DMA((nz,))
    return pl.pallas_call(
        functools.partial(block_sum_kernel, nz),
        out_shape=jax.ShapeDtypeStruct((ch, width), BF16),
        in_specs=[pl.BlockSpec(memory_space=pltpu.VMEM)],
        out_specs=pl.BlockSpec(memory_space=pltpu.VMEM),
        scratch_shapes=[pltpu.VMEM((nz, ch, width), BF16)] * 3 + [dma] * 4,
        compiler_params=pltpu.CompilerParams(
            collective_id=cid, has_side_effects=True, vmem_limit_bytes=40 << 20
        ),
    )(x)


def prep_kernel(
    nb, nz,
    tokens, cotangent, ids, gain, router, heads, lh, lm, le, lr,
    tok_o, cot_o, first_o, gate_o, q_o, kv_o, lh_o, lm_o, le_o, lr_o,
    picks, sib, sib_s, sib_r, own_s, w_s, w_r, wf_s, wf_r, kv_s, kv_r, kf_s, kf_r,
):
    b, z, c = here()
    twin = (b, z, 1 - c)
    bpeers = others(b, nb)
    zpeers = others(z, nz)
    cap, D = tok_o.shape
    half = cap // 2
    rw = q_o.shape[1]
    greet([twin] + [(j, z, c) for j in bpeers] + [(b, j, c) for j in zpeers])

    pairs = [(lh, lh_o), (lm, lm_o), (le, le_o), (lr, lr_o)]

    def cut(ref, array, core):
        if array == 0:
            size = ref.shape[1] // 2
            return ref.at[:, band(core * size, size)]
        size = ref.shape[0] // 2
        return ref.at[band(core * size, size)]

    sends = []
    for i, (src, dst) in enumerate(pairs):
        own = pltpu.make_async_copy(src, dst.at[b], own_s.at[i])
        own.start()
        sends.append(own)
        for j in bpeers:
            copy = remote(cut(src, i, c), cut(dst.at[b], i, c), w_s.at[i, j], w_r.at[i, b], (j, z, c))
            copy.start()
            sends.append(copy)

    step = cap // 4
    for k in range(4):
        at = pl.ds(k * step, step)
        spot = lax.broadcasted_iota(jnp.int32, (step, tokens.shape[0]), 1)
        hot = jnp.where(ids[at] == spot, 1.0, 0.0).astype(BF16)
        picks[at, :D] = mm(hot, tokens[...], 1, 0).astype(BF16)
        picks[at, D:] = mm(hot, cotangent[...], 1, 0).astype(BF16)
        copy = remote(picks.at[at], sib.at[at], sib_s.at[k], sib_r.at[k], twin)
        copy.start()
        sends.append(copy)
    for k in range(4):
        at = pl.ds(k * step, step)
        remote(picks.at[at], sib.at[at], sib_s.at[k], sib_r.at[k], twin).wait_recv()
        tok = picks[at, :D].astype(F32) + sib[at, :D].astype(F32)
        tok_o[at] = tok.astype(BF16)
        cot_o[at] = (picks[at, D:].astype(F32) + sib[at, D:].astype(F32)).astype(BF16)
        r = lax.rsqrt(jnp.mean(tok * tok, axis=-1, keepdims=True) + EPSILON)
        first = (tok * r * gain[...]).astype(BF16)
        first_o[at] = first
        logit = jnp.sum(first.astype(F32) * router[...], axis=-1, keepdims=True)
        gate_o[at] = 1.0 / (1.0 + jnp.exp(-logit))

    own_rows = first_o[band(c * half, half)]
    q_o[...] = mm(own_rows, heads[0], 1, 1).astype(BF16)
    mine = kv_o.at[band((2 * z + c) * half, half)]
    mine[:, :rw] = mm(own_rows, heads[1], 1, 1).astype(BF16)
    mine[:, rw:] = mm(own_rows, heads[2], 1, 1).astype(BF16)
    for j in zpeers:
        copy = remote(mine, mine, kv_s.at[j], kv_r.at[z], (b, j, c))
        copy.start()
        sends.append(copy)
    copy = remote(mine, mine, kf_s.at[z], kf_r.at[z], twin)
    copy.start()
    sends.append(copy)

    def pass_weights(i):
        for j in bpeers:
            dst = cut(pairs[i][1].at[j], i, c)
            remote(dst, dst, w_s.at[i, j], w_r.at[i, j], (j, z, c)).wait_recv()
            copy = remote(dst, dst, wf_s.at[i, j], wf_r.at[i, j], twin)
            copy.start()
            sends.append(copy)

    pass_weights(0)
    for j in zpeers:
        piece = kv_o.at[band((2 * j + c) * half, half)]
        remote(piece, piece, kv_s.at[j], kv_r.at[j], (b, j, c)).wait_recv()
        copy = remote(piece, piece, kf_s.at[j], kf_r.at[j], twin)
        copy.start()
        sends.append(copy)
    for i in range(1, 4):
        pass_weights(i)
    for j in zpeers + [z]:
        piece = kv_o.at[band((2 * j + 1 - c) * half, half)]
        remote(piece, piece, kf_s.at[j], kf_r.at[j], twin).wait_recv()
    for i in range(4):
        for j in bpeers:
            dst = cut(pairs[i][1].at[j], i, 1 - c)
            remote(dst, dst, wf_s.at[i, j], wf_r.at[i, j], twin).wait_recv()
    for copy in sends:
        if copy.is_remote:
            copy.wait_send()
        else:
            copy.wait()


def prep(nb, nz, tokens, cotangent, ids, gain, router, heads, lh, lm, le, lr):
    cap = ids.shape[0]
    D = tokens.shape[1]
    rw = heads.shape[1]
    half = cap // 2
    vmem = pl.BlockSpec(memory_space=pltpu.VMEM)
    hbm = pl.BlockSpec(memory_space=pl.ANY)
    like = lambda x: jax.ShapeDtypeStruct((nb,) + x.shape, BF16)
    rows = jax.ShapeDtypeStruct((cap, D), BF16)
    dma = lambda *shape: pltpu.SemaphoreType.DMA(shape)
    return pl.pallas_call(
        functools.partial(prep_kernel, nb, nz),
        out_shape=(
            rows, rows, rows,
            jax.ShapeDtypeStruct((cap, 1), F32),
            jax.ShapeDtypeStruct((half, rw), BF16),
            jax.ShapeDtypeStruct((2 * nz * half, 2 * rw), BF16),
            like(lh), like(lm), like(le), like(lr),
        ),
        in_specs=[vmem] * 6 + [hbm] * 4,
        out_specs=(vmem,) * 6 + (hbm,) * 4,
        scratch_shapes=[
            pltpu.VMEM((cap, 2 * D), BF16),
            pltpu.VMEM((cap, 2 * D), BF16),
            dma(4), dma(4), dma(4),
            dma(4, nb), dma(4, nb), dma(4, nb), dma(4, nb),
            dma(nz), dma(nz), dma(nz), dma(nz),
        ],
        compiler_params=pltpu.CompilerParams(
            collective_id=0, has_side_effects=True, vmem_limit_bytes=40 << 20
        ),
    )(tokens, cotangent, ids, gain, router, heads, lh, lm, le, lr)


def per_device(
    tokens,
    cotangent,
    gain_before,
    gain_middle,
    router_vector,
    local_heads,
    local_merge,
    routed_heads,
    routed_merge,
    local_expand,
    local_reduce,
    routed_expand,
    routed_reduce,
    routed_slots,
    routed_counts,
):
    nb = lax.axis_size("branch")
    nz = lax.axis_size("zz")
    ndp = 2 * nz
    b = lax.axis_index("branch")
    z = lax.axis_index("zz")
    core = lax.axis_index("core")
    d = 2 * z + core
    rows, D = tokens.shape
    own = rows // nb
    cap = routed_slots.shape[0]
    half = cap // 2
    hl = local_heads.shape[2]
    fl = local_expand.shape[2]
    fh = routed_expand.shape[2] // 2
    rw = routed_heads.shape[2]
    heads_l = nb * hl // DH
    heads_r = rw // DH
    blocks = own // WIN

    n_own = routed_counts[d]
    offset = jnp.where(core == 0, 0, cap - n_own)
    ranks = jnp.arange(cap, dtype=jnp.int32)
    live = (ranks >= offset) & (ranks < offset + n_own)
    twice = jnp.concatenate([routed_slots, routed_slots])
    rolled = lax.dynamic_slice(twice, (jnp.mod(cap - offset, cap),), (cap,))
    ids = jnp.where(live, rolled, -1)
    own_ids = ids[:, None] - b * own
    pick_own = (own_ids == jnp.arange(own, dtype=jnp.int32)[None, :]).astype(BF16)
    mask_own = (jnp.sum(pick_own.astype(F32), 0) > 0.5)[:, None]

    tok_r, cot_r, first_r, gate, qr, kv, lh, lm, le, lr = prep(
        nb, nz, tokens, cotangent, ids[:, None], gain_before[None], router_vector[None],
        routed_heads.transpose(1, 2, 0),
        local_heads.transpose(1, 0, 2), local_merge, local_expand.transpose(1, 0, 2), local_reduce,
    )
    tok_r, cot_r = tok_r.astype(F32), cot_r.astype(F32)
    r1r, xh1r = norm_parts(tok_r)
    first_half = lax.dynamic_slice(first_r, (core * half, 0), (half, D))
    gate_half = lax.dynamic_slice(gate, (core * half, 0), (half, 1))
    lm = lm.reshape(nb * hl, D)
    lr = lr.reshape(nb * fl, D)
    lh3 = lh.transpose(1, 2, 0, 3).reshape(3, D, nb * hl)
    le2 = le.transpose(1, 2, 0, 3).reshape(2, D, nb * fl)

    perm_up = [(i, i + 1) for i in range(ndp - 1)]
    perm_down = [(i + 1, i) for i in range(ndp - 1)]
    before = lax.ppermute(tokens[rows - WIN :], DP, perm_up)
    after = lax.ppermute(tokens[:WIN], DP, perm_down)
    wide = jnp.concatenate([before, tokens, after], 0)
    wide_own = lax.dynamic_slice(wide, (b * own, 0), (own + 2 * WIN, D)).astype(F32)
    cot_own = lax.dynamic_slice(cotangent, (b * own, 0), (own, D))
    r1w, xh1w = norm_parts(wide_own)
    first_w = (xh1w * gain_before).astype(BF16)
    first_own = first_w[WIN : WIN + own]
    tok_own, r1, xh1 = (v[WIN : WIN + own] for v in (wide_own, r1w, xh1w))

    q = mm(first_own, lh3[0], 1, 0).astype(BF16)
    k = mm(first_w, lh3[1], 1, 0).astype(BF16)
    v = mm(first_w, lh3[2], 1, 0).astype(BF16)
    q4 = q.reshape(blocks, WIN, heads_l, DH)
    kw = windows(k.reshape(-1, heads_l, DH), blocks)
    vw = windows(v.reshape(-1, heads_l, DH), blocks)
    qpos = jnp.arange(WIN, dtype=jnp.int32)
    kpos = jnp.arange(3 * WIN, dtype=jnp.int32)
    near = jnp.abs(qpos[:, None] + WIN - kpos[None, :]) <= WIN
    first_key = d * rows + b * own - WIN + jnp.arange(blocks, dtype=jnp.int32)[:, None] * WIN + kpos[None, :]
    inside = (first_key >= 0) & (first_key < ndp * rows)
    allowed = near[None] & inside[:, None, :]
    s = local_scores(q4, kw, allowed)
    peak = jnp.max(s, -1, keepdims=True)
    w = jnp.exp(s - peak)
    tot = jnp.sum(w, -1, keepdims=True)
    lse_l = peak + jnp.log(tot)
    probs = (w / tot).astype(BF16)
    ctx_l = jnp.einsum("nhqk,nkhe->nqhe", probs, vw, preferred_element_type=F32).astype(BF16)
    ctx_l = ctx_l.reshape(own, heads_l * DH)
    local_attn = mm(ctx_l, lm, 1, 0)

    qr = qr.reshape(half, heads_r, DH)
    kr = kv[:, :rw].reshape(-1, heads_r, DH)
    vr = kv[:, rw:].reshape(-1, heads_r, DH)
    sr = jnp.einsum("qhe,khe->hqk", qr, kr, preferred_element_type=F32) * SCALE
    peak_r = jnp.max(sr, -1, keepdims=True)
    wr = jnp.exp(sr - peak_r)
    tot_r = jnp.sum(wr, -1, keepdims=True)
    lse_r = peak_r + jnp.log(tot_r)
    ctx_r = jnp.einsum("hqk,khe->qhe", (wr / tot_r).astype(BF16), vr, preferred_element_type=F32)
    ctx_r = ctx_r.astype(BF16).reshape(half, rw)
    attn_r = mm(ctx_r, routed_merge, 1, 0)

    def at_half(x):
        return lax.dynamic_update_slice(jnp.zeros((cap, x.shape[1]), x.dtype), x, (core * half, 0))

    part = mm(pick_own, local_attn.astype(BF16), 1, 0) + at_half(gate_half * attn_r)
    mixed_r = group_sum(part.astype(BF16), nb, 1)
    mixed_own = jnp.where(mask_own, mm(pick_own, mixed_r, 0, 0), local_attn)
    middle_own = tok_own + mixed_own
    middle_r = tok_r + mixed_r.astype(F32)
    r2, xh2 = norm_parts(middle_own)
    second_own = (xh2 * gain_middle).astype(BF16)
    r2r, xh2r = norm_parts(middle_r)
    second_r = (xh2r * gain_middle).astype(BF16)

    ff_l, dn_l, d_lg, d_lu, d_ld = feed(second_own, cot_own, le2[0], le2[1], lr)
    re_half = lax.dynamic_slice(routed_expand, (0, 0, core * fh), (D, 2, fh))
    rr_half = lax.dynamic_slice(routed_reduce, (core * fh, 0), (fh, D))
    seed_r = (gate * cot_r).astype(BF16)
    ff_r, dn_r, d_rg, d_ru, d_rd = feed(second_r, seed_r, re_half[:, 0], re_half[:, 1], rr_half)
    gate_feed = jnp.sum(cot_r * ff_r, -1, keepdims=True)

    both = jnp.concatenate(
        [ff_r.astype(BF16), (dn_r + mm(pick_own, dn_l.astype(BF16), 1, 0)).astype(BF16)], 1
    )
    both = group_sum(both, nb, 2)
    ffr_sum, dn2_r = both[:, :D].astype(F32), both[:, D:]
    layer_own = (
        middle_own + ff_l + mm(pick_own, (gate * ffr_sum).astype(BF16), 0, 0)
    ).astype(BF16)
    layer_output = lax.all_gather(layer_own, "branch", axis=0, tiled=True).astype(F32)

    dn2_own = jnp.where(mask_own, mm(pick_own, dn2_r, 0, 0), dn_l)
    gm_own = cot_own.astype(F32) + norm_back(dn2_own, xh2, r2, gain_middle)
    gm_r = cot_r + norm_back(dn2_r.astype(F32), xh2r, r2r, gain_middle)
    delta_gain_middle = jnp.sum(dn2_own * xh2, 0)

    gm_low = gm_own.astype(BF16)
    dctx = mm(gm_low, lm, 1, 1).astype(BF16)
    d_lm = mm(ctx_l, gm_low, 0, 0)
    do4 = dctx.reshape(blocks, WIN, heads_l, DH)
    p = jnp.exp(local_scores(q4, kw, allowed) - lse_l)
    dp_ = jnp.einsum("nqhe,nkhe->nhqk", do4, vw, preferred_element_type=F32)
    inner = jnp.sum(p * dp_, -1, keepdims=True)
    ds = (p * (dp_ - inner)).astype(BF16)
    dq = jnp.einsum("nhqk,nkhe->nqhe", ds, kw, preferred_element_type=F32) * SCALE
    dkw = jnp.einsum("nhqk,nqhe->nkhe", ds, q4, preferred_element_type=F32) * SCALE
    dvw = jnp.einsum("nhqk,nqhe->nkhe", p.astype(BF16), do4, preferred_element_type=F32)
    dkv = jnp.concatenate(
        [dkw.reshape(blocks, 3 * WIN, -1), dvw.reshape(blocks, 3 * WIN, -1)], 2
    )
    ext = jnp.zeros((own + 2 * WIN, dkv.shape[2]), F32)
    for i in range(blocks):
        ext = ext.at[i * WIN : (i + 3) * WIN].add(dkv[i])
    total_dev = nb * ndp
    place = [(i % nb) * ndp + i // nb for i in range(total_dev)]
    up = [(place[i], place[i + 1]) for i in range(total_dev - 1)]
    down = [(place[i + 1], place[i]) for i in range(total_dev - 1)]
    everyone = ("branch",) + DP
    from_prev = lax.ppermute(ext[own + WIN :].astype(BF16), everyone, up).astype(F32)
    from_next = lax.ppermute(ext[:WIN].astype(BF16), everyone, down).astype(F32)
    dkv_own = ext[WIN : WIN + own].at[:WIN].add(from_prev).at[own - WIN :].add(from_next)
    dkv_own = dkv_own.astype(BF16)
    wl = heads_l * DH
    dq_own = dq.reshape(own, wl).astype(BF16)
    dk_own, dv_own = dkv_own[:, :wl], dkv_own[:, wl:]
    gf_l = mm(dq_own, lh3[0], 1, 1) + mm(dk_own, lh3[1], 1, 1) + mm(dv_own, lh3[2], 1, 1)
    d_lh = jnp.stack([mm(first_own, x, 0, 0) for x in (dq_own, dk_own, dv_own)], 0)

    gm_half = lax.dynamic_slice(gm_r, (core * half, 0), (half, D))
    seed_a = (gate_half * gm_half).astype(BF16)
    dctx_r = mm(seed_a, routed_merge, 1, 1).astype(BF16).reshape(half, heads_r, DH)
    d_rm = mm(ctx_r, seed_a, 0, 0)
    gate_attn = jnp.sum(gm_half * attn_r, -1, keepdims=True)
    pr = jnp.exp(sr - lse_r)
    dpr = jnp.einsum("qhe,khe->hqk", dctx_r, vr, preferred_element_type=F32)
    inner_r = jnp.sum(pr * dpr, -1, keepdims=True)
    dsr = (pr * (dpr - inner_r)).astype(BF16)
    dqr = jnp.einsum("hqk,khe->qhe", dsr, kr, preferred_element_type=F32) * SCALE
    dkr = jnp.einsum("hqk,qhe->khe", dsr, qr, preferred_element_type=F32) * SCALE
    dvr = jnp.einsum("hqk,qhe->khe", pr.astype(BF16), dctx_r, preferred_element_type=F32)
    dkvr = jnp.concatenate([dkr.reshape(-1, rw), dvr.reshape(-1, rw)], 1).astype(BF16)
    dkvr = block_sum(dkvr, nz, 4)
    triple = jnp.stack([dqr.reshape(half, rw).astype(BF16), dkvr[:, :rw], dkvr[:, rw:]], 1)
    picked = jnp.einsum("rcf,dcf->rd", triple, routed_heads, preferred_element_type=F32)
    d_rh = jnp.einsum("rd,rcf->dcf", first_half, triple, preferred_element_type=F32)
    d_logit = (at_half(gate_attn) + gate_feed) * gate * (1.0 - gate)
    router_part = jnp.sum(d_logit * first_r.astype(F32), 0)

    part3 = at_half(picked) + d_logit * router_vector[None, :] + mm(pick_own, gf_l.astype(BF16), 1, 0)
    gf_r = group_sum(part3.astype(BF16), nb, 3)
    gf_own = jnp.where(mask_own, mm(pick_own, gf_r, 0, 0), gf_l)
    td_own = (gm_own + norm_back(gf_own, xh1, r1, gain_before)).astype(BF16)
    delta_gain_before = jnp.sum(gf_own * xh1, 0)
    tokens_delta = lax.all_gather(td_own, "branch", axis=0, tiled=True).astype(F32)

    vectors = lax.psum(
        jnp.stack([delta_gain_before, delta_gain_middle, router_part]).astype(F32),
        ("branch",) + DP,
    )

    def over_branch(x, dim):
        return lax.psum_scatter(x.astype(BF16), "branch", scatter_dimension=dim, tiled=True)

    g_le = lax.psum(over_branch(jnp.stack([d_lg, d_lu], 0), 2), DP)
    g_lr = lax.psum(over_branch(d_ld, 0), DP)
    g_lh = lax.psum(over_branch(d_lh, 2), DP)
    g_lm = lax.psum(over_branch(d_lm, 0), DP)
    g_re = lax.all_gather(
        lax.psum(jnp.stack([d_rg, d_ru], 0).astype(BF16), "zz"), "core", axis=2, tiled=True
    )
    g_rr = lax.all_gather(lax.psum(d_rd.astype(BF16), "zz"), "core", axis=0, tiled=True)
    g_rh = lax.psum(d_rh.astype(BF16), DP)
    g_rm = lax.psum(d_rm.astype(BF16), DP)
    return (
        layer_output,
        tokens_delta,
        vectors[0],
        vectors[1],
        vectors[2],
        g_lh.transpose(1, 0, 2).astype(F32),
        g_lm.astype(F32),
        g_rh.astype(F32),
        g_rm.astype(F32),
        g_le.transpose(1, 0, 2).astype(F32),
        g_lr.astype(F32),
        g_re.transpose(1, 0, 2).astype(F32),
        g_rr.astype(F32),
    )


def solution(mesh):
    nb = mesh.shape["branch"]
    fine = Mesh(mesh.devices.reshape(nb, -1, 2), ("branch", "zz", "core"))
    rows = P(DP, None)
    cols = P(None, None, "branch")
    deep = P("branch", None)
    return jax.shard_map(
        per_device,
        mesh=fine,
        in_specs=(
            rows, rows, P(), P(), P(), cols, deep, cols, deep, cols, deep, cols, deep, P(DP), P(),
        ),
        out_specs=(
            rows, rows, P(), P(), P(), cols, deep, cols, deep, cols, deep, cols, deep,
        ),
        check_vma=False,
    )
```

```python
import functools

import jax
import jax.numpy as jnp
from jax import lax
from jax.experimental import pallas as pl
from jax.experimental.pallas import tpu as pltpu
from jax.sharding import Mesh
from jax.sharding import PartitionSpec as P

DH = 64
WIN = 128
EPSILON = 1e-06
NEGATIVE = -1e30
HIGHEST = lax.Precision.HIGHEST
F32 = jnp.float32
BF16 = jnp.bfloat16
SCALE = DH ** (-0.5)
DP = ("zz", "core")


def mm(a, b, ca, cb):
    return lax.dot_general(a, b, (((ca,), (cb,)), ((), ())), preferred_element_type=F32)


def norm_parts(values):
    r = lax.rsqrt(jnp.mean(values * values, axis=-1, keepdims=True) + EPSILON)
    return r, values * r


def norm_back(dn, xh, r, gain):
    g = dn * gain
    return r * (g - xh * jnp.mean(g * xh, axis=-1, keepdims=True))


def gelu_parts(u):
    c = 0.7978845608028654
    t = jnp.tanh(c * (u + 0.044715 * u * u * u))
    g = 0.5 * u * (1.0 + t)
    dg = 0.5 * (1.0 + t) + 0.5 * u * (1.0 - t * t) * c * (1.0 + 3 * 0.044715 * u * u)
    return g, dg


def feed(n, seed, w_gate, w_up, w_down):
    u = mm(n, w_gate, 1, 0)
    v = mm(n, w_up, 1, 0)
    g, dg = gelu_parts(u)
    hidden = (g * v).astype(BF16)
    out = mm(hidden, w_down, 1, 0)
    dh = mm(seed, w_down, 1, 1)
    du = (dh * v * dg).astype(BF16)
    dv = (dh * g).astype(BF16)
    dn = mm(du, w_gate, 1, 1) + mm(dv, w_up, 1, 1)
    dwg = mm(n, du, 0, 0)
    dwu = mm(n, dv, 0, 0)
    dwd = mm(hidden, seed, 0, 0)
    return out, dn, dwg, dwu, dwd


MESH = pl.DeviceIdType.MESH


def remote(src, dst, send, recv, device):
    return pltpu.make_async_remote_copy(
        src_ref=src, dst_ref=dst, send_sem=send, recv_sem=recv, device_id=device, device_id_type=MESH
    )


def greet(devices):
    barrier = pltpu.get_barrier_semaphore()
    for device in devices:
        pl.semaphore_signal(barrier, inc=1, device_id=device, device_id_type=MESH)
    pl.semaphore_wait(barrier, len(devices))


def here():
    return lax.axis_index("branch"), lax.axis_index("zz"), lax.axis_index("core")


def others(me, count):
    return [lax.rem(me + k, count) for k in range(1, count)]


def band(start, size):
    return pl.ds(pl.multiple_of(start, size), size)


def finish(copies):
    for copy in copies:
        if copy.is_remote:
            copy.wait_send()
        else:
            copy.wait()


class Pool:
    def __init__(self):
        self.names = []
        self.shapes = []

    def add(self, name, shape):
        self.names.append(name)
        self.shapes.append(shape)

    def vmem(self, name, shape, dtype=BF16):
        self.add(name, pltpu.VMEM(shape, dtype))

    def dma(self, name, *shape):
        self.add(name, pltpu.SemaphoreType.DMA(shape))

    def bind(self, refs):
        return dict(zip(self.names, refs, strict=True))


def group_sum_scratch(pool, nb, rows, width):
    for name in ("gs_sib", "gs_part", "gs_came"):
        pool.vmem(name, (nb, rows // 2 // nb, width))
    for name in ("sib", "rs", "ag", "fw"):
        pool.dma(f"gs_{name}_s", nb)
        pool.dma(f"gs_{name}_r", nb)


def group_sum_steps(nb, x, o, m, meanwhile=()):
    b, z, c = here()
    half = x.shape[0] // 2
    ch = half // nb
    twin = (b, z, 1 - c)
    peers = others(b, nb)
    sib, part, came = m["gs_sib"], m["gs_part"], m["gs_came"]
    work = list(meanwhile)

    def aside():
        if work:
            work.pop(0)()

    def rows(core, j):
        return band(core * half + j * ch, ch)

    order = peers + [b]
    to_twin = [
        remote(x.at[rows(1 - c, j)], sib.at[j], m["gs_sib_s"].at[j], m["gs_sib_r"].at[j], twin)
        for j in order
    ]
    for copy in to_twin:
        copy.start()
    sends = []
    for j, copy in zip(peers, to_twin):
        copy.wait_recv()
        part[j] = (x[rows(c, j)].astype(F32) + sib[j].astype(F32)).astype(BF16)
        send = remote(part.at[j], came.at[b], m["gs_rs_s"].at[j], m["gs_rs_r"].at[b], (j, z, c))
        send.start()
        sends.append(send)
    aside()
    to_twin[-1].wait_recv()
    total = x[rows(c, b)].astype(F32) + sib[b].astype(F32)
    for j in peers:
        remote(part.at[j], came.at[j], m["gs_rs_s"].at[j], m["gs_rs_r"].at[j], (j, z, c)).wait_recv()
        total = total + came[j].astype(F32)
    mine = o.at[rows(c, b)]
    mine[...] = total.astype(BF16)
    for j in peers:
        send = remote(mine, mine, m["gs_ag_s"].at[j], m["gs_ag_r"].at[b], (j, z, c))
        send.start()
        sends.append(send)
    send = remote(mine, mine, m["gs_fw_s"].at[b], m["gs_fw_r"].at[b], twin)
    send.start()
    sends.append(send)
    aside()
    for j in peers:
        piece = o.at[rows(c, j)]
        remote(piece, piece, m["gs_ag_s"].at[j], m["gs_ag_r"].at[j], (j, z, c)).wait_recv()
        send = remote(piece, piece, m["gs_fw_s"].at[j], m["gs_fw_r"].at[j], twin)
        send.start()
        sends.append(send)
    while work:
        aside()
    for j in order:
        piece = o.at[rows(1 - c, j)]
        remote(piece, piece, m["gs_fw_s"].at[j], m["gs_fw_r"].at[j], twin).wait_recv()
    finish(to_twin + sends)


def sum_kernel(nb, pool, x, o, *scratch):
    b, z, c = here()
    greet([(b, z, 1 - c)] + [(j, z, c) for j in others(b, nb)])
    group_sum_steps(nb, x, o, pool.bind(scratch))


def group_sum(x, nb, cid):
    rows, width = x.shape
    pool = Pool()
    group_sum_scratch(pool, nb, rows, width)
    return pl.pallas_call(
        functools.partial(sum_kernel, nb, pool),
        out_shape=jax.ShapeDtypeStruct(x.shape, BF16),
        in_specs=[VM],
        out_specs=VM,
        scratch_shapes=pool.shapes,
        compiler_params=pltpu.CompilerParams(
            collective_id=cid, has_side_effects=True, vmem_limit_bytes=40 << 20
        ),
    )(x)


VM = pl.BlockSpec(memory_space=pltpu.VMEM)
HB = pl.BlockSpec(memory_space=pl.ANY)


def normed(x, gain):
    x = x.astype(F32)
    r = lax.rsqrt(jnp.mean(x * x, axis=-1, keepdims=True) + EPSILON)
    return (x * r * gain).astype(BF16)


def head_lanes(shape, h, dim):
    place = lax.broadcasted_iota(jnp.int32, shape, dim)
    return (place >= h * DH) & (place < (h + 1) * DH)


def only_head(x, h):
    return jnp.where(head_lanes(x.shape, h, 1), x, jnp.zeros_like(x))


def near_keys(shape, key_dim, first, total):
    key = lax.broadcasted_iota(jnp.int32, shape, key_dim)
    query = lax.broadcasted_iota(jnp.int32, shape, 1 - key_dim)
    gap = key - query
    return (gap >= 0) & (gap <= 2 * WIN) & (key + first >= 0) & (key + first < total)


def hot_rows(ids, count):
    spot = lax.broadcasted_iota(jnp.int32, (ids.shape[0], count), 1)
    return jnp.where(ids == spot, 1.0, 0.0).astype(BF16)


FRONT_OUT = (
    "tok_r", "cot_r", "first_r", "gate", "qr", "kv", "lh", "lm", "le", "lr", "first_w",
    "q", "k", "v", "ctx_l", "attn_l", "ctx_r", "attn_r", "mixed",
)


def front_kernel(nb, nz, pool, *refs):
    tokens, cotangent, ids, gain, router, rheads, rmerge, s_lh, s_lm, s_le, s_lr = refs[:11]
    out = dict(zip(FRONT_OUT, refs[11 : 11 + len(FRONT_OUT)]))
    m = pool.bind(refs[11 + len(FRONT_OUT) :])
    b, z, c = here()
    twin = (b, z, 1 - c)
    bpeers, zpeers = others(b, nb), others(z, nz)
    rows, D = tokens.shape
    own = rows // nb
    cap = ids.shape[0]
    half = cap // 2
    rw = rmerge.shape[0]
    after = (b, lax.rem(z + c, nz), 1 - c)
    before = (b, lax.rem(z + nz - 1 + c, nz), 1 - c)
    far = (b, lax.rem(z + nz - 1 + 2 * c, nz), 1 - c)
    greet([twin, far] + [(j, z, c) for j in bpeers] + [(b, j, c) for j in zpeers])
    sends = []

    def go(copy):
        copy.start()
        sends.append(copy)

    pairs = [(s_lh, out["lh"]), (s_lm, out["lm"]), (s_le, out["le"]), (s_lr, out["lr"])]

    def place(i, j):
        src, dst = pairs[i]
        if i in (0, 2):
            return dst.at[:, :, band(j * src.shape[2], src.shape[2])]
        return dst.at[band(j * src.shape[0], src.shape[0])]

    def cut(i, ref, core):
        if i in (0, 2):
            size = ref.shape[1] // 2
            return ref.at[:, band(core * size, size)]
        size = ref.shape[0] // 2
        return ref.at[band(core * size, size)]

    for i in range(4):
        for j in bpeers:
            go(remote(cut(i, pairs[i][0], c), cut(i, place(i, b), c), m["w_s"].at[i, j], m["w_r"].at[i, b], (j, z, c)))
    for i in range(4):
        go(pltpu.make_async_copy(pairs[i][0], place(i, b), m["own_s"].at[i]))
    halo = m["halo"]
    go(remote(tokens.at[pl.ds(rows - WIN, WIN)], halo.at[0], m["halo_s"].at[0], m["halo_r"].at[0], after))
    go(remote(tokens.at[pl.ds(0, WIN)], halo.at[1], m["halo_s"].at[1], m["halo_r"].at[1], before))

    picks, sib = m["picks"], m["sib"]
    step = cap // 4
    for k in range(4):
        at = pl.ds(k * step, step)
        hot = hot_rows(ids[at], rows)
        picks[at, :D] = mm(hot, tokens[...], 1, 0).astype(BF16)
        picks[at, D:] = mm(hot, cotangent[...], 1, 0).astype(BF16)
        go(remote(picks.at[at], sib.at[at], m["pick_s"].at[k], m["pick_r"].at[k], twin))
    for k in range(4):
        at = pl.ds(k * step, step)
        remote(picks.at[at], sib.at[at], m["pick_s"].at[k], m["pick_r"].at[k], twin).wait_recv()
        tok = picks[at, :D].astype(F32) + sib[at, :D].astype(F32)
        out["tok_r"][at] = tok.astype(BF16)
        out["cot_r"][at] = (picks[at, D:].astype(F32) + sib[at, D:].astype(F32)).astype(BF16)
        first = normed(tok, gain[...])
        out["first_r"][at] = first
        logit = jnp.sum(first.astype(F32) * router[...], axis=-1, keepdims=True)
        out["gate"][at] = 1.0 / (1.0 + jnp.exp(-logit))

    own_rows = out["first_r"][band(c * half, half)]
    out["qr"][...] = mm(own_rows, rheads[0], 1, 1).astype(BF16)
    kv = out["kv"]
    mine = kv.at[band((2 * z + c) * half, half)]
    mine[:, :rw] = mm(own_rows, rheads[1], 1, 1).astype(BF16)
    mine[:, rw:] = mm(own_rows, rheads[2], 1, 1).astype(BF16)
    for j in zpeers:
        go(remote(mine, mine, m["kv_s"].at[j], m["kv_r"].at[z], (b, j, c)))
    go(remote(mine, mine, m["kf_s"].at[z], m["kf_r"].at[z], twin))

    first_w = out["first_w"]
    first_w[pl.ds(WIN, own)] = normed(tokens[band(b * own, own)], gain[...])
    for i in range(2):
        remote(halo.at[i], halo.at[i], m["halo_s"].at[i], m["halo_r"].at[i], twin).wait_recv()
    lead = tokens[band(jnp.maximum(b * own - WIN, 0), WIN)]
    trail = tokens[band(jnp.minimum((b + 1) * own, rows - WIN), WIN)]
    first_w[pl.ds(0, WIN)] = normed(jnp.where(b > 0, lead, halo[0]), gain[...])
    first_w[pl.ds(WIN + own, WIN)] = normed(jnp.where(b < nb - 1, trail, halo[1]), gain[...])

    def pass_weights(i):
        for j in bpeers:
            dst = cut(i, place(i, j), c)
            remote(dst, dst, m["w_s"].at[i, j], m["w_r"].at[i, j], (j, z, c)).wait_recv()
            go(remote(dst, dst, m["wf_s"].at[i, j], m["wf_r"].at[i, j], twin))

    def take_weights(i):
        for j in bpeers:
            dst = cut(i, place(i, j), 1 - c)
            remote(dst, dst, m["wf_s"].at[i, j], m["wf_r"].at[i, j], twin).wait_recv()

    pass_weights(0)
    for j in zpeers:
        piece = kv.at[band((2 * j + c) * half, half)]
        remote(piece, piece, m["kv_s"].at[j], m["kv_r"].at[j], (b, j, c)).wait_recv()
        go(remote(piece, piece, m["kf_s"].at[j], m["kf_r"].at[j], twin))
    take_weights(0)
    pltpu.make_async_copy(pairs[0][0], place(0, b), m["own_s"].at[0]).wait()
    lh, q, k, v = out["lh"], out["q"], out["k"], out["v"]
    q[...] = mm(first_w[pl.ds(WIN, own)], lh[0], 1, 0).astype(BF16)
    k[...] = mm(first_w[...], lh[1], 1, 0).astype(BF16)
    v[...] = mm(first_w[...], lh[2], 1, 0).astype(BF16)
    pass_weights(1)

    blocks = own // WIN
    ctx = out["ctx_l"]
    first_key = (2 * z + c) * rows + b * own - WIN
    total = 2 * nz * rows

    def light(i, carry):
        g, n = i // blocks, lax.rem(i, blocks)
        lanes = band(g * 2 * DH, 2 * DH)
        at = band(n * WIN, WIN)
        keys = pl.ds(pl.multiple_of(n * WIN, WIN), 3 * WIN)
        q2, k2, v2 = q[at, lanes], k[keys, lanes], v[keys, lanes]
        allowed = near_keys((WIN, 3 * WIN), 1, first_key + n * WIN, total)
        parts = []
        for h in range(2):
            s = jnp.where(allowed, mm(only_head(q2, h), k2, 1, 1) * SCALE, NEGATIVE)
            w = jnp.exp(s - jnp.max(s, axis=-1, keepdims=True))
            p = (w / jnp.sum(w, axis=-1, keepdims=True)).astype(BF16)
            parts.append(mm(p, v2, 1, 0))
        ctx[at, lanes] = jnp.where(head_lanes((WIN, 2 * DH), 0, 1), parts[0], parts[1]).astype(BF16)
        return carry

    lax.fori_loop(0, blocks * (q.shape[1] // (2 * DH)), light, 0)
    take_weights(1)
    pltpu.make_async_copy(pairs[1][0], place(1, b), m["own_s"].at[1]).wait()
    attn_l = out["attn_l"]
    attn_l[...] = mm(ctx[...], out["lm"][...], 1, 0)

    for j in zpeers + [z]:
        piece = kv.at[band((2 * j + 1 - c) * half, half)]
        remote(piece, piece, m["kf_s"].at[j], m["kf_r"].at[j], twin).wait_recv()
    keys, values, qr, ctx_r = m["keys"], m["values"], out["qr"], out["ctx_r"]
    keys[...] = kv[:, :rw]
    values[...] = kv[:, rw:]
    some = 64

    def heavy(i, carry):
        at = band(i * some, some)
        got = jnp.zeros((some, rw), F32)
        for h in range(rw // DH):
            s = mm(only_head(qr[at], h), keys[...], 1, 1) * SCALE
            w = jnp.exp(s - jnp.max(s, axis=-1, keepdims=True))
            p = (w / jnp.sum(w, axis=-1, keepdims=True)).astype(BF16)
            got = jnp.where(head_lanes((some, rw), h, 1), mm(p, values[...], 1, 0), got)
        ctx_r[at] = got.astype(BF16)
        return carry

    lax.fori_loop(0, half // some, heavy, 0)
    attn_r = out["attn_r"]
    attn_r[...] = mm(ctx_r[...], rmerge[...], 1, 0)

    part = m["part"]
    mine_at, other_at = band(c * half, half), band((1 - c) * half, half)
    low = attn_l[...].astype(BF16)
    part[other_at] = mm(hot_rows(ids[other_at] - b * own, own), low, 1, 0).astype(BF16)
    part[mine_at] = (
        mm(hot_rows(ids[mine_at] - b * own, own), low, 1, 0) + out["gate"][mine_at] * attn_r[...]
    ).astype(BF16)
    group_sum_steps(nb, part, out["mixed"], m, [lambda: pass_weights(2), lambda: pass_weights(3)])
    take_weights(2)
    take_weights(3)
    finish([copy for copy in sends if copy.is_remote])
    for i in (2, 3):
        pltpu.make_async_copy(pairs[i][0], place(i, b), m["own_s"].at[i]).wait()


def front(nb, nz, tokens, cotangent, ids, gain, router, rheads, rmerge, s_lh, s_lm, s_le, s_lr):
    rows, D = tokens.shape
    own = rows // nb
    cap = ids.shape[0]
    half = cap // 2
    rw = rmerge.shape[0]
    wl = nb * s_lm.shape[0]
    shape = lambda *dims: jax.ShapeDtypeStruct(dims, BF16)
    shape32 = lambda *dims: jax.ShapeDtypeStruct(dims, F32)
    outs = dict(
        tok_r=shape(cap, D), cot_r=shape(cap, D), first_r=shape(cap, D), gate=shape32(cap, 1),
        qr=shape(half, rw), kv=shape(2 * nz * half, 2 * rw),
        lh=shape(3, D, wl), lm=shape(wl, D),
        le=shape(2, D, nb * s_le.shape[2]), lr=shape(nb * s_lr.shape[0], D),
        first_w=shape(own + 2 * WIN, D), q=shape(own, wl), k=shape(own + 2 * WIN, wl),
        v=shape(own + 2 * WIN, wl), ctx_l=shape(own, wl), attn_l=shape32(own, D),
        ctx_r=shape(half, rw), attn_r=shape32(half, D), mixed=shape(cap, D),
    )
    pool = Pool()
    pool.vmem("picks", (cap, 2 * D))
    pool.vmem("sib", (cap, 2 * D))
    pool.vmem("halo", (2, WIN, D))
    pool.vmem("keys", (2 * nz * half, rw))
    pool.vmem("values", (2 * nz * half, rw))
    pool.vmem("part", (cap, D))
    group_sum_scratch(pool, nb, cap, D)
    pool.dma("own_s", 4)
    pool.dma("halo_s", 2)
    pool.dma("halo_r", 2)
    pool.dma("pick_s", 4)
    pool.dma("pick_r", 4)
    for name in ("w", "wf"):
        pool.dma(f"{name}_s", 4, nb)
        pool.dma(f"{name}_r", 4, nb)
    for name in ("kv", "kf"):
        pool.dma(f"{name}_s", nz)
        pool.dma(f"{name}_r", nz)
    got = pl.pallas_call(
        functools.partial(front_kernel, nb, nz, pool),
        out_shape=tuple(outs[name] for name in FRONT_OUT),
        in_specs=[VM] * 7 + [HB] * 4,
        out_specs=tuple(HB if name in ("le", "lr") else VM for name in FRONT_OUT),
        scratch_shapes=pool.shapes,
        compiler_params=pltpu.CompilerParams(
            collective_id=0, has_side_effects=True, vmem_limit_bytes=56 << 20
        ),
    )(tokens, cotangent, ids, gain, router, rheads, rmerge, s_lh, s_lm, s_le, s_lr)
    return dict(zip(FRONT_OUT, got))


BACK_OUT = ("gf_r", "gf_l", "d_lh", "d_lm", "d_rh", "d_rm", "router")
BACK_IN = (
    "gm_own", "gm_r", "gate", "gate_feed", "ids", "q", "k", "v", "lm", "lh", "first_w", "ctx_l",
    "qr", "kv", "rmerge", "rheads", "first_r", "ctx_r", "attn_r", "router_vector",
)


def back_names(inner):
    return BACK_IN if inner else BACK_IN + ("trio",)


def heavy_back(i, m, seed, x):
    kv, qr = i["kv"], i["qr"]
    half, rw = qr.shape
    keys, values, keys_t, dk, dv, dq_t, do = (
        m[n] for n in ("keys", "values", "keys_t", "dk", "dv", "dq_t", "do")
    )
    keys[...] = kv[:, :rw]
    values[...] = kv[:, rw:]
    keys_t[...] = keys[...].T
    do[...] = mm(seed, i["rmerge"][...], 1, 1).astype(BF16)
    dk[...] = jnp.zeros_like(dk)
    dv[...] = jnp.zeros_like(dv)
    dq_t[...] = jnp.zeros_like(dq_t)
    some = 128

    def heavy(n, carry):
        at = band(n * some, some)
        for h in range(rw // DH):
            qh, doh = only_head(qr[at], h), only_head(do[at], h)
            s = mm(keys[...], qh, 1, 1) * SCALE
            w = jnp.exp(s - jnp.max(s, axis=0, keepdims=True))
            p = w * (1.0 / jnp.sum(w, axis=0, keepdims=True))
            dp = mm(values[...], doh, 1, 1)
            ds = (p * (dp - jnp.sum(p * dp, axis=0, keepdims=True))).astype(BF16)
            dk[...] += mm(ds, qh, 1, 0)
            dv[...] += mm(p.astype(BF16), doh, 1, 0)
            got = mm(keys_t[...], ds, 1, 0)
            dq_t[:, at] += jnp.where(head_lanes(got.shape, h, 0), got, 0.0)
        return carry

    lax.fori_loop(0, half // some, heavy, 0)
    x[:, :rw] = (dk[...] * SCALE).astype(BF16)
    x[:, rw:] = dv[...].astype(BF16)


def heavy_back_plain(i):
    half, rw = i["qr"].shape
    split = lambda y: y.reshape(y.shape[0], -1, DH)
    at = lax.axis_index("core") * half
    seed = (i["gate"] * i["gm_r"]).astype(BF16)
    seed = lax.dynamic_slice(seed, (at, 0), (half, seed.shape[1]))
    do = split(mm(seed, i["rmerge"], 1, 1).astype(BF16))
    q, k, v = split(i["qr"]), split(i["kv"][:, :rw]), split(i["kv"][:, rw:])
    p = jax.nn.softmax(jnp.einsum("qhe,khe->hqk", q, k, preferred_element_type=F32) * SCALE, axis=-1)
    dp = jnp.einsum("qhe,khe->hqk", do, v, preferred_element_type=F32)
    ds = (p * (dp - jnp.sum(p * dp, -1, keepdims=True))).astype(BF16)
    dq = jnp.einsum("hqk,khe->qhe", ds, k, preferred_element_type=F32) * SCALE
    dk = jnp.einsum("hqk,qhe->khe", ds, q, preferred_element_type=F32) * SCALE
    dv = jnp.einsum("hqk,qhe->khe", p.astype(BF16), do, preferred_element_type=F32)
    both = jnp.concatenate([dk.reshape(-1, rw), dv.reshape(-1, rw)], 1).astype(BF16)
    both = lax.psum_scatter(both, DP, scatter_dimension=0, tiled=True)
    return jnp.stack([dq.reshape(half, rw).astype(BF16), both[:, :rw], both[:, rw:]], 0)


def back_kernel(nb, nz, pool, inner, *refs):
    names = back_names(inner)
    i = dict(zip(names, refs[: len(names)]))
    out = dict(zip(BACK_OUT, refs[len(names) : len(names) + len(BACK_OUT)]))
    m = pool.bind(refs[len(names) + len(BACK_OUT) :])
    b, z, c = here()
    twin = (b, z, 1 - c)
    bpeers, zpeers = others(b, nb), others(z, nz)
    own, D = i["gm_own"].shape
    rows = own * nb
    cap = i["ids"].shape[0]
    half = cap // 2
    rw = i["rmerge"].shape[0]
    wl = i["q"].shape[1]
    last, first = b == nb - 1, b == 0
    after = (
        jnp.where(last, 0, b + 1), jnp.where(last, lax.rem(z + c, nz), z), jnp.where(last, 1 - c, c),
    )
    before = (
        jnp.where(first, nb - 1, b - 1),
        jnp.where(first, lax.rem(z + nz - 1 + c, nz), z),
        jnp.where(first, 1 - c, c),
    )
    greet([twin, after, before] + [(j, z, c) for j in bpeers] + [(b, j, c) for j in zpeers])
    mine_at, other_at = band(c * half, half), band((1 - c) * half, half)
    sends = []

    def go(copy):
        copy.start()
        sends.append(copy)

    gm_half = i["gm_r"][mine_at]
    gate_half = i["gate"][mine_at]
    seed = (gate_half * gm_half).astype(BF16)
    out["d_rm"][...] = mm(i["ctx_r"][...], seed, 0, 0).astype(BF16)
    trio = m["trio"] if inner else i["trio"]

    def spot(core, j):
        return band((2 * j + core) * half, half)

    def to_twin(j):
        return remote(x.at[spot(1 - c, j)], sib.at[j], m["bs_sib_s"].at[j], m["bs_sib_r"].at[j], twin)

    if inner:
        x, sib, part, came = m["dkv"], m["bs_sib"], m["bs_part"], m["bs_came"]
        heavy_back(i, m, seed, x)
        for j in zpeers + [z]:
            go(to_twin(j))

    low, do_l = m["low"], m["do_l"]
    low[...] = i["gm_own"][...].astype(BF16)
    do_l[...] = mm(low[...], i["lm"][...], 1, 1).astype(BF16)
    for j in zpeers if inner else []:
        to_twin(j).wait_recv()
        part[j] = (x[spot(c, j)].astype(F32) + sib[j].astype(F32)).astype(BF16)
        go(remote(part.at[j], came.at[z], m["bs_rs_s"].at[j], m["bs_rs_r"].at[z], (b, j, c)))

    q, k, v = i["q"], i["k"], i["v"]
    lk_t, dkl, dvl, dql = m["lk_t"], m["dkl"], m["dvl"], m["dql"]
    lk_t[...] = k[...].T
    dkl[...] = jnp.zeros_like(dkl)
    dvl[...] = jnp.zeros_like(dvl)
    blocks = own // WIN
    first_key = (2 * z + c) * rows + b * own - WIN
    total = 2 * nz * rows

    def light(n_, carry):
        g, n = n_ // blocks, lax.rem(n_, blocks)
        lanes = band(g * 2 * DH, 2 * DH)
        at = band(n * WIN, WIN)
        near = pl.ds(pl.multiple_of(n * WIN, WIN), 3 * WIN)
        q2, do2, k2, v2, kt2 = q[at, lanes], do_l[at, lanes], k[near, lanes], v[near, lanes], lk_t[lanes, near]
        allowed = near_keys((3 * WIN, WIN), 0, first_key + n * WIN, total)
        got_k = got_v = None
        got_q = []
        for h in range(2):
            qh, doh = only_head(q2, h), only_head(do2, h)
            s = jnp.where(allowed, mm(k2, qh, 1, 1) * SCALE, NEGATIVE)
            w = jnp.exp(s - jnp.max(s, axis=0, keepdims=True))
            p = w * (1.0 / jnp.sum(w, axis=0, keepdims=True))
            dp = mm(v2, doh, 1, 1)
            ds = (p * (dp - jnp.sum(p * dp, axis=0, keepdims=True))).astype(BF16)
            one_k, one_v = mm(ds, qh, 1, 0), mm(p.astype(BF16), doh, 1, 0)
            got_k = one_k if got_k is None else got_k + one_k
            got_v = one_v if got_v is None else got_v + one_v
            got_q.append(mm(kt2, ds, 1, 0))
        dkl[near, lanes] += got_k
        dvl[near, lanes] += got_v
        both = jnp.where(head_lanes((2 * DH, WIN), 0, 0), got_q[0], got_q[1])
        dql[at, lanes] = (both.T * SCALE).astype(BF16)
        return carry

    lax.fori_loop(0, blocks * (wl // (2 * DH)), light, 0)
    rim, came_rim = m["rim"], m["came_rim"]
    for n, start in ((0, WIN + own), (1, 0)):
        rim[n, :, :wl] = (dkl[pl.ds(start, WIN)] * SCALE).astype(BF16)
        rim[n, :, wl:] = dvl[pl.ds(start, WIN)].astype(BF16)
    go(remote(rim.at[0], came_rim.at[0], m["rim_s"].at[0], m["rim_r"].at[0], after))
    go(remote(rim.at[1], came_rim.at[1], m["rim_s"].at[1], m["rim_r"].at[1], before))

    if inner:
        to_twin(z).wait_recv()
        mine = x[spot(c, z)].astype(F32) + sib[z].astype(F32)
        for j in zpeers:
            remote(part.at[j], came.at[j], m["bs_rs_s"].at[j], m["bs_rs_r"].at[j], (b, j, c)).wait_recv()
            mine = mine + came[j].astype(F32)
        trio[0] = (m["dq_t"][...].T * SCALE).astype(BF16)
        trio[1] = mine[:, :rw].astype(BF16)
        trio[2] = mine[:, rw:].astype(BF16)
    rheads = i["rheads"]
    picked = mm(trio[0], rheads[0], 1, 0) + mm(trio[1], rheads[1], 1, 0) + mm(trio[2], rheads[2], 1, 0)

    for n, device in ((0, before), (1, after)):
        remote(rim.at[n], came_rim.at[n], m["rim_s"].at[n], m["rim_r"].at[n], device).wait_recv()
    dkl[pl.ds(WIN, WIN)] += came_rim[0, :, :wl].astype(F32) * (1.0 / SCALE)
    dvl[pl.ds(WIN, WIN)] += came_rim[0, :, wl:].astype(F32)
    dkl[pl.ds(own, WIN)] += came_rim[1, :, :wl].astype(F32) * (1.0 / SCALE)
    dvl[pl.ds(own, WIN)] += came_rim[1, :, wl:].astype(F32)
    dk_own, dv_own = m["dk_own"], m["dv_own"]
    dk_own[...] = (dkl[pl.ds(WIN, own)] * SCALE).astype(BF16)
    dv_own[...] = dvl[pl.ds(WIN, own)].astype(BF16)
    lh = i["lh"]
    gf_l = out["gf_l"]
    gf_l[...] = mm(dql[...], lh[0], 1, 1) + mm(dk_own[...], lh[1], 1, 1) + mm(dv_own[...], lh[2], 1, 1)

    gate, first_r = i["gate"], i["first_r"]
    gate_attn = jnp.sum(gm_half * i["attn_r"][...], axis=-1, keepdims=True)
    total_part = m["part"]
    low_gf = gf_l[...].astype(BF16)
    router_sum = None
    for at, extra, more in ((other_at, None, None), (mine_at, gate_attn, picked)):
        g = gate[at]
        d_gate = i["gate_feed"][at] if extra is None else i["gate_feed"][at] + extra
        d_logit = d_gate * g * (1.0 - g)
        one = jnp.sum(d_logit * first_r[at].astype(F32), axis=0, keepdims=True)
        router_sum = one if router_sum is None else router_sum + one
        sum_ = mm(hot_rows(i["ids"][at] - b * own, own), low_gf, 1, 0) + d_logit * i["router_vector"][...]
        if more is not None:
            sum_ = sum_ + more
        total_part[at] = sum_.astype(BF16)
    out["router"][...] = router_sum

    def weights_light():
        first_t = m["first_t"]
        first_t[...] = i["first_w"][pl.ds(WIN, own)].T
        out["d_lh"][0] = mm(first_t[...], dql[...], 1, 0).astype(BF16)
        out["d_lh"][1] = mm(first_t[...], dk_own[...], 1, 0).astype(BF16)

    def weights_rest():
        out["d_lh"][2] = mm(m["first_t"][...], dv_own[...], 1, 0).astype(BF16)
        out["d_lm"][...] = mm(i["ctx_l"][...], low[...], 0, 0).astype(BF16)
        first_half = first_r[mine_at]
        for n in range(3):
            out["d_rh"][n] = mm(trio[n], first_half, 0, 0).astype(BF16)

    group_sum_steps(nb, total_part, out["gf_r"], m, [weights_light, weights_rest])
    finish(sends)


def back(nb, nz, given):
    own, D = given["gm_own"].shape
    cap = given["ids"].shape[0]
    half = cap // 2
    rw = given["rmerge"].shape[0]
    wl = given["q"].shape[1]
    deep = 2 * nz * half
    shape = lambda *dims: jax.ShapeDtypeStruct(dims, BF16)
    outs = dict(
        gf_r=shape(cap, D), gf_l=jax.ShapeDtypeStruct((own, D), F32), d_lh=shape(3, D, wl),
        d_lm=shape(wl, D), d_rh=shape(3, rw, D), d_rm=shape(rw, D),
        router=jax.ShapeDtypeStruct((1, D), F32),
    )
    pool = Pool()
    inner = deep <= 4096
    if inner:
        pool.vmem("keys", (deep, rw))
        pool.vmem("values", (deep, rw))
        pool.vmem("keys_t", (rw, deep))
        pool.vmem("dk", (deep, rw), F32)
        pool.vmem("dv", (deep, rw), F32)
        pool.vmem("dq_t", (rw, half), F32)
        pool.vmem("do", (half, rw))
        pool.vmem("trio", (3, half, rw))
        pool.vmem("dkv", (deep, 2 * rw))
        for name in ("bs_sib", "bs_part", "bs_came"):
            pool.vmem(name, (nz, half, 2 * rw))
    pool.vmem("low", (own, D))
    pool.vmem("do_l", (own, wl))
    pool.vmem("lk_t", (wl, own + 2 * WIN))
    pool.vmem("dkl", (own + 2 * WIN, wl), F32)
    pool.vmem("dvl", (own + 2 * WIN, wl), F32)
    pool.vmem("dql", (own, wl))
    pool.vmem("dk_own", (own, wl))
    pool.vmem("dv_own", (own, wl))
    pool.vmem("rim", (2, WIN, 2 * wl))
    pool.vmem("came_rim", (2, WIN, 2 * wl))
    pool.vmem("first_t", (D, own))
    pool.vmem("part", (cap, D))
    group_sum_scratch(pool, nb, cap, D)
    for name in ("bs_sib", "bs_rs") if inner else ():
        pool.dma(f"{name}_s", nz)
        pool.dma(f"{name}_r", nz)
    if not inner:
        given = dict(given, trio=heavy_back_plain(given))
    pool.dma("rim_s", 2)
    pool.dma("rim_r", 2)
    got = pl.pallas_call(
        functools.partial(back_kernel, nb, nz, pool, inner),
        out_shape=tuple(outs[name] for name in BACK_OUT),
        in_specs=[VM] * len(back_names(inner)),
        out_specs=(VM,) * len(BACK_OUT),
        scratch_shapes=pool.shapes,
        compiler_params=pltpu.CompilerParams(
            collective_id=3, has_side_effects=True, vmem_limit_bytes=60 << 20
        ),
    )(*(given[name] for name in back_names(inner)))
    return dict(zip(BACK_OUT, got))


def per_device(
    tokens,
    cotangent,
    gain_before,
    gain_middle,
    router_vector,
    local_heads,
    local_merge,
    routed_heads,
    routed_merge,
    local_expand,
    local_reduce,
    routed_expand,
    routed_reduce,
    routed_slots,
    routed_counts,
):
    nb = lax.axis_size("branch")
    nz = lax.axis_size("zz")
    b = lax.axis_index("branch")
    z = lax.axis_index("zz")
    core = lax.axis_index("core")
    d = 2 * z + core
    rows, D = tokens.shape
    own = rows // nb
    cap = routed_slots.shape[0]
    half = cap // 2
    fh = routed_expand.shape[2] // 2

    n_own = routed_counts[d]
    offset = jnp.where(core == 0, 0, cap - n_own)
    ranks = jnp.arange(cap, dtype=jnp.int32)
    live = (ranks >= offset) & (ranks < offset + n_own)
    twice = jnp.concatenate([routed_slots, routed_slots])
    rolled = lax.dynamic_slice(twice, (jnp.mod(cap - offset, cap),), (cap,))
    ids = jnp.where(live, rolled, -1)[:, None]
    pick_own = (ids - b * own == jnp.arange(own, dtype=jnp.int32)[None, :]).astype(BF16)
    mask_own = (jnp.sum(pick_own.astype(F32), 0) > 0.5)[:, None]

    rheads = routed_heads.transpose(1, 2, 0)
    f = front(
        nb, nz, tokens, cotangent, ids, gain_before[None], router_vector[None], rheads, routed_merge,
        local_heads.transpose(1, 0, 2), local_merge, local_expand.transpose(1, 0, 2), local_reduce,
    )
    gate, mixed_r, local_attn = f["gate"], f["mixed"], f["attn_l"]
    tok_r, cot_r = f["tok_r"].astype(F32), f["cot_r"].astype(F32)
    tok_own = lax.dynamic_slice(tokens, (b * own, 0), (own, D)).astype(F32)
    cot_own = lax.dynamic_slice(cotangent, (b * own, 0), (own, D))
    r1, xh1 = norm_parts(tok_own)

    mixed_own = jnp.where(mask_own, mm(pick_own, mixed_r, 0, 0), local_attn)
    middle_own = tok_own + mixed_own
    middle_r = tok_r + mixed_r.astype(F32)
    r2, xh2 = norm_parts(middle_own)
    second_own = (xh2 * gain_middle).astype(BF16)
    r2r, xh2r = norm_parts(middle_r)
    second_r = (xh2r * gain_middle).astype(BF16)

    ff_l, dn_l, d_lg, d_lu, d_ld = feed(second_own, cot_own, f["le"][0], f["le"][1], f["lr"])
    re_half = lax.dynamic_slice(routed_expand, (0, 0, core * fh), (D, 2, fh))
    rr_half = lax.dynamic_slice(routed_reduce, (core * fh, 0), (fh, D))
    seed_r = (gate * cot_r).astype(BF16)
    ff_r, dn_r, d_rg, d_ru, d_rd = feed(second_r, seed_r, re_half[:, 0], re_half[:, 1], rr_half)
    gate_feed = jnp.sum(cot_r * ff_r, -1, keepdims=True)

    both = jnp.concatenate(
        [ff_r.astype(BF16), (dn_r + mm(pick_own, dn_l.astype(BF16), 1, 0)).astype(BF16)], 1
    )
    both = group_sum(both, nb, 2)
    ffr_sum, dn2_r = both[:, :D].astype(F32), both[:, D:]
    layer_own = (
        middle_own + ff_l + mm(pick_own, (gate * ffr_sum).astype(BF16), 0, 0)
    ).astype(BF16)
    layer_output = lax.all_gather(layer_own, "branch", axis=0, tiled=True).astype(F32)

    dn2_own = jnp.where(mask_own, mm(pick_own, dn2_r, 0, 0), dn_l)
    gm_own = cot_own.astype(F32) + norm_back(dn2_own, xh2, r2, gain_middle)
    gm_r = cot_r + norm_back(dn2_r.astype(F32), xh2r, r2r, gain_middle)
    delta_gain_middle = jnp.sum(dn2_own * xh2, 0)

    k = back(
        nb, nz,
        dict(
            f, gm_own=gm_own, gm_r=gm_r, gate_feed=gate_feed, ids=ids, rmerge=routed_merge,
            rheads=rheads, router_vector=router_vector[None],
        ),
    )
    gf_own = jnp.where(mask_own, mm(pick_own, k["gf_r"], 0, 0), k["gf_l"])
    td_own = (gm_own + norm_back(gf_own, xh1, r1, gain_before)).astype(BF16)
    delta_gain_before = jnp.sum(gf_own * xh1, 0)
    tokens_delta = lax.all_gather(td_own, "branch", axis=0, tiled=True).astype(F32)

    vectors = lax.psum(
        jnp.stack([delta_gain_before, delta_gain_middle, k["router"][0]]).astype(F32),
        ("branch",) + DP,
    )

    def over_branch(x, dim):
        return lax.psum_scatter(x.astype(BF16), "branch", scatter_dimension=dim, tiled=True)

    g_le = lax.psum(over_branch(jnp.stack([d_lg, d_lu], 0), 2), DP)
    g_lr = lax.psum(over_branch(d_ld, 0), DP)
    g_lh = lax.psum(over_branch(k["d_lh"], 2), DP)
    g_lm = lax.psum(over_branch(k["d_lm"], 0), DP)
    g_re = lax.all_gather(
        lax.psum(jnp.stack([d_rg, d_ru], 0).astype(BF16), "zz"), "core", axis=2, tiled=True
    )
    g_rr = lax.all_gather(lax.psum(d_rd.astype(BF16), "zz"), "core", axis=0, tiled=True)
    g_rh = lax.psum(k["d_rh"], DP)
    g_rm = lax.psum(k["d_rm"], DP)
    return (
        layer_output,
        tokens_delta,
        vectors[0],
        vectors[1],
        vectors[2],
        g_lh.transpose(1, 0, 2).astype(F32),
        g_lm.astype(F32),
        g_rh.transpose(2, 0, 1).astype(F32),
        g_rm.astype(F32),
        g_le.transpose(1, 0, 2).astype(F32),
        g_lr.astype(F32),
        g_re.transpose(1, 0, 2).astype(F32),
        g_rr.astype(F32),
    )


def solution(mesh):
    nb = mesh.shape["branch"]
    fine = Mesh(mesh.devices.reshape(nb, -1, 2), ("branch", "zz", "core"))
    rows = P(DP, None)
    cols = P(None, None, "branch")
    deep = P("branch", None)
    return jax.shard_map(
        per_device,
        mesh=fine,
        in_specs=(
            rows, rows, P(), P(), P(), cols, deep, cols, deep, cols, deep, cols, deep, P(DP), P(),
        ),
        out_specs=(
            rows, rows, P(), P(), P(), cols, deep, cols, deep, cols, deep, cols, deep,
        ),
        check_vma=False,
    )
```

```python
import functools

import jax
import jax.numpy as jnp
from jax import lax
from jax.experimental import pallas as pl
from jax.experimental.pallas import tpu as pltpu
from jax.sharding import Mesh
from jax.sharding import PartitionSpec as P

DH = 64
WIN = 128
EPSILON = 1e-06
NEGATIVE = -1e30
HIGHEST = lax.Precision.HIGHEST
F32 = jnp.float32
BF16 = jnp.bfloat16
SCALE = DH ** (-0.5)
DP = ("zz", "core")


def mm(a, b, ca, cb):
    return lax.dot_general(a, b, (((ca,), (cb,)), ((), ())), preferred_element_type=F32)


def norm_parts(values):
    r = lax.rsqrt(jnp.mean(values * values, axis=-1, keepdims=True) + EPSILON)
    return r, values * r


def norm_back(dn, xh, r, gain):
    g = dn * gain
    return r * (g - xh * jnp.mean(g * xh, axis=-1, keepdims=True))


def gelu_parts(u):
    c = 0.7978845608028654
    t = jnp.tanh(c * (u + 0.044715 * u * u * u))
    g = 0.5 * u * (1.0 + t)
    dg = 0.5 * (1.0 + t) + 0.5 * u * (1.0 - t * t) * c * (1.0 + 3 * 0.044715 * u * u)
    return g, dg


def feed(n, seed, w_gate, w_up, w_down):
    u = mm(n, w_gate, 1, 0)
    v = mm(n, w_up, 1, 0)
    g, dg = gelu_parts(u)
    hidden = (g * v).astype(BF16)
    out = mm(hidden, w_down, 1, 0)
    dh = mm(seed, w_down, 1, 1)
    du = (dh * v * dg).astype(BF16)
    dv = (dh * g).astype(BF16)
    dn = mm(du, w_gate, 1, 1) + mm(dv, w_up, 1, 1)
    dwg = mm(n, du, 0, 0)
    dwu = mm(n, dv, 0, 0)
    dwd = mm(hidden, seed, 0, 0)
    return out, dn, dwg, dwu, dwd


MESH = pl.DeviceIdType.MESH


def remote(src, dst, send, recv, device):
    return pltpu.make_async_remote_copy(
        src_ref=src, dst_ref=dst, send_sem=send, recv_sem=recv, device_id=device, device_id_type=MESH
    )


def greet(devices):
    barrier = pltpu.get_barrier_semaphore()
    for device in devices:
        pl.semaphore_signal(barrier, inc=1, device_id=device, device_id_type=MESH)
    pl.semaphore_wait(barrier, len(devices))


def here():
    return lax.axis_index("branch"), lax.axis_index("zz"), lax.axis_index("core")


def others(me, count):
    return [lax.rem(me + k, count) for k in range(1, count)]


def band(start, size):
    return pl.ds(pl.multiple_of(start, size), size)


def finish(copies):
    for copy in copies:
        if copy.is_remote:
            copy.wait_send()
        else:
            copy.wait()


class Pool:
    def __init__(self):
        self.names = []
        self.shapes = []

    def add(self, name, shape):
        self.names.append(name)
        self.shapes.append(shape)

    def vmem(self, name, shape, dtype=BF16):
        self.add(name, pltpu.VMEM(shape, dtype))

    def dma(self, name, *shape):
        self.add(name, pltpu.SemaphoreType.DMA(shape))

    def bind(self, refs):
        return dict(zip(self.names, refs, strict=True))


def group_sum_scratch(pool, nb, rows, width):
    for name in ("gs_sib", "gs_part", "gs_came"):
        pool.vmem(name, (nb, rows // 2 // nb, width))
    for name in ("sib", "rs", "ag", "fw"):
        pool.dma(f"gs_{name}_s", nb)
        pool.dma(f"gs_{name}_r", nb)


def group_sum_steps(nb, x, o, m, meanwhile=()):
    b, z, c = here()
    half = x.shape[0] // 2
    ch = half // nb
    twin = (b, z, 1 - c)
    peers = others(b, nb)
    sib, part, came = m["gs_sib"], m["gs_part"], m["gs_came"]
    work = list(meanwhile)

    def aside():
        if work:
            work.pop(0)()

    def rows(core, j):
        return band(core * half + j * ch, ch)

    order = peers + [b]
    to_twin = [
        remote(x.at[rows(1 - c, j)], sib.at[j], m["gs_sib_s"].at[j], m["gs_sib_r"].at[j], twin)
        for j in order
    ]
    for copy in to_twin:
        copy.start()
    sends = []
    for j, copy in zip(peers, to_twin):
        copy.wait_recv()
        part[j] = (x[rows(c, j)].astype(F32) + sib[j].astype(F32)).astype(BF16)
        send = remote(part.at[j], came.at[b], m["gs_rs_s"].at[j], m["gs_rs_r"].at[b], (j, z, c))
        send.start()
        sends.append(send)
    aside()
    to_twin[-1].wait_recv()
    total = x[rows(c, b)].astype(F32) + sib[b].astype(F32)
    for j in peers:
        remote(part.at[j], came.at[j], m["gs_rs_s"].at[j], m["gs_rs_r"].at[j], (j, z, c)).wait_recv()
        total = total + came[j].astype(F32)
    mine = o.at[rows(c, b)]
    mine[...] = total.astype(BF16)
    for j in peers:
        send = remote(mine, mine, m["gs_ag_s"].at[j], m["gs_ag_r"].at[b], (j, z, c))
        send.start()
        sends.append(send)
    send = remote(mine, mine, m["gs_fw_s"].at[b], m["gs_fw_r"].at[b], twin)
    send.start()
    sends.append(send)
    aside()
    for j in peers:
        piece = o.at[rows(c, j)]
        remote(piece, piece, m["gs_ag_s"].at[j], m["gs_ag_r"].at[j], (j, z, c)).wait_recv()
        send = remote(piece, piece, m["gs_fw_s"].at[j], m["gs_fw_r"].at[j], twin)
        send.start()
        sends.append(send)
    while work:
        aside()
    for j in order:
        piece = o.at[rows(1 - c, j)]
        remote(piece, piece, m["gs_fw_s"].at[j], m["gs_fw_r"].at[j], twin).wait_recv()
    finish(to_twin + sends)


def sum_kernel(nb, pool, x, o, *scratch):
    b, z, c = here()
    greet([(b, z, 1 - c)] + [(j, z, c) for j in others(b, nb)])
    group_sum_steps(nb, x, o, pool.bind(scratch))


def group_sum(x, nb, cid):
    rows, width = x.shape
    pool = Pool()
    group_sum_scratch(pool, nb, rows, width)
    return pl.pallas_call(
        functools.partial(sum_kernel, nb, pool),
        out_shape=jax.ShapeDtypeStruct(x.shape, BF16),
        in_specs=[VM],
        out_specs=VM,
        scratch_shapes=pool.shapes,
        compiler_params=pltpu.CompilerParams(
            collective_id=cid, has_side_effects=True, vmem_limit_bytes=40 << 20
        ),
    )(x)


VM = pl.BlockSpec(memory_space=pltpu.VMEM)
HB = pl.BlockSpec(memory_space=pl.ANY)


def normed(x, gain):
    x = x.astype(F32)
    r = lax.rsqrt(jnp.mean(x * x, axis=-1, keepdims=True) + EPSILON)
    return (x * r * gain).astype(BF16)


def head_lanes(shape, h, dim):
    place = lax.broadcasted_iota(jnp.int32, shape, dim)
    return (place >= h * DH) & (place < (h + 1) * DH)


def only_head(x, h):
    return jnp.where(head_lanes(x.shape, h, 1), x, jnp.zeros_like(x))


def near_keys(shape, key_dim, first, total):
    key = lax.broadcasted_iota(jnp.int32, shape, key_dim)
    query = lax.broadcasted_iota(jnp.int32, shape, 1 - key_dim)
    gap = key - query
    return (gap >= 0) & (gap <= 2 * WIN) & (key + first >= 0) & (key + first < total)


def hot_rows(ids, count):
    spot = lax.broadcasted_iota(jnp.int32, (ids.shape[0], count), 1)
    return jnp.where(ids == spot, 1.0, 0.0).astype(BF16)


FRONT_OUT = (
    "tok_r", "cot_r", "first_r", "gate", "qr", "kv", "lh", "lm", "le", "lr", "first_w",
    "q", "k", "v", "ctx_l", "attn_l", "ctx_r", "attn_r", "mixed",
)


def front_kernel(nb, nz, pool, *refs):
    tokens, cotangent, ids, gain, router, rheads, rmerge, s_lh, s_lm, s_le, s_lr = refs[:11]
    out = dict(zip(FRONT_OUT, refs[11 : 11 + len(FRONT_OUT)]))
    m = pool.bind(refs[11 + len(FRONT_OUT) :])
    b, z, c = here()
    twin = (b, z, 1 - c)
    bpeers, zpeers = others(b, nb), others(z, nz)
    rows, D = tokens.shape
    own = rows // nb
    cap = ids.shape[0]
    half = cap // 2
    rw = rmerge.shape[0]
    after = (b, lax.rem(z + c, nz), 1 - c)
    before = (b, lax.rem(z + nz - 1 + c, nz), 1 - c)
    far = (b, lax.rem(z + nz - 1 + 2 * c, nz), 1 - c)
    greet([twin, far] + [(j, z, c) for j in bpeers] + [(b, j, c) for j in zpeers])
    sends = []

    def go(copy):
        copy.start()
        sends.append(copy)

    pairs = [(s_lh, out["lh"]), (s_lm, out["lm"]), (s_le, out["le"]), (s_lr, out["lr"])]

    def place(i, j):
        src, dst = pairs[i]
        if i in (0, 2):
            return dst.at[:, :, band(j * src.shape[2], src.shape[2])]
        return dst.at[band(j * src.shape[0], src.shape[0])]

    def cut(i, ref, core):
        if i in (0, 2):
            size = ref.shape[1] // 2
            return ref.at[:, band(core * size, size)]
        size = ref.shape[0] // 2
        return ref.at[band(core * size, size)]

    for i in range(4):
        for j in bpeers:
            go(remote(cut(i, pairs[i][0], c), cut(i, place(i, b), c), m["w_s"].at[i, j], m["w_r"].at[i, b], (j, z, c)))
    for i in range(4):
        go(pltpu.make_async_copy(pairs[i][0], place(i, b), m["own_s"].at[i]))
    halo = m["halo"]
    go(remote(tokens.at[pl.ds(rows - WIN, WIN)], halo.at[0], m["halo_s"].at[0], m["halo_r"].at[0], after))
    go(remote(tokens.at[pl.ds(0, WIN)], halo.at[1], m["halo_s"].at[1], m["halo_r"].at[1], before))

    picks, sib = m["picks"], m["sib"]
    step = cap // 4
    for k in range(4):
        at = pl.ds(k * step, step)
        hot = hot_rows(ids[at], rows)
        picks[at, :D] = mm(hot, tokens[...], 1, 0).astype(BF16)
        picks[at, D:] = mm(hot, cotangent[...], 1, 0).astype(BF16)
        go(remote(picks.at[at], sib.at[at], m["pick_s"].at[k], m["pick_r"].at[k], twin))
    for k in range(4):
        at = pl.ds(k * step, step)
        remote(picks.at[at], sib.at[at], m["pick_s"].at[k], m["pick_r"].at[k], twin).wait_recv()
        tok = picks[at, :D].astype(F32) + sib[at, :D].astype(F32)
        out["tok_r"][at] = tok.astype(BF16)
        out["cot_r"][at] = (picks[at, D:].astype(F32) + sib[at, D:].astype(F32)).astype(BF16)
        first = normed(tok, gain[...])
        out["first_r"][at] = first
        logit = jnp.sum(first.astype(F32) * router[...], axis=-1, keepdims=True)
        out["gate"][at] = 1.0 / (1.0 + jnp.exp(-logit))

    own_rows = out["first_r"][band(c * half, half)]
    out["qr"][...] = mm(own_rows, rheads[0], 1, 1).astype(BF16)
    kv = out["kv"]
    mine = kv.at[band((2 * z + c) * half, half)]
    mine[:, :rw] = mm(own_rows, rheads[1], 1, 1).astype(BF16)
    mine[:, rw:] = mm(own_rows, rheads[2], 1, 1).astype(BF16)
    for j in zpeers:
        go(remote(mine, mine, m["kv_s"].at[j], m["kv_r"].at[z], (b, j, c)))
    go(remote(mine, mine, m["kf_s"].at[z], m["kf_r"].at[z], twin))

    first_w = out["first_w"]
    first_w[pl.ds(WIN, own)] = normed(tokens[band(b * own, own)], gain[...])
    for i in range(2):
        remote(halo.at[i], halo.at[i], m["halo_s"].at[i], m["halo_r"].at[i], twin).wait_recv()
    lead = tokens[band(jnp.maximum(b * own - WIN, 0), WIN)]
    trail = tokens[band(jnp.minimum((b + 1) * own, rows - WIN), WIN)]
    first_w[pl.ds(0, WIN)] = normed(jnp.where(b > 0, lead, halo[0]), gain[...])
    first_w[pl.ds(WIN + own, WIN)] = normed(jnp.where(b < nb - 1, trail, halo[1]), gain[...])

    def pass_weights(i):
        for j in bpeers:
            dst = cut(i, place(i, j), c)
            remote(dst, dst, m["w_s"].at[i, j], m["w_r"].at[i, j], (j, z, c)).wait_recv()
            go(remote(dst, dst, m["wf_s"].at[i, j], m["wf_r"].at[i, j], twin))

    def take_weights(i):
        for j in bpeers:
            dst = cut(i, place(i, j), 1 - c)
            remote(dst, dst, m["wf_s"].at[i, j], m["wf_r"].at[i, j], twin).wait_recv()

    pass_weights(0)
    for j in zpeers:
        piece = kv.at[band((2 * j + c) * half, half)]
        remote(piece, piece, m["kv_s"].at[j], m["kv_r"].at[j], (b, j, c)).wait_recv()
        go(remote(piece, piece, m["kf_s"].at[j], m["kf_r"].at[j], twin))
    take_weights(0)
    pltpu.make_async_copy(pairs[0][0], place(0, b), m["own_s"].at[0]).wait()
    lh, q, k, v = out["lh"], out["q"], out["k"], out["v"]
    q[...] = mm(first_w[pl.ds(WIN, own)], lh[0], 1, 0).astype(BF16)
    k[...] = mm(first_w[...], lh[1], 1, 0).astype(BF16)
    v[...] = mm(first_w[...], lh[2], 1, 0).astype(BF16)
    pass_weights(1)

    blocks = own // WIN
    ctx = out["ctx_l"]
    first_key = (2 * z + c) * rows + b * own - WIN
    total = 2 * nz * rows

    def light(i, carry):
        g, n = i // blocks, lax.rem(i, blocks)
        lanes = band(g * 2 * DH, 2 * DH)
        at = band(n * WIN, WIN)
        keys = pl.ds(pl.multiple_of(n * WIN, WIN), 3 * WIN)
        q2, k2, v2 = q[at, lanes], k[keys, lanes], v[keys, lanes]
        allowed = near_keys((WIN, 3 * WIN), 1, first_key + n * WIN, total)
        parts = []
        for h in range(2):
            s = jnp.where(allowed, mm(only_head(q2, h), k2, 1, 1) * SCALE, NEGATIVE)
            w = jnp.exp(s - jnp.max(s, axis=-1, keepdims=True))
            p = (w / jnp.sum(w, axis=-1, keepdims=True)).astype(BF16)
            parts.append(mm(p, v2, 1, 0))
        ctx[at, lanes] = jnp.where(head_lanes((WIN, 2 * DH), 0, 1), parts[0], parts[1]).astype(BF16)
        return carry

    lax.fori_loop(0, blocks * (q.shape[1] // (2 * DH)), light, 0)
    take_weights(1)
    pltpu.make_async_copy(pairs[1][0], place(1, b), m["own_s"].at[1]).wait()
    attn_l = out["attn_l"]
    attn_l[...] = mm(ctx[...], out["lm"][...], 1, 0)

    for j in zpeers + [z]:
        piece = kv.at[band((2 * j + 1 - c) * half, half)]
        remote(piece, piece, m["kf_s"].at[j], m["kf_r"].at[j], twin).wait_recv()
    keys, values, qr, ctx_r = m["keys"], m["values"], out["qr"], out["ctx_r"]
    keys[...] = kv[:, :rw]
    values[...] = kv[:, rw:]
    some = 64

    def heavy(i, carry):
        at = band(i * some, some)
        got = jnp.zeros((some, rw), F32)
        for h in range(rw // DH):
            s = mm(only_head(qr[at], h), keys[...], 1, 1) * SCALE
            w = jnp.exp(s - jnp.max(s, axis=-1, keepdims=True))
            p = (w / jnp.sum(w, axis=-1, keepdims=True)).astype(BF16)
            got = jnp.where(head_lanes((some, rw), h, 1), mm(p, values[...], 1, 0), got)
        ctx_r[at] = got.astype(BF16)
        return carry

    lax.fori_loop(0, half // some, heavy, 0)
    attn_r = out["attn_r"]
    attn_r[...] = mm(ctx_r[...], rmerge[...], 1, 0)

    part = m["part"]
    mine_at, other_at = band(c * half, half), band((1 - c) * half, half)
    low = attn_l[...].astype(BF16)
    part[other_at] = mm(hot_rows(ids[other_at] - b * own, own), low, 1, 0).astype(BF16)
    part[mine_at] = (
        mm(hot_rows(ids[mine_at] - b * own, own), low, 1, 0) + out["gate"][mine_at] * attn_r[...]
    ).astype(BF16)
    group_sum_steps(nb, part, out["mixed"], m, [lambda: pass_weights(2), lambda: pass_weights(3)])
    take_weights(2)
    take_weights(3)
    finish([copy for copy in sends if copy.is_remote])
    for i in (2, 3):
        pltpu.make_async_copy(pairs[i][0], place(i, b), m["own_s"].at[i]).wait()


def front(nb, nz, tokens, cotangent, ids, gain, router, rheads, rmerge, s_lh, s_lm, s_le, s_lr):
    rows, D = tokens.shape
    own = rows // nb
    cap = ids.shape[0]
    half = cap // 2
    rw = rmerge.shape[0]
    wl = nb * s_lm.shape[0]
    shape = lambda *dims: jax.ShapeDtypeStruct(dims, BF16)
    shape32 = lambda *dims: jax.ShapeDtypeStruct(dims, F32)
    outs = dict(
        tok_r=shape(cap, D), cot_r=shape(cap, D), first_r=shape(cap, D), gate=shape32(cap, 1),
        qr=shape(half, rw), kv=shape(2 * nz * half, 2 * rw),
        lh=shape(3, D, wl), lm=shape(wl, D),
        le=shape(2, D, nb * s_le.shape[2]), lr=shape(nb * s_lr.shape[0], D),
        first_w=shape(own + 2 * WIN, D), q=shape(own, wl), k=shape(own + 2 * WIN, wl),
        v=shape(own + 2 * WIN, wl), ctx_l=shape(own, wl), attn_l=shape32(own, D),
        ctx_r=shape(half, rw), attn_r=shape32(half, D), mixed=shape(cap, D),
    )
    pool = Pool()
    pool.vmem("picks", (cap, 2 * D))
    pool.vmem("sib", (cap, 2 * D))
    pool.vmem("halo", (2, WIN, D))
    pool.vmem("keys", (2 * nz * half, rw))
    pool.vmem("values", (2 * nz * half, rw))
    pool.vmem("part", (cap, D))
    group_sum_scratch(pool, nb, cap, D)
    pool.dma("own_s", 4)
    pool.dma("halo_s", 2)
    pool.dma("halo_r", 2)
    pool.dma("pick_s", 4)
    pool.dma("pick_r", 4)
    for name in ("w", "wf"):
        pool.dma(f"{name}_s", 4, nb)
        pool.dma(f"{name}_r", 4, nb)
    for name in ("kv", "kf"):
        pool.dma(f"{name}_s", nz)
        pool.dma(f"{name}_r", nz)
    got = pl.pallas_call(
        functools.partial(front_kernel, nb, nz, pool),
        out_shape=tuple(outs[name] for name in FRONT_OUT),
        in_specs=[VM] * 7 + [HB] * 4,
        out_specs=tuple(HB if name in ("le", "lr") else VM for name in FRONT_OUT),
        scratch_shapes=pool.shapes,
        compiler_params=pltpu.CompilerParams(
            collective_id=0, has_side_effects=True, vmem_limit_bytes=56 << 20
        ),
    )(tokens, cotangent, ids, gain, router, rheads, rmerge, s_lh, s_lm, s_le, s_lr)
    return dict(zip(FRONT_OUT, got))


MID_IN = (
    "tok_own", "cot_own", "ids", "gain", "tok_r", "cot_r", "gate", "mixed", "attn_l",
    "le", "lr", "re", "rr",
)
MID_OUT = ("layer", "gm_own", "gm_r", "gate_feed", "gain_part", "g_feed", "g_rx")


def lane_blocks(x):
    return [x[:, n * 128 : (n + 1) * 128] for n in range(x.shape[1] // 128)]


def pack_rows(g, start, parts):
    for part in parts:
        size = part.shape[0] // 2
        for core in range(2):
            g[core, pl.ds(start, size)] = part[core * size : (core + 1) * size].astype(BF16)
        start += size
    return start


def down_pieces(rows, D):
    steps = 8
    per, step = D // steps // 32, rows // steps
    pieces = []
    for n in range(steps):
        spots = [(r, k) for k in range(D // 128) for r in range(0, step, 32)]
        pieces += [(p // per, n * (D // steps) + p % per * 32, n * step + r, k) for p, (r, k) in enumerate(spots)]
    return pieces


def pack_down(g, start, x):
    for block, at, row, k in down_pieces(*x.shape):
        g[start + block, pl.ds(at, 32)] = x[row : row + 32, k * 128 : (k + 1) * 128].astype(BF16)


def mid_kernel(nb, pool, *refs):
    i = dict(zip(MID_IN, refs[: len(MID_IN)]))
    out = dict(zip(MID_OUT, refs[len(MID_IN) : len(MID_IN) + len(MID_OUT)]))
    m = pool.bind(refs[len(MID_IN) + len(MID_OUT) :])
    b, z, c = here()
    greet([(b, z, 1 - c)] + [(j, z, c) for j in others(b, nb)])
    own, D = i["tok_own"].shape
    cap = i["ids"].shape[0]
    fl = i["le"].shape[2] // nb
    fh = i["re"].shape[2]
    gain = i["gain"][...]

    pick, pick_t = m["pick"], m["pick_t"]
    hot = hot_rows(i["ids"][...] - b * own, own)
    pick[...] = hot
    pick_t[...] = hot.T
    owned = jnp.sum(pick_t[...].astype(F32), axis=1, keepdims=True) > 0.5
    mid_o, mid_r = m["mid_o"], m["mid_r"]
    mid_o[...] = i["tok_own"][...].astype(F32) + jnp.where(
        owned, mm(pick_t[...], i["mixed"][...], 1, 0), i["attn_l"][...]
    )
    mid_r[...] = i["tok_r"][...].astype(F32) + i["mixed"][...].astype(F32)
    n_o, n_r = m["n_o"], m["n_r"]
    n_o[...] = normed(mid_o[...], gain)
    n_r[...] = normed(mid_r[...], gain)
    gate = i["gate"][...]
    seed_r = m["seed_r"]
    seed_r[...] = (gate * i["cot_r"][...].astype(F32)).astype(BF16)

    def both_ways(n, seed, expand, narrow, row0, tile, count, hid, du, dv, ff, dn):
        def one(t, carry):
            lanes = band(t * tile, tile)
            wd = narrow[band(row0 + t * tile, tile)]
            u = mm(n[...], expand[0, :, lanes], 1, 0)
            v = mm(n[...], expand[1, :, lanes], 1, 0)
            g, dg = gelu_parts(u)
            low = (g * v).astype(BF16)
            hid[:, lanes] = low
            dh = mm(seed[...], wd, 1, 1)
            du[:, lanes] = (dh * v * dg).astype(BF16)
            dv[:, lanes] = (dh * g).astype(BF16)
            one_ff = mm(low, wd, 1, 0)
            one_dn = mm(du[:, lanes], expand[0, :, lanes], 1, 1) + mm(dv[:, lanes], expand[1, :, lanes], 1, 1)
            ff[...] = jnp.where(t == 0, one_ff, ff[...] + one_ff)
            dn[...] = jnp.where(t == 0, one_dn, dn[...] + one_dn)
            return carry

        lax.fori_loop(0, count, one, 0)

    ff_r, dn_r, ff_o, dn_o = m["ff_r"], m["dn_r"], m["ff_o"], m["dn_o"]
    both_ways(
        n_r, seed_r, i["re"], i["rr"], c * fh, fl, fh // fl, m["hid_r"], m["du_r"], m["dv_r"], ff_r, dn_r
    )
    both_ways(
        n_o, i["cot_own"], i["le"], i["lr"], 0, fl, nb, m["hid_o"], m["du_o"], m["dv_o"], ff_o, dn_o
    )
    out["gate_feed"][...] = jnp.sum(i["cot_r"][...].astype(F32) * ff_r[...], axis=-1, keepdims=True)
    part = m["part"]
    part[:, :D] = ff_r[...].astype(BF16)
    part[:, D:] = (dn_r[...] + mm(pick[...], dn_o[...].astype(BF16), 1, 0)).astype(BF16)

    n_t = m["n_t"]

    def weights_heavy():
        n_t[...] = n_r[...].T
        gx = out["g_rx"]
        for k, x in enumerate(lane_blocks(mm(n_t[...], m["du_r"][...], 1, 0)) + lane_blocks(mm(n_t[...], m["dv_r"][...], 1, 0))):
            gx[k] = x.astype(BF16)
        pack_down(gx, 2 * fh // 128, mm(m["hid_r"][...], seed_r[...], 0, 0))

    def weights_light():
        n_t[...] = n_o[...].T
        g = out["g_feed"]

        def one(t, carry):
            lanes = band(t * fl, fl)
            gate_part = mm(n_t[...], m["du_o"][:, lanes], 1, 0)
            up_part = mm(n_t[...], m["dv_o"][:, lanes], 1, 0)
            down = mm(m["hid_o"][:, lanes], i["cot_own"][...], 0, 0)
            pack_rows(g.at[t], 0, lane_blocks(gate_part) + lane_blocks(up_part) + lane_blocks(down))
            return carry

        lax.fori_loop(0, nb, one, 0)

    sums = m["sums"]
    group_sum_steps(nb, part, sums, m, [weights_heavy, weights_light])
    dn_sum = sums[:, D:]
    scaled = (gate * sums[:, :D].astype(F32)).astype(BF16)
    out["layer"][...] = (mid_o[...] + ff_o[...] + mm(pick_t[...], scaled, 1, 0)).astype(BF16)
    dn_own = jnp.where(owned, mm(pick_t[...], dn_sum, 1, 0), dn_o[...])
    r, xh = norm_parts(mid_o[...])
    out["gm_own"][...] = i["cot_own"][...].astype(F32) + norm_back(dn_own, xh, r, gain)
    out["gain_part"][...] = jnp.sum(dn_own * xh, axis=0, keepdims=True)
    r, xh = norm_parts(mid_r[...])
    out["gm_r"][...] = i["cot_r"][...].astype(F32) + norm_back(dn_sum.astype(F32), xh, r, gain)


def middle(nb, given):
    own, D = given["tok_own"].shape
    cap = given["ids"].shape[0]
    wide = given["le"].shape[2]
    fl = wide // nb
    fh = given["re"].shape[2]
    shape = lambda *dims: jax.ShapeDtypeStruct(dims, BF16)
    shape32 = lambda *dims: jax.ShapeDtypeStruct(dims, F32)
    packed = (2 * D * fl + fl * D) // 2 // 128
    outs = dict(
        layer=shape(own, D), gm_own=shape32(own, D), gm_r=shape32(cap, D), gate_feed=shape32(cap, 1),
        gain_part=shape32(1, D), g_feed=shape(nb, 2, packed, 128), g_rx=shape(3 * fh // 128, D, 128),
    )
    pool = Pool()
    pool.vmem("pick", (cap, own))
    pool.vmem("pick_t", (own, cap))
    for name, count in (("o", own), ("r", cap)):
        pool.vmem(f"mid_{name}", (count, D), F32)
        pool.vmem(f"n_{name}", (count, D))
        pool.vmem(f"ff_{name}", (count, D), F32)
        pool.vmem(f"dn_{name}", (count, D), F32)
        for kind in ("hid", "du", "dv"):
            pool.vmem(f"{kind}_{name}", (count, wide if name == "o" else fh))
    pool.vmem("seed_r", (cap, D))
    pool.vmem("n_t", (D, own))
    pool.vmem("part", (cap, 2 * D))
    pool.vmem("sums", (cap, 2 * D))
    group_sum_scratch(pool, nb, cap, 2 * D)
    got = pl.pallas_call(
        functools.partial(mid_kernel, nb, pool),
        out_shape=tuple(outs[name] for name in MID_OUT),
        in_specs=[VM] * len(MID_IN),
        out_specs=(VM,) * len(MID_OUT),
        scratch_shapes=pool.shapes,
        compiler_params=pltpu.CompilerParams(
            collective_id=2, has_side_effects=True, vmem_limit_bytes=60 << 20
        ),
    )(*(given[name] for name in MID_IN))
    return dict(zip(MID_OUT, got))


class Gather:
    def __init__(self, nb, src, dst, m, name):
        b, z, c = here()
        self.own = pltpu.make_async_copy(src, dst.at[b], m[f"{name}_own"])
        self.out = [
            remote(src, dst.at[b], m[f"{name}_s"].at[j], m[f"{name}_r"].at[b], (j, z, c)) for j in others(b, nb)
        ]
        self.come = [
            remote(dst.at[j], dst.at[j], m[f"{name}_s"].at[j], m[f"{name}_r"].at[j], (j, z, c))
            for j in others(b, nb)
        ]

    def start(self):
        self.own.start()
        for copy in self.out:
            copy.start()

    def wait(self):
        for copy in self.come:
            copy.wait_recv()
        for copy in self.out:
            copy.wait_send()
        self.own.wait()

    @staticmethod
    def scratch(pool, nb, name):
        pool.shapes.append(pltpu.SemaphoreType.DMA)
        pool.names.append(f"{name}_own")
        pool.dma(f"{name}_s", nb)
        pool.dma(f"{name}_r", nb)


class ShardSum:
    def __init__(self, nb, g, h, m, name):
        self.b, self.z, self.c = here()
        self.peers = others(self.b, nb)
        self.g, self.h, self.m, self.name = g, h, m, name
        self.sends = []

    def pair(self, j):
        m, n = self.m, self.name
        return remote(
            self.g.at[j, 1 - self.c], m[f"{n}_sib"].at[j], m[f"{n}_a_s"].at[j], m[f"{n}_a_r"].at[j],
            (self.b, self.z, 1 - self.c),
        )

    def start(self):
        for j in self.peers + [self.b]:
            copy = self.pair(j)
            copy.start()
            self.sends.append(copy)

    def spread(self):
        m, n = self.m, self.name
        for j in self.peers:
            self.pair(j).wait_recv()
            sib = m[f"{n}_sib"]
            sib[j] = (self.g[j, self.c].astype(F32) + sib[j].astype(F32)).astype(BF16)
            copy = remote(
                sib.at[j], m[f"{n}_came"].at[self.b], m[f"{n}_b_s"].at[j], m[f"{n}_b_r"].at[self.b],
                (j, self.z, self.c),
            )
            copy.start()
            self.sends.append(copy)

    def collect(self):
        m, n = self.m, self.name
        sib, came, b = m[f"{n}_sib"], m[f"{n}_came"], self.b
        self.pair(b).wait_recv()
        total = self.g[b, self.c].astype(F32) + sib[b].astype(F32)
        for j in self.peers:
            remote(sib.at[j], came.at[j], m[f"{n}_b_s"].at[j], m[f"{n}_b_r"].at[j], (j, self.z, self.c)).wait_recv()
            total = total + came[j].astype(F32)
        self.h[...] = total.astype(BF16)

    def end(self):
        finish(self.sends)

    @staticmethod
    def scratch(pool, nb, rows, name):
        pool.vmem(f"{name}_sib", (nb, rows, 128))
        pool.vmem(f"{name}_came", (nb, rows, 128))
        for step in ("a", "b"):
            pool.dma(f"{name}_{step}_s", nb)
            pool.dma(f"{name}_{step}_r", nb)


class BlockSum:
    def __init__(self, nz, h, f, m, name):
        self.b, self.z, self.c = here()
        self.peers = others(self.z, nz)
        self.h, self.f, self.m, self.name = h, f, m, name
        self.ch = h.shape[0] // nz
        self.sends = []

    def go(self, copy):
        copy.start()
        self.sends.append(copy)

    def rows(self, j):
        return band(j * self.ch, self.ch)

    def start(self):
        m, n = self.m, self.name
        for j in self.peers:
            self.go(
                remote(
                    self.h.at[self.rows(j)], m[f"{n}_came"].at[self.z], m[f"{n}_a_s"].at[j],
                    m[f"{n}_a_r"].at[self.z], (self.b, j, self.c),
                )
            )

    def spread(self):
        m, n = self.m, self.name
        came, z, c = m[f"{n}_came"], self.z, self.c
        total = self.h[self.rows(z)].astype(F32)
        for j in self.peers:
            remote(
                self.h.at[self.rows(j)], came.at[j], m[f"{n}_a_s"].at[j], m[f"{n}_a_r"].at[j], (self.b, j, c)
            ).wait_recv()
            total = total + came[j].astype(F32)
        mine = self.f.at[c, self.rows(z)]
        mine[...] = total.astype(BF16)
        for j in self.peers:
            self.go(remote(mine, mine, m[f"{n}_b_s"].at[j], m[f"{n}_b_r"].at[z], (self.b, j, c)))
        self.go(remote(mine, mine, m[f"{n}_c_s"].at[z], m[f"{n}_c_r"].at[z], (self.b, z, 1 - c)))

    def forward(self):
        m, n, c = self.m, self.name, self.c
        for j in self.peers:
            piece = self.f.at[c, self.rows(j)]
            remote(piece, piece, m[f"{n}_b_s"].at[j], m[f"{n}_b_r"].at[j], (self.b, j, c)).wait_recv()
            self.go(remote(piece, piece, m[f"{n}_c_s"].at[j], m[f"{n}_c_r"].at[j], (self.b, self.z, 1 - c)))

    def end(self):
        m, n, c = self.m, self.name, self.c
        for j in self.peers + [self.z]:
            piece = self.f.at[1 - c, self.rows(j)]
            remote(piece, piece, m[f"{n}_c_s"].at[j], m[f"{n}_c_r"].at[j], (self.b, self.z, 1 - c)).wait_recv()
        finish(self.sends)

    @staticmethod
    def scratch(pool, nz, rows, name):
        pool.vmem(f"{name}_came", (nz, rows // nz, 128))
        for step in ("a", "b", "c"):
            pool.dma(f"{name}_{step}_s", nz)
            pool.dma(f"{name}_{step}_r", nz)


TAIL_IN = ("g_att", "g_heavy", "gm_own", "gf_l", "gf_r", "ids", "tok_own", "gain", "vec")
TAIL_OUT = ("delta", "f_att", "f_heavy", "vectors")


def tail_kernel(nb, nz, pool, *refs):
    i = dict(zip(TAIL_IN, refs[: len(TAIL_IN)]))
    out = dict(zip(TAIL_OUT, refs[len(TAIL_IN) : len(TAIL_IN) + len(TAIL_OUT)]))
    m = pool.bind(refs[len(TAIL_IN) + len(TAIL_OUT) :])
    b, z, c = here()
    twin = (b, z, 1 - c)
    bpeers, zpeers = others(b, nb), others(z, nz)
    own, D = i["gm_own"].shape
    greet([twin] + [(j, z, c) for j in bpeers] + [(b, j, c) for j in zpeers])
    gh, sib_h, h_heavy = i["g_heavy"], m["sib_h"], m["h_heavy"]
    to_twin = remote(gh.at[1 - c], sib_h, m["sib_h_s"].at[0], m["sib_h_r"].at[0], twin)
    to_twin.start()
    shard = ShardSum(nb, i["g_att"], m["h_att"], m, "ga")
    shard.start()
    att = BlockSum(nz, m["h_att"], out["f_att"], m, "za")
    heavy = BlockSum(nz, h_heavy, out["f_heavy"], m, "zh")
    to_twin.wait_recv()
    h_heavy[...] = (gh[c].astype(F32) + sib_h[...].astype(F32)).astype(BF16)
    heavy.start()
    shard.spread()

    hot_t = hot_rows(i["ids"][...] - b * own, own).T
    owned = jnp.sum(hot_t.astype(F32), axis=1, keepdims=True) > 0.5
    gf = jnp.where(owned, mm(hot_t, i["gf_r"][...], 1, 0), i["gf_l"][...])
    r, xh = norm_parts(i["tok_own"][...].astype(F32))
    gain_part = jnp.sum(gf * xh, axis=0, keepdims=True)
    low = m["low"]
    low[...] = (i["gm_own"][...] + norm_back(gf, xh, r, i["gain"][...])).astype(BF16)
    rows = Gather(nb, low, out["delta"], m, "td")
    rows.start()

    vec = m["vec_mine"]
    vec[pl.ds(0, 8)] = i["vec"][...]
    vec[pl.ds(0, 1)] = gain_part
    sends = [to_twin]

    def vec_step(name, me, peers, device):
        got = m[f"{name}_got"]
        got[me] = vec[...]
        for j in peers:
            copy = remote(vec, got.at[me], m[f"{name}_s"].at[j], m[f"{name}_r"].at[me], device(j))
            copy.start()
            sends.append(copy)

    def vec_end(name, peers, device):
        got = m[f"{name}_got"]
        for j in peers:
            remote(got.at[j], got.at[j], m[f"{name}_s"].at[j], m[f"{name}_r"].at[j], device(j)).wait_recv()
        return functools.reduce(lambda x, y: x + y, [got[j] for j in range(got.shape[0])])

    by_core, by_branch, by_block = (lambda j: (b, z, j)), (lambda j: (j, z, c)), (lambda j: (b, j, c))
    vec_step("vc", c, [1 - c], by_core)
    shard.collect()
    att.start()
    total = vec_end("vc", [1 - c], by_core)
    vec2 = m["vec_pair"]
    vec2[...] = total
    vec = vec2
    vec_step("vb", b, bpeers, by_branch)
    heavy.spread()
    total = vec_end("vb", bpeers, by_branch)
    vec3 = m["vec_group"]
    vec3[...] = total
    vec = vec3
    vec_step("vz", z, zpeers, by_block)
    att.spread()
    heavy.forward()
    out["vectors"][...] = vec_end("vz", zpeers, by_block)
    att.forward()
    heavy.end()
    att.end()
    shard.end()
    rows.wait()
    finish(sends)


def tail(nb, nz, given):
    own, D = given["gm_own"].shape
    ra, rh = given["g_att"].shape[2], given["g_heavy"].shape[1]
    shape = lambda *dims: jax.ShapeDtypeStruct(dims, BF16)
    outs = dict(
        delta=shape(nb, own, D), f_att=shape(2, ra, 128), f_heavy=shape(2, rh, 128),
        vectors=jax.ShapeDtypeStruct((8, D), F32),
    )
    pool = Pool()
    pool.vmem("sib_h", (rh, 128))
    pool.vmem("h_heavy", (rh, 128))
    pool.vmem("h_att", (ra, 128))
    pool.vmem("low", (own, D))
    pool.dma("sib_h_s", 1)
    pool.dma("sib_h_r", 1)
    ShardSum.scratch(pool, nb, ra, "ga")
    BlockSum.scratch(pool, nz, ra, "za")
    BlockSum.scratch(pool, nz, rh, "zh")
    Gather.scratch(pool, nb, "td")
    for name in ("vec_mine", "vec_pair", "vec_group"):
        pool.vmem(name, (8, D), F32)
    for name, count in (("vc", 2), ("vb", nb), ("vz", nz)):
        pool.vmem(f"{name}_got", (count, 8, D), F32)
        pool.dma(f"{name}_s", count)
        pool.dma(f"{name}_r", count)
    got = pl.pallas_call(
        functools.partial(tail_kernel, nb, nz, pool),
        out_shape=tuple(outs[name] for name in TAIL_OUT),
        in_specs=[VM] * len(TAIL_IN),
        out_specs=(HB,) + (VM,) * (len(TAIL_OUT) - 1),
        scratch_shapes=pool.shapes,
        compiler_params=pltpu.CompilerParams(
            collective_id=4, has_side_effects=True, vmem_limit_bytes=56 << 20
        ),
        cost_estimate=pl.CostEstimate(flops=40 * 10**9, bytes_accessed=200 * 2**20, transcendentals=0),
    )(*(given[name] for name in TAIL_IN))
    return dict(zip(TAIL_OUT, got))


BACK_OUT = ("gf_r", "gf_l", "g_att", "g_heavy", "router", "lay", "f_feed")
BACK_IN = (
    "gm_own", "gm_r", "gate", "gate_feed", "ids", "q", "k", "v", "lm", "lh", "first_w", "ctx_l",
    "qr", "kv", "rmerge", "rheads", "first_r", "ctx_r", "attn_r", "router_vector",
    "layer", "g_feed",
)


def back_names(inner):
    return BACK_IN if inner else BACK_IN + ("trio",)


def heavy_back(i, m, seed, x):
    kv, qr = i["kv"], i["qr"]
    half, rw = qr.shape
    keys, values, keys_t, dk, dv, dq_t, do = (
        m[n] for n in ("keys", "values", "keys_t", "dk", "dv", "dq_t", "do")
    )
    keys[...] = kv[:, :rw]
    values[...] = kv[:, rw:]
    keys_t[...] = keys[...].T
    do[...] = mm(seed, i["rmerge"][...], 1, 1).astype(BF16)
    dk[...] = jnp.zeros_like(dk)
    dv[...] = jnp.zeros_like(dv)
    dq_t[...] = jnp.zeros_like(dq_t)
    some = 128

    def heavy(n, carry):
        at = band(n * some, some)
        for h in range(rw // DH):
            qh, doh = only_head(qr[at], h), only_head(do[at], h)
            s = mm(keys[...], qh, 1, 1) * SCALE
            w = jnp.exp(s - jnp.max(s, axis=0, keepdims=True))
            p = w * (1.0 / jnp.sum(w, axis=0, keepdims=True))
            dp = mm(values[...], doh, 1, 1)
            ds = (p * (dp - jnp.sum(p * dp, axis=0, keepdims=True))).astype(BF16)
            dk[...] += mm(ds, qh, 1, 0)
            dv[...] += mm(p.astype(BF16), doh, 1, 0)
            got = mm(keys_t[...], ds, 1, 0)
            dq_t[:, at] += jnp.where(head_lanes(got.shape, h, 0), got, 0.0)
        return carry

    lax.fori_loop(0, half // some, heavy, 0)
    x[:, :rw] = (dk[...] * SCALE).astype(BF16)
    x[:, rw:] = dv[...].astype(BF16)


def heavy_back_plain(i):
    half, rw = i["qr"].shape
    split = lambda y: y.reshape(y.shape[0], -1, DH)
    at = lax.axis_index("core") * half
    seed = (i["gate"] * i["gm_r"]).astype(BF16)
    seed = lax.dynamic_slice(seed, (at, 0), (half, seed.shape[1]))
    do = split(mm(seed, i["rmerge"], 1, 1).astype(BF16))
    q, k, v = split(i["qr"]), split(i["kv"][:, :rw]), split(i["kv"][:, rw:])
    p = jax.nn.softmax(jnp.einsum("qhe,khe->hqk", q, k, preferred_element_type=F32) * SCALE, axis=-1)
    dp = jnp.einsum("qhe,khe->hqk", do, v, preferred_element_type=F32)
    ds = (p * (dp - jnp.sum(p * dp, -1, keepdims=True))).astype(BF16)
    dq = jnp.einsum("hqk,khe->qhe", ds, k, preferred_element_type=F32) * SCALE
    dk = jnp.einsum("hqk,qhe->khe", ds, q, preferred_element_type=F32) * SCALE
    dv = jnp.einsum("hqk,qhe->khe", p.astype(BF16), do, preferred_element_type=F32)
    both = jnp.concatenate([dk.reshape(-1, rw), dv.reshape(-1, rw)], 1).astype(BF16)
    both = lax.psum_scatter(both, DP, scatter_dimension=0, tiled=True)
    return jnp.stack([dq.reshape(half, rw).astype(BF16), both[:, :rw], both[:, rw:]], 0)


def back_kernel(nb, nz, pool, inner, *refs):
    names = back_names(inner)
    i = dict(zip(names, refs[: len(names)]))
    out = dict(zip(BACK_OUT, refs[len(names) : len(names) + len(BACK_OUT)]))
    m = pool.bind(refs[len(names) + len(BACK_OUT) :])
    b, z, c = here()
    twin = (b, z, 1 - c)
    bpeers, zpeers = others(b, nb), others(z, nz)
    own, D = i["gm_own"].shape
    rows = own * nb
    cap = i["ids"].shape[0]
    half = cap // 2
    rw = i["rmerge"].shape[0]
    wl = i["q"].shape[1]
    last, first = b == nb - 1, b == 0
    after = (
        jnp.where(last, 0, b + 1), jnp.where(last, lax.rem(z + c, nz), z), jnp.where(last, 1 - c, c),
    )
    before = (
        jnp.where(first, nb - 1, b - 1),
        jnp.where(first, lax.rem(z + nz - 1 + c, nz), z),
        jnp.where(first, 1 - c, c),
    )
    greet([twin, after, before] + [(j, z, c) for j in bpeers] + [(b, j, c) for j in zpeers])
    mine_at, other_at = band(c * half, half), band((1 - c) * half, half)
    sends = []
    layer = Gather(nb, i["layer"], out["lay"], m, "ly")
    shard = ShardSum(nb, i["g_feed"], m["h_feed"], m, "gf")
    feeds = BlockSum(nz, m["h_feed"], out["f_feed"], m, "zf")
    shard.start()
    layer.start()

    def go(copy):
        copy.start()
        sends.append(copy)

    gm_half = i["gm_r"][mine_at]
    gate_half = i["gate"][mine_at]
    seed = (gate_half * gm_half).astype(BF16)
    pack_rows(out["g_heavy"], 3 * rw // 2 * (D // 128), lane_blocks(mm(i["ctx_r"][...], seed, 0, 0)))
    trio = m["trio"] if inner else i["trio"]

    def spot(core, j):
        return band((2 * j + core) * half, half)

    def to_twin(j):
        return remote(x.at[spot(1 - c, j)], sib.at[j], m["bs_sib_s"].at[j], m["bs_sib_r"].at[j], twin)

    if inner:
        x, sib, part, came = m["dkv"], m["bs_sib"], m["bs_part"], m["bs_came"]
        heavy_back(i, m, seed, x)
        for j in zpeers + [z]:
            go(to_twin(j))

    shard.spread()
    low, do_l = m["low"], m["do_l"]
    low[...] = i["gm_own"][...].astype(BF16)
    do_l[...] = mm(low[...], i["lm"][...], 1, 1).astype(BF16)
    for j in zpeers if inner else []:
        to_twin(j).wait_recv()
        part[j] = (x[spot(c, j)].astype(F32) + sib[j].astype(F32)).astype(BF16)
        go(remote(part.at[j], came.at[z], m["bs_rs_s"].at[j], m["bs_rs_r"].at[z], (b, j, c)))

    q, k, v = i["q"], i["k"], i["v"]
    lk_t, dkl, dvl, dql = m["lk_t"], m["dkl"], m["dvl"], m["dql"]
    lk_t[...] = k[...].T
    dkl[...] = jnp.zeros_like(dkl)
    dvl[...] = jnp.zeros_like(dvl)
    blocks = own // WIN
    first_key = (2 * z + c) * rows + b * own - WIN
    total = 2 * nz * rows

    def light(n_, carry):
        g, n = n_ // blocks, lax.rem(n_, blocks)
        lanes = band(g * 2 * DH, 2 * DH)
        at = band(n * WIN, WIN)
        near = pl.ds(pl.multiple_of(n * WIN, WIN), 3 * WIN)
        q2, do2, k2, v2, kt2 = q[at, lanes], do_l[at, lanes], k[near, lanes], v[near, lanes], lk_t[lanes, near]
        allowed = near_keys((3 * WIN, WIN), 0, first_key + n * WIN, total)
        got_k = got_v = None
        got_q = []
        for h in range(2):
            qh, doh = only_head(q2, h), only_head(do2, h)
            s = jnp.where(allowed, mm(k2, qh, 1, 1) * SCALE, NEGATIVE)
            w = jnp.exp(s - jnp.max(s, axis=0, keepdims=True))
            p = w * (1.0 / jnp.sum(w, axis=0, keepdims=True))
            dp = mm(v2, doh, 1, 1)
            ds = (p * (dp - jnp.sum(p * dp, axis=0, keepdims=True))).astype(BF16)
            one_k, one_v = mm(ds, qh, 1, 0), mm(p.astype(BF16), doh, 1, 0)
            got_k = one_k if got_k is None else got_k + one_k
            got_v = one_v if got_v is None else got_v + one_v
            got_q.append(mm(kt2, ds, 1, 0))
        dkl[near, lanes] += got_k
        dvl[near, lanes] += got_v
        both = jnp.where(head_lanes((2 * DH, WIN), 0, 0), got_q[0], got_q[1])
        dql[at, lanes] = (both.T * SCALE).astype(BF16)
        return carry

    lax.fori_loop(0, blocks * (wl // (2 * DH)), light, 0)
    shard.collect()
    feeds.start()
    rim, came_rim = m["rim"], m["came_rim"]
    for n, start in ((0, WIN + own), (1, 0)):
        rim[n, :, :wl] = (dkl[pl.ds(start, WIN)] * SCALE).astype(BF16)
        rim[n, :, wl:] = dvl[pl.ds(start, WIN)].astype(BF16)
    go(remote(rim.at[0], came_rim.at[0], m["rim_s"].at[0], m["rim_r"].at[0], after))
    go(remote(rim.at[1], came_rim.at[1], m["rim_s"].at[1], m["rim_r"].at[1], before))

    if inner:
        to_twin(z).wait_recv()
        mine = x[spot(c, z)].astype(F32) + sib[z].astype(F32)
        for j in zpeers:
            remote(part.at[j], came.at[j], m["bs_rs_s"].at[j], m["bs_rs_r"].at[j], (b, j, c)).wait_recv()
            mine = mine + came[j].astype(F32)
        trio[0] = (m["dq_t"][...].T * SCALE).astype(BF16)
        trio[1] = mine[:, :rw].astype(BF16)
        trio[2] = mine[:, rw:].astype(BF16)
    rheads = i["rheads"]
    picked = mm(trio[0], rheads[0], 1, 0) + mm(trio[1], rheads[1], 1, 0) + mm(trio[2], rheads[2], 1, 0)

    for n, device in ((0, before), (1, after)):
        remote(rim.at[n], came_rim.at[n], m["rim_s"].at[n], m["rim_r"].at[n], device).wait_recv()
    dkl[pl.ds(WIN, WIN)] += came_rim[0, :, :wl].astype(F32) * (1.0 / SCALE)
    dvl[pl.ds(WIN, WIN)] += came_rim[0, :, wl:].astype(F32)
    dkl[pl.ds(own, WIN)] += came_rim[1, :, :wl].astype(F32) * (1.0 / SCALE)
    dvl[pl.ds(own, WIN)] += came_rim[1, :, wl:].astype(F32)
    dk_own, dv_own = m["dk_own"], m["dv_own"]
    dk_own[...] = (dkl[pl.ds(WIN, own)] * SCALE).astype(BF16)
    dv_own[...] = dvl[pl.ds(WIN, own)].astype(BF16)
    lh = i["lh"]
    gf_l = out["gf_l"]
    gf_l[...] = mm(dql[...], lh[0], 1, 1) + mm(dk_own[...], lh[1], 1, 1) + mm(dv_own[...], lh[2], 1, 1)

    feeds.spread()
    gate, first_r = i["gate"], i["first_r"]
    gate_attn = jnp.sum(gm_half * i["attn_r"][...], axis=-1, keepdims=True)
    total_part = m["part"]
    low_gf = gf_l[...].astype(BF16)
    router_sum = None
    for at, extra, more in ((other_at, None, None), (mine_at, gate_attn, picked)):
        g = gate[at]
        d_gate = i["gate_feed"][at] if extra is None else i["gate_feed"][at] + extra
        d_logit = d_gate * g * (1.0 - g)
        one = jnp.sum(d_logit * first_r[at].astype(F32), axis=0, keepdims=True)
        router_sum = one if router_sum is None else router_sum + one
        sum_ = mm(hot_rows(i["ids"][at] - b * own, own), low_gf, 1, 0) + d_logit * i["router_vector"][...]
        if more is not None:
            sum_ = sum_ + more
        total_part[at] = sum_.astype(BF16)
    out["router"][...] = router_sum

    first_t, g_att = m["first_t"], out["g_att"]
    hl = wl // nb

    def weights_light():
        first_t[...] = i["first_w"][pl.ds(WIN, own)].T

        def one(t, carry):
            lanes = band(t * 2 * hl, 2 * hl)
            for n, x in enumerate((dql, dk_own, dv_own)):
                both = mm(first_t[...], x[:, lanes], 1, 0)
                for k in range(2):
                    pack_rows(g_att.at[2 * t + k], n * D // 2, [both[:, k * hl : (k + 1) * hl]])
            return carry

        lax.fori_loop(0, nb // 2, one, 0)

    def weights_rest():
        def one(t, carry):
            both = mm(i["ctx_l"][:, band(t * 2 * hl, 2 * hl)], low[...], 0, 0)
            for k in range(2):
                pack_rows(g_att.at[2 * t + k], 3 * D // 2, lane_blocks(both[k * hl : (k + 1) * hl]))
            return carry

        lax.fori_loop(0, nb // 2, one, 0)
        first_half = first_r[mine_at]
        for n in range(3):
            pack_rows(out["g_heavy"], n * rw // 2 * (D // 128), lane_blocks(mm(trio[n], first_half, 0, 0)))
        feeds.forward()

    group_sum_steps(nb, total_part, out["gf_r"], m, [weights_light, weights_rest])
    feeds.end()
    shard.end()
    layer.wait()
    finish(sends)


def back(nb, nz, given):
    own, D = given["gm_own"].shape
    cap = given["ids"].shape[0]
    half = cap // 2
    rw = given["rmerge"].shape[0]
    wl = given["q"].shape[1]
    deep = 2 * nz * half
    feed_rows = given["g_feed"].shape[2]
    shape = lambda *dims: jax.ShapeDtypeStruct(dims, BF16)
    outs = dict(
        gf_r=shape(cap, D), gf_l=jax.ShapeDtypeStruct((own, D), F32),
        g_att=shape(nb, 2, 2 * D * wl // nb // 128, 128), g_heavy=shape(2, 2 * D * rw // 128, 128),
        router=jax.ShapeDtypeStruct((1, D), F32),
        lay=shape(nb, own, D), f_feed=shape(2, feed_rows, 128),
    )
    pool = Pool()
    inner = deep <= 4096
    if inner:
        pool.vmem("keys", (deep, rw))
        pool.vmem("values", (deep, rw))
        pool.vmem("keys_t", (rw, deep))
        pool.vmem("dk", (deep, rw), F32)
        pool.vmem("dv", (deep, rw), F32)
        pool.vmem("dq_t", (rw, half), F32)
        pool.vmem("do", (half, rw))
        pool.vmem("trio", (3, half, rw))
        pool.vmem("dkv", (deep, 2 * rw))
        for name in ("bs_sib", "bs_part", "bs_came"):
            pool.vmem(name, (nz, half, 2 * rw))
    pool.vmem("low", (own, D))
    pool.vmem("do_l", (own, wl))
    pool.vmem("lk_t", (wl, own + 2 * WIN))
    pool.vmem("dkl", (own + 2 * WIN, wl), F32)
    pool.vmem("dvl", (own + 2 * WIN, wl), F32)
    pool.vmem("dql", (own, wl))
    pool.vmem("dk_own", (own, wl))
    pool.vmem("dv_own", (own, wl))
    pool.vmem("rim", (2, WIN, 2 * wl))
    pool.vmem("came_rim", (2, WIN, 2 * wl))
    pool.vmem("first_t", (D, own))
    pool.vmem("part", (cap, D))
    group_sum_scratch(pool, nb, cap, D)
    for name in ("bs_sib", "bs_rs") if inner else ():
        pool.dma(f"{name}_s", nz)
        pool.dma(f"{name}_r", nz)
    if not inner:
        given = dict(given, trio=heavy_back_plain(given))
    pool.vmem("h_feed", (feed_rows, 128))
    ShardSum.scratch(pool, nb, feed_rows, "gf")
    BlockSum.scratch(pool, nz, feed_rows, "zf")
    Gather.scratch(pool, nb, "ly")
    pool.dma("rim_s", 2)
    pool.dma("rim_r", 2)
    got = pl.pallas_call(
        functools.partial(back_kernel, nb, nz, pool, inner),
        out_shape=tuple(outs[name] for name in BACK_OUT),
        in_specs=[VM] * len(back_names(inner)),
        out_specs=tuple(HB if name == "lay" else VM for name in BACK_OUT),
        scratch_shapes=pool.shapes,
        compiler_params=pltpu.CompilerParams(
            collective_id=3, has_side_effects=True, vmem_limit_bytes=62 << 20
        ),
        cost_estimate=pl.CostEstimate(flops=80 * 10**9, bytes_accessed=200 * 2**20, transcendentals=0),
    )(*(given[name] for name in back_names(inner)))
    return dict(zip(BACK_OUT, got))


FIN_OUT = ("layer", "delta", "re", "rr", "lh", "lm", "rh", "rm", "le", "lr")


def finish_kernel(lay, dlt, rx, att, heavy, feed_in, *outs):
    o = dict(zip(FIN_OUT, outs))
    o["layer"][...] = lay[...].astype(F32)
    o["delta"][...] = dlt[...].astype(F32)
    size = rx.shape[2]
    blocks = rx.shape[1] // 3
    for core in range(2):
        for part in range(2):
            for k in range(blocks):
                at = 2 * (core * blocks + k) + part
                o["re"][pl.ds(at, size, 4 * blocks), :] = rx[core, part * blocks + k].astype(F32)
        for block, at, row, k in down_pieces(blocks * 128, size * 8):
            if row < blocks * 16:
                o["rr"][core, pl.ds(row, 32), k * 128 : (k + 1) * 128] = rx[core, 2 * blocks + block, pl.ds(at, 32)].astype(F32)

    @pl.when(pl.program_id(0) == 0)
    def _():
        for core in range(2):
            D, hl = o["lh"].shape[1:]
            start = 0
            for n in range(3):
                size = D // 2
                o["lh"][n, pl.ds(core * size, size)] = att[core, pl.ds(start, size)].astype(F32)
                start += size
            for k in range(D // 128):
                size = hl // 2
                o["lm"][pl.ds(core * size, size), k * 128 : (k + 1) * 128] = att[core, pl.ds(start, size)].astype(F32)
                start += size
            start = 0
            size = o["rm"].shape[0] // 2
            for n in range(4):
                dst = o["rm"] if n == 3 else o["rh"].at[n]
                for k in range(D // 128):
                    dst[pl.ds(core * size, size), k * 128 : (k + 1) * 128] = heavy[core, pl.ds(start, size)].astype(F32)
                    start += size
            start = 0
            fl = o["lr"].shape[0]
            lanes = fl // 128
            size = D // 2
            for part in range(2):
                for k in range(lanes):
                    o["le"][pl.ds(core * size * 2 * lanes + 2 * k + part, size, 2 * lanes), :] = feed_in[
                        core, pl.ds(start, size)
                    ].astype(F32)
                    start += size
            size = fl // 2
            for k in range(D // 128):
                o["lr"][pl.ds(core * size, size), k * 128 : (k + 1) * 128] = feed_in[core, pl.ds(start, size)].astype(F32)
                start += size


def finish_all(lay, dlt, rx, att, heavy, feed_in, hl, fl, rw):
    steps = 8
    rows, D = lay.shape
    fh = rx.shape[1] // 3 * 128
    shape = lambda *dims: jax.ShapeDtypeStruct(dims, F32)
    whole = lambda *dims: pl.BlockSpec(dims, lambda n: (0,) * len(dims))
    tall = lambda count, width: pl.BlockSpec((count // steps, width), lambda n: (n, 0))
    return dict(
        zip(
            FIN_OUT,
            pl.pallas_call(
                finish_kernel,
                grid=(steps,),
                out_shape=(
                    shape(rows, D), shape(rows, D), shape(D * 4 * fh // 128, 128), shape(2, fh, D),
                    shape(3, D, hl), shape(hl, D), shape(3, rw, D), shape(rw, D),
                    shape(D * 2 * fl // 128, 128), shape(fl, D),
                ),
                in_specs=[
                    tall(rows, D), tall(rows, D),
                    pl.BlockSpec((2, 3 * fh // 128, D // steps, 128), lambda n: (0, 0, n, 0)),
                    whole(*att.shape), whole(*heavy.shape), whole(*feed_in.shape),
                ],
                out_specs=(
                    tall(rows, D), tall(rows, D), tall(D * 4 * fh // 128, 128),
                    pl.BlockSpec((2, fh // steps, D), lambda n: (0, n, 0)),
                    whole(3, D, hl), whole(hl, D), whole(3, rw, D), whole(rw, D),
                    whole(D * 2 * fl // 128, 128), whole(fl, D),
                ),
                compiler_params=pltpu.CompilerParams(vmem_limit_bytes=50 << 20),
            )(lay, dlt, rx, att, heavy, feed_in),
        )
    )


def woven(x, width):
    blocks = width // 128
    return x.reshape(-1, blocks, 2, 128).transpose(0, 2, 1, 3).reshape(-1, 2, width)


def per_device(
    tokens,
    cotangent,
    gain_before,
    gain_middle,
    router_vector,
    local_heads,
    local_merge,
    routed_heads,
    routed_merge,
    local_expand,
    local_reduce,
    routed_expand,
    routed_reduce,
    routed_slots,
    routed_counts,
):
    nb = lax.axis_size("branch")
    nz = lax.axis_size("zz")
    b = lax.axis_index("branch")
    z = lax.axis_index("zz")
    core = lax.axis_index("core")
    d = 2 * z + core
    rows, D = tokens.shape
    own = rows // nb
    cap = routed_slots.shape[0]
    half = cap // 2
    fh = routed_expand.shape[2] // 2

    n_own = routed_counts[d]
    offset = jnp.where(core == 0, 0, cap - n_own)
    ranks = jnp.arange(cap, dtype=jnp.int32)
    live = (ranks >= offset) & (ranks < offset + n_own)
    twice = jnp.concatenate([routed_slots, routed_slots])
    rolled = lax.dynamic_slice(twice, (jnp.mod(cap - offset, cap),), (cap,))
    ids = jnp.where(live, rolled, -1)[:, None]
    rheads = routed_heads.transpose(1, 2, 0)
    f = front(
        nb, nz, tokens, cotangent, ids, gain_before[None], router_vector[None], rheads, routed_merge,
        local_heads.transpose(1, 0, 2), local_merge, local_expand.transpose(1, 0, 2), local_reduce,
    )
    tok_own = lax.dynamic_slice(tokens, (b * own, 0), (own, D))
    cot_own = lax.dynamic_slice(cotangent, (b * own, 0), (own, D))
    re_half = lax.dynamic_slice(routed_expand, (0, 0, core * fh), (D, 2, fh)).transpose(1, 0, 2)
    f = dict(
        f, tok_own=tok_own, cot_own=cot_own, ids=ids, gain=gain_middle[None], re=re_half, rr=routed_reduce,
        rmerge=routed_merge, rheads=rheads, router_vector=router_vector[None],
    )
    f = dict(f, **middle(nb, f))
    rx_sum = lax.psum(f["g_rx"], "zz")
    f = dict(f, **back(nb, nz, f))
    rx_sum, f["gf_r"] = lax.optimization_barrier((rx_sum, f["gf_r"]))
    vec = jnp.concatenate(
        [jnp.zeros((1, D), F32), f["gain_part"], f["router"], jnp.zeros((5, D), F32)], 0
    )
    f = dict(f, gain=gain_before[None], vec=vec)
    f = dict(f, **tail(nb, nz, f))
    rx_sum = lax.all_gather(rx_sum, "core")
    g = finish_all(
        f["lay"].reshape(rows, D), f["delta"].reshape(rows, D), rx_sum,
        f["f_att"], f["f_heavy"], f["f_feed"], hl=local_merge.shape[0], fl=local_reduce.shape[0],
        rw=routed_merge.shape[0],
    )
    return (
        g["layer"],
        g["delta"],
        f["vectors"][0],
        f["vectors"][1],
        f["vectors"][2],
        g["lh"].transpose(1, 0, 2),
        g["lm"],
        g["rh"].transpose(2, 0, 1),
        g["rm"],
        woven(g["le"], local_reduce.shape[0]),
        g["lr"],
        woven(g["re"], 2 * fh),
        g["rr"].reshape(2 * fh, D),
    )


def solution(mesh):
    nb = mesh.shape["branch"]
    fine = Mesh(mesh.devices.reshape(nb, -1, 2), ("branch", "zz", "core"))
    rows = P(DP, None)
    cols = P(None, None, "branch")
    deep = P("branch", None)
    return jax.shard_map(
        per_device,
        mesh=fine,
        in_specs=(
            rows, rows, P(), P(), P(), cols, deep, cols, deep, cols, deep, cols, deep, P(DP), P(),
        ),
        out_specs=(
            rows, rows, P(), P(), P(), cols, deep, cols, deep, cols, deep, cols, deep,
        ),
        check_vma=False,
    )
```

```python
import functools

import jax
import jax.numpy as jnp
from jax import lax
from jax.experimental import pallas as pl
from jax.experimental.pallas import tpu as pltpu
from jax.sharding import Mesh
from jax.sharding import PartitionSpec as P

DH = 64
WIN = 128
EPSILON = 1e-06
NEGATIVE = -1e30
HIGHEST = lax.Precision.HIGHEST
F32 = jnp.float32
BF16 = jnp.bfloat16
SCALE = DH ** (-0.5)
DP = ("zz", "core")


def mm(a, b, ca, cb):
    return lax.dot_general(a, b, (((ca,), (cb,)), ((), ())), preferred_element_type=F32)


def norm_parts(values):
    r = lax.rsqrt(jnp.mean(values * values, axis=-1, keepdims=True) + EPSILON)
    return r, values * r


def norm_back(dn, xh, r, gain):
    g = dn * gain
    return r * (g - xh * jnp.mean(g * xh, axis=-1, keepdims=True))


def gelu_parts(u):
    c = 0.7978845608028654
    t = jnp.tanh(c * (u + 0.044715 * u * u * u))
    g = 0.5 * u * (1.0 + t)
    dg = 0.5 * (1.0 + t) + 0.5 * u * (1.0 - t * t) * c * (1.0 + 3 * 0.044715 * u * u)
    return g, dg


def feed(n, seed, w_gate, w_up, w_down):
    u = mm(n, w_gate, 1, 0)
    v = mm(n, w_up, 1, 0)
    g, dg = gelu_parts(u)
    hidden = (g * v).astype(BF16)
    out = mm(hidden, w_down, 1, 0)
    dh = mm(seed, w_down, 1, 1)
    du = (dh * v * dg).astype(BF16)
    dv = (dh * g).astype(BF16)
    dn = mm(du, w_gate, 1, 1) + mm(dv, w_up, 1, 1)
    dwg = mm(n, du, 0, 0)
    dwu = mm(n, dv, 0, 0)
    dwd = mm(hidden, seed, 0, 0)
    return out, dn, dwg, dwu, dwd


MESH = pl.DeviceIdType.MESH


def remote(src, dst, send, recv, device):
    return pltpu.make_async_remote_copy(
        src_ref=src, dst_ref=dst, send_sem=send, recv_sem=recv, device_id=device, device_id_type=MESH
    )


def greet(devices):
    barrier = pltpu.get_barrier_semaphore()
    for device in devices:
        pl.semaphore_signal(barrier, inc=1, device_id=device, device_id_type=MESH)
    pl.semaphore_wait(barrier, len(devices))


def here():
    return lax.axis_index("branch"), lax.axis_index("zz"), lax.axis_index("core")


def others(me, count):
    return [lax.rem(me + k, count) for k in range(1, count)]


def band(start, size):
    return pl.ds(pl.multiple_of(start, size), size)


def finish(copies):
    for copy in copies:
        if copy.is_remote:
            copy.wait_send()
        else:
            copy.wait()


class Pool:
    def __init__(self):
        self.names = []
        self.shapes = []

    def add(self, name, shape):
        self.names.append(name)
        self.shapes.append(shape)

    def vmem(self, name, shape, dtype=BF16):
        self.add(name, pltpu.VMEM(shape, dtype))

    def dma(self, name, *shape):
        self.add(name, pltpu.SemaphoreType.DMA(shape))

    def bind(self, refs):
        return dict(zip(self.names, refs, strict=True))


def group_sum_scratch(pool, nb, rows, width):
    for name in ("gs_sib", "gs_part", "gs_came"):
        pool.vmem(name, (nb, rows // 2 // nb, width))
    for name in ("sib", "rs", "ag", "fw"):
        pool.dma(f"gs_{name}_s", nb)
        pool.dma(f"gs_{name}_r", nb)


def group_sum_steps(nb, x, o, m, meanwhile=()):
    b, z, c = here()
    half = x.shape[0] // 2
    ch = half // nb
    twin = (b, z, 1 - c)
    peers = others(b, nb)
    sib, part, came = m["gs_sib"], m["gs_part"], m["gs_came"]
    work = list(meanwhile)

    def aside():
        if work:
            work.pop(0)()

    def rows(core, j):
        return band(core * half + j * ch, ch)

    order = peers + [b]
    to_twin = [
        remote(x.at[rows(1 - c, j)], sib.at[j], m["gs_sib_s"].at[j], m["gs_sib_r"].at[j], twin)
        for j in order
    ]
    for copy in to_twin:
        copy.start()
    sends = []
    for j, copy in zip(peers, to_twin):
        copy.wait_recv()
        part[j] = (x[rows(c, j)].astype(F32) + sib[j].astype(F32)).astype(BF16)
        send = remote(part.at[j], came.at[b], m["gs_rs_s"].at[j], m["gs_rs_r"].at[b], (j, z, c))
        send.start()
        sends.append(send)
    aside()
    to_twin[-1].wait_recv()
    total = x[rows(c, b)].astype(F32) + sib[b].astype(F32)
    for j in peers:
        remote(part.at[j], came.at[j], m["gs_rs_s"].at[j], m["gs_rs_r"].at[j], (j, z, c)).wait_recv()
        total = total + came[j].astype(F32)
    mine = o.at[rows(c, b)]
    mine[...] = total.astype(BF16)
    for j in peers:
        send = remote(mine, mine, m["gs_ag_s"].at[j], m["gs_ag_r"].at[b], (j, z, c))
        send.start()
        sends.append(send)
    send = remote(mine, mine, m["gs_fw_s"].at[b], m["gs_fw_r"].at[b], twin)
    send.start()
    sends.append(send)
    aside()
    for j in peers:
        piece = o.at[rows(c, j)]
        remote(piece, piece, m["gs_ag_s"].at[j], m["gs_ag_r"].at[j], (j, z, c)).wait_recv()
        send = remote(piece, piece, m["gs_fw_s"].at[j], m["gs_fw_r"].at[j], twin)
        send.start()
        sends.append(send)
    while work:
        aside()
    for j in order:
        piece = o.at[rows(1 - c, j)]
        remote(piece, piece, m["gs_fw_s"].at[j], m["gs_fw_r"].at[j], twin).wait_recv()
    finish(to_twin + sends)


def sum_kernel(nb, pool, x, o, *scratch):
    b, z, c = here()
    greet([(b, z, 1 - c)] + [(j, z, c) for j in others(b, nb)])
    group_sum_steps(nb, x, o, pool.bind(scratch))


def group_sum(x, nb, cid):
    rows, width = x.shape
    pool = Pool()
    group_sum_scratch(pool, nb, rows, width)
    return pl.pallas_call(
        functools.partial(sum_kernel, nb, pool),
        out_shape=jax.ShapeDtypeStruct(x.shape, BF16),
        in_specs=[VM],
        out_specs=VM,
        scratch_shapes=pool.shapes,
        compiler_params=pltpu.CompilerParams(
            collective_id=cid, has_side_effects=True, vmem_limit_bytes=40 << 20
        ),
    )(x)


VM = pl.BlockSpec(memory_space=pltpu.VMEM)
HB = pl.BlockSpec(memory_space=pl.ANY)


def normed(x, gain):
    x = x.astype(F32)
    r = lax.rsqrt(jnp.mean(x * x, axis=-1, keepdims=True) + EPSILON)
    return (x * r * gain).astype(BF16)


def head_lanes(shape, h, dim):
    place = lax.broadcasted_iota(jnp.int32, shape, dim)
    return (place >= h * DH) & (place < (h + 1) * DH)


def only_head(x, h):
    return jnp.where(head_lanes(x.shape, h, 1), x, jnp.zeros_like(x))


def near_keys(shape, key_dim, first, total):
    key = lax.broadcasted_iota(jnp.int32, shape, key_dim)
    query = lax.broadcasted_iota(jnp.int32, shape, 1 - key_dim)
    gap = key - query
    return (gap >= 0) & (gap <= 2 * WIN) & (key + first >= 0) & (key + first < total)


def hot_rows(ids, count):
    spot = lax.broadcasted_iota(jnp.int32, (ids.shape[0], count), 1)
    return jnp.where(ids == spot, 1.0, 0.0).astype(BF16)


FRONT_OUT = (
    "tok_r", "cot_r", "first_r", "gate", "qr", "kv", "lh", "lm", "le", "lr", "first_w",
    "q", "k", "v", "ctx_l", "attn_l", "ctx_r", "attn_r", "mixed", "ids", "tok_own", "cot_own",
)


def front_kernel(nb, nz, pool, *refs):
    tokens, cotangent, slots, counts, vecs, rheads, rmerge, s_lh, s_lm, s_le, s_lr = refs[:11]
    out = dict(zip(FRONT_OUT, refs[11 : 11 + len(FRONT_OUT)]))
    m = pool.bind(refs[11 + len(FRONT_OUT) :])
    ids = out["ids"]
    gain, router = vecs[0:1], vecs[2:3]
    b, z, c = here()
    twin = (b, z, 1 - c)
    bpeers, zpeers = others(b, nb), others(z, nz)
    rows, D = tokens.shape
    own = rows // nb
    cap = slots.shape[0]
    half = cap // 2
    rw = rmerge.shape[0]
    after = (b, lax.rem(z + c, nz), 1 - c)
    before = (b, lax.rem(z + nz - 1 + c, nz), 1 - c)
    far = (b, lax.rem(z + nz - 1 + 2 * c, nz), 1 - c)
    greet([twin, far] + [(j, z, c) for j in bpeers] + [(b, j, c) for j in zpeers])
    sends = []

    def go(copy):
        copy.start()
        sends.append(copy)

    pairs = [(s_lh, out["lh"]), (s_lm, out["lm"]), (s_le, out["le"]), (s_lr, out["lr"])]

    def place(i, j):
        src, dst = pairs[i]
        if i in (0, 2):
            return dst.at[:, :, band(j * src.shape[2], src.shape[2])]
        return dst.at[band(j * src.shape[0], src.shape[0])]

    def cut(i, ref, core):
        if i in (0, 2):
            size = ref.shape[1] // 2
            return ref.at[:, band(core * size, size)]
        size = ref.shape[0] // 2
        return ref.at[band(core * size, size)]

    def send_weights(i):
        for j in bpeers:
            go(remote(cut(i, pairs[i][0], c), cut(i, place(i, b), c), m["w_s"].at[i, j], m["w_r"].at[i, b], (j, z, c)))

    send_weights(0)
    send_weights(1)
    for i in range(4):
        go(pltpu.make_async_copy(pairs[i][0], place(i, b), m["own_s"].at[i]))
    halo = m["halo"]
    go(remote(tokens.at[pl.ds(rows - WIN, WIN)], halo.at[0], m["halo_s"].at[0], m["halo_r"].at[0], after))
    go(remote(tokens.at[pl.ds(0, WIN)], halo.at[1], m["halo_s"].at[1], m["halo_r"].at[1], before))

    n_own = counts[2 * z + c]
    offset = jnp.where(c == 0, 0, cap - n_own)
    rank = lax.broadcasted_iota(jnp.int32, (cap, cap), 0)
    slot = lax.broadcasted_iota(jnp.int32, (cap, cap), 1)
    shift = jnp.where((rank == slot + offset) & (slot < n_own), 1.0, 0.0).astype(BF16)
    lane = lax.broadcasted_iota(jnp.int32, (cap, 128), 1)
    high, rest = slots[...] // 64, slots[...] % 64
    digits = jnp.where(lane == 0, high, jnp.where(lane == 1, rest, jnp.where(lane == 2, 1, 0)))
    found = mm(shift, digits.astype(F32).astype(BF16), 1, 0)
    ids[...] = jnp.where(found[:, 2:3] > 0.5, found[:, 0:1] * 64.0 + found[:, 1:2], -1.0).astype(jnp.int32)
    out["tok_own"][...] = tokens[band(b * own, own)]
    out["cot_own"][...] = cotangent[band(b * own, own)]
    picks, sib = m["picks"], m["sib"]
    step = cap // 4
    for k in range(4):
        at = pl.ds(k * step, step)
        hot = hot_rows(ids[at], rows)
        picks[at, :D] = mm(hot, tokens[...], 1, 0).astype(BF16)
        picks[at, D:] = mm(hot, cotangent[...], 1, 0).astype(BF16)
        go(remote(picks.at[at], sib.at[at], m["pick_s"].at[k], m["pick_r"].at[k], twin))
    for k in range(4):
        at = pl.ds(k * step, step)
        remote(picks.at[at], sib.at[at], m["pick_s"].at[k], m["pick_r"].at[k], twin).wait_recv()
        tok = picks[at, :D].astype(F32) + sib[at, :D].astype(F32)
        out["tok_r"][at] = tok.astype(BF16)
        out["cot_r"][at] = (picks[at, D:].astype(F32) + sib[at, D:].astype(F32)).astype(BF16)
        first = normed(tok, gain)
        out["first_r"][at] = first
        logit = jnp.sum(first.astype(F32) * router, axis=-1, keepdims=True)
        out["gate"][at] = 1.0 / (1.0 + jnp.exp(-logit))

    own_rows = out["first_r"][band(c * half, half)]
    out["qr"][...] = mm(own_rows, rheads[0], 1, 1).astype(BF16)
    kv = out["kv"]
    mine = kv.at[band((2 * z + c) * half, half)]
    mine[:, :rw] = mm(own_rows, rheads[1], 1, 1).astype(BF16)
    mine[:, rw:] = mm(own_rows, rheads[2], 1, 1).astype(BF16)
    for j in zpeers:
        go(remote(mine, mine, m["kv_s"].at[j], m["kv_r"].at[z], (b, j, c)))
    go(remote(mine, mine, m["kf_s"].at[z], m["kf_r"].at[z], twin))

    first_w = out["first_w"]
    first_w[pl.ds(WIN, own)] = normed(tokens[band(b * own, own)], gain)
    for i in range(2):
        remote(halo.at[i], halo.at[i], m["halo_s"].at[i], m["halo_r"].at[i], twin).wait_recv()
    lead = tokens[band(jnp.maximum(b * own - WIN, 0), WIN)]
    trail = tokens[band(jnp.minimum((b + 1) * own, rows - WIN), WIN)]
    first_w[pl.ds(0, WIN)] = normed(jnp.where(b > 0, lead, halo[0]), gain)
    first_w[pl.ds(WIN + own, WIN)] = normed(jnp.where(b < nb - 1, trail, halo[1]), gain)

    def pass_weights(i):
        for j in bpeers:
            dst = cut(i, place(i, j), c)
            remote(dst, dst, m["w_s"].at[i, j], m["w_r"].at[i, j], (j, z, c)).wait_recv()
            go(remote(dst, dst, m["wf_s"].at[i, j], m["wf_r"].at[i, j], twin))

    def take_weights(i):
        for j in bpeers:
            dst = cut(i, place(i, j), 1 - c)
            remote(dst, dst, m["wf_s"].at[i, j], m["wf_r"].at[i, j], twin).wait_recv()

    pass_weights(0)
    for j in zpeers:
        piece = kv.at[band((2 * j + c) * half, half)]
        remote(piece, piece, m["kv_s"].at[j], m["kv_r"].at[j], (b, j, c)).wait_recv()
        go(remote(piece, piece, m["kf_s"].at[j], m["kf_r"].at[j], twin))
    take_weights(0)
    send_weights(2)
    send_weights(3)
    pltpu.make_async_copy(pairs[0][0], place(0, b), m["own_s"].at[0]).wait()
    lh, q, k, v = out["lh"], out["q"], out["k"], out["v"]
    q[...] = mm(first_w[pl.ds(WIN, own)], lh[0], 1, 0).astype(BF16)
    k[...] = mm(first_w[...], lh[1], 1, 0).astype(BF16)
    v[...] = mm(first_w[...], lh[2], 1, 0).astype(BF16)
    pass_weights(1)

    blocks = own // WIN
    ctx = out["ctx_l"]
    first_key = (2 * z + c) * rows + b * own - WIN
    total = 2 * nz * rows

    def light(i, carry):
        g, n = i // blocks, lax.rem(i, blocks)
        lanes = band(g * 2 * DH, 2 * DH)
        at = band(n * WIN, WIN)
        keys = pl.ds(pl.multiple_of(n * WIN, WIN), 3 * WIN)
        q2, k2, v2 = q[at, lanes], k[keys, lanes], v[keys, lanes]
        allowed = near_keys((WIN, 3 * WIN), 1, first_key + n * WIN, total)
        parts = []
        for h in range(2):
            s = jnp.where(allowed, mm(only_head(q2, h), k2, 1, 1) * SCALE, NEGATIVE)
            w = jnp.exp(s - jnp.max(s, axis=-1, keepdims=True))
            p = (w / jnp.sum(w, axis=-1, keepdims=True)).astype(BF16)
            parts.append(mm(p, v2, 1, 0))
        ctx[at, lanes] = jnp.where(head_lanes((WIN, 2 * DH), 0, 1), parts[0], parts[1]).astype(BF16)
        return carry

    lax.fori_loop(0, blocks * (q.shape[1] // (2 * DH)), light, 0)
    take_weights(1)
    pltpu.make_async_copy(pairs[1][0], place(1, b), m["own_s"].at[1]).wait()
    attn_l = out["attn_l"]
    attn_l[...] = mm(ctx[...], out["lm"][...], 1, 0)

    for j in zpeers + [z]:
        piece = kv.at[band((2 * j + 1 - c) * half, half)]
        remote(piece, piece, m["kf_s"].at[j], m["kf_r"].at[j], twin).wait_recv()
    keys, values, qr, ctx_r = m["keys"], m["values"], out["qr"], out["ctx_r"]
    keys[...] = kv[:, :rw]
    values[...] = kv[:, rw:]
    some = 128

    def heavy(i, carry):
        at = band(i * some, some)
        got = jnp.zeros((some, rw), F32)
        for h in range(rw // DH):
            s = mm(only_head(qr[at], h), keys[...], 1, 1) * SCALE
            w = jnp.exp(s - jnp.max(s, axis=-1, keepdims=True))
            p = (w / jnp.sum(w, axis=-1, keepdims=True)).astype(BF16)
            got = jnp.where(head_lanes((some, rw), h, 1), mm(p, values[...], 1, 0), got)
        ctx_r[at] = got.astype(BF16)
        return carry

    lax.fori_loop(0, half // some, heavy, 0)
    pass_weights(2)
    attn_r = out["attn_r"]
    attn_r[...] = mm(ctx_r[...], rmerge[...], 1, 0)

    part = m["part"]
    mine_at, other_at = band(c * half, half), band((1 - c) * half, half)
    low = attn_l[...].astype(BF16)
    part[other_at] = mm(hot_rows(ids[other_at] - b * own, own), low, 1, 0).astype(BF16)
    part[mine_at] = (
        mm(hot_rows(ids[mine_at] - b * own, own), low, 1, 0) + out["gate"][mine_at] * attn_r[...]
    ).astype(BF16)
    group_sum_steps(nb, part, out["mixed"], m, [lambda: pass_weights(3)])
    take_weights(2)
    take_weights(3)
    finish([copy for copy in sends if copy.is_remote])
    for i in (2, 3):
        pltpu.make_async_copy(pairs[i][0], place(i, b), m["own_s"].at[i]).wait()


def front(nb, nz, tokens, cotangent, slots, counts, vecs, rheads, rmerge, s_lh, s_lm, s_le, s_lr):
    rows, D = tokens.shape
    own = rows // nb
    cap = slots.shape[0]
    half = cap // 2
    rw = rmerge.shape[0]
    wl = nb * s_lm.shape[0]
    shape = lambda *dims: jax.ShapeDtypeStruct(dims, BF16)
    shape32 = lambda *dims: jax.ShapeDtypeStruct(dims, F32)
    outs = dict(
        tok_r=shape(cap, D), cot_r=shape(cap, D), first_r=shape(cap, D), gate=shape32(cap, 1),
        qr=shape(half, rw), kv=shape(2 * nz * half, 2 * rw),
        lh=shape(3, D, wl), lm=shape(wl, D),
        le=shape(2, D, nb * s_le.shape[2]), lr=shape(nb * s_lr.shape[0], D),
        first_w=shape(own + 2 * WIN, D), q=shape(own, wl), k=shape(own + 2 * WIN, wl),
        v=shape(own + 2 * WIN, wl), ctx_l=shape(own, wl), attn_l=shape32(own, D),
        ctx_r=shape(half, rw), attn_r=shape32(half, D), mixed=shape(cap, D),
        ids=jax.ShapeDtypeStruct((cap, 1), jnp.int32), tok_own=shape(own, D), cot_own=shape(own, D),
    )
    pool = Pool()
    pool.vmem("picks", (cap, 2 * D))
    pool.vmem("sib", (cap, 2 * D))
    pool.vmem("halo", (2, WIN, D))
    pool.vmem("keys", (2 * nz * half, rw))
    pool.vmem("values", (2 * nz * half, rw))
    pool.vmem("part", (cap, D))
    group_sum_scratch(pool, nb, cap, D)
    pool.dma("own_s", 4)
    pool.dma("halo_s", 2)
    pool.dma("halo_r", 2)
    pool.dma("pick_s", 4)
    pool.dma("pick_r", 4)
    for name in ("w", "wf"):
        pool.dma(f"{name}_s", 4, nb)
        pool.dma(f"{name}_r", 4, nb)
    for name in ("kv", "kf"):
        pool.dma(f"{name}_s", nz)
        pool.dma(f"{name}_r", nz)
    got = pl.pallas_call(
        functools.partial(front_kernel, nb, nz, pool),
        out_shape=tuple(outs[name] for name in FRONT_OUT),
        in_specs=[VM] * 3 + [pl.BlockSpec(memory_space=pltpu.SMEM)] + [VM] * 3 + [HB] * 4,
        out_specs=tuple(HB if name in ("le", "lr") else VM for name in FRONT_OUT),
        scratch_shapes=pool.shapes,
        compiler_params=pltpu.CompilerParams(
            collective_id=0, has_side_effects=True, vmem_limit_bytes=56 << 20
        ),
    )(tokens, cotangent, slots, counts, vecs, rheads, rmerge, s_lh, s_lm, s_le, s_lr)
    return dict(zip(FRONT_OUT, got))


MID_IN = (
    "tok_own", "cot_own", "ids", "vecs", "tok_r", "cot_r", "gate", "mixed", "attn_l",
    "le", "lr", "re", "rr",
)
MID_OUT = ("layer", "gm_own", "gm_r", "gate_feed", "gain_part", "g_feed", "g_rx")


def lane_blocks(x):
    return [x[:, n * 128 : (n + 1) * 128] for n in range(x.shape[1] // 128)]


def pack_rows(g, start, parts):
    for part in parts:
        size = part.shape[0] // 2
        for core in range(2):
            g[core, pl.ds(start, size)] = part[core * size : (core + 1) * size].astype(BF16)
        start += size
    return start


def down_pieces(rows, D):
    steps = 8
    per, step = D // steps // 32, rows // steps
    pieces = []
    for n in range(steps):
        spots = [(r, k) for k in range(D // 128) for r in range(0, step, 32)]
        pieces += [(p // per, n * (D // steps) + p % per * 32, n * step + r, k) for p, (r, k) in enumerate(spots)]
    return pieces


def pack_down(g, start, x):
    for block, at, row, k in down_pieces(*x.shape):
        g[start + block, pl.ds(at, 32)] = x[row : row + 32, k * 128 : (k + 1) * 128].astype(BF16)


def mid_kernel(nb, pool, *refs):
    i = dict(zip(MID_IN, refs[: len(MID_IN)]))
    out = dict(zip(MID_OUT, refs[len(MID_IN) : len(MID_IN) + len(MID_OUT)]))
    m = pool.bind(refs[len(MID_IN) + len(MID_OUT) :])
    b, z, c = here()
    greet([(b, z, 1 - c)] + [(j, z, c) for j in others(b, nb)])
    own, D = i["tok_own"].shape
    cap = i["ids"].shape[0]
    fl = i["le"].shape[2] // nb
    fh = i["re"].shape[2]
    gain = i["vecs"][1:2]

    pick, pick_t = m["pick"], m["pick_t"]
    hot = hot_rows(i["ids"][...] - b * own, own)
    pick[...] = hot
    pick_t[...] = hot.T
    owned = jnp.sum(pick_t[...].astype(F32), axis=1, keepdims=True) > 0.5
    mid_o, mid_r = m["mid_o"], m["mid_r"]
    mid_o[...] = i["tok_own"][...].astype(F32) + jnp.where(
        owned, mm(pick_t[...], i["mixed"][...], 1, 0), i["attn_l"][...]
    )
    mid_r[...] = i["tok_r"][...].astype(F32) + i["mixed"][...].astype(F32)
    n_o, n_r = m["n_o"], m["n_r"]
    n_o[...] = normed(mid_o[...], gain)
    n_r[...] = normed(mid_r[...], gain)
    gate = i["gate"][...]
    seed_r = m["seed_r"]
    seed_r[...] = (gate * i["cot_r"][...].astype(F32)).astype(BF16)

    def both_ways(n, seed, expand, narrow, row0, tile, count, hid, du, dv, ff, dn):
        def one(t, carry):
            lanes = band(t * tile, tile)
            wd = narrow[band(row0 + t * tile, tile)]
            u = mm(n[...], expand[0, :, lanes], 1, 0)
            v = mm(n[...], expand[1, :, lanes], 1, 0)
            g, dg = gelu_parts(u)
            low = (g * v).astype(BF16)
            hid[:, lanes] = low
            dh = mm(seed[...], wd, 1, 1)
            du[:, lanes] = (dh * v * dg).astype(BF16)
            dv[:, lanes] = (dh * g).astype(BF16)
            one_ff = mm(low, wd, 1, 0)
            one_dn = mm(du[:, lanes], expand[0, :, lanes], 1, 1) + mm(dv[:, lanes], expand[1, :, lanes], 1, 1)
            ff[...] = jnp.where(t == 0, one_ff, ff[...] + one_ff)
            dn[...] = jnp.where(t == 0, one_dn, dn[...] + one_dn)
            return carry

        lax.fori_loop(0, count, one, 0)

    ff_r, dn_r, ff_o, dn_o = m["ff_r"], m["dn_r"], m["ff_o"], m["dn_o"]
    both_ways(
        n_r, seed_r, i["re"], i["rr"], c * fh, fl, fh // fl, m["hid_r"], m["du_r"], m["dv_r"], ff_r, dn_r
    )
    both_ways(
        n_o, i["cot_own"], i["le"], i["lr"], 0, fl, nb, m["hid_o"], m["du_o"], m["dv_o"], ff_o, dn_o
    )
    out["gate_feed"][...] = jnp.sum(i["cot_r"][...].astype(F32) * ff_r[...], axis=-1, keepdims=True)
    part = m["part"]
    part[:, :D] = ff_r[...].astype(BF16)
    part[:, D:] = (dn_r[...] + mm(pick[...], dn_o[...].astype(BF16), 1, 0)).astype(BF16)

    n_t = m["n_t"]

    def weights_heavy():
        n_t[...] = n_r[...].T
        gx = out["g_rx"]
        for k, x in enumerate(lane_blocks(mm(n_t[...], m["du_r"][...], 1, 0)) + lane_blocks(mm(n_t[...], m["dv_r"][...], 1, 0))):
            gx[k] = x.astype(BF16)
        pack_down(gx, 2 * fh // 128, mm(m["hid_r"][...], seed_r[...], 0, 0))

    def weights_light():
        n_t[...] = n_o[...].T
        g = out["g_feed"]

        def one(t, carry):
            lanes = band(t * fl, fl)
            gate_part = mm(n_t[...], m["du_o"][:, lanes], 1, 0)
            up_part = mm(n_t[...], m["dv_o"][:, lanes], 1, 0)
            down = mm(m["hid_o"][:, lanes], i["cot_own"][...], 0, 0)
            pack_rows(g.at[t], 0, lane_blocks(gate_part) + lane_blocks(up_part) + lane_blocks(down))
            return carry

        lax.fori_loop(0, nb, one, 0)

    sums = m["sums"]
    group_sum_steps(nb, part, sums, m, [weights_heavy, weights_light])
    dn_sum = sums[:, D:]
    scaled = (gate * sums[:, :D].astype(F32)).astype(BF16)
    out["layer"][...] = (mid_o[...] + ff_o[...] + mm(pick_t[...], scaled, 1, 0)).astype(BF16)
    dn_own = jnp.where(owned, mm(pick_t[...], dn_sum, 1, 0), dn_o[...])
    r, xh = norm_parts(mid_o[...])
    out["gm_own"][...] = i["cot_own"][...].astype(F32) + norm_back(dn_own, xh, r, gain)
    out["gain_part"][...] = jnp.sum(dn_own * xh, axis=0, keepdims=True)
    r, xh = norm_parts(mid_r[...])
    out["gm_r"][...] = i["cot_r"][...].astype(F32) + norm_back(dn_sum.astype(F32), xh, r, gain)


def middle(nb, given):
    own, D = given["tok_own"].shape
    cap = given["ids"].shape[0]
    wide = given["le"].shape[2]
    fl = wide // nb
    fh = given["re"].shape[2]
    shape = lambda *dims: jax.ShapeDtypeStruct(dims, BF16)
    shape32 = lambda *dims: jax.ShapeDtypeStruct(dims, F32)
    packed = (2 * D * fl + fl * D) // 2 // 128
    outs = dict(
        layer=shape(own, D), gm_own=shape32(own, D), gm_r=shape32(cap, D), gate_feed=shape32(cap, 1),
        gain_part=shape32(1, D), g_feed=shape(nb, 2, packed, 128), g_rx=shape(3 * fh // 128, D, 128),
    )
    pool = Pool()
    pool.vmem("pick", (cap, own))
    pool.vmem("pick_t", (own, cap))
    for name, count in (("o", own), ("r", cap)):
        pool.vmem(f"mid_{name}", (count, D), F32)
        pool.vmem(f"n_{name}", (count, D))
        pool.vmem(f"ff_{name}", (count, D), F32)
        pool.vmem(f"dn_{name}", (count, D), F32)
        for kind in ("hid", "du", "dv"):
            pool.vmem(f"{kind}_{name}", (count, wide if name == "o" else fh))
    pool.vmem("seed_r", (cap, D))
    pool.vmem("n_t", (D, own))
    pool.vmem("part", (cap, 2 * D))
    pool.vmem("sums", (cap, 2 * D))
    group_sum_scratch(pool, nb, cap, 2 * D)
    got = pl.pallas_call(
        functools.partial(mid_kernel, nb, pool),
        out_shape=tuple(outs[name] for name in MID_OUT),
        in_specs=[VM] * len(MID_IN),
        out_specs=(VM,) * len(MID_OUT),
        scratch_shapes=pool.shapes,
        compiler_params=pltpu.CompilerParams(
            collective_id=2, has_side_effects=True, vmem_limit_bytes=60 << 20
        ),
    )(*(given[name] for name in MID_IN))
    return dict(zip(MID_OUT, got))


def neighbours(b):
    return b + 1 - 2 * lax.rem(b, 2), lax.rem(b + 2, 4), 3 - b


class Gather:
    def __init__(self, src, dst, m, name):
        b, z, c = here()
        self.src, self.dst, self.m, self.name, self.b = src, dst, m, name, b
        self.bx, self.by, self.bd = neighbours(b)
        self.dx, self.dy = (self.bx, z, c), (self.by, z, c)
        self.sends = []

    def half(self, ref, k):
        size = self.src.shape[0] // 2
        return ref.at[pl.ds(k * size, size)]

    def go(self, copy):
        copy.start()
        self.sends.append(copy)

    def copy(self, way, k, src, slot, device):
        m, n = self.m, self.name
        return remote(
            self.half(src, k), self.half(self.dst.at[slot], k), m[f"{n}_{way}_s"].at[k], m[f"{n}_{way}_r"].at[k], device
        )

    def start(self):
        own = pltpu.make_async_copy(self.src, self.dst.at[self.b], self.m[f"{self.name}_own"].at[0])
        self.go(own)
        for first, second in ((0, 1), (1, 0)):
            self.go(self.copy("x", second, self.src, self.b, self.dx))
            self.go(self.copy("y", first, self.src, self.b, self.dy))

    def relay(self):
        came = self.dst.at[self.bx]
        self.copy("x", 1, came, self.bx, self.dx).wait_recv()
        self.go(self.copy("f", 1, came, self.bx, self.dy))
        came = self.dst.at[self.by]
        self.copy("y", 0, came, self.by, self.dy).wait_recv()
        self.go(self.copy("f", 0, came, self.by, self.dx))

    def wait(self):
        self.copy("x", 0, self.dst.at[self.bx], self.bx, self.dx).wait_recv()
        self.copy("y", 1, self.dst.at[self.by], self.by, self.dy).wait_recv()
        far = self.dst.at[self.bd]
        self.copy("f", 0, far, self.bd, self.dx).wait_recv()
        self.copy("f", 1, far, self.bd, self.dy).wait_recv()
        finish(self.sends)

    @staticmethod
    def scratch(pool, name):
        pool.dma(f"{name}_own", 1)
        for way in ("x", "y", "f"):
            pool.dma(f"{name}_{way}_s", 2)
            pool.dma(f"{name}_{way}_r", 2)


class ShardSum:
    def __init__(self, g, h, m, name):
        self.b, self.z, self.c = here()
        self.bx, self.by, self.bd = neighbours(self.b)
        self.g, self.h, self.m, self.name = g, h, m, name
        self.sib = m[f"{name}_sib"]
        size = g.shape[2] // 2
        self.parts = (pl.ds(0, size), pl.ds(size, size))
        self.sends = []

    def go(self, copy):
        copy.start()
        self.sends.append(copy)

    def pair(self, j):
        m, n = self.m, self.name
        return remote(
            self.g.at[j, 1 - self.c], self.sib.at[j], m[f"{n}_a_s"].at[j], m[f"{n}_a_r"].at[j],
            (self.b, self.z, 1 - self.c),
        )

    def start(self):
        for j in (self.bd, self.bx, self.by, self.b):
            self.go(self.pair(j))

    def step(self, n, src, k):
        m = self.m
        device = (self.bx if n in (0, 1, 5) else self.by, self.z, self.c)
        return remote(
            src.at[self.parts[k]], m[f"{self.name}_came"].at[n], m[f"{self.name}_b_s"].at[n], m[f"{self.name}_b_r"].at[n],
            device,
        )

    def add(self, j):
        self.pair(j).wait_recv()
        self.sib[j] = (self.g[j, self.c].astype(F32) + self.sib[j].astype(F32)).astype(BF16)

    def spread(self):
        self.add(self.bd)
        self.go(self.step(1, self.sib.at[self.bd], 0))
        self.go(self.step(3, self.sib.at[self.bd], 1))
        self.add(self.bx)
        self.go(self.step(0, self.sib.at[self.bx], 0))
        self.add(self.by)
        self.go(self.step(2, self.sib.at[self.by], 1))
        self.add(self.b)

    def relay(self):
        came = self.m[f"{self.name}_came"]
        for n, j, k, then in ((1, self.by, 0, 4), (3, self.bx, 1, 5)):
            self.step(n, self.sib.at[j], k).wait_recv()
            at = self.parts[k]
            self.sib[j, at] = (self.sib[j, at].astype(F32) + came[n].astype(F32)).astype(BF16)
            self.go(self.step(then, self.sib.at[j], k))

    def collect(self):
        came = self.m[f"{self.name}_came"]
        for k, one, two in ((0, 0, 4), (1, 2, 5)):
            at = self.parts[k]
            self.step(one, self.sib.at[self.b], k).wait_recv()
            self.step(two, self.sib.at[self.b], k).wait_recv()
            total = self.sib[self.b, at].astype(F32) + came[one].astype(F32) + came[two].astype(F32)
            self.h[at] = total.astype(BF16)

    def end(self):
        finish(self.sends)

    @staticmethod
    def scratch(pool, rows, name):
        pool.vmem(f"{name}_sib", (4, rows, 128))
        pool.vmem(f"{name}_came", (6, rows // 2, 128))
        pool.dma(f"{name}_a_s", 4)
        pool.dma(f"{name}_a_r", 4)
        pool.dma(f"{name}_b_s", 6)
        pool.dma(f"{name}_b_r", 6)


class ChainSum:
    def __init__(self, nz, pieces, h, f, m, name):
        self.b, self.z, self.c = here()
        self.nz, self.pieces, self.h, self.f, self.m, self.name = nz, pieces, h, f, m, name
        self.ch = h.shape[0] // 2 // pieces
        self.steps = pieces + 2 * (nz - 1)
        self.next = 0

    def rows(self, side, p):
        return band(side * self.pieces * self.ch + p * self.ch, self.ch)

    def copies(self, side, p):
        m, n = self.m, self.name
        came = m[f"{n}_came"].at[side, p]
        piece = self.f.at[self.c, self.rows(side, p)]
        step = 1 - 2 * side
        on = (self.b, lax.rem(self.z + step + self.nz, self.nz), self.c)
        back = (self.b, lax.rem(self.z - step + self.nz, self.nz), self.c)
        over = (self.b, self.z, 1 - self.c)
        sem = lambda kind: m[f"{n}_{kind}"].at[side, p]
        return (
            lambda src: remote(src, came, sem("a_s"), sem("a_r"), on),
            lambda src: remote(src, piece, sem("b_s"), sem("b_r"), back),
            lambda src: remote(src, piece, sem("c_s"), sem("c_r"), over),
            piece,
        )

    def pump(self, s):
        last = self.nz - 1
        for side in range(2):
            pos = self.z if side == 0 else last - self.z
            p = s - pos

            @pl.when((p >= 0) & (p < self.pieces))
            def _():
                on, back, over, piece = self.copies(side, p)
                own = self.h.at[self.rows(side, p)]
                came = self.m[f"{self.name}_came"].at[side, p]

                @pl.when(pos == 0)
                def _():
                    on(own).start()

                @pl.when(pos > 0)
                def _():
                    on(came).wait_recv()
                    came[...] = (own[...].astype(F32) + came[...].astype(F32)).astype(BF16)

                @pl.when((pos > 0) & (pos < last))
                def _():
                    on(came).start()

                @pl.when(pos == last)
                def _():
                    pltpu.make_async_copy(came, piece, self.m[f"{self.name}_own"].at[side, p]).start()
                    back(came).start()
                    over(came).start()

            q = s - last - (last - pos)

            @pl.when((q >= 0) & (q < self.pieces) & (pos < last))
            def _():
                on, back, over, piece = self.copies(side, q)
                back(piece).wait_recv()
                over(piece).start()

                @pl.when(pos > 0)
                def _():
                    back(piece).start()

    def go(self, count=None):
        upto = self.steps if count is None else min(self.steps, self.next + count)
        if upto - self.next > 4:
            lax.fori_loop(self.next, upto, lambda s, carry: (self.pump(s), carry)[1], 0)
        else:
            for s in range(self.next, upto):
                self.pump(s)
        self.next = upto

    def end(self):
        self.go()
        last = self.nz - 1

        def one(p, carry):
            for side in range(2):
                pos = self.z if side == 0 else last - self.z
                on, back, over, piece = self.copies(side, p)
                other = self.f.at[1 - self.c, self.rows(side, p)]
                came = self.m[f"{self.name}_came"].at[side, p]
                sem = lambda kind: self.m[f"{self.name}_{kind}"].at[side, p]
                remote(other, other, sem("c_s"), sem("c_r"), (self.b, self.z, 1 - self.c)).wait_recv()
                over(piece).wait_send()

                @pl.when(pos < last)
                def _():
                    on(came).wait_send()

                @pl.when(pos > 0)
                def _():
                    back(piece).wait_send()

                @pl.when(pos == last)
                def _():
                    pltpu.make_async_copy(came, piece, self.m[f"{self.name}_own"].at[side, p]).wait()

            return carry

        lax.fori_loop(0, self.pieces, one, 0)

    @staticmethod
    def scratch(pool, rows, pieces, name):
        pool.vmem(f"{name}_came", (2, pieces, rows // 2 // pieces, 128))
        for kind in ("a_s", "a_r", "b_s", "b_r", "c_s", "c_r", "own"):
            pool.dma(f"{name}_{kind}", 2, pieces)


TAIL_IN = ("g_att", "g_heavy", "h_feed", "gm_own", "gf_l", "gf_r", "ids", "tok_own", "vecs", "gain_part", "router")
TAIL_OUT = ("delta", "f_att", "f_heavy", "f_feed", "vectors")


def tail_kernel(nb, nz, pool, *refs):
    i = dict(zip(TAIL_IN, refs[: len(TAIL_IN)]))
    out = dict(zip(TAIL_OUT, refs[len(TAIL_IN) : len(TAIL_IN) + len(TAIL_OUT)]))
    m = pool.bind(refs[len(TAIL_IN) + len(TAIL_OUT) :])
    b, z, c = here()
    twin = (b, z, 1 - c)
    bpeers, zpeers = others(b, nb), others(z, nz)
    own, D = i["gm_own"].shape
    greet([twin] + [(j, z, c) for j in bpeers] + [(b, j, c) for j in zpeers])
    gh, sib_h, h_heavy = i["g_heavy"], m["sib_h"], m["h_heavy"]
    to_twin = remote(gh.at[1 - c], sib_h, m["sib_h_s"].at[0], m["sib_h_r"].at[0], twin)
    to_twin.start()
    shard = ShardSum(i["g_att"], m["h_att"], m, "ga")
    shard.start()
    feeds = ChainSum(nz, 4, i["h_feed"], out["f_feed"], m, "zf")
    heavy = ChainSum(nz, 4, h_heavy, out["f_heavy"], m, "zh")
    att = ChainSum(nz, 4, m["h_att"], out["f_att"], m, "za")
    feeds.go(1)
    shard.spread()
    to_twin.wait_recv()
    h_heavy[...] = (gh[c].astype(F32) + sib_h[...].astype(F32)).astype(BF16)
    feeds.go(1)
    heavy.go(1)

    hot_t = hot_rows(i["ids"][...] - b * own, own).T
    owned = jnp.sum(hot_t.astype(F32), axis=1, keepdims=True) > 0.5
    gf = jnp.where(owned, mm(hot_t, i["gf_r"][...], 1, 0), i["gf_l"][...])
    r, xh = norm_parts(i["tok_own"][...].astype(F32))
    gain_part = jnp.sum(gf * xh, axis=0, keepdims=True)
    low = m["low"]
    low[...] = (i["gm_own"][...] + norm_back(gf, xh, r, i["vecs"][0:1])).astype(BF16)
    rows = Gather(low, out["delta"], m, "td")
    rows.start()
    shard.relay()
    feeds.go(1)
    heavy.go(1)

    vec = m["vec_mine"]
    vec[...] = jnp.zeros_like(vec)
    vec[pl.ds(0, 1)] = gain_part
    vec[pl.ds(1, 1)] = i["gain_part"][...]
    vec[pl.ds(2, 1)] = i["router"][...]
    sends = [to_twin]

    def vec_step(name, me, peers, device):
        got = m[f"{name}_got"]
        got[me] = vec[...]
        for j in peers:
            copy = remote(vec, got.at[me], m[f"{name}_s"].at[j], m[f"{name}_r"].at[me], device(j))
            copy.start()
            sends.append(copy)

    def vec_end(name, peers, device):
        got = m[f"{name}_got"]
        for j in peers:
            remote(got.at[j], got.at[j], m[f"{name}_s"].at[j], m[f"{name}_r"].at[j], device(j)).wait_recv()
        return functools.reduce(lambda x, y: x + y, [got[j] for j in range(got.shape[0])])

    by_core, by_branch, by_block = (lambda j: (b, z, j)), (lambda j: (j, z, c)), (lambda j: (b, j, c))
    vec_step("vc", c, [1 - c], by_core)
    feeds.go(1)
    heavy.go(1)
    shard.collect()
    att.go(1)
    total = vec_end("vc", [1 - c], by_core)
    vec2 = m["vec_pair"]
    vec2[...] = total
    vec = vec2
    vec_step("vb", b, bpeers, by_branch)
    feeds.go(1)
    heavy.go(1)
    att.go(1)
    rows.relay()
    total = vec_end("vb", bpeers, by_branch)
    vec3 = m["vec_group"]
    vec3[...] = total
    vec = vec3
    vec_step("vz", z, zpeers, by_block)
    while att.next < att.steps:
        feeds.go(1)
        heavy.go(1)
        att.go(1)
    out["vectors"][...] = vec_end("vz", zpeers, by_block)
    feeds.end()
    heavy.end()
    att.end()
    shard.end()
    rows.wait()
    finish(sends)


def tail(nb, nz, given):
    own, D = given["gm_own"].shape
    ra, rh, rf = given["g_att"].shape[2], given["g_heavy"].shape[1], given["h_feed"].shape[0]
    shape = lambda *dims: jax.ShapeDtypeStruct(dims, BF16)
    outs = dict(
        delta=shape(nb, own, D), f_att=shape(2, ra, 128), f_heavy=shape(2, rh, 128), f_feed=shape(2, rf, 128),
        vectors=jax.ShapeDtypeStruct((8, D), F32),
    )
    pool = Pool()
    pool.vmem("sib_h", (rh, 128))
    pool.vmem("h_heavy", (rh, 128))
    pool.vmem("h_att", (ra, 128))
    pool.vmem("low", (own, D))
    pool.dma("sib_h_s", 1)
    pool.dma("sib_h_r", 1)
    ShardSum.scratch(pool, ra, "ga")
    ChainSum.scratch(pool, ra, 4, "za")
    ChainSum.scratch(pool, rh, 4, "zh")
    ChainSum.scratch(pool, rf, 4, "zf")
    Gather.scratch(pool, "td")
    for name in ("vec_mine", "vec_pair", "vec_group"):
        pool.vmem(name, (8, D), F32)
    for name, count in (("vc", 2), ("vb", nb), ("vz", nz)):
        pool.vmem(f"{name}_got", (count, 8, D), F32)
        pool.dma(f"{name}_s", count)
        pool.dma(f"{name}_r", count)
    got = pl.pallas_call(
        functools.partial(tail_kernel, nb, nz, pool),
        out_shape=tuple(outs[name] for name in TAIL_OUT),
        in_specs=[VM] * len(TAIL_IN),
        out_specs=(HB,) * 4 + (VM,),
        scratch_shapes=pool.shapes,
        compiler_params=pltpu.CompilerParams(
            collective_id=4, has_side_effects=True, vmem_limit_bytes=56 << 20
        ),
    )(*(given[name] for name in TAIL_IN))
    return dict(zip(TAIL_OUT, got))


RX_PIECES = 8
BACK_OUT = ("gf_r", "gf_l", "g_att", "g_heavy", "router", "lay", "h_feed", "f_rx")
BACK_IN = (
    "gm_own", "gm_r", "gate", "gate_feed", "ids", "q", "k", "v", "lm", "lh", "first_w", "ctx_l",
    "qr", "kv", "rmerge", "rheads", "first_r", "ctx_r", "attn_r", "vecs",
    "layer", "g_feed", "g_rx",
)


def back_names(inner):
    return BACK_IN if inner else BACK_IN + ("trio",)


def heavy_back(i, m, seed, x, chain):
    kv, qr = i["kv"], i["qr"]
    half, rw = qr.shape
    keys, values, keys_t, dk, dv, dq_t, do = (
        m[n] for n in ("keys", "values", "keys_t", "dk", "dv", "dq_t", "do")
    )
    keys[...] = kv[:, :rw]
    values[...] = kv[:, rw:]
    keys_t[...] = keys[...].T
    do[...] = mm(seed, i["rmerge"][...], 1, 1).astype(BF16)
    dk[...] = jnp.zeros_like(dk)
    dv[...] = jnp.zeros_like(dv)
    dq_t[...] = jnp.zeros_like(dq_t)
    some = 128

    def heavy(n, carry):
        at = band(n * some, some)
        for h in range(rw // DH):
            chain.pump(n * (rw // DH) + h)
            qh, doh = only_head(qr[at], h), only_head(do[at], h)
            s = mm(keys[...], qh, 1, 1) * SCALE
            w = jnp.exp(s - jnp.max(s, axis=0, keepdims=True))
            p = w * (1.0 / jnp.sum(w, axis=0, keepdims=True))
            dp = mm(values[...], doh, 1, 1)
            ds = (p * (dp - jnp.sum(p * dp, axis=0, keepdims=True))).astype(BF16)
            dk[...] += mm(ds, qh, 1, 0)
            dv[...] += mm(p.astype(BF16), doh, 1, 0)
            got = mm(keys_t[...], ds, 1, 0)
            dq_t[:, at] += jnp.where(head_lanes(got.shape, h, 0), got, 0.0)
        return carry

    lax.fori_loop(0, half // some, heavy, 0)
    chain.next = half // some * (rw // DH)
    x[:, :rw] = (dk[...] * SCALE).astype(BF16)
    x[:, rw:] = dv[...].astype(BF16)


def heavy_back_plain(i):
    half, rw = i["qr"].shape
    split = lambda y: y.reshape(y.shape[0], -1, DH)
    at = lax.axis_index("core") * half
    seed = (i["gate"] * i["gm_r"]).astype(BF16)
    seed = lax.dynamic_slice(seed, (at, 0), (half, seed.shape[1]))
    do = split(mm(seed, i["rmerge"], 1, 1).astype(BF16))
    q, k, v = split(i["qr"]), split(i["kv"][:, :rw]), split(i["kv"][:, rw:])
    p = jax.nn.softmax(jnp.einsum("qhe,khe->hqk", q, k, preferred_element_type=F32) * SCALE, axis=-1)
    dp = jnp.einsum("qhe,khe->hqk", do, v, preferred_element_type=F32)
    ds = (p * (dp - jnp.sum(p * dp, -1, keepdims=True))).astype(BF16)
    dq = jnp.einsum("hqk,khe->qhe", ds, k, preferred_element_type=F32) * SCALE
    dk = jnp.einsum("hqk,qhe->khe", ds, q, preferred_element_type=F32) * SCALE
    dv = jnp.einsum("hqk,qhe->khe", p.astype(BF16), do, preferred_element_type=F32)
    both = jnp.concatenate([dk.reshape(-1, rw), dv.reshape(-1, rw)], 1).astype(BF16)
    both = lax.psum_scatter(both, DP, scatter_dimension=0, tiled=True)
    return jnp.stack([dq.reshape(half, rw).astype(BF16), both[:, :rw], both[:, rw:]], 0)


def back_kernel(nb, nz, pool, inner, *refs):
    names = back_names(inner)
    i = dict(zip(names, refs[: len(names)]))
    out = dict(zip(BACK_OUT, refs[len(names) : len(names) + len(BACK_OUT)]))
    m = pool.bind(refs[len(names) + len(BACK_OUT) :])
    b, z, c = here()
    twin = (b, z, 1 - c)
    bpeers, zpeers = others(b, nb), others(z, nz)
    own, D = i["gm_own"].shape
    rows = own * nb
    cap = i["ids"].shape[0]
    half = cap // 2
    rw = i["rmerge"].shape[0]
    wl = i["q"].shape[1]
    last, first = b == nb - 1, b == 0
    after = (
        jnp.where(last, 0, b + 1), jnp.where(last, lax.rem(z + c, nz), z), jnp.where(last, 1 - c, c),
    )
    before = (
        jnp.where(first, nb - 1, b - 1),
        jnp.where(first, lax.rem(z + nz - 1 + c, nz), z),
        jnp.where(first, 1 - c, c),
    )
    greet([twin, after, before] + [(j, z, c) for j in bpeers] + [(b, j, c) for j in zpeers])
    mine_at, other_at = band(c * half, half), band((1 - c) * half, half)
    sends = []
    layer = Gather(i["layer"], out["lay"], m, "ly")
    shard = ShardSum(i["g_feed"], out["h_feed"], m, "gf")
    chain = ChainSum(nz, RX_PIECES, i["g_rx"], out["f_rx"], m, "zx")
    shard.start()
    layer.start()

    def go(copy):
        copy.start()
        sends.append(copy)

    gm_half = i["gm_r"][mine_at]
    gate_half = i["gate"][mine_at]
    seed = (gate_half * gm_half).astype(BF16)
    pack_rows(out["g_heavy"], 3 * rw // 2 * (D // 128), lane_blocks(mm(i["ctx_r"][...], seed, 0, 0)))
    trio = m["trio"] if inner else i["trio"]

    def spot(core, j):
        return band((2 * j + core) * half, half)

    def to_twin(j):
        return remote(x.at[spot(1 - c, j)], sib.at[j], m["bs_sib_s"].at[j], m["bs_sib_r"].at[j], twin)

    shard.spread()
    if inner:
        x, sib, part, came = m["dkv"], m["bs_sib"], m["bs_part"], m["bs_came"]
        heavy_back(i, m, seed, x, chain)
        for j in zpeers + [z]:
            go(to_twin(j))

    shard.relay()
    layer.relay()
    low, do_l = m["low"], m["do_l"]
    low[...] = i["gm_own"][...].astype(BF16)
    do_l[...] = mm(low[...], i["lm"][...], 1, 1).astype(BF16)
    for j in zpeers if inner else []:
        to_twin(j).wait_recv()
        part[j] = (x[spot(c, j)].astype(F32) + sib[j].astype(F32)).astype(BF16)
        go(remote(part.at[j], came.at[z], m["bs_rs_s"].at[j], m["bs_rs_r"].at[z], (b, j, c)))

    q, k, v = i["q"], i["k"], i["v"]
    lk_t, dkl, dvl, dql = m["lk_t"], m["dkl"], m["dvl"], m["dql"]
    lk_t[...] = k[...].T
    dkl[...] = jnp.zeros_like(dkl)
    dvl[...] = jnp.zeros_like(dvl)
    blocks = own // WIN
    first_key = (2 * z + c) * rows + b * own - WIN
    total = 2 * nz * rows

    def light(n_, carry):
        g, n = n_ // blocks, lax.rem(n_, blocks)
        lanes = band(g * 2 * DH, 2 * DH)
        at = band(n * WIN, WIN)
        near = pl.ds(pl.multiple_of(n * WIN, WIN), 3 * WIN)
        q2, do2, k2, v2, kt2 = q[at, lanes], do_l[at, lanes], k[near, lanes], v[near, lanes], lk_t[lanes, near]
        allowed = near_keys((3 * WIN, WIN), 0, first_key + n * WIN, total)
        got_k = got_v = None
        got_q = []
        for h in range(2):
            qh, doh = only_head(q2, h), only_head(do2, h)
            s = jnp.where(allowed, mm(k2, qh, 1, 1) * SCALE, NEGATIVE)
            w = jnp.exp(s - jnp.max(s, axis=0, keepdims=True))
            p = w * (1.0 / jnp.sum(w, axis=0, keepdims=True))
            dp = mm(v2, doh, 1, 1)
            ds = (p * (dp - jnp.sum(p * dp, axis=0, keepdims=True))).astype(BF16)
            one_k, one_v = mm(ds, qh, 1, 0), mm(p.astype(BF16), doh, 1, 0)
            got_k = one_k if got_k is None else got_k + one_k
            got_v = one_v if got_v is None else got_v + one_v
            got_q.append(mm(kt2, ds, 1, 0))
        dkl[near, lanes] += got_k
        dvl[near, lanes] += got_v
        both = jnp.where(head_lanes((2 * DH, WIN), 0, 0), got_q[0], got_q[1])
        dql[at, lanes] = (both.T * SCALE).astype(BF16)
        pl.when(lax.rem(n_, 4) == 3)(lambda: chain.pump(pumped + n_ // 4))
        return carry

    pumped = chain.next
    lax.fori_loop(0, blocks * (wl // (2 * DH)), light, 0)
    chain.next = pumped + blocks * (wl // (2 * DH)) // 4
    shard.collect()
    rim, came_rim = m["rim"], m["came_rim"]
    for n, start in ((0, WIN + own), (1, 0)):
        rim[n, :, :wl] = (dkl[pl.ds(start, WIN)] * SCALE).astype(BF16)
        rim[n, :, wl:] = dvl[pl.ds(start, WIN)].astype(BF16)
    go(remote(rim.at[0], came_rim.at[0], m["rim_s"].at[0], m["rim_r"].at[0], after))
    go(remote(rim.at[1], came_rim.at[1], m["rim_s"].at[1], m["rim_r"].at[1], before))

    if inner:
        to_twin(z).wait_recv()
        mine = x[spot(c, z)].astype(F32) + sib[z].astype(F32)
        for j in zpeers:
            remote(part.at[j], came.at[j], m["bs_rs_s"].at[j], m["bs_rs_r"].at[j], (b, j, c)).wait_recv()
            mine = mine + came[j].astype(F32)
        trio[0] = (m["dq_t"][...].T * SCALE).astype(BF16)
        trio[1] = mine[:, :rw].astype(BF16)
        trio[2] = mine[:, rw:].astype(BF16)
    rheads = i["rheads"]
    picked = mm(trio[0], rheads[0], 1, 0) + mm(trio[1], rheads[1], 1, 0) + mm(trio[2], rheads[2], 1, 0)

    for n, device in ((0, before), (1, after)):
        remote(rim.at[n], came_rim.at[n], m["rim_s"].at[n], m["rim_r"].at[n], device).wait_recv()
    dkl[pl.ds(WIN, WIN)] += came_rim[0, :, :wl].astype(F32) * (1.0 / SCALE)
    dvl[pl.ds(WIN, WIN)] += came_rim[0, :, wl:].astype(F32)
    dkl[pl.ds(own, WIN)] += came_rim[1, :, :wl].astype(F32) * (1.0 / SCALE)
    dvl[pl.ds(own, WIN)] += came_rim[1, :, wl:].astype(F32)
    dk_own, dv_own = m["dk_own"], m["dv_own"]
    dk_own[...] = (dkl[pl.ds(WIN, own)] * SCALE).astype(BF16)
    dv_own[...] = dvl[pl.ds(WIN, own)].astype(BF16)
    lh = i["lh"]
    gf_l = out["gf_l"]
    gf_l[...] = mm(dql[...], lh[0], 1, 1) + mm(dk_own[...], lh[1], 1, 1) + mm(dv_own[...], lh[2], 1, 1)

    chain.go(1)
    gate, first_r = i["gate"], i["first_r"]
    gate_attn = jnp.sum(gm_half * i["attn_r"][...], axis=-1, keepdims=True)
    total_part = m["part"]
    low_gf = gf_l[...].astype(BF16)
    router_sum = None
    for at, extra, more in ((other_at, None, None), (mine_at, gate_attn, picked)):
        g = gate[at]
        d_gate = i["gate_feed"][at] if extra is None else i["gate_feed"][at] + extra
        d_logit = d_gate * g * (1.0 - g)
        one = jnp.sum(d_logit * first_r[at].astype(F32), axis=0, keepdims=True)
        router_sum = one if router_sum is None else router_sum + one
        sum_ = mm(hot_rows(i["ids"][at] - b * own, own), low_gf, 1, 0) + d_logit * i["vecs"][2:3]
        if more is not None:
            sum_ = sum_ + more
        total_part[at] = sum_.astype(BF16)
    out["router"][...] = router_sum

    first_t, g_att = m["first_t"], out["g_att"]
    hl = wl // nb

    def weights_light():
        first_t[...] = i["first_w"][pl.ds(WIN, own)].T

        def one(t, carry):
            lanes = band(t * 2 * hl, 2 * hl)
            for n, x in enumerate((dql, dk_own, dv_own)):
                both = mm(first_t[...], x[:, lanes], 1, 0)
                for k in range(2):
                    pack_rows(g_att.at[2 * t + k], n * D // 2, [both[:, k * hl : (k + 1) * hl]])
            return carry

        lax.fori_loop(0, nb // 2, one, 0)
        chain.go(1)

    def weights_rest():
        def one(t, carry):
            both = mm(i["ctx_l"][:, band(t * 2 * hl, 2 * hl)], low[...], 0, 0)
            for k in range(2):
                pack_rows(g_att.at[2 * t + k], 3 * D // 2, lane_blocks(both[k * hl : (k + 1) * hl]))
            return carry

        lax.fori_loop(0, nb // 2, one, 0)
        first_half = first_r[mine_at]
        for n in range(3):
            pack_rows(out["g_heavy"], n * rw // 2 * (D // 128), lane_blocks(mm(trio[n], first_half, 0, 0)))
        chain.go(1)

    group_sum_steps(nb, total_part, out["gf_r"], m, [weights_light, weights_rest])
    chain.end()
    shard.end()
    layer.wait()
    finish(sends)


def back(nb, nz, given):
    own, D = given["gm_own"].shape
    cap = given["ids"].shape[0]
    half = cap // 2
    rw = given["rmerge"].shape[0]
    wl = given["q"].shape[1]
    deep = 2 * nz * half
    feed_rows, rx_rows = given["g_feed"].shape[2], given["g_rx"].shape[0]
    shape = lambda *dims: jax.ShapeDtypeStruct(dims, BF16)
    outs = dict(
        gf_r=shape(cap, D), gf_l=jax.ShapeDtypeStruct((own, D), F32),
        g_att=shape(nb, 2, 2 * D * wl // nb // 128, 128), g_heavy=shape(2, 2 * D * rw // 128, 128),
        router=jax.ShapeDtypeStruct((1, D), F32),
        lay=shape(nb, own, D), h_feed=shape(feed_rows, 128), f_rx=shape(2, rx_rows, 128),
    )
    pool = Pool()
    inner = deep <= 4096
    if inner:
        pool.vmem("keys", (deep, rw))
        pool.vmem("values", (deep, rw))
        pool.vmem("keys_t", (rw, deep))
        pool.vmem("dk", (deep, rw), F32)
        pool.vmem("dv", (deep, rw), F32)
        pool.vmem("dq_t", (rw, half), F32)
        pool.vmem("do", (half, rw))
        pool.vmem("trio", (3, half, rw))
        pool.vmem("dkv", (deep, 2 * rw))
        for name in ("bs_sib", "bs_part", "bs_came"):
            pool.vmem(name, (nz, half, 2 * rw))
    pool.vmem("low", (own, D))
    pool.vmem("do_l", (own, wl))
    pool.vmem("lk_t", (wl, own + 2 * WIN))
    pool.vmem("dkl", (own + 2 * WIN, wl), F32)
    pool.vmem("dvl", (own + 2 * WIN, wl), F32)
    pool.vmem("dql", (own, wl))
    pool.vmem("dk_own", (own, wl))
    pool.vmem("dv_own", (own, wl))
    pool.vmem("rim", (2, WIN, 2 * wl))
    pool.vmem("came_rim", (2, WIN, 2 * wl))
    pool.vmem("first_t", (D, own))
    pool.vmem("part", (cap, D))
    group_sum_scratch(pool, nb, cap, D)
    for name in ("bs_sib", "bs_rs") if inner else ():
        pool.dma(f"{name}_s", nz)
        pool.dma(f"{name}_r", nz)
    if not inner:
        given = dict(given, trio=heavy_back_plain(given))
    ShardSum.scratch(pool, feed_rows, "gf")
    ChainSum.scratch(pool, rx_rows, RX_PIECES, "zx")
    Gather.scratch(pool, "ly")
    pool.dma("rim_s", 2)
    pool.dma("rim_r", 2)
    got = pl.pallas_call(
        functools.partial(back_kernel, nb, nz, pool, inner),
        out_shape=tuple(outs[name] for name in BACK_OUT),
        in_specs=[VM] * len(back_names(inner)),
        out_specs=tuple(HB if name in ("lay", "f_rx") else VM for name in BACK_OUT),
        scratch_shapes=pool.shapes,
        compiler_params=pltpu.CompilerParams(
            collective_id=3, has_side_effects=True, vmem_limit_bytes=62 << 20
        ),
    )(*(given[name] for name in back_names(inner)))
    return dict(zip(BACK_OUT, got))


FIN_OUT = ("layer", "delta", "re", "rr", "lh", "lm", "rh", "rm", "le", "lr")


def finish_kernel(lay, dlt, rx, att, heavy, feed_in, *outs):
    o = dict(zip(FIN_OUT, outs))
    o["layer"][...] = lay[...].astype(F32)
    o["delta"][...] = dlt[...].astype(F32)
    size = rx.shape[2]
    blocks = rx.shape[1] // 3
    for core in range(2):
        for part in range(2):
            for k in range(blocks):
                at = 2 * (core * blocks + k) + part
                o["re"][pl.ds(at, size, 4 * blocks), :] = rx[core, part * blocks + k].astype(F32)
        for block, at, row, k in down_pieces(blocks * 128, size * 8):
            if row < blocks * 16:
                o["rr"][core, pl.ds(row, 32), k * 128 : (k + 1) * 128] = rx[core, 2 * blocks + block, pl.ds(at, 32)].astype(F32)

    @pl.when(pl.program_id(0) == 0)
    def _():
        for core in range(2):
            D, hl = o["lh"].shape[1:]
            start = 0
            for n in range(3):
                size = D // 2
                o["lh"][n, pl.ds(core * size, size)] = att[core, pl.ds(start, size)].astype(F32)
                start += size
            for k in range(D // 128):
                size = hl // 2
                o["lm"][pl.ds(core * size, size), k * 128 : (k + 1) * 128] = att[core, pl.ds(start, size)].astype(F32)
                start += size
            start = 0
            size = o["rm"].shape[0] // 2
            for n in range(4):
                dst = o["rm"] if n == 3 else o["rh"].at[n]
                for k in range(D // 128):
                    dst[pl.ds(core * size, size), k * 128 : (k + 1) * 128] = heavy[core, pl.ds(start, size)].astype(F32)
                    start += size
            start = 0
            fl = o["lr"].shape[0]
            lanes = fl // 128
            size = D // 2
            for part in range(2):
                for k in range(lanes):
                    o["le"][pl.ds(core * size * 2 * lanes + 2 * k + part, size, 2 * lanes), :] = feed_in[
                        core, pl.ds(start, size)
                    ].astype(F32)
                    start += size
            size = fl // 2
            for k in range(D // 128):
                o["lr"][pl.ds(core * size, size), k * 128 : (k + 1) * 128] = feed_in[core, pl.ds(start, size)].astype(F32)
                start += size


def finish_all(lay, dlt, rx, att, heavy, feed_in, hl, fl, rw):
    steps = 8
    rows, D = lay.shape
    fh = rx.shape[1] // 3 * 128
    shape = lambda *dims: jax.ShapeDtypeStruct(dims, F32)
    whole = lambda *dims: pl.BlockSpec(dims, lambda n: (0,) * len(dims))
    tall = lambda count, width: pl.BlockSpec((count // steps, width), lambda n: (n, 0))
    return dict(
        zip(
            FIN_OUT,
            pl.pallas_call(
                finish_kernel,
                grid=(steps,),
                out_shape=(
                    shape(rows, D), shape(rows, D), shape(D * 4 * fh // 128, 128), shape(2, fh, D),
                    shape(3, D, hl), shape(hl, D), shape(3, rw, D), shape(rw, D),
                    shape(D * 2 * fl // 128, 128), shape(fl, D),
                ),
                in_specs=[
                    tall(rows, D), tall(rows, D),
                    pl.BlockSpec((2, 3 * fh // 128, D // steps, 128), lambda n: (0, 0, n, 0)),
                    whole(*att.shape), whole(*heavy.shape), whole(*feed_in.shape),
                ],
                out_specs=(
                    tall(rows, D), tall(rows, D), tall(D * 4 * fh // 128, 128),
                    pl.BlockSpec((2, fh // steps, D), lambda n: (0, n, 0)),
                    whole(3, D, hl), whole(hl, D), whole(3, rw, D), whole(rw, D),
                    whole(D * 2 * fl // 128, 128), whole(fl, D),
                ),
                compiler_params=pltpu.CompilerParams(vmem_limit_bytes=50 << 20),
            )(lay, dlt, rx, att, heavy, feed_in),
        )
    )


def woven(x, width):
    blocks = width // 128
    return x.reshape(-1, blocks, 2, 128).transpose(0, 2, 1, 3).reshape(-1, 2, width)


def per_device(
    tokens,
    cotangent,
    gain_before,
    gain_middle,
    router_vector,
    local_heads,
    local_merge,
    routed_heads,
    routed_merge,
    local_expand,
    local_reduce,
    routed_expand,
    routed_reduce,
    routed_slots,
    routed_counts,
):
    nb = lax.axis_size("branch")
    nz = lax.axis_size("zz")
    core = lax.axis_index("core")
    rows, D = tokens.shape
    fh = routed_expand.shape[2] // 2
    vecs = jnp.stack([gain_before, gain_middle, router_vector])
    rheads = routed_heads.transpose(1, 2, 0)
    f = front(
        nb, nz, tokens, cotangent, routed_slots[:, None], routed_counts, vecs, rheads, routed_merge,
        local_heads.transpose(1, 0, 2), local_merge, local_expand.transpose(1, 0, 2), local_reduce,
    )
    re_half = lax.dynamic_slice(routed_expand, (0, 0, core * fh), (D, 2, fh)).transpose(1, 0, 2)
    f = dict(f, vecs=vecs, re=re_half, rr=routed_reduce, rmerge=routed_merge, rheads=rheads)
    f = dict(f, **middle(nb, f))
    f["g_rx"] = f["g_rx"].reshape(-1, 128)
    f = dict(f, **back(nb, nz, f))
    f = dict(f, **tail(nb, nz, f))
    g = finish_all(
        f["lay"].reshape(rows, D), f["delta"].reshape(rows, D), f["f_rx"].reshape(2, -1, D, 128),
        f["f_att"], f["f_heavy"], f["f_feed"], hl=local_merge.shape[0], fl=local_reduce.shape[0],
        rw=routed_merge.shape[0],
    )
    return (
        g["layer"],
        g["delta"],
        f["vectors"][0],
        f["vectors"][1],
        f["vectors"][2],
        g["lh"].transpose(1, 0, 2),
        g["lm"],
        g["rh"].transpose(2, 0, 1),
        g["rm"],
        woven(g["le"], local_reduce.shape[0]),
        g["lr"],
        woven(g["re"], 2 * fh),
        g["rr"].reshape(2 * fh, D),
    )


def solution(mesh):
    nb = mesh.shape["branch"]
    fine = Mesh(mesh.devices.reshape(nb, -1, 2), ("branch", "zz", "core"))
    rows = P(DP, None)
    cols = P(None, None, "branch")
    deep = P("branch", None)
    return jax.shard_map(
        per_device,
        mesh=fine,
        in_specs=(
            rows, rows, P(), P(), P(), cols, deep, cols, deep, cols, deep, cols, deep, P(DP), P(),
        ),
        out_specs=(
            rows, rows, P(), P(), P(), cols, deep, cols, deep, cols, deep, cols, deep,
        ),
        check_vma=False,
    )
```

```python
import functools

import jax
import jax.numpy as jnp
from jax import lax
from jax.experimental import pallas as pl
from jax.experimental.pallas import tpu as pltpu
from jax.sharding import Mesh
from jax.sharding import PartitionSpec as P

DH = 64
WIN = 128
EPSILON = 1e-06
NEGATIVE = -1e30
HIGHEST = lax.Precision.HIGHEST
F32 = jnp.float32
BF16 = jnp.bfloat16
SCALE = DH ** (-0.5)
DP = ("zz", "core")


def mm(a, b, ca, cb):
    return lax.dot_general(a, b, (((ca,), (cb,)), ((), ())), preferred_element_type=F32)


def norm_parts(values):
    r = lax.rsqrt(jnp.mean(values * values, axis=-1, keepdims=True) + EPSILON)
    return r, values * r


def norm_back(dn, xh, r, gain):
    g = dn * gain
    return r * (g - xh * jnp.mean(g * xh, axis=-1, keepdims=True))


def gelu_parts(u):
    c = 0.7978845608028654
    t = jnp.tanh(c * (u + 0.044715 * u * u * u))
    g = 0.5 * u * (1.0 + t)
    dg = 0.5 * (1.0 + t) + 0.5 * u * (1.0 - t * t) * c * (1.0 + 3 * 0.044715 * u * u)
    return g, dg


def feed(n, seed, w_gate, w_up, w_down):
    u = mm(n, w_gate, 1, 0)
    v = mm(n, w_up, 1, 0)
    g, dg = gelu_parts(u)
    hidden = (g * v).astype(BF16)
    out = mm(hidden, w_down, 1, 0)
    dh = mm(seed, w_down, 1, 1)
    du = (dh * v * dg).astype(BF16)
    dv = (dh * g).astype(BF16)
    dn = mm(du, w_gate, 1, 1) + mm(dv, w_up, 1, 1)
    dwg = mm(n, du, 0, 0)
    dwu = mm(n, dv, 0, 0)
    dwd = mm(hidden, seed, 0, 0)
    return out, dn, dwg, dwu, dwd


MESH = pl.DeviceIdType.MESH


def remote(src, dst, send, recv, device):
    return pltpu.make_async_remote_copy(
        src_ref=src, dst_ref=dst, send_sem=send, recv_sem=recv, device_id=device, device_id_type=MESH
    )


def greet(devices):
    barrier = pltpu.get_barrier_semaphore()
    for device in devices:
        pl.semaphore_signal(barrier, inc=1, device_id=device, device_id_type=MESH)
    pl.semaphore_wait(barrier, len(devices))


def here():
    return lax.axis_index("branch"), lax.axis_index("zz"), lax.axis_index("core")


def others(me, count):
    return [lax.rem(me + k, count) for k in range(1, count)]


def band(start, size):
    return pl.ds(pl.multiple_of(start, size), size)


def finish(copies):
    for copy in copies:
        if copy.is_remote:
            copy.wait_send()
        else:
            copy.wait()


class Pool:
    def __init__(self):
        self.names = []
        self.shapes = []

    def add(self, name, shape):
        self.names.append(name)
        self.shapes.append(shape)

    def vmem(self, name, shape, dtype=BF16):
        self.add(name, pltpu.VMEM(shape, dtype))

    def dma(self, name, *shape):
        self.add(name, pltpu.SemaphoreType.DMA(shape))

    def bind(self, refs):
        return dict(zip(self.names, refs, strict=True))


def group_sum_scratch(pool, nb, rows, width, tag="gs"):
    for name in ("sib", "part", "came"):
        pool.vmem(f"{tag}_{name}", (nb, rows // 2 // nb, width))
    for name in ("sib", "rs", "ag", "fw"):
        pool.dma(f"{tag}_{name}_s", nb)
        pool.dma(f"{tag}_{name}_r", nb)


def group_sum_steps(nb, x, o, m, meanwhile=(), tag="gs"):
    m = {name[len(tag) + 1 :]: ref for name, ref in m.items() if name.startswith(tag + "_")}
    b, z, c = here()
    half = x.shape[0] // 2
    ch = half // nb
    twin = (b, z, 1 - c)
    peers = others(b, nb)
    sib, part, came = m["sib"], m["part"], m["came"]
    work = list(meanwhile)

    def aside():
        if work:
            work.pop(0)()

    def rows(core, j):
        return band(core * half + j * ch, ch)

    order = peers + [b]
    to_twin = [
        remote(x.at[rows(1 - c, j)], sib.at[j], m["sib_s"].at[j], m["sib_r"].at[j], twin)
        for j in order
    ]
    for copy in to_twin:
        copy.start()
    sends = []
    for j, copy in zip(peers, to_twin):
        copy.wait_recv()
        part[j] = (x[rows(c, j)].astype(F32) + sib[j].astype(F32)).astype(BF16)
        send = remote(part.at[j], came.at[b], m["rs_s"].at[j], m["rs_r"].at[b], (j, z, c))
        send.start()
        sends.append(send)
    aside()
    to_twin[-1].wait_recv()
    total = x[rows(c, b)].astype(F32) + sib[b].astype(F32)
    for j in peers:
        remote(part.at[j], came.at[j], m["rs_s"].at[j], m["rs_r"].at[j], (j, z, c)).wait_recv()
        total = total + came[j].astype(F32)
    mine = o.at[rows(c, b)]
    mine[...] = total.astype(BF16)
    for j in peers:
        send = remote(mine, mine, m["ag_s"].at[j], m["ag_r"].at[b], (j, z, c))
        send.start()
        sends.append(send)
    send = remote(mine, mine, m["fw_s"].at[b], m["fw_r"].at[b], twin)
    send.start()
    sends.append(send)
    aside()
    for j in peers:
        piece = o.at[rows(c, j)]
        remote(piece, piece, m["ag_s"].at[j], m["ag_r"].at[j], (j, z, c)).wait_recv()
        send = remote(piece, piece, m["fw_s"].at[j], m["fw_r"].at[j], twin)
        send.start()
        sends.append(send)
    while work:
        aside()
    for j in order:
        piece = o.at[rows(1 - c, j)]
        remote(piece, piece, m["fw_s"].at[j], m["fw_r"].at[j], twin).wait_recv()
    finish(to_twin + sends)


VM = pl.BlockSpec(memory_space=pltpu.VMEM)
HB = pl.BlockSpec(memory_space=pl.ANY)


def normed(x, gain):
    x = x.astype(F32)
    r = lax.rsqrt(jnp.mean(x * x, axis=-1, keepdims=True) + EPSILON)
    return (x * r * gain).astype(BF16)


def head_lanes(shape, h, dim):
    place = lax.broadcasted_iota(jnp.int32, shape, dim)
    return (place >= h * DH) & (place < (h + 1) * DH)


def only_head(x, h):
    return jnp.where(head_lanes(x.shape, h, 1), x, jnp.zeros_like(x))


def near_keys(shape, key_dim, first, total):
    key = lax.broadcasted_iota(jnp.int32, shape, key_dim)
    query = lax.broadcasted_iota(jnp.int32, shape, 1 - key_dim)
    gap = key - query
    return (gap >= 0) & (gap <= 2 * WIN) & (key + first >= 0) & (key + first < total)


def hot_rows(ids, count):
    spot = lax.broadcasted_iota(jnp.int32, (ids.shape[0], count), 1)
    return jnp.where(ids == spot, 1.0, 0.0).astype(BF16)


FRONT_OUT = (
    "tok_r", "cot_r", "first_r", "gate", "qr", "kv", "lh", "lm", "le", "lr", "first_w",
    "q", "k", "v", "ctx_l", "attn_l", "ctx_r", "attn_r", "mixed", "ids", "tok_own", "cot_own",
)


def front_kernel(nb, nz, pool, *refs):
    tokens, cotangent, slots, counts, vecs, rheads, rmerge, s_lh, s_lm, s_le, s_lr = refs[:11]
    out = dict(zip(FRONT_OUT, refs[11 : 11 + len(FRONT_OUT)]))
    m = pool.bind(refs[11 + len(FRONT_OUT) :])
    ids = out["ids"]
    gain, router = vecs[0:1], vecs[2:3]
    b, z, c = here()
    twin = (b, z, 1 - c)
    bpeers, zpeers = others(b, nb), others(z, nz)
    rows, D = tokens.shape
    own = rows // nb
    cap = slots.shape[0]
    half = cap // 2
    rw = rmerge.shape[0]
    after = (b, lax.rem(z + c, nz), 1 - c)
    before = (b, lax.rem(z + nz - 1 + c, nz), 1 - c)
    far = (b, lax.rem(z + nz - 1 + 2 * c, nz), 1 - c)
    greet([twin, far] + [(j, z, c) for j in bpeers] + [(b, j, c) for j in zpeers])
    sends = []

    def go(copy):
        copy.start()
        sends.append(copy)

    pairs = [(s_lh, out["lh"]), (s_lm, out["lm"]), (s_le, out["le"]), (s_lr, out["lr"])]

    def place(i, j):
        src, dst = pairs[i]
        if i in (0, 2):
            return dst.at[:, :, band(j * src.shape[2], src.shape[2])]
        return dst.at[band(j * src.shape[0], src.shape[0])]

    def cut(i, ref, core):
        if i in (0, 2):
            size = ref.shape[1] // 2
            return ref.at[:, band(core * size, size)]
        size = ref.shape[0] // 2
        return ref.at[band(core * size, size)]

    def send_weights(i):
        for j in bpeers:
            go(remote(cut(i, pairs[i][0], c), cut(i, place(i, b), c), m["w_s"].at[i, j], m["w_r"].at[i, b], (j, z, c)))

    send_weights(0)
    send_weights(1)
    for i in range(4):
        go(pltpu.make_async_copy(pairs[i][0], place(i, b), m["own_s"].at[i]))
    halo = m["halo"]
    go(remote(tokens.at[pl.ds(rows - WIN, WIN)], halo.at[0], m["halo_s"].at[0], m["halo_r"].at[0], after))
    go(remote(tokens.at[pl.ds(0, WIN)], halo.at[1], m["halo_s"].at[1], m["halo_r"].at[1], before))

    n_own = counts[2 * z + c]
    offset = jnp.where(c == 0, 0, cap - n_own)
    rank = lax.broadcasted_iota(jnp.int32, (cap, cap), 0)
    slot = lax.broadcasted_iota(jnp.int32, (cap, cap), 1)
    shift = jnp.where((rank == slot + offset) & (slot < n_own), 1.0, 0.0).astype(BF16)
    lane = lax.broadcasted_iota(jnp.int32, (cap, 128), 1)
    high, rest = slots[...] // 64, slots[...] % 64
    digits = jnp.where(lane == 0, high, jnp.where(lane == 1, rest, jnp.where(lane == 2, 1, 0)))
    found = mm(shift, digits.astype(F32).astype(BF16), 1, 0)
    ids[...] = jnp.where(found[:, 2:3] > 0.5, found[:, 0:1] * 64.0 + found[:, 1:2], -1.0).astype(jnp.int32)
    out["tok_own"][...] = tokens[band(b * own, own)]
    out["cot_own"][...] = cotangent[band(b * own, own)]
    picks, sib = m["picks"], m["sib"]
    step = cap // 4
    for k in range(4):
        at = pl.ds(k * step, step)
        hot = hot_rows(ids[at], rows)
        picks[at, :D] = mm(hot, tokens[...], 1, 0).astype(BF16)
        picks[at, D:] = mm(hot, cotangent[...], 1, 0).astype(BF16)
        go(remote(picks.at[at], sib.at[at], m["pick_s"].at[k], m["pick_r"].at[k], twin))
    for k in range(4):
        at = pl.ds(k * step, step)
        remote(picks.at[at], sib.at[at], m["pick_s"].at[k], m["pick_r"].at[k], twin).wait_recv()
        tok = picks[at, :D].astype(F32) + sib[at, :D].astype(F32)
        out["tok_r"][at] = tok.astype(BF16)
        out["cot_r"][at] = (picks[at, D:].astype(F32) + sib[at, D:].astype(F32)).astype(BF16)
        first = normed(tok, gain)
        out["first_r"][at] = first
        logit = jnp.sum(first.astype(F32) * router, axis=-1, keepdims=True)
        out["gate"][at] = 1.0 / (1.0 + jnp.exp(-logit))

    own_rows = out["first_r"][band(c * half, half)]
    out["qr"][...] = mm(own_rows, rheads[0], 1, 1).astype(BF16)
    kv = out["kv"]
    mine = kv.at[band((2 * z + c) * half, half)]
    mine[:, :rw] = mm(own_rows, rheads[1], 1, 1).astype(BF16)
    mine[:, rw:] = mm(own_rows, rheads[2], 1, 1).astype(BF16)
    for j in zpeers:
        go(remote(mine, mine, m["kv_s"].at[j], m["kv_r"].at[z], (b, j, c)))
    go(remote(mine, mine, m["kf_s"].at[z], m["kf_r"].at[z], twin))

    first_w = out["first_w"]
    first_w[pl.ds(WIN, own)] = normed(tokens[band(b * own, own)], gain)
    for i in range(2):
        remote(halo.at[i], halo.at[i], m["halo_s"].at[i], m["halo_r"].at[i], twin).wait_recv()
    lead = tokens[band(jnp.maximum(b * own - WIN, 0), WIN)]
    trail = tokens[band(jnp.minimum((b + 1) * own, rows - WIN), WIN)]
    first_w[pl.ds(0, WIN)] = normed(jnp.where(b > 0, lead, halo[0]), gain)
    first_w[pl.ds(WIN + own, WIN)] = normed(jnp.where(b < nb - 1, trail, halo[1]), gain)

    def pass_weights(i):
        for j in bpeers:
            dst = cut(i, place(i, j), c)
            remote(dst, dst, m["w_s"].at[i, j], m["w_r"].at[i, j], (j, z, c)).wait_recv()
            go(remote(dst, dst, m["wf_s"].at[i, j], m["wf_r"].at[i, j], twin))

    def take_weights(i):
        for j in bpeers:
            dst = cut(i, place(i, j), 1 - c)
            remote(dst, dst, m["wf_s"].at[i, j], m["wf_r"].at[i, j], twin).wait_recv()

    pass_weights(0)
    for j in zpeers:
        piece = kv.at[band((2 * j + c) * half, half)]
        remote(piece, piece, m["kv_s"].at[j], m["kv_r"].at[j], (b, j, c)).wait_recv()
        go(remote(piece, piece, m["kf_s"].at[j], m["kf_r"].at[j], twin))
    take_weights(0)
    send_weights(2)
    send_weights(3)
    pltpu.make_async_copy(pairs[0][0], place(0, b), m["own_s"].at[0]).wait()
    lh, q, k, v = out["lh"], out["q"], out["k"], out["v"]
    q[...] = mm(first_w[pl.ds(WIN, own)], lh[0], 1, 0).astype(BF16)
    k[...] = mm(first_w[...], lh[1], 1, 0).astype(BF16)
    v[...] = mm(first_w[...], lh[2], 1, 0).astype(BF16)
    pass_weights(1)

    blocks = own // WIN
    ctx = out["ctx_l"]
    first_key = (2 * z + c) * rows + b * own - WIN
    total = 2 * nz * rows

    def light(i, carry):
        g, n = i // blocks, lax.rem(i, blocks)
        lanes = band(g * 2 * DH, 2 * DH)
        at = band(n * WIN, WIN)
        keys = pl.ds(pl.multiple_of(n * WIN, WIN), 3 * WIN)
        q2, k2, v2 = q[at, lanes], k[keys, lanes], v[keys, lanes]
        allowed = near_keys((WIN, 3 * WIN), 1, first_key + n * WIN, total)
        parts = []
        for h in range(2):
            s = jnp.where(allowed, mm(only_head(q2, h), k2, 1, 1) * SCALE, NEGATIVE)
            w = jnp.exp(s - jnp.max(s, axis=-1, keepdims=True))
            p = (w / jnp.sum(w, axis=-1, keepdims=True)).astype(BF16)
            parts.append(mm(p, v2, 1, 0))
        ctx[at, lanes] = jnp.where(head_lanes((WIN, 2 * DH), 0, 1), parts[0], parts[1]).astype(BF16)
        return carry

    lax.fori_loop(0, blocks * (q.shape[1] // (2 * DH)), light, 0)
    take_weights(1)
    pltpu.make_async_copy(pairs[1][0], place(1, b), m["own_s"].at[1]).wait()
    attn_l = out["attn_l"]
    attn_l[...] = mm(ctx[...], out["lm"][...], 1, 0)

    for j in zpeers + [z]:
        piece = kv.at[band((2 * j + 1 - c) * half, half)]
        remote(piece, piece, m["kf_s"].at[j], m["kf_r"].at[j], twin).wait_recv()
    keys, values, qr, ctx_r = m["keys"], m["values"], out["qr"], out["ctx_r"]
    keys[...] = kv[:, :rw]
    values[...] = kv[:, rw:]
    some = 128

    def heavy(i, carry):
        at = band(i * some, some)
        got = jnp.zeros((some, rw), F32)
        for h in range(rw // DH):
            s = mm(only_head(qr[at], h), keys[...], 1, 1) * SCALE
            w = jnp.exp(s - jnp.max(s, axis=-1, keepdims=True))
            p = (w / jnp.sum(w, axis=-1, keepdims=True)).astype(BF16)
            got = jnp.where(head_lanes((some, rw), h, 1), mm(p, values[...], 1, 0), got)
        ctx_r[at] = got.astype(BF16)
        return carry

    lax.fori_loop(0, half // some, heavy, 0)
    pass_weights(2)
    attn_r = out["attn_r"]
    attn_r[...] = mm(ctx_r[...], rmerge[...], 1, 0)

    part = m["part"]
    mine_at, other_at = band(c * half, half), band((1 - c) * half, half)
    low = attn_l[...].astype(BF16)
    part[other_at] = mm(hot_rows(ids[other_at] - b * own, own), low, 1, 0).astype(BF16)
    part[mine_at] = (
        mm(hot_rows(ids[mine_at] - b * own, own), low, 1, 0) + out["gate"][mine_at] * attn_r[...]
    ).astype(BF16)
    group_sum_steps(nb, part, out["mixed"], m, [lambda: pass_weights(3)])
    take_weights(2)
    take_weights(3)
    finish([copy for copy in sends if copy.is_remote])
    for i in (2, 3):
        pltpu.make_async_copy(pairs[i][0], place(i, b), m["own_s"].at[i]).wait()


def front(nb, nz, tokens, cotangent, slots, counts, vecs, rheads, rmerge, s_lh, s_lm, s_le, s_lr):
    rows, D = tokens.shape
    own = rows // nb
    cap = slots.shape[0]
    half = cap // 2
    rw = rmerge.shape[0]
    wl = nb * s_lm.shape[0]
    shape = lambda *dims: jax.ShapeDtypeStruct(dims, BF16)
    shape32 = lambda *dims: jax.ShapeDtypeStruct(dims, F32)
    outs = dict(
        tok_r=shape(cap, D), cot_r=shape(cap, D), first_r=shape(cap, D), gate=shape32(cap, 1),
        qr=shape(half, rw), kv=shape(2 * nz * half, 2 * rw),
        lh=shape(3, D, wl), lm=shape(wl, D),
        le=shape(2, D, nb * s_le.shape[2]), lr=shape(nb * s_lr.shape[0], D),
        first_w=shape(own + 2 * WIN, D), q=shape(own, wl), k=shape(own + 2 * WIN, wl),
        v=shape(own + 2 * WIN, wl), ctx_l=shape(own, wl), attn_l=shape32(own, D),
        ctx_r=shape(half, rw), attn_r=shape32(half, D), mixed=shape(cap, D),
        ids=jax.ShapeDtypeStruct((cap, 1), jnp.int32), tok_own=shape(own, D), cot_own=shape(own, D),
    )
    pool = Pool()
    pool.vmem("picks", (cap, 2 * D))
    pool.vmem("sib", (cap, 2 * D))
    pool.vmem("halo", (2, WIN, D))
    pool.vmem("keys", (2 * nz * half, rw))
    pool.vmem("values", (2 * nz * half, rw))
    pool.vmem("part", (cap, D))
    group_sum_scratch(pool, nb, cap, D)
    pool.dma("own_s", 4)
    pool.dma("halo_s", 2)
    pool.dma("halo_r", 2)
    pool.dma("pick_s", 4)
    pool.dma("pick_r", 4)
    for name in ("w", "wf"):
        pool.dma(f"{name}_s", 4, nb)
        pool.dma(f"{name}_r", 4, nb)
    for name in ("kv", "kf"):
        pool.dma(f"{name}_s", nz)
        pool.dma(f"{name}_r", nz)
    got = pl.pallas_call(
        functools.partial(front_kernel, nb, nz, pool),
        out_shape=tuple(outs[name] for name in FRONT_OUT),
        in_specs=[VM] * 3 + [pl.BlockSpec(memory_space=pltpu.SMEM)] + [VM] * 3 + [HB] * 4,
        out_specs=tuple(HB if name in ("le", "lr") else VM for name in FRONT_OUT),
        scratch_shapes=pool.shapes,
        compiler_params=pltpu.CompilerParams(
            collective_id=0, has_side_effects=True, vmem_limit_bytes=56 << 20
        ),
    )(tokens, cotangent, slots, counts, vecs, rheads, rmerge, s_lh, s_lm, s_le, s_lr)
    return dict(zip(FRONT_OUT, got))


def neighbours(b):
    return b + 1 - 2 * lax.rem(b, 2), lax.rem(b + 2, 4), 3 - b


class Gather:
    def __init__(self, src, dst, m, name):
        b, z, c = here()
        self.src, self.dst, self.m, self.name, self.b = src, dst, m, name, b
        self.bx, self.by, self.bd = neighbours(b)
        self.dx, self.dy = (self.bx, z, c), (self.by, z, c)
        self.sends = []

    def half(self, ref, k):
        size = self.src.shape[0] // 2
        return ref.at[pl.ds(k * size, size)]

    def go(self, copy):
        copy.start()
        self.sends.append(copy)

    def copy(self, way, k, src, slot, device):
        m, n = self.m, self.name
        return remote(
            self.half(src, k), self.half(self.dst.at[slot], k), m[f"{n}_{way}_s"].at[k], m[f"{n}_{way}_r"].at[k], device
        )

    def start(self):
        own = pltpu.make_async_copy(self.src, self.dst.at[self.b], self.m[f"{self.name}_own"].at[0])
        self.go(own)
        for first, second in ((0, 1), (1, 0)):
            self.go(self.copy("x", second, self.src, self.b, self.dx))
            self.go(self.copy("y", first, self.src, self.b, self.dy))

    def relay(self):
        came = self.dst.at[self.bx]
        self.copy("x", 1, came, self.bx, self.dx).wait_recv()
        self.go(self.copy("f", 1, came, self.bx, self.dy))
        came = self.dst.at[self.by]
        self.copy("y", 0, came, self.by, self.dy).wait_recv()
        self.go(self.copy("f", 0, came, self.by, self.dx))

    def wait(self):
        self.copy("x", 0, self.dst.at[self.bx], self.bx, self.dx).wait_recv()
        self.copy("y", 1, self.dst.at[self.by], self.by, self.dy).wait_recv()
        far = self.dst.at[self.bd]
        self.copy("f", 0, far, self.bd, self.dx).wait_recv()
        self.copy("f", 1, far, self.bd, self.dy).wait_recv()
        finish(self.sends)

    @staticmethod
    def scratch(pool, name):
        pool.dma(f"{name}_own", 1)
        for way in ("x", "y", "f"):
            pool.dma(f"{name}_{way}_s", 2)
            pool.dma(f"{name}_{way}_r", 2)


class ShardSum:
    def __init__(self, g, h, m, name):
        self.b, self.z, self.c = here()
        self.bx, self.by, self.bd = neighbours(self.b)
        self.g, self.h, self.m, self.name = g, h, m, name
        self.sib = m[f"{name}_sib"]
        size = g.shape[2] // 2
        self.parts = (pl.ds(0, size), pl.ds(size, size))
        self.sends = []

    def go(self, copy):
        copy.start()
        self.sends.append(copy)

    def pair(self, j):
        m, n = self.m, self.name
        return remote(
            self.g.at[j, 1 - self.c], self.sib.at[j], m[f"{n}_a_s"].at[j], m[f"{n}_a_r"].at[j],
            (self.b, self.z, 1 - self.c),
        )

    def kept(self, j):
        return pltpu.make_async_copy(
            self.g.at[j, self.c], self.m[f"{self.name}_kept"].at[j], self.m[f"{self.name}_kept_s"].at[j]
        )

    def start(self):
        for j in (self.bd, self.bx, self.by, self.b):
            self.go(self.pair(j))
            self.kept(j).start()

    def step(self, n, src, k):
        m = self.m
        device = (self.bx if n in (0, 1, 5) else self.by, self.z, self.c)
        return remote(
            src.at[self.parts[k]], m[f"{self.name}_came"].at[n], m[f"{self.name}_b_s"].at[n], m[f"{self.name}_b_r"].at[n],
            device,
        )

    def add(self, j):
        self.kept(j).wait()
        self.pair(j).wait_recv()
        self.sib[j] = (self.m[f"{self.name}_kept"][j].astype(F32) + self.sib[j].astype(F32)).astype(BF16)

    def spread(self):
        self.add(self.bd)
        self.go(self.step(1, self.sib.at[self.bd], 0))
        self.go(self.step(3, self.sib.at[self.bd], 1))
        self.add(self.bx)
        self.go(self.step(0, self.sib.at[self.bx], 0))
        self.add(self.by)
        self.go(self.step(2, self.sib.at[self.by], 1))
        self.add(self.b)

    def relay(self):
        came = self.m[f"{self.name}_came"]
        for n, j, k, then in ((1, self.by, 0, 4), (3, self.bx, 1, 5)):
            self.step(n, self.sib.at[j], k).wait_recv()
            at = self.parts[k]
            self.sib[j, at] = (self.sib[j, at].astype(F32) + came[n].astype(F32)).astype(BF16)
            self.go(self.step(then, self.sib.at[j], k))

    def collect(self):
        came = self.m[f"{self.name}_came"]
        for k, one, two in ((0, 0, 4), (1, 2, 5)):
            at = self.parts[k]
            self.step(one, self.sib.at[self.b], k).wait_recv()
            self.step(two, self.sib.at[self.b], k).wait_recv()
            total = self.sib[self.b, at].astype(F32) + came[one].astype(F32) + came[two].astype(F32)
            self.h[at] = total.astype(BF16)

    def end(self):
        finish(self.sends)

    @staticmethod
    def scratch(pool, rows, name):
        pool.vmem(f"{name}_sib", (4, rows, 128))
        pool.vmem(f"{name}_kept", (4, rows, 128))
        pool.dma(f"{name}_kept_s", 4)
        pool.vmem(f"{name}_came", (6, rows // 2, 128))
        pool.dma(f"{name}_a_s", 4)
        pool.dma(f"{name}_a_r", 4)
        pool.dma(f"{name}_b_s", 6)
        pool.dma(f"{name}_b_r", 6)


class BlockSum:
    def __init__(self, nz, h, f, m, name):
        self.b, self.z, self.c = here()
        self.peers = others(self.z, nz)
        self.h, self.f, self.m, self.name = h, f, m, name
        self.ch = h.shape[0] // nz
        self.sends = []

    def go(self, copy):
        copy.start()
        self.sends.append(copy)

    def rows(self, j):
        return band(j * self.ch, self.ch)

    def sem(self, kind, j):
        return self.m[f"{self.name}_{kind}_s"].at[j], self.m[f"{self.name}_{kind}_r"].at[j]

    def start(self):
        for j in self.peers:
            self.go(
                remote(
                    self.h.at[self.rows(j)], self.m[f"{self.name}_came"].at[self.z], self.sem("a", j)[0],
                    self.sem("a", self.z)[1], (self.b, j, self.c),
                )
            )

    def spread(self):
        came, z, c = self.m[f"{self.name}_came"], self.z, self.c
        total = self.h[self.rows(z)].astype(F32)
        for j in self.peers:
            remote(self.h.at[self.rows(j)], came.at[j], *self.sem("a", j), (self.b, j, c)).wait_recv()
            total = total + came[j].astype(F32)
        stage = came.at[z]
        stage[...] = total.astype(BF16)
        piece = self.f.at[c, self.rows(z)]
        for j in self.peers:
            self.go(remote(stage, piece, self.sem("b", j)[0], self.sem("b", z)[1], (self.b, j, c)))
        self.go(remote(stage, piece, *self.sem("c", z), (self.b, z, 1 - c)))
        self.go(pltpu.make_async_copy(stage, piece, self.m[f"{self.name}_own"].at[0]))

    def forward(self):
        c = self.c
        for j in self.peers:
            piece = self.f.at[c, self.rows(j)]
            remote(piece, piece, *self.sem("b", j), (self.b, j, c)).wait_recv()
            self.go(remote(piece, piece, *self.sem("c", j), (self.b, self.z, 1 - c)))

    def end(self):
        for j in self.peers + [self.z]:
            piece = self.f.at[1 - self.c, self.rows(j)]
            remote(piece, piece, *self.sem("c", j), (self.b, self.z, 1 - self.c)).wait_recv()
        finish(self.sends)

    @staticmethod
    def scratch(pool, nz, rows, name):
        pool.vmem(f"{name}_came", (nz, rows // nz, 128))
        pool.dma(f"{name}_own", 1)
        for step in ("a", "b", "c"):
            pool.dma(f"{name}_{step}_s", nz)
            pool.dma(f"{name}_{step}_r", nz)


class ChainSum:
    def __init__(self, nz, pieces, slack, h, f, m, name):
        self.b, self.z, self.c = here()
        self.nz, self.pieces, self.h, self.f, self.m, self.name = nz, pieces, h, f, m, name
        self.ch = h.shape[0] // 2 // pieces
        self.slack = slack
        self.steps = pieces + 2 * slack * (nz - 1)
        self.next = 0

    def rows(self, side, p):
        return band(side * self.pieces * self.ch + p * self.ch, self.ch)

    def copies(self, side, p):
        m, n = self.m, self.name
        came = m[f"{n}_came"].at[side, p]
        piece = self.f.at[self.c, self.rows(side, p)]
        step = 1 - 2 * side
        on = (self.b, lax.rem(self.z + step + self.nz, self.nz), self.c)
        back = (self.b, lax.rem(self.z - step + self.nz, self.nz), self.c)
        over = (self.b, self.z, 1 - self.c)
        sem = lambda kind: m[f"{n}_{kind}"].at[side, p]
        return (
            lambda src: remote(src, came, sem("a_s"), sem("a_r"), on),
            lambda src: remote(src, piece, sem("b_s"), sem("b_r"), back),
            lambda src: remote(src, piece, sem("c_s"), sem("c_r"), over),
            piece,
        )

    def pump(self, s):
        last = self.nz - 1
        for side in range(2):
            pos = self.z if side == 0 else last - self.z
            p = s - self.slack * pos

            @pl.when((p >= 0) & (p < self.pieces))
            def _():
                on, back, over, piece = self.copies(side, p)
                own = self.h.at[self.rows(side, p)]
                came = self.m[f"{self.name}_came"].at[side, p]

                @pl.when(pos == 0)
                def _():
                    on(own).start()

                @pl.when(pos > 0)
                def _():
                    on(came).wait_recv()
                    came[...] = (own[...].astype(F32) + came[...].astype(F32)).astype(BF16)

                @pl.when((pos > 0) & (pos < last))
                def _():
                    on(came).start()

                @pl.when(pos == last)
                def _():
                    pltpu.make_async_copy(came, piece, self.m[f"{self.name}_own"].at[side, p]).start()
                    back(came).start()
                    over(came).start()

            q = s - self.slack * (last + last - pos)

            @pl.when((q >= 0) & (q < self.pieces) & (pos < last))
            def _():
                on, back, over, piece = self.copies(side, q)
                back(piece).wait_recv()
                over(piece).start()

                @pl.when(pos > 0)
                def _():
                    back(piece).start()

    def go(self, count=None):
        upto = self.steps if count is None else min(self.steps, self.next + count)
        if upto - self.next > 4:
            lax.fori_loop(self.next, upto, lambda s, carry: (self.pump(s), carry)[1], 0)
        else:
            for s in range(self.next, upto):
                self.pump(s)
        self.next = upto

    def end(self):
        self.go()
        last = self.nz - 1

        def one(p, carry):
            for side in range(2):
                pos = self.z if side == 0 else last - self.z
                on, back, over, piece = self.copies(side, p)
                other = self.f.at[1 - self.c, self.rows(side, p)]
                came = self.m[f"{self.name}_came"].at[side, p]
                sem = lambda kind: self.m[f"{self.name}_{kind}"].at[side, p]
                remote(other, other, sem("c_s"), sem("c_r"), (self.b, self.z, 1 - self.c)).wait_recv()
                over(piece).wait_send()

                @pl.when(pos < last)
                def _():
                    on(came).wait_send()

                @pl.when(pos > 0)
                def _():
                    back(piece).wait_send()

                @pl.when(pos == last)
                def _():
                    pltpu.make_async_copy(came, piece, self.m[f"{self.name}_own"].at[side, p]).wait()

            return carry

        lax.fori_loop(0, self.pieces, one, 0)

    @staticmethod
    def scratch(pool, rows, pieces, name):
        pool.vmem(f"{name}_came", (2, pieces, rows // 2 // pieces, 128))
        for kind in ("a_s", "a_r", "b_s", "b_r", "c_s", "c_r", "own"):
            pool.dma(f"{name}_{kind}", 2, pieces)


TAIL_IN = ("g_att", "g_heavy", "h_feed", "gm_own", "gf_l", "gf_r", "ids", "tok_own", "vecs", "gain_part", "router")
TAIL_OUT = ("delta", "f_att", "f_both", "vectors")


def tail_kernel(nb, nz, pool, *refs):
    i = dict(zip(TAIL_IN, refs[: len(TAIL_IN)]))
    out = dict(zip(TAIL_OUT, refs[len(TAIL_IN) : len(TAIL_IN) + len(TAIL_OUT)]))
    m = pool.bind(refs[len(TAIL_IN) + len(TAIL_OUT) :])
    b, z, c = here()
    twin = (b, z, 1 - c)
    bpeers, zpeers = others(b, nb), others(z, nz)
    own, D = i["gm_own"].shape
    greet([twin] + [(j, z, c) for j in bpeers] + [(b, j, c) for j in zpeers])
    gh, sib_h, both_h = i["g_heavy"], m["sib_h"], m["both_h"]
    rf, rh = i["h_feed"].shape[0], sib_h.shape[0]
    to_twin = remote(gh.at[1 - c], sib_h, m["sib_h_s"].at[0], m["sib_h_r"].at[0], twin)
    to_twin.start()
    shard = ShardSum(i["g_att"], m["h_att"], m, "ga")
    shard.start()
    both = ChainSum(nz, 8, 2, both_h, out["f_both"], m, "zb")
    att = BlockSum(nz, m["h_att"], out["f_att"], m, "za")
    both_h[pl.ds(0, rf)] = i["h_feed"][...]
    to_twin.wait_recv()
    both_h[pl.ds(rf, rh)] = (gh[c].astype(F32) + sib_h[...].astype(F32)).astype(BF16)
    both.go(1)
    shard.spread()
    both.go(2)

    hot_t = hot_rows(i["ids"][...] - b * own, own).T
    owned = jnp.sum(hot_t.astype(F32), axis=1, keepdims=True) > 0.5
    gf = jnp.where(owned, mm(hot_t, i["gf_r"][...], 1, 0), i["gf_l"][...])
    r, xh = norm_parts(i["tok_own"][...].astype(F32))
    gain_part = jnp.sum(gf * xh, axis=0, keepdims=True)
    low = m["low"]
    low[...] = (i["gm_own"][...] + norm_back(gf, xh, r, i["vecs"][0:1])).astype(BF16)
    rows = Gather(low, out["delta"], m, "td")
    both.go(2)
    shard.relay()
    rows.start()
    both.go(3)

    vec = m["vec_mine"]
    vec[...] = jnp.zeros_like(vec)
    vec[pl.ds(0, 1)] = gain_part
    vec[pl.ds(1, 1)] = i["gain_part"][...]
    vec[pl.ds(2, 1)] = i["router"][...]
    sends = [to_twin]

    def vec_step(name, me, peers, device):
        got = m[f"{name}_got"]
        got[me] = vec[...]
        for j in peers:
            copy = remote(vec, got.at[me], m[f"{name}_s"].at[j], m[f"{name}_r"].at[me], device(j))
            copy.start()
            sends.append(copy)

    def vec_end(name, peers, device):
        got = m[f"{name}_got"]
        for j in peers:
            remote(got.at[j], got.at[j], m[f"{name}_s"].at[j], m[f"{name}_r"].at[j], device(j)).wait_recv()
        return functools.reduce(lambda x, y: x + y, [got[j] for j in range(got.shape[0])])

    by_core, by_branch, by_block = (lambda j: (b, z, j)), (lambda j: (j, z, c)), (lambda j: (b, j, c))
    vec_step("vc", c, [1 - c], by_core)
    both.go(1)
    shard.collect()
    att.start()
    total = vec_end("vc", [1 - c], by_core)
    vec2 = m["vec_pair"]
    vec2[...] = total
    vec = vec2
    vec_step("vb", b, bpeers, by_branch)
    both.go(3)
    total = vec_end("vb", bpeers, by_branch)
    vec3 = m["vec_group"]
    vec3[...] = total
    vec = vec3
    vec_step("vz", z, zpeers, by_block)
    both.go(2)
    att.spread()
    rows.relay()
    both.go(4)
    out["vectors"][...] = vec_end("vz", zpeers, by_block)
    both.go()
    att.forward()
    both.end()
    att.end()
    shard.end()
    rows.wait()
    finish(sends)


def tail(nb, nz, given):
    own, D = given["gm_own"].shape
    ra, rh, rf = given["g_att"].shape[2], given["g_heavy"].shape[1], given["h_feed"].shape[0]
    shape = lambda *dims: jax.ShapeDtypeStruct(dims, BF16)
    outs = dict(
        delta=shape(nb, own, D), f_att=shape(2, ra, 128), f_both=shape(2, rf + rh, 128),
        vectors=jax.ShapeDtypeStruct((8, D), F32),
    )
    pool = Pool()
    pool.vmem("sib_h", (rh, 128))
    pool.vmem("both_h", (rf + rh, 128))
    pool.vmem("h_att", (ra, 128))
    pool.vmem("low", (own, D))
    pool.dma("sib_h_s", 1)
    pool.dma("sib_h_r", 1)
    ShardSum.scratch(pool, ra, "ga")
    BlockSum.scratch(pool, nz, ra, "za")
    ChainSum.scratch(pool, rf + rh, 8, "zb")
    Gather.scratch(pool, "td")
    for name in ("vec_mine", "vec_pair", "vec_group"):
        pool.vmem(name, (8, D), F32)
    for name, count in (("vc", 2), ("vb", nb), ("vz", nz)):
        pool.vmem(f"{name}_got", (count, 8, D), F32)
        pool.dma(f"{name}_s", count)
        pool.dma(f"{name}_r", count)
    got = pl.pallas_call(
        functools.partial(tail_kernel, nb, nz, pool),
        out_shape=tuple(outs[name] for name in TAIL_OUT),
        in_specs=[HB if name == "g_att" else VM for name in TAIL_IN],
        out_specs=(HB,) * 3 + (VM,),
        scratch_shapes=pool.shapes,
        compiler_params=pltpu.CompilerParams(
            collective_id=4, has_side_effects=True, vmem_limit_bytes=56 << 20
        ),
    )(*(given[name] for name in TAIL_IN))
    return dict(zip(TAIL_OUT, got))


MID_IN = (
    "tok_own", "cot_own", "ids", "vecs", "tok_r", "cot_r", "gate", "mixed", "attn_l",
    "le", "lr", "re", "rr",
)
MID_OUT = ("base", "ff", "gm_own", "gm_r", "gate_feed", "gain_part", "g_feed", "g_rx", "f_gate")


def lane_blocks(x):
    return [x[:, n * 128 : (n + 1) * 128] for n in range(x.shape[1] // 128)]


def pack_rows(g, start, parts):
    for part in parts:
        size = part.shape[0] // 2
        for core in range(2):
            g[core, pl.ds(start, size)] = part[core * size : (core + 1) * size].astype(BF16)
        start += size
    return start


def down_pieces(rows, D):
    steps = 8
    per, step = D // steps // 32, rows // steps
    pieces = []
    for n in range(steps):
        spots = [(r, k) for k in range(D // 128) for r in range(0, step, 32)]
        pieces += [(p // per, n * (D // steps) + p % per * 32, n * step + r, k) for p, (r, k) in enumerate(spots)]
    return pieces


def pack_down(g, start, x):
    for block, at, row, k in down_pieces(*x.shape):
        g[start + block, pl.ds(at, 32)] = x[row : row + 32, k * 128 : (k + 1) * 128].astype(BF16)


def mid_kernel(nb, nz, pool, *refs):
    i = dict(zip(MID_IN, refs[: len(MID_IN)]))
    out = dict(zip(MID_OUT, refs[len(MID_IN) : len(MID_IN) + len(MID_OUT)]))
    m = pool.bind(refs[len(MID_IN) + len(MID_OUT) :])
    b, z, c = here()
    greet([(b, z, 1 - c)] + [(j, z, c) for j in others(b, nb)] + [(b, j, c) for j in others(z, nz)])
    own, D = i["tok_own"].shape
    cap = i["ids"].shape[0]
    fl = i["le"].shape[2] // nb
    fh = i["re"].shape[2]
    gain = i["vecs"][1:2]

    pick, pick_t = m["pick"], m["pick_t"]
    hot = hot_rows(i["ids"][...] - b * own, own)
    pick[...] = hot
    pick_t[...] = hot.T
    owned = jnp.sum(pick_t[...].astype(F32), axis=1, keepdims=True) > 0.5
    mid_o, mid_r = m["mid_o"], m["mid_r"]
    mid_o[...] = i["tok_own"][...].astype(F32) + jnp.where(
        owned, mm(pick_t[...], i["mixed"][...], 1, 0), i["attn_l"][...]
    )
    mid_r[...] = i["tok_r"][...].astype(F32) + i["mixed"][...].astype(F32)
    n_o, n_r = m["n_o"], m["n_r"]
    n_o[...] = normed(mid_o[...], gain)
    n_r[...] = normed(mid_r[...], gain)
    gate = i["gate"][...]
    seed_r = m["seed_r"]
    seed_r[...] = (gate * i["cot_r"][...].astype(F32)).astype(BF16)

    def both_ways(n, seed, expand, narrow, row0, tile, count, hid, du, dv, ff, dn):
        def one(t, carry):
            lanes = band(t * tile, tile)
            wd = narrow[band(row0 + t * tile, tile)]
            u = mm(n[...], expand[0, :, lanes], 1, 0)
            v = mm(n[...], expand[1, :, lanes], 1, 0)
            g, dg = gelu_parts(u)
            low = (g * v).astype(BF16)
            hid[:, lanes] = low
            dh = mm(seed[...], wd, 1, 1)
            du[:, lanes] = (dh * v * dg).astype(BF16)
            dv[:, lanes] = (dh * g).astype(BF16)
            one_ff = mm(low, wd, 1, 0)
            one_dn = mm(du[:, lanes], expand[0, :, lanes], 1, 1) + mm(dv[:, lanes], expand[1, :, lanes], 1, 1)
            ff[...] = jnp.where(t == 0, one_ff, ff[...] + one_ff)
            dn[...] = jnp.where(t == 0, one_dn, dn[...] + one_dn)
            return carry

        lax.fori_loop(0, count, one, 0)

    ff_r, dn_r, ff_o, dn_o = m["ff_r"], m["dn_r"], m["ff_o"], m["dn_o"]
    both_ways(
        n_r, seed_r, i["re"], i["rr"], c * fh, fl, fh // fl, m["hid_r"], m["du_r"], m["dv_r"], ff_r, dn_r
    )
    n_t = m["n_t"]
    n_t[...] = n_r[...].T
    g_gate = m["g_gate"]
    for k, x in enumerate(lane_blocks(mm(n_t[...], m["du_r"][...], 1, 0))):
        g_gate[pl.ds(k * D, D)] = x.astype(BF16)
    chain = BlockSum(nz, g_gate, out["f_gate"], m, "zg")
    chain.start()
    both_ways(
        n_o, i["cot_own"], i["le"], i["lr"], 0, fl, nb, m["hid_o"], m["du_o"], m["dv_o"], ff_o, dn_o,
    )
    out["gate_feed"][...] = jnp.sum(i["cot_r"][...].astype(F32) * ff_r[...], axis=-1, keepdims=True)
    part = m["part"]
    out["ff"][...] = ff_r[...].astype(BF16)
    part[...] = (dn_r[...] + mm(pick[...], dn_o[...].astype(BF16), 1, 0)).astype(BF16)

    def weights_heavy():
        gx = out["g_rx"]
        for k, x in enumerate(lane_blocks(mm(n_t[...], m["dv_r"][...], 1, 0))):
            gx[k] = x.astype(BF16)
        pack_down(gx, fh // 128, mm(m["hid_r"][...], seed_r[...], 0, 0))
        chain.spread()

    def weights_light():
        n_t[...] = n_o[...].T
        g = out["g_feed"]

        def one(t, carry):
            lanes = band(t * fl, fl)
            gate_part = mm(n_t[...], m["du_o"][:, lanes], 1, 0)
            up_part = mm(n_t[...], m["dv_o"][:, lanes], 1, 0)
            down = mm(m["hid_o"][:, lanes], i["cot_own"][...], 0, 0)
            pack_rows(g.at[t], 0, lane_blocks(gate_part) + lane_blocks(up_part) + lane_blocks(down))
            return carry

        lax.fori_loop(0, nb, one, 0)

    sums = m["sums"]
    group_sum_steps(nb, part, sums, m, [weights_heavy, weights_light])
    dn_sum = sums[...]
    out["base"][...] = mid_o[...] + ff_o[...]
    dn_own = jnp.where(owned, mm(pick_t[...], dn_sum, 1, 0), dn_o[...])
    r, xh = norm_parts(mid_o[...])
    out["gm_own"][...] = i["cot_own"][...].astype(F32) + norm_back(dn_own, xh, r, gain)
    out["gain_part"][...] = jnp.sum(dn_own * xh, axis=0, keepdims=True)
    r, xh = norm_parts(mid_r[...])
    out["gm_r"][...] = i["cot_r"][...].astype(F32) + norm_back(dn_sum.astype(F32), xh, r, gain)
    chain.forward()
    chain.end()


def middle(nb, nz, given):
    own, D = given["tok_own"].shape
    cap = given["ids"].shape[0]
    wide = given["le"].shape[2]
    fl = wide // nb
    fh = given["re"].shape[2]
    shape = lambda *dims: jax.ShapeDtypeStruct(dims, BF16)
    shape32 = lambda *dims: jax.ShapeDtypeStruct(dims, F32)
    packed = (2 * D * fl + fl * D) // 2 // 128
    outs = dict(
        base=shape32(own, D), ff=shape(cap, D), gm_own=shape32(own, D), gm_r=shape32(cap, D), gate_feed=shape32(cap, 1),
        gain_part=shape32(1, D), g_feed=shape(nb, 2, packed, 128), g_rx=shape(2 * fh // 128, D, 128), f_gate=shape(2, D * fh // 128, 128),
    )
    pool = Pool()
    pool.vmem("pick", (cap, own))
    pool.vmem("pick_t", (own, cap))
    for name, count in (("o", own), ("r", cap)):
        pool.vmem(f"mid_{name}", (count, D), F32)
        pool.vmem(f"n_{name}", (count, D))
        pool.vmem(f"ff_{name}", (count, D), F32)
        pool.vmem(f"dn_{name}", (count, D), F32)
        for kind in ("hid", "du", "dv"):
            pool.vmem(f"{kind}_{name}", (count, wide if name == "o" else fh))
    pool.vmem("seed_r", (cap, D))
    pool.vmem("n_t", (D, own))
    pool.vmem("part", (cap, D))
    pool.vmem("sums", (cap, D))
    pool.vmem("g_gate", (D * fh // 128, 128))
    group_sum_scratch(pool, nb, cap, D)
    BlockSum.scratch(pool, nz, D * fh // 128, "zg")
    got = pl.pallas_call(
        functools.partial(mid_kernel, nb, nz, pool),
        out_shape=tuple(outs[name] for name in MID_OUT),
        in_specs=[VM] * len(MID_IN),
        out_specs=tuple(HB if name == "f_gate" else VM for name in MID_OUT),
        scratch_shapes=pool.shapes,
        compiler_params=pltpu.CompilerParams(
            collective_id=2, has_side_effects=True, vmem_limit_bytes=60 << 20
        ),
    )(*(given[name] for name in MID_IN))
    return dict(zip(MID_OUT, got))


BACK_OUT = ("gf_r", "gf_l", "g_att", "g_heavy", "router", "lay", "h_feed", "f_rx")
BACK_IN = (
    "gm_own", "gm_r", "gate", "gate_feed", "ids", "q", "k", "v", "lm", "lh", "first_w", "ctx_l",
    "qr", "kv", "rmerge", "rheads", "first_r", "ctx_r", "attn_r", "vecs",
    "base", "ff", "g_feed", "g_rx",
)


def back_names(inner):
    return BACK_IN if inner else BACK_IN + ("trio",)


def heavy_back(i, m, seed, x):
    kv, qr = i["kv"], i["qr"]
    half, rw = qr.shape
    keys, values, keys_t, dk, dv, dq_t, do = (
        m[n] for n in ("keys", "values", "keys_t", "dk", "dv", "dq_t", "do")
    )
    keys[...] = kv[:, :rw]
    values[...] = kv[:, rw:]
    keys_t[...] = keys[...].T
    do[...] = mm(seed, i["rmerge"][...], 1, 1).astype(BF16)
    dk[...] = jnp.zeros_like(dk)
    dv[...] = jnp.zeros_like(dv)
    dq_t[...] = jnp.zeros_like(dq_t)
    some = 128

    def heavy(n):
        at = band(n * some, some)
        for h in range(rw // DH):
            qh, doh = only_head(qr[at], h), only_head(do[at], h)
            s = mm(keys[...], qh, 1, 1) * SCALE
            w = jnp.exp(s - jnp.max(s, axis=0, keepdims=True))
            p = w * (1.0 / jnp.sum(w, axis=0, keepdims=True))
            dp = mm(values[...], doh, 1, 1)
            ds = (p * (dp - jnp.sum(p * dp, axis=0, keepdims=True))).astype(BF16)
            dk[...] += mm(ds, qh, 1, 0)
            dv[...] += mm(p.astype(BF16), doh, 1, 0)
            got = mm(keys_t[...], ds, 1, 0)
            dq_t[:, at] += jnp.where(head_lanes(got.shape, h, 0), got, 0.0)

    def end():
        x[:, :rw] = (dk[...] * SCALE).astype(BF16)
        x[:, rw:] = dv[...].astype(BF16)

    return [functools.partial(heavy, n) for n in range(half // some)] + [end]


def heavy_back_plain(i):
    half, rw = i["qr"].shape
    split = lambda y: y.reshape(y.shape[0], -1, DH)
    at = lax.axis_index("core") * half
    seed = (i["gate"] * i["gm_r"]).astype(BF16)
    seed = lax.dynamic_slice(seed, (at, 0), (half, seed.shape[1]))
    do = split(mm(seed, i["rmerge"], 1, 1).astype(BF16))
    q, k, v = split(i["qr"]), split(i["kv"][:, :rw]), split(i["kv"][:, rw:])
    p = jax.nn.softmax(jnp.einsum("qhe,khe->hqk", q, k, preferred_element_type=F32) * SCALE, axis=-1)
    dp = jnp.einsum("qhe,khe->hqk", do, v, preferred_element_type=F32)
    ds = (p * (dp - jnp.sum(p * dp, -1, keepdims=True))).astype(BF16)
    dq = jnp.einsum("hqk,khe->qhe", ds, k, preferred_element_type=F32) * SCALE
    dk = jnp.einsum("hqk,qhe->khe", ds, q, preferred_element_type=F32) * SCALE
    dv = jnp.einsum("hqk,qhe->khe", p.astype(BF16), do, preferred_element_type=F32)
    both = jnp.concatenate([dk.reshape(-1, rw), dv.reshape(-1, rw)], 1).astype(BF16)
    both = lax.psum_scatter(both, DP, scatter_dimension=0, tiled=True)
    return jnp.stack([dq.reshape(half, rw).astype(BF16), both[:, :rw], both[:, rw:]], 0)


def back_kernel(nb, nz, pool, inner, *refs):
    names = back_names(inner)
    i = dict(zip(names, refs[: len(names)]))
    out = dict(zip(BACK_OUT, refs[len(names) : len(names) + len(BACK_OUT)]))
    m = pool.bind(refs[len(names) + len(BACK_OUT) :])
    b, z, c = here()
    twin = (b, z, 1 - c)
    bpeers, zpeers = others(b, nb), others(z, nz)
    own, D = i["gm_own"].shape
    rows = own * nb
    cap = i["ids"].shape[0]
    half = cap // 2
    rw = i["rmerge"].shape[0]
    wl = i["q"].shape[1]
    last, first = b == nb - 1, b == 0
    after = (
        jnp.where(last, 0, b + 1), jnp.where(last, lax.rem(z + c, nz), z), jnp.where(last, 1 - c, c),
    )
    before = (
        jnp.where(first, nb - 1, b - 1),
        jnp.where(first, lax.rem(z + nz - 1 + c, nz), z),
        jnp.where(first, 1 - c, c),
    )
    greet([twin, after, before] + [(j, z, c) for j in bpeers] + [(b, j, c) for j in zpeers])
    mine_at, other_at = band(c * half, half), band((1 - c) * half, half)
    sends = []
    layer = Gather(m["layer"], out["lay"], m, "ly")
    shard = ShardSum(i["g_feed"], out["h_feed"], m, "gf")
    chain = BlockSum(nz, i["g_rx"], out["f_rx"], m, "zx")
    chain.start()
    shard.start()

    def go(copy):
        copy.start()
        sends.append(copy)

    gm_half = i["gm_r"][mine_at]
    gate_half = i["gate"][mine_at]
    seed = (gate_half * gm_half).astype(BF16)
    pack_rows(out["g_heavy"], 3 * rw // 2 * (D // 128), lane_blocks(mm(i["ctx_r"][...], seed, 0, 0)))
    trio = m["trio"] if inner else i["trio"]

    def spot(core, j):
        return band((2 * j + core) * half, half)

    def to_twin(j):
        return remote(x.at[spot(1 - c, j)], sib.at[j], m["bs_sib_s"].at[j], m["bs_sib_r"].at[j], twin)

    shard.spread()
    if inner:
        x, sib, came = m["dkv"], m["bs_sib"], m["bs_came"]
        pieces = heavy_back(i, m, seed, x)
        pieces[-1:] = [functools.partial(lambda f: (f(), [go(to_twin(j)) for j in zpeers + [z]]), pieces[-1])]
    else:
        pieces = []
    group_sum_steps(nb, i["ff"], m["ff_sum"], m, pieces, "fs")
    pick_t = hot_rows(i["ids"][...] - b * own, own).T
    scaled = (i["gate"][...] * m["ff_sum"][...].astype(F32)).astype(BF16)
    m["layer"][...] = (i["base"][...] + mm(pick_t, scaled, 1, 0)).astype(BF16)
    shard.relay()
    layer.start()

    low, do_l = m["low"], m["do_l"]
    low[...] = i["gm_own"][...].astype(BF16)
    do_l[...] = mm(low[...], i["lm"][...], 1, 1).astype(BF16)
    for j in zpeers if inner else []:
        to_twin(j).wait_recv()
        sib[j] = (x[spot(c, j)].astype(F32) + sib[j].astype(F32)).astype(BF16)
        go(remote(sib.at[j], came.at[z], m["bs_rs_s"].at[j], m["bs_rs_r"].at[z], (b, j, c)))

    q, k, v = i["q"], i["k"], i["v"]
    lk_t, dkl, dvl, dql = m["lk_t"], m["dkl"], m["dvl"], m["dql"]
    lk_t[...] = k[...].T
    dkl[...] = jnp.zeros_like(dkl)
    dvl[...] = jnp.zeros_like(dvl)
    blocks = own // WIN
    first_key = (2 * z + c) * rows + b * own - WIN
    total = 2 * nz * rows

    def light(n_, carry):
        g, n = n_ // blocks, lax.rem(n_, blocks)
        lanes = band(g * 2 * DH, 2 * DH)
        at = band(n * WIN, WIN)
        near = pl.ds(pl.multiple_of(n * WIN, WIN), 3 * WIN)
        q2, do2, k2, v2, kt2 = q[at, lanes], do_l[at, lanes], k[near, lanes], v[near, lanes], lk_t[lanes, near]
        allowed = near_keys((3 * WIN, WIN), 0, first_key + n * WIN, total)
        got_k = got_v = None
        got_q = []
        for h in range(2):
            qh, doh = only_head(q2, h), only_head(do2, h)
            s = jnp.where(allowed, mm(k2, qh, 1, 1) * SCALE, NEGATIVE)
            w = jnp.exp(s - jnp.max(s, axis=0, keepdims=True))
            p = w * (1.0 / jnp.sum(w, axis=0, keepdims=True))
            dp = mm(v2, doh, 1, 1)
            ds = (p * (dp - jnp.sum(p * dp, axis=0, keepdims=True))).astype(BF16)
            one_k, one_v = mm(ds, qh, 1, 0), mm(p.astype(BF16), doh, 1, 0)
            got_k = one_k if got_k is None else got_k + one_k
            got_v = one_v if got_v is None else got_v + one_v
            got_q.append(mm(kt2, ds, 1, 0))
        dkl[near, lanes] += got_k
        dvl[near, lanes] += got_v
        both = jnp.where(head_lanes((2 * DH, WIN), 0, 0), got_q[0], got_q[1])
        dql[at, lanes] = (both.T * SCALE).astype(BF16)
        return carry

    lax.fori_loop(0, blocks * (wl // (2 * DH)), light, 0)
    layer.relay()
    shard.collect()
    rim, came_rim = m["rim"], m["came_rim"]
    for n, start in ((0, WIN + own), (1, 0)):
        rim[n, :, :wl] = (dkl[pl.ds(start, WIN)] * SCALE).astype(BF16)
        rim[n, :, wl:] = dvl[pl.ds(start, WIN)].astype(BF16)
    go(remote(rim.at[0], came_rim.at[0], m["rim_s"].at[0], m["rim_r"].at[0], after))
    go(remote(rim.at[1], came_rim.at[1], m["rim_s"].at[1], m["rim_r"].at[1], before))

    if inner:
        to_twin(z).wait_recv()
        mine = x[spot(c, z)].astype(F32) + sib[z].astype(F32)
        for j in zpeers:
            remote(sib.at[j], came.at[j], m["bs_rs_s"].at[j], m["bs_rs_r"].at[j], (b, j, c)).wait_recv()
            mine = mine + came[j].astype(F32)
        trio[0] = (m["dq_t"][...].T * SCALE).astype(BF16)
        trio[1] = mine[:, :rw].astype(BF16)
        trio[2] = mine[:, rw:].astype(BF16)
    chain.spread()
    rheads = i["rheads"]
    picked = mm(trio[0], rheads[0], 1, 0) + mm(trio[1], rheads[1], 1, 0) + mm(trio[2], rheads[2], 1, 0)

    for n, device in ((0, before), (1, after)):
        remote(rim.at[n], came_rim.at[n], m["rim_s"].at[n], m["rim_r"].at[n], device).wait_recv()
    dkl[pl.ds(WIN, WIN)] += came_rim[0, :, :wl].astype(F32) * (1.0 / SCALE)
    dvl[pl.ds(WIN, WIN)] += came_rim[0, :, wl:].astype(F32)
    dkl[pl.ds(own, WIN)] += came_rim[1, :, :wl].astype(F32) * (1.0 / SCALE)
    dvl[pl.ds(own, WIN)] += came_rim[1, :, wl:].astype(F32)
    dk_own, dv_own = m["dk_own"], m["dv_own"]
    dk_own[...] = (dkl[pl.ds(WIN, own)] * SCALE).astype(BF16)
    dv_own[...] = dvl[pl.ds(WIN, own)].astype(BF16)
    lh = i["lh"]
    gf_l = out["gf_l"]
    gf_l[...] = mm(dql[...], lh[0], 1, 1) + mm(dk_own[...], lh[1], 1, 1) + mm(dv_own[...], lh[2], 1, 1)

    gate, first_r = i["gate"], i["first_r"]
    gate_attn = jnp.sum(gm_half * i["attn_r"][...], axis=-1, keepdims=True)
    total_part = m["part"]
    low_gf = gf_l[...].astype(BF16)
    router_sum = None
    for at, extra, more in ((other_at, None, None), (mine_at, gate_attn, picked)):
        g = gate[at]
        d_gate = i["gate_feed"][at] if extra is None else i["gate_feed"][at] + extra
        d_logit = d_gate * g * (1.0 - g)
        one = jnp.sum(d_logit * first_r[at].astype(F32), axis=0, keepdims=True)
        router_sum = one if router_sum is None else router_sum + one
        sum_ = mm(hot_rows(i["ids"][at] - b * own, own), low_gf, 1, 0) + d_logit * i["vecs"][2:3]
        if more is not None:
            sum_ = sum_ + more
        total_part[at] = sum_.astype(BF16)
    out["router"][...] = router_sum

    first_t, g_att = m["first_t"], out["g_att"]
    hl = wl // nb

    def weights_light():
        first_t[...] = i["first_w"][pl.ds(WIN, own)].T

        def one(t, carry):
            lanes = band(t * 2 * hl, 2 * hl)
            for n, x in enumerate((dql, dk_own, dv_own)):
                both = mm(first_t[...], x[:, lanes], 1, 0)
                for k in range(2):
                    pack_rows(g_att.at[2 * t + k], n * D // 2, [both[:, k * hl : (k + 1) * hl]])
            return carry

        lax.fori_loop(0, nb // 2, one, 0)

    def weights_rest():
        def one(t, carry):
            both = mm(i["ctx_l"][:, band(t * 2 * hl, 2 * hl)], low[...], 0, 0)
            for k in range(2):
                pack_rows(g_att.at[2 * t + k], 3 * D // 2, lane_blocks(both[k * hl : (k + 1) * hl]))
            return carry

        lax.fori_loop(0, nb // 2, one, 0)
        first_half = first_r[mine_at]
        for n in range(3):
            pack_rows(out["g_heavy"], n * rw // 2 * (D // 128), lane_blocks(mm(trio[n], first_half, 0, 0)))

    group_sum_steps(nb, total_part, out["gf_r"], m, [weights_light, weights_rest])
    chain.forward()
    chain.end()
    shard.end()
    layer.wait()
    finish(sends)


def back(nb, nz, given):
    own, D = given["gm_own"].shape
    cap = given["ids"].shape[0]
    half = cap // 2
    rw = given["rmerge"].shape[0]
    wl = given["q"].shape[1]
    deep = 2 * nz * half
    feed_rows, rx_rows = given["g_feed"].shape[2], given["g_rx"].shape[0]
    shape = lambda *dims: jax.ShapeDtypeStruct(dims, BF16)
    outs = dict(
        gf_r=shape(cap, D), gf_l=jax.ShapeDtypeStruct((own, D), F32),
        g_att=shape(nb, 2, 2 * D * wl // nb // 128, 128), g_heavy=shape(2, 2 * D * rw // 128, 128),
        router=jax.ShapeDtypeStruct((1, D), F32),
        lay=shape(nb, own, D), h_feed=shape(feed_rows, 128), f_rx=shape(2, rx_rows, 128),
    )
    pool = Pool()
    inner = deep <= 4096
    if inner:
        pool.vmem("keys", (deep, rw))
        pool.vmem("values", (deep, rw))
        pool.vmem("keys_t", (rw, deep))
        pool.vmem("dk", (deep, rw), F32)
        pool.vmem("dv", (deep, rw), F32)
        pool.vmem("dq_t", (rw, half), F32)
        pool.vmem("do", (half, rw))
        pool.vmem("trio", (3, half, rw))
        pool.vmem("dkv", (deep, 2 * rw))
        for name in ("bs_sib", "bs_came"):
            pool.vmem(name, (nz, half, 2 * rw))
    pool.vmem("low", (own, D))
    pool.vmem("do_l", (own, wl))
    pool.vmem("lk_t", (wl, own + 2 * WIN))
    pool.vmem("dkl", (own + 2 * WIN, wl), F32)
    pool.vmem("dvl", (own + 2 * WIN, wl), F32)
    pool.vmem("dql", (own, wl))
    pool.vmem("dk_own", (own, wl))
    pool.vmem("dv_own", (own, wl))
    pool.vmem("rim", (2, WIN, 2 * wl))
    pool.vmem("came_rim", (2, WIN, 2 * wl))
    pool.vmem("first_t", (D, own))
    pool.vmem("part", (cap, D))
    group_sum_scratch(pool, nb, cap, D)
    for name in ("bs_sib", "bs_rs") if inner else ():
        pool.dma(f"{name}_s", nz)
        pool.dma(f"{name}_r", nz)
    if not inner:
        given = dict(given, trio=heavy_back_plain(given))
    pool.vmem("layer", (own, D))
    pool.vmem("ff_sum", (cap, D))
    group_sum_scratch(pool, nb, cap, D, "fs")
    ShardSum.scratch(pool, feed_rows, "gf")
    BlockSum.scratch(pool, nz, rx_rows, "zx")
    Gather.scratch(pool, "ly")
    pool.dma("rim_s", 2)
    pool.dma("rim_r", 2)
    got = pl.pallas_call(
        functools.partial(back_kernel, nb, nz, pool, inner),
        out_shape=tuple(outs[name] for name in BACK_OUT),
        in_specs=[HB if name == "g_feed" else VM for name in back_names(inner)],
        out_specs=tuple(HB if name in ("lay", "f_rx") else VM for name in BACK_OUT),
        scratch_shapes=pool.shapes,
        compiler_params=pltpu.CompilerParams(
            collective_id=3, has_side_effects=True, vmem_limit_bytes=62 << 20
        ),
    )(*(given[name] for name in back_names(inner)))
    return dict(zip(BACK_OUT, got))


FIN_OUT = ("layer", "delta", "re", "rr", "lh", "lm", "rh", "rm", "le", "lr")


def finish_kernel(lay, dlt, gate, rx, att, both, *outs):
    o = dict(zip(FIN_OUT, outs))
    o["layer"][...] = lay[...].astype(F32)
    o["delta"][...] = dlt[...].astype(F32)
    size = rx.shape[2]
    blocks = gate.shape[1]
    for core in range(2):
        for part in range(2):
            for k in range(blocks):
                at = 2 * (core * blocks + k) + part
                o["re"][pl.ds(at, size, 4 * blocks), :] = (rx if part else gate)[core, k].astype(F32)
        for block, at, row, k in down_pieces(blocks * 128, size * 8):
            if row < blocks * 16:
                o["rr"][core, pl.ds(row, 32), k * 128 : (k + 1) * 128] = rx[core, blocks + block, pl.ds(at, 32)].astype(F32)

    @pl.when(pl.program_id(0) == 0)
    def _():
        for core in range(2):
            D, hl = o["lh"].shape[1:]
            start = 0
            for n in range(3):
                size = D // 2
                o["lh"][n, pl.ds(core * size, size)] = att[core, pl.ds(start, size)].astype(F32)
                start += size
            for k in range(D // 128):
                size = hl // 2
                o["lm"][pl.ds(core * size, size), k * 128 : (k + 1) * 128] = att[core, pl.ds(start, size)].astype(F32)
                start += size
            start = D * 3 * o["lr"].shape[0] // 256
            size = o["rm"].shape[0] // 2
            for n in range(4):
                dst = o["rm"] if n == 3 else o["rh"].at[n]
                for k in range(D // 128):
                    dst[pl.ds(core * size, size), k * 128 : (k + 1) * 128] = both[core, pl.ds(start, size)].astype(F32)
                    start += size
            start = 0
            fl = o["lr"].shape[0]
            lanes = fl // 128
            size = D // 2
            for part in range(2):
                for k in range(lanes):
                    o["le"][pl.ds(core * size * 2 * lanes + 2 * k + part, size, 2 * lanes), :] = both[
                        core, pl.ds(start, size)
                    ].astype(F32)
                    start += size
            size = fl // 2
            for k in range(D // 128):
                o["lr"][pl.ds(core * size, size), k * 128 : (k + 1) * 128] = both[core, pl.ds(start, size)].astype(F32)
                start += size


def finish_all(lay, dlt, gate, rx, att, both, hl, fl, rw):
    steps = 8
    rows, D = lay.shape
    fh = gate.shape[1] * 128
    shape = lambda *dims: jax.ShapeDtypeStruct(dims, F32)
    whole = lambda *dims: pl.BlockSpec(dims, lambda n: (0,) * len(dims))
    tall = lambda count, width: pl.BlockSpec((count // steps, width), lambda n: (n, 0))
    return dict(
        zip(
            FIN_OUT,
            pl.pallas_call(
                finish_kernel,
                grid=(steps,),
                out_shape=(
                    shape(rows, D), shape(rows, D), shape(D * 4 * fh // 128, 128), shape(2, fh, D),
                    shape(3, D, hl), shape(hl, D), shape(3, rw, D), shape(rw, D),
                    shape(D * 2 * fl // 128, 128), shape(fl, D),
                ),
                in_specs=[
                    tall(rows, D), tall(rows, D),
                    pl.BlockSpec((2, fh // 128, D // steps, 128), lambda n: (0, 0, n, 0)),
                    pl.BlockSpec((2, 2 * fh // 128, D // steps, 128), lambda n: (0, 0, n, 0)),
                    whole(*att.shape), whole(*both.shape),
                ],
                out_specs=(
                    tall(rows, D), tall(rows, D), tall(D * 4 * fh // 128, 128),
                    pl.BlockSpec((2, fh // steps, D), lambda n: (0, n, 0)),
                    whole(3, D, hl), whole(hl, D), whole(3, rw, D), whole(rw, D),
                    whole(D * 2 * fl // 128, 128), whole(fl, D),
                ),
                compiler_params=pltpu.CompilerParams(vmem_limit_bytes=50 << 20),
            )(lay, dlt, gate, rx, att, both),
        )
    )


def woven(x, width):
    blocks = width // 128
    return x.reshape(-1, blocks, 2, 128).transpose(0, 2, 1, 3).reshape(-1, 2, width)


def per_device(
    tokens,
    cotangent,
    gain_before,
    gain_middle,
    router_vector,
    local_heads,
    local_merge,
    routed_heads,
    routed_merge,
    local_expand,
    local_reduce,
    routed_expand,
    routed_reduce,
    routed_slots,
    routed_counts,
):
    nb = lax.axis_size("branch")
    nz = lax.axis_size("zz")
    core = lax.axis_index("core")
    rows, D = tokens.shape
    fh = routed_expand.shape[2] // 2
    vecs = jnp.stack([gain_before, gain_middle, router_vector])
    rheads = routed_heads.transpose(1, 2, 0)
    f = front(
        nb, nz, tokens, cotangent, routed_slots[:, None], routed_counts, vecs, rheads, routed_merge,
        local_heads.transpose(1, 0, 2), local_merge, local_expand.transpose(1, 0, 2), local_reduce,
    )
    re_half = lax.dynamic_slice(routed_expand, (0, 0, core * fh), (D, 2, fh)).transpose(1, 0, 2)
    f = dict(f, vecs=vecs, re=re_half, rr=routed_reduce, rmerge=routed_merge, rheads=rheads)
    f = dict(f, **middle(nb, nz, f))
    f["g_rx"] = f["g_rx"].reshape(-1, 128)
    f = dict(f, **back(nb, nz, f))
    f = dict(f, **tail(nb, nz, f))
    g = finish_all(
        f["lay"].reshape(rows, D), f["delta"].reshape(rows, D), f["f_gate"].reshape(2, -1, D, 128),
        f["f_rx"].reshape(2, -1, D, 128), f["f_att"], f["f_both"], hl=local_merge.shape[0], fl=local_reduce.shape[0],
        rw=routed_merge.shape[0],
    )
    return (
        g["layer"],
        g["delta"],
        f["vectors"][0],
        f["vectors"][1],
        f["vectors"][2],
        g["lh"].transpose(1, 0, 2),
        g["lm"],
        g["rh"].transpose(2, 0, 1),
        g["rm"],
        woven(g["le"], local_reduce.shape[0]),
        g["lr"],
        woven(g["re"], 2 * fh),
        g["rr"].reshape(2 * fh, D),
    )


def solution(mesh):
    nb = mesh.shape["branch"]
    fine = Mesh(mesh.devices.reshape(nb, -1, 2), ("branch", "zz", "core"))
    rows = P(DP, None)
    cols = P(None, None, "branch")
    deep = P("branch", None)
    return jax.shard_map(
        per_device,
        mesh=fine,
        in_specs=(
            rows, rows, P(), P(), P(), cols, deep, cols, deep, cols, deep, cols, deep, P(DP), P(),
        ),
        out_specs=(
            rows, rows, P(), P(), P(), cols, deep, cols, deep, cols, deep, cols, deep,
        ),
        check_vma=False,
    )
```

```python
import functools

import jax
import jax.numpy as jnp
from jax import lax
from jax.experimental import pallas as pl
from jax.experimental.pallas import tpu as pltpu
from jax.sharding import Mesh
from jax.sharding import PartitionSpec as P

DH = 64
WIN = 128
EPSILON = 1e-06
NEGATIVE = -1e30
HIGHEST = lax.Precision.HIGHEST
F32 = jnp.float32
BF16 = jnp.bfloat16
SCALE = DH ** (-0.5)
DP = ("zz", "core")


def mm(a, b, ca, cb):
    return lax.dot_general(a, b, (((ca,), (cb,)), ((), ())), preferred_element_type=F32)


def norm_parts(values):
    r = lax.rsqrt(jnp.mean(values * values, axis=-1, keepdims=True) + EPSILON)
    return r, values * r


def norm_back(dn, xh, r, gain):
    g = dn * gain
    return r * (g - xh * jnp.mean(g * xh, axis=-1, keepdims=True))


def gelu_parts(u):
    c = 0.7978845608028654
    t = jnp.tanh(c * (u + 0.044715 * u * u * u))
    g = 0.5 * u * (1.0 + t)
    dg = 0.5 * (1.0 + t) + 0.5 * u * (1.0 - t * t) * c * (1.0 + 3 * 0.044715 * u * u)
    return g, dg


def feed(n, seed, w_gate, w_up, w_down):
    u = mm(n, w_gate, 1, 0)
    v = mm(n, w_up, 1, 0)
    g, dg = gelu_parts(u)
    hidden = (g * v).astype(BF16)
    out = mm(hidden, w_down, 1, 0)
    dh = mm(seed, w_down, 1, 1)
    du = (dh * v * dg).astype(BF16)
    dv = (dh * g).astype(BF16)
    dn = mm(du, w_gate, 1, 1) + mm(dv, w_up, 1, 1)
    dwg = mm(n, du, 0, 0)
    dwu = mm(n, dv, 0, 0)
    dwd = mm(hidden, seed, 0, 0)
    return out, dn, dwg, dwu, dwd


MESH = pl.DeviceIdType.MESH


def remote(src, dst, send, recv, device):
    return pltpu.make_async_remote_copy(
        src_ref=src, dst_ref=dst, send_sem=send, recv_sem=recv, device_id=device, device_id_type=MESH
    )


def greet(devices):
    barrier = pltpu.get_barrier_semaphore()
    for device in devices:
        pl.semaphore_signal(barrier, inc=1, device_id=device, device_id_type=MESH)
    pl.semaphore_wait(barrier, len(devices))


def here():
    return lax.axis_index("branch"), lax.axis_index("zz"), lax.axis_index("core")


def others(me, count):
    return [lax.rem(me + k, count) for k in range(1, count)]


def band(start, size):
    return pl.ds(pl.multiple_of(start, size), size)


def finish(copies):
    for copy in copies:
        if copy.is_remote:
            copy.wait_send()
        else:
            copy.wait()


class Pool:
    def __init__(self):
        self.names = []
        self.shapes = []

    def add(self, name, shape):
        self.names.append(name)
        self.shapes.append(shape)

    def vmem(self, name, shape, dtype=BF16):
        self.add(name, pltpu.VMEM(shape, dtype))

    def dma(self, name, *shape):
        self.add(name, pltpu.SemaphoreType.DMA(shape))

    def bind(self, refs):
        return dict(zip(self.names, refs, strict=True))


class Early:
    def __init__(self, names, out, m):
        self.names, self.out, self.m = names, dict(out), m
        self.copies = []
        for name in names:
            out[name] = m[f"out_{name}"]

    def put(self, *names):
        for name in names:
            sem = self.m["out_s"].at[self.names.index(name)]
            copy = pltpu.make_async_copy(self.m[f"out_{name}"], self.out[name], sem)
            copy.start()
            self.copies.append(copy)

    def end(self):
        assert len(self.copies) == len(self.names)
        finish(self.copies)

    @staticmethod
    def scratch(pool, names, shapes):
        for name in names:
            pool.vmem(f"out_{name}", shapes[name].shape, shapes[name].dtype)
        pool.dma("out_s", len(names))


class Late:
    def __init__(self, names, given, m):
        self.copies = {}
        for k, name in enumerate(names):
            copy = pltpu.make_async_copy(given[name], m[f"in_{name}"], m["in_s"].at[k])
            copy.start()
            self.copies[name] = copy
            given[name] = m[f"in_{name}"]

    def need(self, *names):
        for name in names or tuple(self.copies):
            self.copies.pop(name).wait()

    @staticmethod
    def scratch(pool, names, given):
        for name in names:
            pool.vmem(f"in_{name}", given[name].shape, given[name].dtype)
        pool.dma("in_s", len(names))


def group_sum_scratch(pool, nb, rows, width, tag="gs"):
    for name in ("sib", "part", "came"):
        pool.vmem(f"{tag}_{name}", (nb, rows // 2 // nb, width))
    for name in ("sib", "rs", "ag", "fw"):
        pool.dma(f"{tag}_{name}_s", nb)
        pool.dma(f"{tag}_{name}_r", nb)


def group_sum_steps(nb, x, o, m, meanwhile=(), tag="gs"):
    m = {name[len(tag) + 1 :]: ref for name, ref in m.items() if name.startswith(tag + "_")}
    b, z, c = here()
    half = x.shape[0] // 2
    ch = half // nb
    twin = (b, z, 1 - c)
    peers = others(b, nb)
    sib, part, came = m["sib"], m["part"], m["came"]
    work = list(meanwhile)

    def aside():
        if work:
            work.pop(0)()

    def rows(core, j):
        return band(core * half + j * ch, ch)

    order = peers + [b]
    to_twin = [
        remote(x.at[rows(1 - c, j)], sib.at[j], m["sib_s"].at[j], m["sib_r"].at[j], twin)
        for j in order
    ]
    for copy in to_twin:
        copy.start()
    sends = []
    for j, copy in zip(peers, to_twin):
        copy.wait_recv()
        part[j] = (x[rows(c, j)].astype(F32) + sib[j].astype(F32)).astype(BF16)
        send = remote(part.at[j], came.at[b], m["rs_s"].at[j], m["rs_r"].at[b], (j, z, c))
        send.start()
        sends.append(send)
    aside()
    to_twin[-1].wait_recv()
    total = x[rows(c, b)].astype(F32) + sib[b].astype(F32)
    for j in peers:
        remote(part.at[j], came.at[j], m["rs_s"].at[j], m["rs_r"].at[j], (j, z, c)).wait_recv()
        total = total + came[j].astype(F32)
    mine = o.at[rows(c, b)]
    mine[...] = total.astype(BF16)
    for j in peers:
        send = remote(mine, mine, m["ag_s"].at[j], m["ag_r"].at[b], (j, z, c))
        send.start()
        sends.append(send)
    send = remote(mine, mine, m["fw_s"].at[b], m["fw_r"].at[b], twin)
    send.start()
    sends.append(send)
    aside()
    for j in peers:
        piece = o.at[rows(c, j)]
        remote(piece, piece, m["ag_s"].at[j], m["ag_r"].at[j], (j, z, c)).wait_recv()
        send = remote(piece, piece, m["fw_s"].at[j], m["fw_r"].at[j], twin)
        send.start()
        sends.append(send)
    while work:
        aside()
    for j in order:
        piece = o.at[rows(1 - c, j)]
        remote(piece, piece, m["fw_s"].at[j], m["fw_r"].at[j], twin).wait_recv()
    finish(to_twin + sends)


VM = pl.BlockSpec(memory_space=pltpu.VMEM)
HB = pl.BlockSpec(memory_space=pl.ANY)


def normed(x, gain):
    x = x.astype(F32)
    r = lax.rsqrt(jnp.mean(x * x, axis=-1, keepdims=True) + EPSILON)
    return (x * r * gain).astype(BF16)


def head_lanes(shape, h, dim):
    place = lax.broadcasted_iota(jnp.int32, shape, dim)
    return (place >= h * DH) & (place < (h + 1) * DH)


def only_head(x, h):
    return jnp.where(head_lanes(x.shape, h, 1), x, jnp.zeros_like(x))


def near_keys(shape, key_dim, first, total):
    key = lax.broadcasted_iota(jnp.int32, shape, key_dim)
    query = lax.broadcasted_iota(jnp.int32, shape, 1 - key_dim)
    gap = key - query
    return (gap >= 0) & (gap <= 2 * WIN) & (key + first >= 0) & (key + first < total)


def hot_rows(ids, count):
    spot = lax.broadcasted_iota(jnp.int32, (ids.shape[0], count), 1)
    return jnp.where(ids == spot, 1.0, 0.0).astype(BF16)


FRONT_OUT = (
    "tok_r", "cot_r", "first_r", "gate", "qr", "kv", "lh", "lm", "le", "lr", "first_w",
    "q", "k", "v", "ctx_l", "attn_l", "ctx_r", "attn_r", "mixed", "ids", "tok_own", "cot_own",
)


FRONT_EARLY = (
    "kv", "lh", "lm", "q", "k", "v", "first_w", "tok_r", "cot_r", "first_r", "ctx_l", "attn_l",
)


def front_kernel(nb, nz, pool, *refs):
    tokens, cotangent, slots, counts, vecs, rheads, rmerge, s_lh, s_lm, s_le, s_lr = refs[:11]
    out = dict(zip(FRONT_OUT, refs[11 : 11 + len(FRONT_OUT)]))
    m = pool.bind(refs[11 + len(FRONT_OUT) :])
    early = Early(FRONT_EARLY, out, m)
    ids = out["ids"]
    gain, router = vecs[0:1], vecs[2:3]
    b, z, c = here()
    twin = (b, z, 1 - c)
    bpeers, zpeers = others(b, nb), others(z, nz)
    rows, D = tokens.shape
    own = rows // nb
    cap = slots.shape[1]
    half = cap // 2
    rw = rmerge.shape[0]
    after = (b, lax.rem(z + c, nz), 1 - c)
    before = (b, lax.rem(z + nz - 1 + c, nz), 1 - c)
    far = (b, lax.rem(z + nz - 1 + 2 * c, nz), 1 - c)
    greet([twin, far] + [(j, z, c) for j in bpeers] + [(b, j, c) for j in zpeers])
    sends = []

    def go(copy):
        copy.start()
        sends.append(copy)

    pairs = [(s_lh, out["lh"]), (s_lm, out["lm"]), (s_le, out["le"]), (s_lr, out["lr"])]

    def place(i, j):
        src, dst = pairs[i]
        if i in (0, 2):
            return dst.at[:, :, band(j * src.shape[2], src.shape[2])]
        return dst.at[band(j * src.shape[0], src.shape[0])]

    def cut(i, ref, core):
        if i in (0, 2):
            size = ref.shape[1] // 2
            return ref.at[:, band(core * size, size)]
        size = ref.shape[0] // 2
        return ref.at[band(core * size, size)]

    def send_weights(i):
        for j in bpeers:
            go(remote(cut(i, pairs[i][0], c), cut(i, place(i, b), c), m["w_s"].at[i, j], m["w_r"].at[i, b], (j, z, c)))

    send_weights(0)
    send_weights(1)
    for i in range(4):
        pltpu.make_async_copy(pairs[i][0], place(i, b), m["own_s"].at[i]).start()
    halo = m["halo"]
    go(remote(tokens.at[pl.ds(rows - WIN, WIN)], halo.at[0], m["halo_s"].at[0], m["halo_r"].at[0], after))
    go(remote(tokens.at[pl.ds(0, WIN)], halo.at[1], m["halo_s"].at[1], m["halo_r"].at[1], before))

    n_own = counts[2 * z + c]
    offset = jnp.where(c == 0, 0, cap - n_own)
    rank = lax.broadcasted_iota(jnp.int32, (cap, cap), 0)
    slot = lax.broadcasted_iota(jnp.int32, (cap, cap), 1)
    shift = jnp.where((rank == slot + offset) & (slot < n_own), 1.0, 0.0).astype(BF16)
    line = lax.broadcasted_iota(jnp.int32, (16, cap), 0)
    high, rest = slots[...] // 64, slots[...] % 64
    digits = jnp.where(line == 0, high, jnp.where(line == 1, rest, jnp.where(line == 2, 1, 0)))
    found = mm(shift, digits.astype(F32).astype(BF16), 1, 1)
    ids[...] = jnp.where(found[:, 2:3] > 0.5, found[:, 0:1] * 64.0 + found[:, 1:2], -1.0).astype(jnp.int32)
    for n, (name, source) in enumerate((("tok_own", tokens), ("cot_own", cotangent))):
        go(pltpu.make_async_copy(source.at[band(b * own, own)], out[name], m["rows_s"].at[n]))
    picks, sib = m["picks"], m["sib"]
    step = cap // 4
    for k in range(4):
        at = pl.ds(k * step, step)
        hot = hot_rows(ids[at], rows)
        picks[at, :D] = mm(hot, tokens[...], 1, 0).astype(BF16)
        picks[at, D:] = mm(hot, cotangent[...], 1, 0).astype(BF16)
        go(remote(picks.at[at], sib.at[at], m["pick_s"].at[k], m["pick_r"].at[k], twin))
    for k in range(4):
        at = pl.ds(k * step, step)
        remote(picks.at[at], sib.at[at], m["pick_s"].at[k], m["pick_r"].at[k], twin).wait_recv()
        tok = picks[at, :D].astype(F32) + sib[at, :D].astype(F32)
        out["tok_r"][at] = tok.astype(BF16)
        out["cot_r"][at] = (picks[at, D:].astype(F32) + sib[at, D:].astype(F32)).astype(BF16)
        first = normed(tok, gain)
        out["first_r"][at] = first
        logit = jnp.sum(first.astype(F32) * router, axis=-1, keepdims=True)
        out["gate"][at] = 1.0 / (1.0 + jnp.exp(-logit))

    early.put("tok_r", "cot_r", "first_r")
    own_rows = out["first_r"][band(c * half, half)]
    out["qr"][...] = mm(own_rows, rheads[0], 1, 1).astype(BF16)
    kv = out["kv"]
    mine = kv.at[band((2 * z + c) * half, half)]
    mine[:, :rw] = mm(own_rows, rheads[1], 1, 1).astype(BF16)
    mine[:, rw:] = mm(own_rows, rheads[2], 1, 1).astype(BF16)
    for j in zpeers:
        go(remote(mine, mine, m["kv_s"].at[j], m["kv_r"].at[z], (b, j, c)))
    go(remote(mine, mine, m["kf_s"].at[z], m["kf_r"].at[z], twin))

    first_w = out["first_w"]
    first_w[pl.ds(WIN, own)] = normed(tokens[band(b * own, own)], gain)
    for i in range(2):
        remote(halo.at[i], halo.at[i], m["halo_s"].at[i], m["halo_r"].at[i], twin).wait_recv()
    lead = tokens[band(jnp.maximum(b * own - WIN, 0), WIN)]
    trail = tokens[band(jnp.minimum((b + 1) * own, rows - WIN), WIN)]
    first_w[pl.ds(0, WIN)] = normed(jnp.where(b > 0, lead, halo[0]), gain)
    first_w[pl.ds(WIN + own, WIN)] = normed(jnp.where(b < nb - 1, trail, halo[1]), gain)

    def pass_weights(i):
        for j in bpeers:
            dst = cut(i, place(i, j), c)
            remote(dst, dst, m["w_s"].at[i, j], m["w_r"].at[i, j], (j, z, c)).wait_recv()
            go(remote(dst, dst, m["wf_s"].at[i, j], m["wf_r"].at[i, j], twin))

    def take_weights(i):
        for j in bpeers:
            dst = cut(i, place(i, j), 1 - c)
            remote(dst, dst, m["wf_s"].at[i, j], m["wf_r"].at[i, j], twin).wait_recv()

    pass_weights(0)
    for j in zpeers:
        piece = kv.at[band((2 * j + c) * half, half)]
        remote(piece, piece, m["kv_s"].at[j], m["kv_r"].at[j], (b, j, c)).wait_recv()
        go(remote(piece, piece, m["kf_s"].at[j], m["kf_r"].at[j], twin))
    take_weights(0)
    send_weights(2)
    send_weights(3)
    pltpu.make_async_copy(pairs[0][0], place(0, b), m["own_s"].at[0]).wait()
    lh, q, k, v = out["lh"], out["q"], out["k"], out["v"]
    q[...] = mm(first_w[pl.ds(WIN, own)], lh[0], 1, 0).astype(BF16)
    k[...] = mm(first_w[...], lh[1], 1, 0).astype(BF16)
    v[...] = mm(first_w[...], lh[2], 1, 0).astype(BF16)
    early.put("lh", "q", "k", "v", "first_w")
    pass_weights(1)

    blocks = own // WIN
    ctx = out["ctx_l"]
    first_key = (2 * z + c) * rows + b * own - WIN
    total = 2 * nz * rows

    def light(i, carry):
        g, n = i // blocks, lax.rem(i, blocks)
        lanes = band(g * 2 * DH, 2 * DH)
        at = band(n * WIN, WIN)
        keys = pl.ds(pl.multiple_of(n * WIN, WIN), 3 * WIN)
        q2, k2, v2 = q[at, lanes], k[keys, lanes], v[keys, lanes]
        allowed = near_keys((WIN, 3 * WIN), 1, first_key + n * WIN, total)
        parts = []
        for h in range(2):
            s = jnp.where(allowed, mm(only_head(q2, h), k2, 1, 1) * SCALE, NEGATIVE)
            w = jnp.exp(s - jnp.max(s, axis=-1, keepdims=True))
            p = (w / jnp.sum(w, axis=-1, keepdims=True)).astype(BF16)
            parts.append(mm(p, v2, 1, 0))
        ctx[at, lanes] = jnp.where(head_lanes((WIN, 2 * DH), 0, 1), parts[0], parts[1]).astype(BF16)
        return carry

    lax.fori_loop(0, blocks * (q.shape[1] // (2 * DH)), light, 0)
    take_weights(1)
    pltpu.make_async_copy(pairs[1][0], place(1, b), m["own_s"].at[1]).wait()
    attn_l = out["attn_l"]
    attn_l[...] = mm(ctx[...], out["lm"][...], 1, 0)
    early.put("lm", "ctx_l", "attn_l")

    for j in zpeers + [z]:
        piece = kv.at[band((2 * j + 1 - c) * half, half)]
        remote(piece, piece, m["kf_s"].at[j], m["kf_r"].at[j], twin).wait_recv()
    keys, values, qr, ctx_r = m["keys"], m["values"], out["qr"], out["ctx_r"]
    early.put("kv")
    keys[...] = kv[:, :rw]
    values[...] = kv[:, rw:]
    some = 128

    def heavy(i, carry):
        at = band(i * some, some)
        got = jnp.zeros((some, rw), F32)
        for h in range(rw // DH):
            s = mm(only_head(qr[at], h), keys[...], 1, 1) * SCALE
            w = jnp.exp(s - jnp.max(s, axis=-1, keepdims=True))
            p = (w / jnp.sum(w, axis=-1, keepdims=True)).astype(BF16)
            got = jnp.where(head_lanes((some, rw), h, 1), mm(p, values[...], 1, 0), got)
        ctx_r[at] = got.astype(BF16)
        return carry

    lax.fori_loop(0, half // some, heavy, 0)
    pass_weights(2)
    attn_r = out["attn_r"]
    attn_r[...] = mm(ctx_r[...], rmerge[...], 1, 0)

    part = m["part"]
    mine_at, other_at = band(c * half, half), band((1 - c) * half, half)
    low = attn_l[...].astype(BF16)
    part[other_at] = mm(hot_rows(ids[other_at] - b * own, own), low, 1, 0).astype(BF16)
    part[mine_at] = (
        mm(hot_rows(ids[mine_at] - b * own, own), low, 1, 0) + out["gate"][mine_at] * attn_r[...]
    ).astype(BF16)
    group_sum_steps(nb, part, out["mixed"], m, [lambda: pass_weights(3)])
    take_weights(2)
    take_weights(3)
    early.end()
    finish(sends)
    for i in (2, 3):
        pltpu.make_async_copy(pairs[i][0], place(i, b), m["own_s"].at[i]).wait()


def front(nb, nz, tokens, cotangent, slots, counts, vecs, rheads, rmerge, s_lh, s_lm, s_le, s_lr):
    rows, D = tokens.shape
    own = rows // nb
    cap = slots.shape[1]
    half = cap // 2
    rw = rmerge.shape[0]
    wl = nb * s_lm.shape[0]
    shape = lambda *dims: jax.ShapeDtypeStruct(dims, BF16)
    shape32 = lambda *dims: jax.ShapeDtypeStruct(dims, F32)
    outs = dict(
        tok_r=shape(cap, D), cot_r=shape(cap, D), first_r=shape(cap, D), gate=shape32(cap, 1),
        qr=shape(half, rw), kv=shape(2 * nz * half, 2 * rw),
        lh=shape(3, D, wl), lm=shape(wl, D),
        le=shape(2, D, nb * s_le.shape[2]), lr=shape(nb * s_lr.shape[0], D),
        first_w=shape(own + 2 * WIN, D), q=shape(own, wl), k=shape(own + 2 * WIN, wl),
        v=shape(own + 2 * WIN, wl), ctx_l=shape(own, wl), attn_l=shape32(own, D),
        ctx_r=shape(half, rw), attn_r=shape32(half, D), mixed=shape(cap, D),
        ids=jax.ShapeDtypeStruct((cap, 1), jnp.int32), tok_own=shape(own, D), cot_own=shape(own, D),
    )
    pool = Pool()
    pool.vmem("picks", (cap, 2 * D))
    pool.vmem("sib", (cap, 2 * D))
    pool.vmem("halo", (2, WIN, D))
    pool.vmem("keys", (2 * nz * half, rw))
    pool.vmem("values", (2 * nz * half, rw))
    pool.vmem("part", (cap, D))
    group_sum_scratch(pool, nb, cap, D)
    pool.dma("own_s", 4)
    pool.dma("rows_s", 2)
    Early.scratch(pool, FRONT_EARLY, outs)
    pool.dma("halo_s", 2)
    pool.dma("halo_r", 2)
    pool.dma("pick_s", 4)
    pool.dma("pick_r", 4)
    for name in ("w", "wf"):
        pool.dma(f"{name}_s", 4, nb)
        pool.dma(f"{name}_r", 4, nb)
    for name in ("kv", "kf"):
        pool.dma(f"{name}_s", nz)
        pool.dma(f"{name}_r", nz)
    got = pl.pallas_call(
        functools.partial(front_kernel, nb, nz, pool),
        out_shape=tuple(outs[name] for name in FRONT_OUT),
        in_specs=[VM] * 3 + [pl.BlockSpec(memory_space=pltpu.SMEM)] + [VM] * 3 + [HB] * 4,
        out_specs=tuple(
            HB if name in ("le", "lr", "tok_own", "cot_own") + FRONT_EARLY else VM for name in FRONT_OUT
        ),
        scratch_shapes=pool.shapes,
        compiler_params=pltpu.CompilerParams(
            collective_id=0, has_side_effects=True, vmem_limit_bytes=56 << 20
        ),
    )(tokens, cotangent, slots, counts, vecs, rheads, rmerge, s_lh, s_lm, s_le, s_lr)
    return dict(zip(FRONT_OUT, got))


def neighbours(b):
    return b + 1 - 2 * lax.rem(b, 2), lax.rem(b + 2, 4), 3 - b


class Gather:
    def __init__(self, src, dst, m, name):
        b, z, c = here()
        self.src, self.dst, self.m, self.name, self.b = src, dst, m, name, b
        self.bx, self.by, self.bd = neighbours(b)
        self.dx, self.dy = (self.bx, z, c), (self.by, z, c)
        self.sends = []

    def half(self, ref, k):
        size = self.src.shape[0] // 2
        return ref.at[pl.ds(k * size, size)]

    def go(self, copy):
        copy.start()
        self.sends.append(copy)

    def copy(self, way, k, src, slot, device):
        m, n = self.m, self.name
        return remote(
            self.half(src, k), self.half(self.dst.at[slot], k), m[f"{n}_{way}_s"].at[k], m[f"{n}_{way}_r"].at[k], device
        )

    def start(self):
        own = pltpu.make_async_copy(self.src, self.dst.at[self.b], self.m[f"{self.name}_own"].at[0])
        self.go(own)
        for first, second in ((0, 1), (1, 0)):
            self.go(self.copy("x", second, self.src, self.b, self.dx))
            self.go(self.copy("y", first, self.src, self.b, self.dy))

    def relay(self):
        came = self.dst.at[self.bx]
        self.copy("x", 1, came, self.bx, self.dx).wait_recv()
        self.go(self.copy("f", 1, came, self.bx, self.dy))
        came = self.dst.at[self.by]
        self.copy("y", 0, came, self.by, self.dy).wait_recv()
        self.go(self.copy("f", 0, came, self.by, self.dx))

    def wait(self):
        self.copy("x", 0, self.dst.at[self.bx], self.bx, self.dx).wait_recv()
        self.copy("y", 1, self.dst.at[self.by], self.by, self.dy).wait_recv()
        far = self.dst.at[self.bd]
        self.copy("f", 0, far, self.bd, self.dx).wait_recv()
        self.copy("f", 1, far, self.bd, self.dy).wait_recv()
        finish(self.sends)

    @staticmethod
    def scratch(pool, name):
        pool.dma(f"{name}_own", 1)
        for way in ("x", "y", "f"):
            pool.dma(f"{name}_{way}_s", 2)
            pool.dma(f"{name}_{way}_r", 2)


class ShardSum:
    def __init__(self, g, h, m, name):
        self.b, self.z, self.c = here()
        self.bx, self.by, self.bd = neighbours(self.b)
        self.g, self.h, self.m, self.name = g, h, m, name
        self.sib = m[f"{name}_sib"]
        size = g.shape[2] // 2
        self.parts = (pl.ds(0, size), pl.ds(size, size))
        self.sends = []

    def go(self, copy):
        copy.start()
        self.sends.append(copy)

    def pair(self, j):
        m, n = self.m, self.name
        return remote(
            self.g.at[j, 1 - self.c], self.sib.at[j], m[f"{n}_a_s"].at[j], m[f"{n}_a_r"].at[j],
            (self.b, self.z, 1 - self.c),
        )

    def kept(self, j):
        return pltpu.make_async_copy(
            self.g.at[j, self.c], self.m[f"{self.name}_kept"].at[j], self.m[f"{self.name}_kept_s"].at[j]
        )

    def start(self):
        for j in (self.bd, self.bx, self.by, self.b):
            self.go(self.pair(j))
            self.kept(j).start()

    def step(self, n, src, k):
        m = self.m
        device = (self.bx if n in (0, 1, 5) else self.by, self.z, self.c)
        return remote(
            src.at[self.parts[k]], m[f"{self.name}_came"].at[n], m[f"{self.name}_b_s"].at[n], m[f"{self.name}_b_r"].at[n],
            device,
        )

    def add(self, j):
        self.kept(j).wait()
        self.pair(j).wait_recv()
        self.sib[j] = (self.m[f"{self.name}_kept"][j].astype(F32) + self.sib[j].astype(F32)).astype(BF16)

    def spread(self):
        self.add(self.bd)
        self.go(self.step(1, self.sib.at[self.bd], 0))
        self.go(self.step(3, self.sib.at[self.bd], 1))
        self.add(self.bx)
        self.go(self.step(0, self.sib.at[self.bx], 0))
        self.add(self.by)
        self.go(self.step(2, self.sib.at[self.by], 1))
        self.add(self.b)

    def relay(self):
        came = self.m[f"{self.name}_came"]
        for n, j, k, then in ((1, self.by, 0, 4), (3, self.bx, 1, 5)):
            self.step(n, self.sib.at[j], k).wait_recv()
            at = self.parts[k]
            self.sib[j, at] = (self.sib[j, at].astype(F32) + came[n].astype(F32)).astype(BF16)
            self.go(self.step(then, self.sib.at[j], k))

    def collect(self):
        came = self.m[f"{self.name}_came"]
        for k, one, two in ((0, 0, 4), (1, 2, 5)):
            at = self.parts[k]
            self.step(one, self.sib.at[self.b], k).wait_recv()
            self.step(two, self.sib.at[self.b], k).wait_recv()
            total = self.sib[self.b, at].astype(F32) + came[one].astype(F32) + came[two].astype(F32)
            self.h[at] = total.astype(BF16)

    def end(self):
        finish(self.sends)

    @staticmethod
    def scratch(pool, rows, name):
        pool.vmem(f"{name}_sib", (4, rows, 128))
        pool.vmem(f"{name}_kept", (4, rows, 128))
        pool.dma(f"{name}_kept_s", 4)
        pool.vmem(f"{name}_came", (6, rows // 2, 128))
        pool.dma(f"{name}_a_s", 4)
        pool.dma(f"{name}_a_r", 4)
        pool.dma(f"{name}_b_s", 6)
        pool.dma(f"{name}_b_r", 6)


class BlockSum:
    def __init__(self, nz, h, f, m, name):
        self.b, self.z, self.c = here()
        self.peers = others(self.z, nz)
        self.h, self.f, self.m, self.name = h, f, m, name
        self.ch = h.shape[0] // nz
        self.sends = []

    def go(self, copy):
        copy.start()
        self.sends.append(copy)

    def rows(self, j):
        return band(j * self.ch, self.ch)

    def sem(self, kind, j):
        return self.m[f"{self.name}_{kind}_s"].at[j], self.m[f"{self.name}_{kind}_r"].at[j]

    def start(self):
        for j in self.peers:
            self.go(
                remote(
                    self.h.at[self.rows(j)], self.m[f"{self.name}_came"].at[self.z], self.sem("a", j)[0],
                    self.sem("a", self.z)[1], (self.b, j, self.c),
                )
            )

    def spread(self):
        came, z, c = self.m[f"{self.name}_came"], self.z, self.c
        total = self.h[self.rows(z)].astype(F32)
        for j in self.peers:
            remote(self.h.at[self.rows(j)], came.at[j], *self.sem("a", j), (self.b, j, c)).wait_recv()
            total = total + came[j].astype(F32)
        stage = came.at[z]
        stage[...] = total.astype(BF16)
        piece = self.f.at[c, self.rows(z)]
        for j in self.peers:
            self.go(remote(stage, piece, self.sem("b", j)[0], self.sem("b", z)[1], (self.b, j, c)))
        self.go(remote(stage, piece, *self.sem("c", z), (self.b, z, 1 - c)))
        self.go(pltpu.make_async_copy(stage, piece, self.m[f"{self.name}_own"].at[0]))

    def forward(self):
        c = self.c
        for j in self.peers:
            piece = self.f.at[c, self.rows(j)]
            remote(piece, piece, *self.sem("b", j), (self.b, j, c)).wait_recv()
            self.go(remote(piece, piece, *self.sem("c", j), (self.b, self.z, 1 - c)))

    def end(self):
        for j in self.peers + [self.z]:
            piece = self.f.at[1 - self.c, self.rows(j)]
            remote(piece, piece, *self.sem("c", j), (self.b, self.z, 1 - self.c)).wait_recv()
        finish(self.sends)

    @staticmethod
    def scratch(pool, nz, rows, name):
        pool.vmem(f"{name}_came", (nz, rows // nz, 128))
        pool.dma(f"{name}_own", 1)
        for step in ("a", "b", "c"):
            pool.dma(f"{name}_{step}_s", nz)
            pool.dma(f"{name}_{step}_r", nz)


class ChainSum:
    def __init__(self, nz, pieces, slack, h, f, m, name):
        self.b, self.z, self.c = here()
        self.nz, self.pieces, self.h, self.f, self.m, self.name = nz, pieces, h, f, m, name
        self.ch = h.shape[0] // 2 // pieces
        self.slack = slack
        self.steps = pieces + 2 * slack * (nz - 1)
        self.next = 0

    def rows(self, side, p):
        return band(side * self.pieces * self.ch + p * self.ch, self.ch)

    def copies(self, side, p):
        m, n = self.m, self.name
        came = m[f"{n}_came"].at[side, p]
        piece = self.f.at[self.c, self.rows(side, p)]
        step = 1 - 2 * side
        on = (self.b, lax.rem(self.z + step + self.nz, self.nz), self.c)
        back = (self.b, lax.rem(self.z - step + self.nz, self.nz), self.c)
        over = (self.b, self.z, 1 - self.c)
        sem = lambda kind: m[f"{n}_{kind}"].at[side, p]
        return (
            lambda src: remote(src, came, sem("a_s"), sem("a_r"), on),
            lambda src: remote(src, piece, sem("b_s"), sem("b_r"), back),
            lambda src: remote(src, piece, sem("c_s"), sem("c_r"), over),
            piece,
        )

    def pump(self, s):
        last = self.nz - 1
        for side in range(2):
            pos = self.z if side == 0 else last - self.z
            p = s - self.slack * pos

            @pl.when((p >= 0) & (p < self.pieces))
            def _():
                on, back, over, piece = self.copies(side, p)
                own = self.h.at[self.rows(side, p)]
                came = self.m[f"{self.name}_came"].at[side, p]

                @pl.when(pos == 0)
                def _():
                    on(own).start()

                @pl.when(pos > 0)
                def _():
                    on(came).wait_recv()
                    came[...] = (own[...].astype(F32) + came[...].astype(F32)).astype(BF16)

                @pl.when((pos > 0) & (pos < last))
                def _():
                    on(came).start()

                @pl.when(pos == last)
                def _():
                    pltpu.make_async_copy(came, piece, self.m[f"{self.name}_own"].at[side, p]).start()
                    back(came).start()
                    over(came).start()

            q = s - self.slack * (last + last - pos)

            @pl.when((q >= 0) & (q < self.pieces) & (pos < last))
            def _():
                on, back, over, piece = self.copies(side, q)
                back(piece).wait_recv()
                over(piece).start()

                @pl.when(pos > 0)
                def _():
                    back(piece).start()

    def go(self, count=None):
        upto = self.steps if count is None else min(self.steps, self.next + count)
        if upto - self.next > 4:
            lax.fori_loop(self.next, upto, lambda s, carry: (self.pump(s), carry)[1], 0)
        else:
            for s in range(self.next, upto):
                self.pump(s)
        self.next = upto

    def end(self):
        self.go()
        last = self.nz - 1

        def one(p, carry):
            for side in range(2):
                pos = self.z if side == 0 else last - self.z
                on, back, over, piece = self.copies(side, p)
                other = self.f.at[1 - self.c, self.rows(side, p)]
                came = self.m[f"{self.name}_came"].at[side, p]
                sem = lambda kind: self.m[f"{self.name}_{kind}"].at[side, p]
                remote(other, other, sem("c_s"), sem("c_r"), (self.b, self.z, 1 - self.c)).wait_recv()
                over(piece).wait_send()

                @pl.when(pos < last)
                def _():
                    on(came).wait_send()

                @pl.when(pos > 0)
                def _():
                    back(piece).wait_send()

                @pl.when(pos == last)
                def _():
                    pltpu.make_async_copy(came, piece, self.m[f"{self.name}_own"].at[side, p]).wait()

            return carry

        lax.fori_loop(0, self.pieces, one, 0)

    @staticmethod
    def scratch(pool, rows, pieces, name):
        pool.vmem(f"{name}_came", (2, pieces, rows // 2 // pieces, 128))
        for kind in ("a_s", "a_r", "b_s", "b_r", "c_s", "c_r", "own"):
            pool.dma(f"{name}_{kind}", 2, pieces)


TAIL_IN = ("g_att", "g_heavy", "h_feed", "gm_own", "gf_l", "gf_r", "ids", "tok_own", "vecs", "gain_part", "router")
TAIL_OUT = ("delta", "f_att", "f_both", "vectors")


def tail_kernel(nb, nz, pool, *refs):
    i = dict(zip(TAIL_IN, refs[: len(TAIL_IN)]))
    out = dict(zip(TAIL_OUT, refs[len(TAIL_IN) : len(TAIL_IN) + len(TAIL_OUT)]))
    m = pool.bind(refs[len(TAIL_IN) + len(TAIL_OUT) :])
    b, z, c = here()
    twin = (b, z, 1 - c)
    bpeers, zpeers = others(b, nb), others(z, nz)
    own, D = i["gm_own"].shape
    greet([twin] + [(j, z, c) for j in bpeers] + [(b, j, c) for j in zpeers])
    gh, sib_h, both_h = i["g_heavy"], m["sib_h"], m["both_h"]
    rf, rh = i["h_feed"].shape[0], sib_h.shape[0]
    to_twin = remote(gh.at[1 - c], sib_h, m["sib_h_s"].at[0], m["sib_h_r"].at[0], twin)
    to_twin.start()
    shard = ShardSum(i["g_att"], m["h_att"], m, "ga")
    shard.start()
    both = ChainSum(nz, 8, 2, both_h, out["f_both"], m, "zb")
    att = BlockSum(nz, m["h_att"], out["f_att"], m, "za")
    both_h[pl.ds(0, rf)] = i["h_feed"][...]
    to_twin.wait_recv()
    both_h[pl.ds(rf, rh)] = (gh[c].astype(F32) + sib_h[...].astype(F32)).astype(BF16)
    both.go(1)
    shard.spread()
    both.go(2)

    hot_t = hot_rows(i["ids"][...] - b * own, own).T
    owned = jnp.sum(hot_t.astype(F32), axis=1, keepdims=True) > 0.5
    gf = jnp.where(owned, mm(hot_t, i["gf_r"][...], 1, 0), i["gf_l"][...])
    r, xh = norm_parts(i["tok_own"][...].astype(F32))
    gain_part = jnp.sum(gf * xh, axis=0, keepdims=True)
    low = m["low"]
    low[...] = (i["gm_own"][...] + norm_back(gf, xh, r, i["vecs"][0:1])).astype(BF16)
    rows = Gather(low, out["delta"], m, "td")
    both.go(2)
    shard.relay()
    rows.start()
    both.go(3)

    vec = m["vec_mine"]
    vec[...] = jnp.zeros_like(vec)
    vec[pl.ds(0, 1)] = gain_part
    vec[pl.ds(1, 1)] = i["gain_part"][...]
    vec[pl.ds(2, 1)] = i["router"][...]
    sends = [to_twin]

    def vec_step(name, me, peers, device):
        got = m[f"{name}_got"]
        got[me] = vec[...]
        for j in peers:
            copy = remote(vec, got.at[me], m[f"{name}_s"].at[j], m[f"{name}_r"].at[me], device(j))
            copy.start()
            sends.append(copy)

    def vec_end(name, peers, device):
        got = m[f"{name}_got"]
        for j in peers:
            remote(got.at[j], got.at[j], m[f"{name}_s"].at[j], m[f"{name}_r"].at[j], device(j)).wait_recv()
        return functools.reduce(lambda x, y: x + y, [got[j] for j in range(got.shape[0])])

    by_core, by_branch, by_block = (lambda j: (b, z, j)), (lambda j: (j, z, c)), (lambda j: (b, j, c))
    vec_step("vc", c, [1 - c], by_core)
    both.go(1)
    shard.collect()
    att.start()
    total = vec_end("vc", [1 - c], by_core)
    vec2 = m["vec_pair"]
    vec2[...] = total
    vec = vec2
    vec_step("vb", b, bpeers, by_branch)
    both.go(3)
    total = vec_end("vb", bpeers, by_branch)
    vec3 = m["vec_group"]
    vec3[...] = total
    vec = vec3
    vec_step("vz", z, zpeers, by_block)
    both.go(2)
    att.spread()
    rows.relay()
    both.go(4)
    out["vectors"][...] = vec_end("vz", zpeers, by_block)
    both.go()
    att.forward()
    both.end()
    att.end()
    shard.end()
    rows.wait()
    finish(sends)


def tail(nb, nz, given):
    own, D = given["gm_own"].shape
    ra, rh, rf = given["g_att"].shape[2], given["g_heavy"].shape[1], given["h_feed"].shape[0]
    shape = lambda *dims: jax.ShapeDtypeStruct(dims, BF16)
    outs = dict(
        delta=shape(nb, own, D), f_att=shape(2, ra, 128), f_both=shape(2, rf + rh, 128),
        vectors=jax.ShapeDtypeStruct((8, D), F32),
    )
    pool = Pool()
    pool.vmem("sib_h", (rh, 128))
    pool.vmem("both_h", (rf + rh, 128))
    pool.vmem("h_att", (ra, 128))
    pool.vmem("low", (own, D))
    pool.dma("sib_h_s", 1)
    pool.dma("sib_h_r", 1)
    ShardSum.scratch(pool, ra, "ga")
    BlockSum.scratch(pool, nz, ra, "za")
    ChainSum.scratch(pool, rf + rh, 8, "zb")
    Gather.scratch(pool, "td")
    for name in ("vec_mine", "vec_pair", "vec_group"):
        pool.vmem(name, (8, D), F32)
    for name, count in (("vc", 2), ("vb", nb), ("vz", nz)):
        pool.vmem(f"{name}_got", (count, 8, D), F32)
        pool.dma(f"{name}_s", count)
        pool.dma(f"{name}_r", count)
    got = pl.pallas_call(
        functools.partial(tail_kernel, nb, nz, pool),
        out_shape=tuple(outs[name] for name in TAIL_OUT),
        in_specs=[HB if name == "g_att" else VM for name in TAIL_IN],
        out_specs=(HB,) * 3 + (VM,),
        scratch_shapes=pool.shapes,
        compiler_params=pltpu.CompilerParams(
            collective_id=4, has_side_effects=True, vmem_limit_bytes=56 << 20
        ),
    )(*(given[name] for name in TAIL_IN))
    return dict(zip(TAIL_OUT, got))


MID_IN = (
    "tok_own", "cot_own", "ids", "vecs", "tok_r", "cot_r", "gate", "mixed", "attn_l",
    "le", "lr", "re", "rr",
)
MID_OUT = ("base", "ff", "gm_own", "gm_r", "gate_feed", "gain_part", "g_feed", "g_rx", "f_gate")


MID_EARLY = ("base", "ff", "g_rx", "g_feed")
MID_LATE = ("re", "rr", "cot_own", "le", "lr")


def lane_blocks(x):
    return [x[:, n * 128 : (n + 1) * 128] for n in range(x.shape[1] // 128)]


def pack_rows(g, start, parts):
    for part in parts:
        size = part.shape[0] // 2
        for core in range(2):
            g[core, pl.ds(start, size)] = part[core * size : (core + 1) * size].astype(BF16)
        start += size
    return start


def down_pieces(rows, D):
    steps = 8
    per, step = D // steps // 32, rows // steps
    pieces = []
    for n in range(steps):
        spots = [(r, k) for k in range(D // 128) for r in range(0, step, 32)]
        pieces += [(p // per, n * (D // steps) + p % per * 32, n * step + r, k) for p, (r, k) in enumerate(spots)]
    return pieces


def pack_down(g, start, x):
    for block, at, row, k in down_pieces(*x.shape):
        g[start + block, pl.ds(at, 32)] = x[row : row + 32, k * 128 : (k + 1) * 128].astype(BF16)


def mid_kernel(nb, nz, pool, *refs):
    i = dict(zip(MID_IN, refs[: len(MID_IN)]))
    out = dict(zip(MID_OUT, refs[len(MID_IN) : len(MID_IN) + len(MID_OUT)]))
    m = pool.bind(refs[len(MID_IN) + len(MID_OUT) :])
    early = Early(MID_EARLY, out, m)
    late = Late(MID_LATE, i, m)
    b, z, c = here()
    greet([(b, z, 1 - c)] + [(j, z, c) for j in others(b, nb)] + [(b, j, c) for j in others(z, nz)])
    own, D = i["tok_own"].shape
    cap = i["ids"].shape[0]
    fl = i["le"].shape[2] // nb
    fh = i["re"].shape[2]
    gain = i["vecs"][1:2]

    pick, pick_t = m["pick"], m["pick_t"]
    hot = hot_rows(i["ids"][...] - b * own, own)
    pick[...] = hot
    pick_t[...] = hot.T
    owned = jnp.sum(pick_t[...].astype(F32), axis=1, keepdims=True) > 0.5
    mid_o, mid_r = m["mid_o"], m["mid_r"]
    mid_o[...] = i["tok_own"][...].astype(F32) + jnp.where(
        owned, mm(pick_t[...], i["mixed"][...], 1, 0), i["attn_l"][...]
    )
    mid_r[...] = i["tok_r"][...].astype(F32) + i["mixed"][...].astype(F32)
    n_o, n_r = m["n_o"], m["n_r"]
    n_o[...] = normed(mid_o[...], gain)
    n_r[...] = normed(mid_r[...], gain)
    gate = i["gate"][...]
    seed_r = m["seed_r"]
    seed_r[...] = (gate * i["cot_r"][...].astype(F32)).astype(BF16)

    def both_ways(n, seed, expand, narrow, row0, tile, count, hid, du, dv, ff, dn):
        def one(t, carry):
            lanes = band(t * tile, tile)
            wd = narrow[band(row0 + t * tile, tile)]
            u = mm(n[...], expand[0, :, lanes], 1, 0)
            v = mm(n[...], expand[1, :, lanes], 1, 0)
            g, dg = gelu_parts(u)
            low = (g * v).astype(BF16)
            hid[:, lanes] = low
            dh = mm(seed[...], wd, 1, 1)
            du[:, lanes] = (dh * v * dg).astype(BF16)
            dv[:, lanes] = (dh * g).astype(BF16)
            one_ff = mm(low, wd, 1, 0)
            one_dn = mm(du[:, lanes], expand[0, :, lanes], 1, 1) + mm(dv[:, lanes], expand[1, :, lanes], 1, 1)
            ff[...] = jnp.where(t == 0, one_ff, ff[...] + one_ff)
            dn[...] = jnp.where(t == 0, one_dn, dn[...] + one_dn)
            return carry

        lax.fori_loop(0, count, one, 0)

    ff_r, dn_r, ff_o, dn_o = m["ff_r"], m["dn_r"], m["ff_o"], m["dn_o"]
    late.need("re", "rr")
    both_ways(
        n_r, seed_r, i["re"], i["rr"], c * fh, fl, fh // fl, m["hid_r"], m["du_r"], m["dv_r"], ff_r, dn_r
    )
    n_t = m["n_t"]
    n_t[...] = n_r[...].T
    g_gate = m["g_gate"]
    for k, x in enumerate(lane_blocks(mm(n_t[...], m["du_r"][...], 1, 0))):
        g_gate[pl.ds(k * D, D)] = x.astype(BF16)
    chain = BlockSum(nz, g_gate, out["f_gate"], m, "zg")
    chain.start()
    late.need()
    both_ways(
        n_o, i["cot_own"], i["le"], i["lr"], 0, fl, nb, m["hid_o"], m["du_o"], m["dv_o"], ff_o, dn_o,
    )
    out["gate_feed"][...] = jnp.sum(i["cot_r"][...].astype(F32) * ff_r[...], axis=-1, keepdims=True)
    part = m["part"]
    out["ff"][...] = ff_r[...].astype(BF16)
    out["base"][...] = mid_o[...] + ff_o[...]
    early.put("ff", "base")
    part[...] = (dn_r[...] + mm(pick[...], dn_o[...].astype(BF16), 1, 0)).astype(BF16)

    def weights_heavy():
        gx = out["g_rx"]
        for k, x in enumerate(lane_blocks(mm(n_t[...], m["dv_r"][...], 1, 0))):
            gx[k] = x.astype(BF16)
        pack_down(gx, fh // 128, mm(m["hid_r"][...], seed_r[...], 0, 0))
        early.put("g_rx")
        chain.spread()

    def weights_light():
        n_t[...] = n_o[...].T
        g = out["g_feed"]

        def one(t, carry):
            lanes = band(t * fl, fl)
            gate_part = mm(n_t[...], m["du_o"][:, lanes], 1, 0)
            up_part = mm(n_t[...], m["dv_o"][:, lanes], 1, 0)
            down = mm(m["hid_o"][:, lanes], i["cot_own"][...], 0, 0)
            pack_rows(g.at[t], 0, lane_blocks(gate_part) + lane_blocks(up_part) + lane_blocks(down))
            return carry

        lax.fori_loop(0, nb, one, 0)
        early.put("g_feed")

    sums = m["sums"]
    group_sum_steps(nb, part, sums, m, [weights_heavy, weights_light])
    dn_sum = sums[...]
    dn_own = jnp.where(owned, mm(pick_t[...], dn_sum, 1, 0), dn_o[...])
    r, xh = norm_parts(mid_o[...])
    out["gm_own"][...] = i["cot_own"][...].astype(F32) + norm_back(dn_own, xh, r, gain)
    out["gain_part"][...] = jnp.sum(dn_own * xh, axis=0, keepdims=True)
    r, xh = norm_parts(mid_r[...])
    out["gm_r"][...] = i["cot_r"][...].astype(F32) + norm_back(dn_sum.astype(F32), xh, r, gain)
    chain.forward()
    chain.end()
    early.end()


def middle(nb, nz, given):
    own, D = given["tok_own"].shape
    cap = given["ids"].shape[0]
    wide = given["le"].shape[2]
    fl = wide // nb
    fh = given["re"].shape[2]
    shape = lambda *dims: jax.ShapeDtypeStruct(dims, BF16)
    shape32 = lambda *dims: jax.ShapeDtypeStruct(dims, F32)
    packed = (2 * D * fl + fl * D) // 2 // 128
    outs = dict(
        base=shape32(own, D), ff=shape(cap, D), gm_own=shape32(own, D), gm_r=shape32(cap, D), gate_feed=shape32(cap, 1),
        gain_part=shape32(1, D), g_feed=shape(nb, 2, packed, 128), g_rx=shape(2 * fh // 128, D, 128), f_gate=shape(2, D * fh // 128, 128),
    )
    pool = Pool()
    Early.scratch(pool, MID_EARLY, outs)
    Late.scratch(pool, MID_LATE, given)
    pool.vmem("pick", (cap, own))
    pool.vmem("pick_t", (own, cap))
    for name, count in (("o", own), ("r", cap)):
        pool.vmem(f"mid_{name}", (count, D), F32)
        pool.vmem(f"n_{name}", (count, D))
        pool.vmem(f"ff_{name}", (count, D), F32)
        pool.vmem(f"dn_{name}", (count, D), F32)
        for kind in ("hid", "du", "dv"):
            pool.vmem(f"{kind}_{name}", (count, wide if name == "o" else fh))
    pool.vmem("seed_r", (cap, D))
    pool.vmem("n_t", (D, own))
    pool.vmem("part", (cap, D))
    pool.vmem("sums", (cap, D))
    pool.vmem("g_gate", (D * fh // 128, 128))
    group_sum_scratch(pool, nb, cap, D)
    BlockSum.scratch(pool, nz, D * fh // 128, "zg")
    got = pl.pallas_call(
        functools.partial(mid_kernel, nb, nz, pool),
        out_shape=tuple(outs[name] for name in MID_OUT),
        in_specs=[HB if name in MID_LATE else VM for name in MID_IN],
        out_specs=tuple(HB if name in ("f_gate",) + MID_EARLY else VM for name in MID_OUT),
        scratch_shapes=pool.shapes,
        compiler_params=pltpu.CompilerParams(
            collective_id=2, has_side_effects=True, vmem_limit_bytes=60 << 20
        ),
    )(*(given[name] for name in MID_IN))
    return dict(zip(MID_OUT, got))


BACK_OUT = ("gf_r", "gf_l", "g_att", "g_heavy", "router", "lay", "h_feed", "f_rx")
BACK_IN = (
    "gm_own", "gm_r", "gate", "gate_feed", "ids", "q", "k", "v", "lm", "lh", "first_w", "ctx_l",
    "qr", "kv", "rmerge", "rheads", "first_r", "ctx_r", "attn_r", "vecs",
    "base", "ff", "g_feed", "g_rx",
)


BACK_LATE = (
    "base", "gm_own", "q", "k", "v", "lm", "lh", "first_w", "ctx_l", "rheads", "first_r", "attn_r",
)


def back_names(inner):
    return BACK_IN if inner else BACK_IN + ("trio",)


def heavy_back(i, m, seed, x):
    kv, qr = i["kv"], i["qr"]
    half, rw = qr.shape
    keys, values, keys_t, dk, dv, dq_t, do = (
        m[n] for n in ("keys", "values", "keys_t", "dk", "dv", "dq_t", "do")
    )
    keys[...] = kv[:, :rw]
    values[...] = kv[:, rw:]
    keys_t[...] = keys[...].T
    do[...] = mm(seed, i["rmerge"][...], 1, 1).astype(BF16)
    dk[...] = jnp.zeros_like(dk)
    dv[...] = jnp.zeros_like(dv)
    dq_t[...] = jnp.zeros_like(dq_t)
    some = 128

    def heavy(n):
        at = band(n * some, some)
        for h in range(rw // DH):
            qh, doh = only_head(qr[at], h), only_head(do[at], h)
            s = mm(keys[...], qh, 1, 1) * SCALE
            w = jnp.exp(s - jnp.max(s, axis=0, keepdims=True))
            p = w * (1.0 / jnp.sum(w, axis=0, keepdims=True))
            dp = mm(values[...], doh, 1, 1)
            ds = (p * (dp - jnp.sum(p * dp, axis=0, keepdims=True))).astype(BF16)
            dk[...] += mm(ds, qh, 1, 0)
            dv[...] += mm(p.astype(BF16), doh, 1, 0)
            got = mm(keys_t[...], ds, 1, 0)
            dq_t[:, at] += jnp.where(head_lanes(got.shape, h, 0), got, 0.0)

    def end():
        x[:, :rw] = (dk[...] * SCALE).astype(BF16)
        x[:, rw:] = dv[...].astype(BF16)

    return [functools.partial(heavy, n) for n in range(half // some)] + [end]


def heavy_back_plain(i):
    half, rw = i["qr"].shape
    split = lambda y: y.reshape(y.shape[0], -1, DH)
    at = lax.axis_index("core") * half
    seed = (i["gate"] * i["gm_r"]).astype(BF16)
    seed = lax.dynamic_slice(seed, (at, 0), (half, seed.shape[1]))
    do = split(mm(seed, i["rmerge"], 1, 1).astype(BF16))
    q, k, v = split(i["qr"]), split(i["kv"][:, :rw]), split(i["kv"][:, rw:])
    p = jax.nn.softmax(jnp.einsum("qhe,khe->hqk", q, k, preferred_element_type=F32) * SCALE, axis=-1)
    dp = jnp.einsum("qhe,khe->hqk", do, v, preferred_element_type=F32)
    ds = (p * (dp - jnp.sum(p * dp, -1, keepdims=True))).astype(BF16)
    dq = jnp.einsum("hqk,khe->qhe", ds, k, preferred_element_type=F32) * SCALE
    dk = jnp.einsum("hqk,qhe->khe", ds, q, preferred_element_type=F32) * SCALE
    dv = jnp.einsum("hqk,qhe->khe", p.astype(BF16), do, preferred_element_type=F32)
    both = jnp.concatenate([dk.reshape(-1, rw), dv.reshape(-1, rw)], 1).astype(BF16)
    both = lax.psum_scatter(both, DP, scatter_dimension=0, tiled=True)
    return jnp.stack([dq.reshape(half, rw).astype(BF16), both[:, :rw], both[:, rw:]], 0)


def back_kernel(nb, nz, pool, inner, *refs):
    names = back_names(inner)
    i = dict(zip(names, refs[: len(names)]))
    out = dict(zip(BACK_OUT, refs[len(names) : len(names) + len(BACK_OUT)]))
    m = pool.bind(refs[len(names) + len(BACK_OUT) :])
    late = Late(BACK_LATE, i, m)
    b, z, c = here()
    twin = (b, z, 1 - c)
    bpeers, zpeers = others(b, nb), others(z, nz)
    own, D = i["gm_own"].shape
    rows = own * nb
    cap = i["ids"].shape[0]
    half = cap // 2
    rw = i["rmerge"].shape[0]
    wl = i["q"].shape[1]
    last, first = b == nb - 1, b == 0
    after = (
        jnp.where(last, 0, b + 1), jnp.where(last, lax.rem(z + c, nz), z), jnp.where(last, 1 - c, c),
    )
    before = (
        jnp.where(first, nb - 1, b - 1),
        jnp.where(first, lax.rem(z + nz - 1 + c, nz), z),
        jnp.where(first, 1 - c, c),
    )
    greet([twin, after, before] + [(j, z, c) for j in bpeers] + [(b, j, c) for j in zpeers])
    mine_at, other_at = band(c * half, half), band((1 - c) * half, half)
    sends = []
    layer = Gather(m["layer"], out["lay"], m, "ly")
    shard = ShardSum(i["g_feed"], out["h_feed"], m, "gf")
    chain = BlockSum(nz, i["g_rx"], out["f_rx"], m, "zx")
    chain.start()
    shard.start()

    def go(copy):
        copy.start()
        sends.append(copy)

    gm_half = i["gm_r"][mine_at]
    gate_half = i["gate"][mine_at]
    seed = (gate_half * gm_half).astype(BF16)
    pack_rows(out["g_heavy"], 3 * rw // 2 * (D // 128), lane_blocks(mm(i["ctx_r"][...], seed, 0, 0)))
    trio = m["trio"] if inner else i["trio"]

    def spot(core, j):
        return band((2 * j + core) * half, half)

    def to_twin(j):
        return remote(x.at[spot(1 - c, j)], sib.at[j], m["bs_sib_s"].at[j], m["bs_sib_r"].at[j], twin)

    shard.spread()
    if inner:
        x, sib, came = m["dkv"], m["bs_sib"], m["bs_came"]
        pieces = heavy_back(i, m, seed, x)
        pieces[-1:] = [functools.partial(lambda f: (f(), [go(to_twin(j)) for j in zpeers + [z]]), pieces[-1])]
    else:
        pieces = []
    group_sum_steps(nb, i["ff"], m["ff_sum"], m, pieces, "fs")
    late.need()
    pick_t = hot_rows(i["ids"][...] - b * own, own).T
    scaled = (i["gate"][...] * m["ff_sum"][...].astype(F32)).astype(BF16)
    m["layer"][...] = (i["base"][...] + mm(pick_t, scaled, 1, 0)).astype(BF16)
    shard.relay()
    layer.start()

    low, do_l = m["low"], m["do_l"]
    low[...] = i["gm_own"][...].astype(BF16)
    do_l[...] = mm(low[...], i["lm"][...], 1, 1).astype(BF16)
    for j in zpeers if inner else []:
        to_twin(j).wait_recv()
        sib[j] = (x[spot(c, j)].astype(F32) + sib[j].astype(F32)).astype(BF16)
        go(remote(sib.at[j], came.at[z], m["bs_rs_s"].at[j], m["bs_rs_r"].at[z], (b, j, c)))

    q, k, v = i["q"], i["k"], i["v"]
    lk_t, dkl, dvl, dql = m["lk_t"], m["dkl"], m["dvl"], m["dql"]
    lk_t[...] = k[...].T
    dkl[...] = jnp.zeros_like(dkl)
    dvl[...] = jnp.zeros_like(dvl)
    blocks = own // WIN
    first_key = (2 * z + c) * rows + b * own - WIN
    total = 2 * nz * rows

    def light(n_, carry):
        g, n = n_ // blocks, lax.rem(n_, blocks)
        lanes = band(g * 2 * DH, 2 * DH)
        at = band(n * WIN, WIN)
        near = pl.ds(pl.multiple_of(n * WIN, WIN), 3 * WIN)
        q2, do2, k2, v2, kt2 = q[at, lanes], do_l[at, lanes], k[near, lanes], v[near, lanes], lk_t[lanes, near]
        allowed = near_keys((3 * WIN, WIN), 0, first_key + n * WIN, total)
        got_k = got_v = None
        got_q = []
        for h in range(2):
            qh, doh = only_head(q2, h), only_head(do2, h)
            s = jnp.where(allowed, mm(k2, qh, 1, 1) * SCALE, NEGATIVE)
            w = jnp.exp(s - jnp.max(s, axis=0, keepdims=True))
            p = w * (1.0 / jnp.sum(w, axis=0, keepdims=True))
            dp = mm(v2, doh, 1, 1)
            ds = (p * (dp - jnp.sum(p * dp, axis=0, keepdims=True))).astype(BF16)
            one_k, one_v = mm(ds, qh, 1, 0), mm(p.astype(BF16), doh, 1, 0)
            got_k = one_k if got_k is None else got_k + one_k
            got_v = one_v if got_v is None else got_v + one_v
            got_q.append(mm(kt2, ds, 1, 0))
        dkl[near, lanes] += got_k
        dvl[near, lanes] += got_v
        both = jnp.where(head_lanes((2 * DH, WIN), 0, 0), got_q[0], got_q[1])
        dql[at, lanes] = (both.T * SCALE).astype(BF16)
        return carry

    lax.fori_loop(0, blocks * (wl // (2 * DH)), light, 0)
    layer.relay()
    shard.collect()
    rim, came_rim = m["rim"], m["came_rim"]
    for n, start in ((0, WIN + own), (1, 0)):
        rim[n, :, :wl] = (dkl[pl.ds(start, WIN)] * SCALE).astype(BF16)
        rim[n, :, wl:] = dvl[pl.ds(start, WIN)].astype(BF16)
    go(remote(rim.at[0], came_rim.at[0], m["rim_s"].at[0], m["rim_r"].at[0], after))
    go(remote(rim.at[1], came_rim.at[1], m["rim_s"].at[1], m["rim_r"].at[1], before))

    if inner:
        to_twin(z).wait_recv()
        mine = x[spot(c, z)].astype(F32) + sib[z].astype(F32)
        for j in zpeers:
            remote(sib.at[j], came.at[j], m["bs_rs_s"].at[j], m["bs_rs_r"].at[j], (b, j, c)).wait_recv()
            mine = mine + came[j].astype(F32)
        trio[0] = (m["dq_t"][...].T * SCALE).astype(BF16)
        trio[1] = mine[:, :rw].astype(BF16)
        trio[2] = mine[:, rw:].astype(BF16)
    chain.spread()
    rheads = i["rheads"]
    picked = mm(trio[0], rheads[0], 1, 0) + mm(trio[1], rheads[1], 1, 0) + mm(trio[2], rheads[2], 1, 0)

    for n, device in ((0, before), (1, after)):
        remote(rim.at[n], came_rim.at[n], m["rim_s"].at[n], m["rim_r"].at[n], device).wait_recv()
    dkl[pl.ds(WIN, WIN)] += came_rim[0, :, :wl].astype(F32) * (1.0 / SCALE)
    dvl[pl.ds(WIN, WIN)] += came_rim[0, :, wl:].astype(F32)
    dkl[pl.ds(own, WIN)] += came_rim[1, :, :wl].astype(F32) * (1.0 / SCALE)
    dvl[pl.ds(own, WIN)] += came_rim[1, :, wl:].astype(F32)
    dk_own, dv_own = m["dk_own"], m["dv_own"]
    dk_own[...] = (dkl[pl.ds(WIN, own)] * SCALE).astype(BF16)
    dv_own[...] = dvl[pl.ds(WIN, own)].astype(BF16)
    lh = i["lh"]
    gf_l = out["gf_l"]
    gf_l[...] = mm(dql[...], lh[0], 1, 1) + mm(dk_own[...], lh[1], 1, 1) + mm(dv_own[...], lh[2], 1, 1)

    gate, first_r = i["gate"], i["first_r"]
    gate_attn = jnp.sum(gm_half * i["attn_r"][...], axis=-1, keepdims=True)
    total_part = m["part"]
    low_gf = gf_l[...].astype(BF16)
    router_sum = None
    for at, extra, more in ((other_at, None, None), (mine_at, gate_attn, picked)):
        g = gate[at]
        d_gate = i["gate_feed"][at] if extra is None else i["gate_feed"][at] + extra
        d_logit = d_gate * g * (1.0 - g)
        one = jnp.sum(d_logit * first_r[at].astype(F32), axis=0, keepdims=True)
        router_sum = one if router_sum is None else router_sum + one
        sum_ = mm(hot_rows(i["ids"][at] - b * own, own), low_gf, 1, 0) + d_logit * i["vecs"][2:3]
        if more is not None:
            sum_ = sum_ + more
        total_part[at] = sum_.astype(BF16)
    out["router"][...] = router_sum

    first_t, g_att = m["first_t"], out["g_att"]
    hl = wl // nb

    def weights_light():
        first_t[...] = i["first_w"][pl.ds(WIN, own)].T

        def one(t, carry):
            lanes = band(t * 2 * hl, 2 * hl)
            for n, x in enumerate((dql, dk_own, dv_own)):
                both = mm(first_t[...], x[:, lanes], 1, 0)
                for k in range(2):
                    pack_rows(g_att.at[2 * t + k], n * D // 2, [both[:, k * hl : (k + 1) * hl]])
            return carry

        lax.fori_loop(0, nb // 2, one, 0)

    def weights_rest():
        def one(t, carry):
            both = mm(i["ctx_l"][:, band(t * 2 * hl, 2 * hl)], low[...], 0, 0)
            for k in range(2):
                pack_rows(g_att.at[2 * t + k], 3 * D // 2, lane_blocks(both[k * hl : (k + 1) * hl]))
            return carry

        lax.fori_loop(0, nb // 2, one, 0)
        first_half = first_r[mine_at]
        for n in range(3):
            pack_rows(out["g_heavy"], n * rw // 2 * (D // 128), lane_blocks(mm(trio[n], first_half, 0, 0)))

    group_sum_steps(nb, total_part, out["gf_r"], m, [weights_light, weights_rest])
    chain.forward()
    chain.end()
    shard.end()
    layer.wait()
    finish(sends)


def back(nb, nz, given):
    own, D = given["gm_own"].shape
    cap = given["ids"].shape[0]
    half = cap // 2
    rw = given["rmerge"].shape[0]
    wl = given["q"].shape[1]
    deep = 2 * nz * half
    feed_rows, rx_rows = given["g_feed"].shape[2], given["g_rx"].shape[0]
    shape = lambda *dims: jax.ShapeDtypeStruct(dims, BF16)
    outs = dict(
        gf_r=shape(cap, D), gf_l=jax.ShapeDtypeStruct((own, D), F32),
        g_att=shape(nb, 2, 2 * D * wl // nb // 128, 128), g_heavy=shape(2, 2 * D * rw // 128, 128),
        router=jax.ShapeDtypeStruct((1, D), F32),
        lay=shape(nb, own, D), h_feed=shape(feed_rows, 128), f_rx=shape(2, rx_rows, 128),
    )
    pool = Pool()
    inner = deep <= 4096
    if inner:
        pool.vmem("keys", (deep, rw))
        pool.vmem("values", (deep, rw))
        pool.vmem("keys_t", (rw, deep))
        pool.vmem("dk", (deep, rw), F32)
        pool.vmem("dv", (deep, rw), F32)
        pool.vmem("dq_t", (rw, half), F32)
        pool.vmem("do", (half, rw))
        pool.vmem("trio", (3, half, rw))
        pool.vmem("dkv", (deep, 2 * rw))
        for name in ("bs_sib", "bs_came"):
            pool.vmem(name, (nz, half, 2 * rw))
    pool.vmem("low", (own, D))
    pool.vmem("do_l", (own, wl))
    pool.vmem("lk_t", (wl, own + 2 * WIN))
    pool.vmem("dkl", (own + 2 * WIN, wl), F32)
    pool.vmem("dvl", (own + 2 * WIN, wl), F32)
    pool.vmem("dql", (own, wl))
    pool.vmem("dk_own", (own, wl))
    pool.vmem("dv_own", (own, wl))
    pool.vmem("rim", (2, WIN, 2 * wl))
    pool.vmem("came_rim", (2, WIN, 2 * wl))
    pool.vmem("first_t", (D, own))
    pool.vmem("part", (cap, D))
    group_sum_scratch(pool, nb, cap, D)
    for name in ("bs_sib", "bs_rs") if inner else ():
        pool.dma(f"{name}_s", nz)
        pool.dma(f"{name}_r", nz)
    if not inner:
        given = dict(given, trio=heavy_back_plain(given))
    Late.scratch(pool, BACK_LATE, given)
    pool.vmem("layer", (own, D))
    pool.vmem("ff_sum", (cap, D))
    group_sum_scratch(pool, nb, cap, D, "fs")
    ShardSum.scratch(pool, feed_rows, "gf")
    BlockSum.scratch(pool, nz, rx_rows, "zx")
    Gather.scratch(pool, "ly")
    pool.dma("rim_s", 2)
    pool.dma("rim_r", 2)
    got = pl.pallas_call(
        functools.partial(back_kernel, nb, nz, pool, inner),
        out_shape=tuple(outs[name] for name in BACK_OUT),
        in_specs=[HB if name in ("g_feed",) + BACK_LATE else VM for name in back_names(inner)],
        out_specs=tuple(HB if name in ("lay", "f_rx") else VM for name in BACK_OUT),
        scratch_shapes=pool.shapes,
        compiler_params=pltpu.CompilerParams(
            collective_id=3, has_side_effects=True, vmem_limit_bytes=62 << 20
        ),
    )(*(given[name] for name in back_names(inner)))
    return dict(zip(BACK_OUT, got))


FIN_OUT = ("layer", "delta", "re", "rr", "lh", "lm", "rh", "rm", "le", "lr")


def finish_kernel(lay, dlt, gate, rx, att, both, *outs):
    o = dict(zip(FIN_OUT, outs))
    o["layer"][...] = lay[...].astype(F32)
    o["delta"][...] = dlt[...].astype(F32)
    size = rx.shape[2]
    blocks = gate.shape[1]
    for core in range(2):
        for part in range(2):
            for k in range(blocks):
                at = 2 * (core * blocks + k) + part
                o["re"][pl.ds(at, size, 4 * blocks), :] = (rx if part else gate)[core, k].astype(F32)
        for block, at, row, k in down_pieces(blocks * 128, size * 8):
            if row < blocks * 16:
                o["rr"][core, pl.ds(row, 32), k * 128 : (k + 1) * 128] = rx[core, blocks + block, pl.ds(at, 32)].astype(F32)

    @pl.when(pl.program_id(0) == 0)
    def _():
        for core in range(2):
            D, hl = o["lh"].shape[1:]
            start = 0
            for n in range(3):
                size = D // 2
                o["lh"][n, pl.ds(core * size, size)] = att[core, pl.ds(start, size)].astype(F32)
                start += size
            for k in range(D // 128):
                size = hl // 2
                o["lm"][pl.ds(core * size, size), k * 128 : (k + 1) * 128] = att[core, pl.ds(start, size)].astype(F32)
                start += size
            start = D * 3 * o["lr"].shape[0] // 256
            size = o["rm"].shape[0] // 2
            for n in range(4):
                dst = o["rm"] if n == 3 else o["rh"].at[n]
                for k in range(D // 128):
                    dst[pl.ds(core * size, size), k * 128 : (k + 1) * 128] = both[core, pl.ds(start, size)].astype(F32)
                    start += size
            start = 0
            fl = o["lr"].shape[0]
            lanes = fl // 128
            size = D // 2
            for part in range(2):
                for k in range(lanes):
                    o["le"][pl.ds(core * size * 2 * lanes + 2 * k + part, size, 2 * lanes), :] = both[
                        core, pl.ds(start, size)
                    ].astype(F32)
                    start += size
            size = fl // 2
            for k in range(D // 128):
                o["lr"][pl.ds(core * size, size), k * 128 : (k + 1) * 128] = both[core, pl.ds(start, size)].astype(F32)
                start += size


def finish_all(lay, dlt, gate, rx, att, both, hl, fl, rw):
    steps = 8
    rows, D = lay.shape
    fh = gate.shape[1] * 128
    shape = lambda *dims: jax.ShapeDtypeStruct(dims, F32)
    whole = lambda *dims: pl.BlockSpec(dims, lambda n: (0,) * len(dims))
    tall = lambda count, width: pl.BlockSpec((count // steps, width), lambda n: (n, 0))
    return dict(
        zip(
            FIN_OUT,
            pl.pallas_call(
                finish_kernel,
                grid=(steps,),
                out_shape=(
                    shape(rows, D), shape(rows, D), shape(D * 4 * fh // 128, 128), shape(2, fh, D),
                    shape(3, D, hl), shape(hl, D), shape(3, rw, D), shape(rw, D),
                    shape(D * 2 * fl // 128, 128), shape(fl, D),
                ),
                in_specs=[
                    tall(rows, D), tall(rows, D),
                    pl.BlockSpec((2, fh // 128, D // steps, 128), lambda n: (0, 0, n, 0)),
                    pl.BlockSpec((2, 2 * fh // 128, D // steps, 128), lambda n: (0, 0, n, 0)),
                    whole(*att.shape), whole(*both.shape),
                ],
                out_specs=(
                    tall(rows, D), tall(rows, D), tall(D * 4 * fh // 128, 128),
                    pl.BlockSpec((2, fh // steps, D), lambda n: (0, n, 0)),
                    whole(3, D, hl), whole(hl, D), whole(3, rw, D), whole(rw, D),
                    whole(D * 2 * fl // 128, 128), whole(fl, D),
                ),
                compiler_params=pltpu.CompilerParams(vmem_limit_bytes=50 << 20),
            )(lay, dlt, gate, rx, att, both),
        )
    )


def woven(x, width):
    blocks = width // 128
    return x.reshape(-1, blocks, 2, 128).transpose(0, 2, 1, 3).reshape(-1, 2, width)


def per_device(
    tokens,
    cotangent,
    gain_before,
    gain_middle,
    router_vector,
    local_heads,
    local_merge,
    routed_heads,
    routed_merge,
    local_expand,
    local_reduce,
    routed_expand,
    routed_reduce,
    routed_slots,
    routed_counts,
):
    nb = lax.axis_size("branch")
    nz = lax.axis_size("zz")
    core = lax.axis_index("core")
    rows, D = tokens.shape
    fh = routed_expand.shape[2] // 2
    vecs = jnp.stack([gain_before, gain_middle, router_vector])
    rheads = routed_heads.transpose(1, 2, 0)
    f = front(
        nb, nz, tokens, cotangent, routed_slots[None], routed_counts, vecs, rheads, routed_merge,
        local_heads.transpose(1, 0, 2), local_merge, local_expand.transpose(1, 0, 2), local_reduce,
    )
    re_half = lax.dynamic_slice(routed_expand, (0, 0, core * fh), (D, 2, fh)).transpose(1, 0, 2)
    f = dict(f, vecs=vecs, re=re_half, rr=routed_reduce, rmerge=routed_merge, rheads=rheads)
    f = dict(f, **middle(nb, nz, f))
    f["g_rx"] = f["g_rx"].reshape(-1, 128)
    f = dict(f, **back(nb, nz, f))
    f = dict(f, **tail(nb, nz, f))
    g = finish_all(
        f["lay"].reshape(rows, D), f["delta"].reshape(rows, D), f["f_gate"].reshape(2, -1, D, 128),
        f["f_rx"].reshape(2, -1, D, 128), f["f_att"], f["f_both"], hl=local_merge.shape[0], fl=local_reduce.shape[0],
        rw=routed_merge.shape[0],
    )
    return (
        g["layer"],
        g["delta"],
        f["vectors"][0],
        f["vectors"][1],
        f["vectors"][2],
        g["lh"].transpose(1, 0, 2),
        g["lm"],
        g["rh"].transpose(2, 0, 1),
        g["rm"],
        woven(g["le"], local_reduce.shape[0]),
        g["lr"],
        woven(g["re"], 2 * fh),
        g["rr"].reshape(2 * fh, D),
    )


def solution(mesh):
    nb = mesh.shape["branch"]
    fine = Mesh(mesh.devices.reshape(nb, -1, 2), ("branch", "zz", "core"))
    rows = P(DP, None)
    cols = P(None, None, "branch")
    deep = P("branch", None)
    return jax.shard_map(
        per_device,
        mesh=fine,
        in_specs=(
            rows, rows, P(), P(), P(), cols, deep, cols, deep, cols, deep, cols, deep, P(DP), P(),
        ),
        out_specs=(
            rows, rows, P(), P(), P(), cols, deep, cols, deep, cols, deep, cols, deep,
        ),
        check_vma=False,
    )
```

```python
import functools

import jax
import jax.numpy as jnp
from jax import lax
from jax.experimental import pallas as pl
from jax.experimental.pallas import tpu as pltpu
from jax.sharding import Mesh
from jax.sharding import PartitionSpec as P

DH = 64
WIN = 128
EPSILON = 1e-06
NEGATIVE = -1e30
HIGHEST = lax.Precision.HIGHEST
F32 = jnp.float32
BF16 = jnp.bfloat16
SCALE = DH ** (-0.5)
DP = ("zz", "core")


def mm(a, b, ca, cb):
    return lax.dot_general(a, b, (((ca,), (cb,)), ((), ())), preferred_element_type=F32)


def norm_parts(values):
    r = lax.rsqrt(jnp.mean(values * values, axis=-1, keepdims=True) + EPSILON)
    return r, values * r


def norm_back(dn, xh, r, gain):
    g = dn * gain
    return r * (g - xh * jnp.mean(g * xh, axis=-1, keepdims=True))


def gelu_parts(u):
    c = 0.7978845608028654
    t = jnp.tanh(c * (u + 0.044715 * u * u * u))
    g = 0.5 * u * (1.0 + t)
    dg = 0.5 * (1.0 + t) + 0.5 * u * (1.0 - t * t) * c * (1.0 + 3 * 0.044715 * u * u)
    return g, dg


def feed(n, seed, w_gate, w_up, w_down):
    u = mm(n, w_gate, 1, 0)
    v = mm(n, w_up, 1, 0)
    g, dg = gelu_parts(u)
    hidden = (g * v).astype(BF16)
    out = mm(hidden, w_down, 1, 0)
    dh = mm(seed, w_down, 1, 1)
    du = (dh * v * dg).astype(BF16)
    dv = (dh * g).astype(BF16)
    dn = mm(du, w_gate, 1, 1) + mm(dv, w_up, 1, 1)
    dwg = mm(n, du, 0, 0)
    dwu = mm(n, dv, 0, 0)
    dwd = mm(hidden, seed, 0, 0)
    return out, dn, dwg, dwu, dwd


MESH = pl.DeviceIdType.MESH


def remote(src, dst, send, recv, device):
    return pltpu.make_async_remote_copy(
        src_ref=src, dst_ref=dst, send_sem=send, recv_sem=recv, device_id=device, device_id_type=MESH
    )


def greet(devices):
    barrier = pltpu.get_barrier_semaphore()
    for device in devices:
        pl.semaphore_signal(barrier, inc=1, device_id=device, device_id_type=MESH)
    pl.semaphore_wait(barrier, len(devices))


def here():
    return lax.axis_index("branch"), lax.axis_index("zz"), lax.axis_index("core")


def others(me, count):
    return [lax.rem(me + k, count) for k in range(1, count)]


def band(start, size):
    return pl.ds(pl.multiple_of(start, size), size)


def finish(copies):
    for copy in copies:
        if copy.is_remote:
            copy.wait_send()
        else:
            copy.wait()


class Pool:
    def __init__(self):
        self.names = []
        self.shapes = []

    def add(self, name, shape):
        self.names.append(name)
        self.shapes.append(shape)

    def vmem(self, name, shape, dtype=BF16):
        self.add(name, pltpu.VMEM(shape, dtype))

    def dma(self, name, *shape):
        self.add(name, pltpu.SemaphoreType.DMA(shape))

    def bind(self, refs):
        return dict(zip(self.names, refs, strict=True))


class Early:
    def __init__(self, names, out, m):
        self.names, self.out, self.m = names, dict(out), m
        self.copies = []
        for name in names:
            out[name] = m[f"out_{name}"]

    def put(self, *names):
        for name in names:
            sem = self.m["out_s"].at[self.names.index(name)]
            copy = pltpu.make_async_copy(self.m[f"out_{name}"], self.out[name], sem)
            copy.start()
            self.copies.append(copy)

    def end(self):
        assert len(self.copies) == len(self.names)
        finish(self.copies)

    @staticmethod
    def scratch(pool, names, shapes):
        for name in names:
            pool.vmem(f"out_{name}", shapes[name].shape, shapes[name].dtype)
        pool.dma("out_s", len(names))


class Late:
    def __init__(self, names, given, m):
        self.copies = {}
        for k, name in enumerate(names):
            copy = pltpu.make_async_copy(given[name], m[f"in_{name}"], m["in_s"].at[k])
            copy.start()
            self.copies[name] = copy
            given[name] = m[f"in_{name}"]

    def need(self, *names):
        for name in names or tuple(self.copies):
            self.copies.pop(name).wait()

    @staticmethod
    def scratch(pool, names, given):
        for name in names:
            pool.vmem(f"in_{name}", given[name].shape, given[name].dtype)
        pool.dma("in_s", len(names))


def group_sum_scratch(pool, nb, rows, width, tag="gs"):
    for name in ("sib", "part", "came"):
        pool.vmem(f"{tag}_{name}", (nb, rows // 2 // nb, width))
    for name in ("sib", "rs", "ag", "fw"):
        pool.dma(f"{tag}_{name}_s", nb)
        pool.dma(f"{tag}_{name}_r", nb)


def group_sum_steps(nb, x, o, m, meanwhile=(), tag="gs"):
    m = {name[len(tag) + 1 :]: ref for name, ref in m.items() if name.startswith(tag + "_")}
    b, z, c = here()
    half = x.shape[0] // 2
    ch = half // nb
    twin = (b, z, 1 - c)
    peers = others(b, nb)
    sib, part, came = m["sib"], m["part"], m["came"]
    work = list(meanwhile)

    def aside():
        if work:
            work.pop(0)()

    def rows(core, j):
        return band(core * half + j * ch, ch)

    order = peers + [b]
    to_twin = [
        remote(x.at[rows(1 - c, j)], sib.at[j], m["sib_s"].at[j], m["sib_r"].at[j], twin)
        for j in order
    ]
    for copy in to_twin:
        copy.start()
    sends = []
    for j, copy in zip(peers, to_twin):
        copy.wait_recv()
        part[j] = (x[rows(c, j)].astype(F32) + sib[j].astype(F32)).astype(BF16)
        send = remote(part.at[j], came.at[b], m["rs_s"].at[j], m["rs_r"].at[b], (j, z, c))
        send.start()
        sends.append(send)
    aside()
    to_twin[-1].wait_recv()
    total = x[rows(c, b)].astype(F32) + sib[b].astype(F32)
    for j in peers:
        remote(part.at[j], came.at[j], m["rs_s"].at[j], m["rs_r"].at[j], (j, z, c)).wait_recv()
        total = total + came[j].astype(F32)
    mine = o.at[rows(c, b)]
    mine[...] = total.astype(BF16)
    for j in peers:
        send = remote(mine, mine, m["ag_s"].at[j], m["ag_r"].at[b], (j, z, c))
        send.start()
        sends.append(send)
    send = remote(mine, mine, m["fw_s"].at[b], m["fw_r"].at[b], twin)
    send.start()
    sends.append(send)
    aside()
    for j in peers:
        piece = o.at[rows(c, j)]
        remote(piece, piece, m["ag_s"].at[j], m["ag_r"].at[j], (j, z, c)).wait_recv()
        send = remote(piece, piece, m["fw_s"].at[j], m["fw_r"].at[j], twin)
        send.start()
        sends.append(send)
    while work:
        aside()
    for j in order:
        piece = o.at[rows(1 - c, j)]
        remote(piece, piece, m["fw_s"].at[j], m["fw_r"].at[j], twin).wait_recv()
    finish(to_twin + sends)


VM = pl.BlockSpec(memory_space=pltpu.VMEM)
HB = pl.BlockSpec(memory_space=pl.ANY)


def normed(x, gain):
    x = x.astype(F32)
    r = lax.rsqrt(jnp.mean(x * x, axis=-1, keepdims=True) + EPSILON)
    return (x * r * gain).astype(BF16)


def head_lanes(shape, h, dim):
    place = lax.broadcasted_iota(jnp.int32, shape, dim)
    return (place >= h * DH) & (place < (h + 1) * DH)


def only_head(x, h):
    return jnp.where(head_lanes(x.shape, h, 1), x, jnp.zeros_like(x))


def near_keys(shape, key_dim, first, total):
    key = lax.broadcasted_iota(jnp.int32, shape, key_dim)
    query = lax.broadcasted_iota(jnp.int32, shape, 1 - key_dim)
    gap = key - query
    return (gap >= 0) & (gap <= 2 * WIN) & (key + first >= 0) & (key + first < total)


def hot_rows(ids, count):
    spot = lax.broadcasted_iota(jnp.int32, (ids.shape[0], count), 1)
    return jnp.where(ids == spot, 1.0, 0.0).astype(BF16)


FRONT_OUT = (
    "tok_r", "cot_r", "first_r", "gate", "qr", "kv", "lh", "lm", "le", "lr", "first_w",
    "q", "k", "v", "ctx_l", "attn_l", "ctx_r", "attn_r", "mixed", "ids", "tok_own", "cot_own",
)


FRONT_EARLY = (
    "kv", "lh", "lm", "q", "k", "v", "first_w", "tok_r", "cot_r", "first_r", "ctx_l", "attn_l",
)


def front_kernel(nb, nz, pool, *refs):
    tokens, cotangent, slots, counts, vecs, rheads, rmerge, s_lh, s_lm, s_le, s_lr = refs[:11]
    out = dict(zip(FRONT_OUT, refs[11 : 11 + len(FRONT_OUT)]))
    m = pool.bind(refs[11 + len(FRONT_OUT) :])
    early = Early(FRONT_EARLY, out, m)
    ids = out["ids"]
    gain, router = vecs[0:1], vecs[2:3]
    b, z, c = here()
    twin = (b, z, 1 - c)
    bpeers, zpeers = others(b, nb), others(z, nz)
    rows, D = tokens.shape
    own = rows // nb
    cap = slots.shape[1]
    half = cap // 2
    rw = rmerge.shape[0]
    after = (b, lax.rem(z + c, nz), 1 - c)
    before = (b, lax.rem(z + nz - 1 + c, nz), 1 - c)
    far = (b, lax.rem(z + nz - 1 + 2 * c, nz), 1 - c)
    greet([twin, far] + [(j, z, c) for j in bpeers] + [(b, j, c) for j in zpeers])
    sends = []

    def go(copy):
        copy.start()
        sends.append(copy)

    pairs = [(s_lh, out["lh"]), (s_lm, out["lm"]), (s_le, out["le"]), (s_lr, out["lr"])]

    def place(i, j):
        src, dst = pairs[i]
        if i in (0, 2):
            return dst.at[:, :, band(j * src.shape[2], src.shape[2])]
        return dst.at[band(j * src.shape[0], src.shape[0])]

    def cut(i, ref, core):
        if i in (0, 2):
            size = ref.shape[1] // 2
            return ref.at[:, band(core * size, size)]
        size = ref.shape[0] // 2
        return ref.at[band(core * size, size)]

    def send_weights(i):
        for j in bpeers:
            go(remote(cut(i, pairs[i][0], c), cut(i, place(i, b), c), m["w_s"].at[i, j], m["w_r"].at[i, b], (j, z, c)))

    send_weights(0)
    send_weights(1)
    for i in range(4):
        pltpu.make_async_copy(pairs[i][0], place(i, b), m["own_s"].at[i]).start()
    halo = m["halo"]
    go(remote(tokens.at[pl.ds(rows - WIN, WIN)], halo.at[0], m["halo_s"].at[0], m["halo_r"].at[0], after))
    go(remote(tokens.at[pl.ds(0, WIN)], halo.at[1], m["halo_s"].at[1], m["halo_r"].at[1], before))

    n_own = counts[2 * z + c]
    offset = jnp.where(c == 0, 0, cap - n_own)
    rank = lax.broadcasted_iota(jnp.int32, (cap, cap), 0)
    slot = lax.broadcasted_iota(jnp.int32, (cap, cap), 1)
    shift = jnp.where((rank == slot + offset) & (slot < n_own), 1.0, 0.0).astype(BF16)
    line = lax.broadcasted_iota(jnp.int32, (16, cap), 0)
    high, rest = slots[...] // 64, slots[...] % 64
    digits = jnp.where(line == 0, high, jnp.where(line == 1, rest, jnp.where(line == 2, 1, 0)))
    found = mm(shift, digits.astype(F32).astype(BF16), 1, 1)
    ids[...] = jnp.where(found[:, 2:3] > 0.5, found[:, 0:1] * 64.0 + found[:, 1:2], -1.0).astype(jnp.int32)
    for n, (name, source) in enumerate((("tok_own", tokens), ("cot_own", cotangent))):
        go(pltpu.make_async_copy(source.at[band(b * own, own)], out[name], m["rows_s"].at[n]))
    picks, sib = m["picks"], m["sib"]
    step = cap // 4
    for k in range(4):
        at = pl.ds(k * step, step)
        hot = hot_rows(ids[at], rows)
        picks[at, :D] = mm(hot, tokens[...], 1, 0).astype(BF16)
        picks[at, D:] = mm(hot, cotangent[...], 1, 0).astype(BF16)
        go(remote(picks.at[at], sib.at[at], m["pick_s"].at[k], m["pick_r"].at[k], twin))
    for k in range(4):
        at = pl.ds(k * step, step)
        remote(picks.at[at], sib.at[at], m["pick_s"].at[k], m["pick_r"].at[k], twin).wait_recv()
        tok = picks[at, :D].astype(F32) + sib[at, :D].astype(F32)
        out["tok_r"][at] = tok.astype(BF16)
        out["cot_r"][at] = (picks[at, D:].astype(F32) + sib[at, D:].astype(F32)).astype(BF16)
        first = normed(tok, gain)
        out["first_r"][at] = first
        logit = jnp.sum(first.astype(F32) * router, axis=-1, keepdims=True)
        out["gate"][at] = 1.0 / (1.0 + jnp.exp(-logit))

    early.put("tok_r", "cot_r", "first_r")
    own_rows = out["first_r"][band(c * half, half)]
    out["qr"][...] = mm(own_rows, rheads[0], 1, 1).astype(BF16)
    kv = out["kv"]
    mine = kv.at[band((2 * z + c) * half, half)]
    mine[:, :rw] = mm(own_rows, rheads[1], 1, 1).astype(BF16)
    mine[:, rw:] = mm(own_rows, rheads[2], 1, 1).astype(BF16)
    for j in zpeers:
        go(remote(mine, mine, m["kv_s"].at[j], m["kv_r"].at[z], (b, j, c)))
    go(remote(mine, mine, m["kf_s"].at[z], m["kf_r"].at[z], twin))

    first_w = out["first_w"]
    first_w[pl.ds(WIN, own)] = normed(tokens[band(b * own, own)], gain)
    for i in range(2):
        remote(halo.at[i], halo.at[i], m["halo_s"].at[i], m["halo_r"].at[i], twin).wait_recv()
    lead = tokens[band(jnp.maximum(b * own - WIN, 0), WIN)]
    trail = tokens[band(jnp.minimum((b + 1) * own, rows - WIN), WIN)]
    first_w[pl.ds(0, WIN)] = normed(jnp.where(b > 0, lead, halo[0]), gain)
    first_w[pl.ds(WIN + own, WIN)] = normed(jnp.where(b < nb - 1, trail, halo[1]), gain)

    def pass_weights(i):
        for j in bpeers:
            dst = cut(i, place(i, j), c)
            remote(dst, dst, m["w_s"].at[i, j], m["w_r"].at[i, j], (j, z, c)).wait_recv()
            go(remote(dst, dst, m["wf_s"].at[i, j], m["wf_r"].at[i, j], twin))

    def take_weights(i):
        for j in bpeers:
            dst = cut(i, place(i, j), 1 - c)
            remote(dst, dst, m["wf_s"].at[i, j], m["wf_r"].at[i, j], twin).wait_recv()

    pass_weights(0)
    for j in zpeers:
        piece = kv.at[band((2 * j + c) * half, half)]
        remote(piece, piece, m["kv_s"].at[j], m["kv_r"].at[j], (b, j, c)).wait_recv()
        go(remote(piece, piece, m["kf_s"].at[j], m["kf_r"].at[j], twin))
    take_weights(0)
    send_weights(2)
    send_weights(3)
    pltpu.make_async_copy(pairs[0][0], place(0, b), m["own_s"].at[0]).wait()
    lh, q, k, v = out["lh"], out["q"], out["k"], out["v"]
    q[...] = mm(first_w[pl.ds(WIN, own)], lh[0], 1, 0).astype(BF16)
    k[...] = mm(first_w[...], lh[1], 1, 0).astype(BF16)
    v[...] = mm(first_w[...], lh[2], 1, 0).astype(BF16)
    early.put("lh", "q", "k", "v", "first_w")
    pass_weights(1)

    blocks = own // WIN
    ctx = out["ctx_l"]
    first_key = (2 * z + c) * rows + b * own - WIN
    total = 2 * nz * rows

    def light(i, carry):
        g, n = i // blocks, lax.rem(i, blocks)
        lanes = band(g * 2 * DH, 2 * DH)
        at = band(n * WIN, WIN)
        keys = pl.ds(pl.multiple_of(n * WIN, WIN), 3 * WIN)
        q2, k2, v2 = q[at, lanes], k[keys, lanes], v[keys, lanes]
        allowed = near_keys((WIN, 3 * WIN), 1, first_key + n * WIN, total)
        parts = []
        for h in range(2):
            s = jnp.where(allowed, mm(only_head(q2, h), k2, 1, 1) * SCALE, NEGATIVE)
            w = jnp.exp(s - jnp.max(s, axis=-1, keepdims=True))
            p = (w / jnp.sum(w, axis=-1, keepdims=True)).astype(BF16)
            parts.append(mm(p, v2, 1, 0))
        ctx[at, lanes] = jnp.where(head_lanes((WIN, 2 * DH), 0, 1), parts[0], parts[1]).astype(BF16)
        return carry

    lax.fori_loop(0, blocks * (q.shape[1] // (2 * DH)), light, 0)
    take_weights(1)
    pltpu.make_async_copy(pairs[1][0], place(1, b), m["own_s"].at[1]).wait()
    attn_l = out["attn_l"]
    attn_l[...] = mm(ctx[...], out["lm"][...], 1, 0)
    early.put("lm", "ctx_l", "attn_l")

    for j in zpeers + [z]:
        piece = kv.at[band((2 * j + 1 - c) * half, half)]
        remote(piece, piece, m["kf_s"].at[j], m["kf_r"].at[j], twin).wait_recv()
    keys, values, qr, ctx_r = m["keys"], m["values"], out["qr"], out["ctx_r"]
    early.put("kv")
    keys[...] = kv[:, :rw]
    values[...] = kv[:, rw:]
    some = 128

    def heavy(i, carry):
        at = band(i * some, some)
        got = jnp.zeros((some, rw), F32)
        for h in range(rw // DH):
            s = mm(only_head(qr[at], h), keys[...], 1, 1) * SCALE
            w = jnp.exp(s - jnp.max(s, axis=-1, keepdims=True))
            p = (w / jnp.sum(w, axis=-1, keepdims=True)).astype(BF16)
            got = jnp.where(head_lanes((some, rw), h, 1), mm(p, values[...], 1, 0), got)
        ctx_r[at] = got.astype(BF16)
        return carry

    lax.fori_loop(0, half // some, heavy, 0)
    pass_weights(2)
    attn_r = out["attn_r"]
    attn_r[...] = mm(ctx_r[...], rmerge[...], 1, 0)

    part = m["part"]
    mine_at, other_at = band(c * half, half), band((1 - c) * half, half)
    low = attn_l[...].astype(BF16)
    part[other_at] = mm(hot_rows(ids[other_at] - b * own, own), low, 1, 0).astype(BF16)
    part[mine_at] = (
        mm(hot_rows(ids[mine_at] - b * own, own), low, 1, 0) + out["gate"][mine_at] * attn_r[...]
    ).astype(BF16)
    group_sum_steps(nb, part, out["mixed"], m, [lambda: pass_weights(3)])
    take_weights(2)
    take_weights(3)
    early.end()
    finish(sends)
    for i in (2, 3):
        pltpu.make_async_copy(pairs[i][0], place(i, b), m["own_s"].at[i]).wait()


def front(nb, nz, tokens, cotangent, slots, counts, vecs, rheads, rmerge, s_lh, s_lm, s_le, s_lr):
    rows, D = tokens.shape
    own = rows // nb
    cap = slots.shape[1]
    half = cap // 2
    rw = rmerge.shape[0]
    wl = nb * s_lm.shape[0]
    shape = lambda *dims: jax.ShapeDtypeStruct(dims, BF16)
    shape32 = lambda *dims: jax.ShapeDtypeStruct(dims, F32)
    outs = dict(
        tok_r=shape(cap, D), cot_r=shape(cap, D), first_r=shape(cap, D), gate=shape32(cap, 1),
        qr=shape(half, rw), kv=shape(2 * nz * half, 2 * rw),
        lh=shape(3, D, wl), lm=shape(wl, D),
        le=shape(2, D, nb * s_le.shape[2]), lr=shape(nb * s_lr.shape[0], D),
        first_w=shape(own + 2 * WIN, D), q=shape(own, wl), k=shape(own + 2 * WIN, wl),
        v=shape(own + 2 * WIN, wl), ctx_l=shape(own, wl), attn_l=shape32(own, D),
        ctx_r=shape(half, rw), attn_r=shape32(half, D), mixed=shape(cap, D),
        ids=jax.ShapeDtypeStruct((cap, 1), jnp.int32), tok_own=shape(own, D), cot_own=shape(own, D),
    )
    pool = Pool()
    pool.vmem("picks", (cap, 2 * D))
    pool.vmem("sib", (cap, 2 * D))
    pool.vmem("halo", (2, WIN, D))
    pool.vmem("keys", (2 * nz * half, rw))
    pool.vmem("values", (2 * nz * half, rw))
    pool.vmem("part", (cap, D))
    group_sum_scratch(pool, nb, cap, D)
    pool.dma("own_s", 4)
    pool.dma("rows_s", 2)
    Early.scratch(pool, FRONT_EARLY, outs)
    pool.dma("halo_s", 2)
    pool.dma("halo_r", 2)
    pool.dma("pick_s", 4)
    pool.dma("pick_r", 4)
    for name in ("w", "wf"):
        pool.dma(f"{name}_s", 4, nb)
        pool.dma(f"{name}_r", 4, nb)
    for name in ("kv", "kf"):
        pool.dma(f"{name}_s", nz)
        pool.dma(f"{name}_r", nz)
    got = pl.pallas_call(
        functools.partial(front_kernel, nb, nz, pool),
        out_shape=tuple(outs[name] for name in FRONT_OUT),
        in_specs=[VM] * 3 + [pl.BlockSpec(memory_space=pltpu.SMEM)] + [VM] * 3 + [HB] * 4,
        out_specs=tuple(
            HB if name in ("le", "lr", "tok_own", "cot_own") + FRONT_EARLY else VM for name in FRONT_OUT
        ),
        scratch_shapes=pool.shapes,
        compiler_params=pltpu.CompilerParams(
            collective_id=0, has_side_effects=True, vmem_limit_bytes=56 << 20
        ),
    )(tokens, cotangent, slots, counts, vecs, rheads, rmerge, s_lh, s_lm, s_le, s_lr)
    return dict(zip(FRONT_OUT, got))


def neighbours(b):
    return b + 1 - 2 * lax.rem(b, 2), lax.rem(b + 2, 4), 3 - b


class Gather:
    def __init__(self, src, dst, m, name):
        b, z, c = here()
        self.src, self.dst, self.m, self.name, self.b = src, dst, m, name, b
        self.bx, self.by, self.bd = neighbours(b)
        self.dx, self.dy = (self.bx, z, c), (self.by, z, c)
        self.sends = []

    def half(self, ref, k):
        size = self.src.shape[0] // 2
        return ref.at[pl.ds(k * size, size)]

    def go(self, copy):
        copy.start()
        self.sends.append(copy)

    def copy(self, way, k, src, slot, device):
        m, n = self.m, self.name
        return remote(
            self.half(src, k), self.half(self.dst.at[slot], k), m[f"{n}_{way}_s"].at[k], m[f"{n}_{way}_r"].at[k], device
        )

    def start(self):
        own = pltpu.make_async_copy(self.src, self.dst.at[self.b], self.m[f"{self.name}_own"].at[0])
        self.go(own)
        for first, second in ((0, 1), (1, 0)):
            self.go(self.copy("x", second, self.src, self.b, self.dx))
            self.go(self.copy("y", first, self.src, self.b, self.dy))

    def relay(self):
        came = self.dst.at[self.bx]
        self.copy("x", 1, came, self.bx, self.dx).wait_recv()
        self.go(self.copy("f", 1, came, self.bx, self.dy))
        came = self.dst.at[self.by]
        self.copy("y", 0, came, self.by, self.dy).wait_recv()
        self.go(self.copy("f", 0, came, self.by, self.dx))

    def wait(self):
        self.copy("x", 0, self.dst.at[self.bx], self.bx, self.dx).wait_recv()
        self.copy("y", 1, self.dst.at[self.by], self.by, self.dy).wait_recv()
        far = self.dst.at[self.bd]
        self.copy("f", 0, far, self.bd, self.dx).wait_recv()
        self.copy("f", 1, far, self.bd, self.dy).wait_recv()
        finish(self.sends)

    @staticmethod
    def scratch(pool, name):
        pool.dma(f"{name}_own", 1)
        for way in ("x", "y", "f"):
            pool.dma(f"{name}_{way}_s", 2)
            pool.dma(f"{name}_{way}_r", 2)


class ShardSum:
    def __init__(self, g, h, m, name):
        self.b, self.z, self.c = here()
        self.bx, self.by, self.bd = neighbours(self.b)
        self.g, self.h, self.m, self.name = g, h, m, name
        self.sib = m[f"{name}_sib"]
        size = g.shape[2] // 2
        self.parts = (pl.ds(0, size), pl.ds(size, size))
        self.sends = []

    def go(self, copy):
        copy.start()
        self.sends.append(copy)

    def pair(self, j):
        m, n = self.m, self.name
        return remote(
            self.g.at[j, 1 - self.c], self.sib.at[j], m[f"{n}_a_s"].at[j], m[f"{n}_a_r"].at[j],
            (self.b, self.z, 1 - self.c),
        )

    def kept(self, j):
        return pltpu.make_async_copy(
            self.g.at[j, self.c], self.m[f"{self.name}_kept"].at[j], self.m[f"{self.name}_kept_s"].at[j]
        )

    def start(self):
        for j in (self.bd, self.bx, self.by, self.b):
            self.go(self.pair(j))
            self.kept(j).start()

    def step(self, n, src, k):
        m = self.m
        device = (self.bx if n in (0, 1, 5) else self.by, self.z, self.c)
        return remote(
            src.at[self.parts[k]], m[f"{self.name}_came"].at[n], m[f"{self.name}_b_s"].at[n], m[f"{self.name}_b_r"].at[n],
            device,
        )

    def add(self, j):
        self.kept(j).wait()
        self.pair(j).wait_recv()
        self.sib[j] = (self.m[f"{self.name}_kept"][j].astype(F32) + self.sib[j].astype(F32)).astype(BF16)

    def spread(self):
        self.add(self.bd)
        self.go(self.step(1, self.sib.at[self.bd], 0))
        self.go(self.step(3, self.sib.at[self.bd], 1))
        self.add(self.bx)
        self.go(self.step(0, self.sib.at[self.bx], 0))
        self.add(self.by)
        self.go(self.step(2, self.sib.at[self.by], 1))
        self.add(self.b)

    def relay(self):
        came = self.m[f"{self.name}_came"]
        for n, j, k, then in ((1, self.by, 0, 4), (3, self.bx, 1, 5)):
            self.step(n, self.sib.at[j], k).wait_recv()
            at = self.parts[k]
            self.sib[j, at] = (self.sib[j, at].astype(F32) + came[n].astype(F32)).astype(BF16)
            self.go(self.step(then, self.sib.at[j], k))

    def collect(self):
        came = self.m[f"{self.name}_came"]
        for k, one, two in ((0, 0, 4), (1, 2, 5)):
            at = self.parts[k]
            self.step(one, self.sib.at[self.b], k).wait_recv()
            self.step(two, self.sib.at[self.b], k).wait_recv()
            total = self.sib[self.b, at].astype(F32) + came[one].astype(F32) + came[two].astype(F32)
            self.h[at] = total.astype(BF16)

    def end(self):
        finish(self.sends)

    @staticmethod
    def scratch(pool, rows, name):
        pool.vmem(f"{name}_sib", (4, rows, 128))
        pool.vmem(f"{name}_kept", (4, rows, 128))
        pool.dma(f"{name}_kept_s", 4)
        pool.vmem(f"{name}_came", (6, rows // 2, 128))
        pool.dma(f"{name}_a_s", 4)
        pool.dma(f"{name}_a_r", 4)
        pool.dma(f"{name}_b_s", 6)
        pool.dma(f"{name}_b_r", 6)


class BlockSum:
    def __init__(self, nz, h, f, m, name):
        self.b, self.z, self.c = here()
        self.peers = others(self.z, nz)
        self.h, self.f, self.m, self.name = h, f, m, name
        self.ch = h.shape[0] // nz
        self.sends = []

    def go(self, copy):
        copy.start()
        self.sends.append(copy)

    def rows(self, j):
        return band(j * self.ch, self.ch)

    def sem(self, kind, j):
        return self.m[f"{self.name}_{kind}_s"].at[j], self.m[f"{self.name}_{kind}_r"].at[j]

    def start(self):
        for j in self.peers:
            self.go(
                remote(
                    self.h.at[self.rows(j)], self.m[f"{self.name}_came"].at[self.z], self.sem("a", j)[0],
                    self.sem("a", self.z)[1], (self.b, j, self.c),
                )
            )

    def spread(self):
        came, z, c = self.m[f"{self.name}_came"], self.z, self.c
        total = self.h[self.rows(z)].astype(F32)
        for j in self.peers:
            remote(self.h.at[self.rows(j)], came.at[j], *self.sem("a", j), (self.b, j, c)).wait_recv()
            total = total + came[j].astype(F32)
        stage = came.at[z]
        stage[...] = total.astype(BF16)
        piece = self.f.at[c, self.rows(z)]
        for j in self.peers:
            self.go(remote(stage, piece, self.sem("b", j)[0], self.sem("b", z)[1], (self.b, j, c)))
        self.go(remote(stage, piece, *self.sem("c", z), (self.b, z, 1 - c)))
        self.go(pltpu.make_async_copy(stage, piece, self.m[f"{self.name}_own"].at[0]))

    def forward(self):
        c = self.c
        for j in self.peers:
            piece = self.f.at[c, self.rows(j)]
            remote(piece, piece, *self.sem("b", j), (self.b, j, c)).wait_recv()
            self.go(remote(piece, piece, *self.sem("c", j), (self.b, self.z, 1 - c)))

    def end(self):
        for j in self.peers + [self.z]:
            piece = self.f.at[1 - self.c, self.rows(j)]
            remote(piece, piece, *self.sem("c", j), (self.b, self.z, 1 - self.c)).wait_recv()
        finish(self.sends)

    @staticmethod
    def scratch(pool, nz, rows, name):
        pool.vmem(f"{name}_came", (nz, rows // nz, 128))
        pool.dma(f"{name}_own", 1)
        for step in ("a", "b", "c"):
            pool.dma(f"{name}_{step}_s", nz)
            pool.dma(f"{name}_{step}_r", nz)


class ChainSum:
    def __init__(self, nz, pieces, slack, h, f, m, name):
        self.b, self.z, self.c = here()
        self.nz, self.pieces, self.h, self.f, self.m, self.name = nz, pieces, h, f, m, name
        self.ch = h.shape[0] // 2 // pieces
        self.slack = slack
        self.steps = pieces + 2 * slack * (nz - 1)
        self.next = 0

    def rows(self, side, p):
        return band(side * self.pieces * self.ch + p * self.ch, self.ch)

    def copies(self, side, p):
        m, n = self.m, self.name
        came = m[f"{n}_came"].at[side, p]
        piece = self.f.at[self.c, self.rows(side, p)]
        step = 1 - 2 * side
        on = (self.b, lax.rem(self.z + step + self.nz, self.nz), self.c)
        back = (self.b, lax.rem(self.z - step + self.nz, self.nz), self.c)
        over = (self.b, self.z, 1 - self.c)
        sem = lambda kind: m[f"{n}_{kind}"].at[side, p]
        return (
            lambda src: remote(src, came, sem("a_s"), sem("a_r"), on),
            lambda src: remote(src, piece, sem("b_s"), sem("b_r"), back),
            lambda src: remote(src, piece, sem("c_s"), sem("c_r"), over),
            piece,
        )

    def pump(self, s):
        last = self.nz - 1
        for side in range(2):
            pos = self.z if side == 0 else last - self.z
            p = s - self.slack * pos

            @pl.when((p >= 0) & (p < self.pieces))
            def _():
                on, back, over, piece = self.copies(side, p)
                own = self.h.at[self.rows(side, p)]
                came = self.m[f"{self.name}_came"].at[side, p]

                @pl.when(pos == 0)
                def _():
                    on(own).start()

                @pl.when(pos > 0)
                def _():
                    on(came).wait_recv()
                    came[...] = (own[...].astype(F32) + came[...].astype(F32)).astype(BF16)

                @pl.when((pos > 0) & (pos < last))
                def _():
                    on(came).start()

                @pl.when(pos == last)
                def _():
                    pltpu.make_async_copy(came, piece, self.m[f"{self.name}_own"].at[side, p]).start()
                    back(came).start()
                    over(came).start()

            q = s - self.slack * (last + last - pos)

            @pl.when((q >= 0) & (q < self.pieces) & (pos < last))
            def _():
                on, back, over, piece = self.copies(side, q)
                back(piece).wait_recv()
                over(piece).start()

                @pl.when(pos > 0)
                def _():
                    back(piece).start()

    def go(self, count=None):
        upto = self.steps if count is None else min(self.steps, self.next + count)
        if upto - self.next > 4:
            lax.fori_loop(self.next, upto, lambda s, carry: (self.pump(s), carry)[1], 0)
        else:
            for s in range(self.next, upto):
                self.pump(s)
        self.next = upto

    def end(self):
        self.go()
        last = self.nz - 1

        def one(p, carry):
            for side in range(2):
                pos = self.z if side == 0 else last - self.z
                on, back, over, piece = self.copies(side, p)
                other = self.f.at[1 - self.c, self.rows(side, p)]
                came = self.m[f"{self.name}_came"].at[side, p]
                sem = lambda kind: self.m[f"{self.name}_{kind}"].at[side, p]
                remote(other, other, sem("c_s"), sem("c_r"), (self.b, self.z, 1 - self.c)).wait_recv()
                over(piece).wait_send()

                @pl.when(pos < last)
                def _():
                    on(came).wait_send()

                @pl.when(pos > 0)
                def _():
                    back(piece).wait_send()

                @pl.when(pos == last)
                def _():
                    pltpu.make_async_copy(came, piece, self.m[f"{self.name}_own"].at[side, p]).wait()

            return carry

        lax.fori_loop(0, self.pieces, one, 0)

    @staticmethod
    def scratch(pool, rows, pieces, name):
        pool.vmem(f"{name}_came", (2, pieces, rows // 2 // pieces, 128))
        for kind in ("a_s", "a_r", "b_s", "b_r", "c_s", "c_r", "own"):
            pool.dma(f"{name}_{kind}", 2, pieces)


TAIL_IN = ("g_att", "g_heavy", "h_feed", "gm_own", "gf_l", "gf_r", "ids", "tok_own", "vecs", "gain_part", "router")
TAIL_LATE = ("gf_r", "gf_l", "tok_own", "gm_own")
TAIL_OUT = ("delta", "f_att", "f_both", "vectors")


def tail_kernel(nb, nz, pool, *refs):
    i = dict(zip(TAIL_IN, refs[: len(TAIL_IN)]))
    out = dict(zip(TAIL_OUT, refs[len(TAIL_IN) : len(TAIL_IN) + len(TAIL_OUT)]))
    m = pool.bind(refs[len(TAIL_IN) + len(TAIL_OUT) :])
    late = Late(TAIL_LATE, i, m)
    b, z, c = here()
    twin = (b, z, 1 - c)
    bpeers, zpeers = others(b, nb), others(z, nz)
    own, D = i["gm_own"].shape
    greet([twin] + [(j, z, c) for j in bpeers] + [(b, j, c) for j in zpeers])
    gh, sib_h, both_h = i["g_heavy"], m["sib_h"], m["both_h"]
    rf, rh = i["h_feed"].shape[0], sib_h.shape[0]
    to_twin = remote(gh.at[1 - c], sib_h, m["sib_h_s"].at[0], m["sib_h_r"].at[0], twin)
    to_twin.start()
    shard = ShardSum(i["g_att"], m["h_att"], m, "ga")
    shard.start()
    both = ChainSum(nz, 6, 2, both_h, out["f_both"], m, "zb")
    att = BlockSum(nz, m["h_att"], out["f_att"], m, "za")
    both_h[pl.ds(0, rf)] = i["h_feed"][...]
    to_twin.wait_recv()
    both_h[pl.ds(rf, rh)] = (gh[c].astype(F32) + sib_h[...].astype(F32)).astype(BF16)
    both.go(1)
    shard.spread()
    both.go(2)

    late.need()
    hot_t = hot_rows(i["ids"][...] - b * own, own).T
    owned = jnp.sum(hot_t.astype(F32), axis=1, keepdims=True) > 0.5
    gf = jnp.where(owned, mm(hot_t, i["gf_r"][...], 1, 0), i["gf_l"][...])
    r, xh = norm_parts(i["tok_own"][...].astype(F32))
    gain_part = jnp.sum(gf * xh, axis=0, keepdims=True)
    low = m["low"]
    low[...] = (i["gm_own"][...] + norm_back(gf, xh, r, i["vecs"][0:1])).astype(BF16)
    rows = Gather(low, out["delta"], m, "td")
    both.go(2)
    shard.relay()
    rows.start()
    both.go(3)

    vec = m["vec_mine"]
    vec[...] = jnp.zeros_like(vec)
    vec[pl.ds(0, 1)] = gain_part
    vec[pl.ds(1, 1)] = i["gain_part"][...]
    vec[pl.ds(2, 1)] = i["router"][...]
    sends = [to_twin]

    def vec_step(name, me, peers, device):
        got = m[f"{name}_got"]
        got[me] = vec[...]
        for j in peers:
            copy = remote(vec, got.at[me], m[f"{name}_s"].at[j], m[f"{name}_r"].at[me], device(j))
            copy.start()
            sends.append(copy)

    def vec_end(name, peers, device):
        got = m[f"{name}_got"]
        for j in peers:
            remote(got.at[j], got.at[j], m[f"{name}_s"].at[j], m[f"{name}_r"].at[j], device(j)).wait_recv()
        return functools.reduce(lambda x, y: x + y, [got[j] for j in range(got.shape[0])])

    by_core, by_branch, by_block = (lambda j: (b, z, j)), (lambda j: (j, z, c)), (lambda j: (b, j, c))
    vec_step("vc", c, [1 - c], by_core)
    both.go(1)
    shard.collect()
    att.start()
    total = vec_end("vc", [1 - c], by_core)
    vec2 = m["vec_pair"]
    vec2[...] = total
    vec = vec2
    vec_step("vb", b, bpeers, by_branch)
    both.go(3)
    total = vec_end("vb", bpeers, by_branch)
    vec3 = m["vec_group"]
    vec3[...] = total
    vec = vec3
    vec_step("vz", z, zpeers, by_block)
    both.go(2)
    att.spread()
    rows.relay()
    both.go(4)
    out["vectors"][...] = vec_end("vz", zpeers, by_block)
    both.go()
    att.forward()
    both.end()
    att.end()
    shard.end()
    rows.wait()
    finish(sends)


def tail(nb, nz, given):
    own, D = given["gm_own"].shape
    ra, rh, rf = given["g_att"].shape[2], given["g_heavy"].shape[1], given["h_feed"].shape[0]
    shape = lambda *dims: jax.ShapeDtypeStruct(dims, BF16)
    outs = dict(
        delta=shape(nb, own, D), f_att=shape(2, ra, 128), f_both=shape(2, rf + rh, 128),
        vectors=jax.ShapeDtypeStruct((8, D), F32),
    )
    pool = Pool()
    Late.scratch(pool, TAIL_LATE, given)
    pool.vmem("sib_h", (rh, 128))
    pool.vmem("both_h", (rf + rh, 128))
    pool.vmem("h_att", (ra, 128))
    pool.vmem("low", (own, D))
    pool.dma("sib_h_s", 1)
    pool.dma("sib_h_r", 1)
    ShardSum.scratch(pool, ra, "ga")
    BlockSum.scratch(pool, nz, ra, "za")
    ChainSum.scratch(pool, rf + rh, 6, "zb")
    Gather.scratch(pool, "td")
    for name in ("vec_mine", "vec_pair", "vec_group"):
        pool.vmem(name, (8, D), F32)
    for name, count in (("vc", 2), ("vb", nb), ("vz", nz)):
        pool.vmem(f"{name}_got", (count, 8, D), F32)
        pool.dma(f"{name}_s", count)
        pool.dma(f"{name}_r", count)
    got = pl.pallas_call(
        functools.partial(tail_kernel, nb, nz, pool),
        out_shape=tuple(outs[name] for name in TAIL_OUT),
        in_specs=[HB if name in ("g_att",) + TAIL_LATE else VM for name in TAIL_IN],
        out_specs=(HB,) * 3 + (VM,),
        scratch_shapes=pool.shapes,
        compiler_params=pltpu.CompilerParams(
            collective_id=4, has_side_effects=True, vmem_limit_bytes=56 << 20
        ),
    )(*(given[name] for name in TAIL_IN))
    return dict(zip(TAIL_OUT, got))


MID_IN = (
    "tok_own", "cot_own", "ids", "vecs", "tok_r", "cot_r", "gate", "mixed", "attn_l",
    "le", "lr", "re", "rr",
)
MID_OUT = ("base", "ff", "gm_own", "gm_r", "gate_feed", "gain_part", "g_feed", "g_rx", "f_gate")


MID_EARLY = ("base", "ff", "g_rx", "g_feed")
MID_LATE = ("re", "rr", "cot_own", "le", "lr")


def lane_blocks(x):
    return [x[:, n * 128 : (n + 1) * 128] for n in range(x.shape[1] // 128)]


def pack_rows(g, start, parts):
    for part in parts:
        size = part.shape[0] // 2
        for core in range(2):
            g[core, pl.ds(start, size)] = part[core * size : (core + 1) * size].astype(BF16)
        start += size
    return start


def down_pieces(rows, D):
    steps = 8
    per, step = D // steps // 32, rows // steps
    pieces = []
    for n in range(steps):
        spots = [(r, k) for k in range(D // 128) for r in range(0, step, 32)]
        pieces += [(p // per, n * (D // steps) + p % per * 32, n * step + r, k) for p, (r, k) in enumerate(spots)]
    return pieces


def pack_down(g, start, x):
    for block, at, row, k in down_pieces(*x.shape):
        g[start + block, pl.ds(at, 32)] = x[row : row + 32, k * 128 : (k + 1) * 128].astype(BF16)


def mid_kernel(nb, nz, pool, *refs):
    i = dict(zip(MID_IN, refs[: len(MID_IN)]))
    out = dict(zip(MID_OUT, refs[len(MID_IN) : len(MID_IN) + len(MID_OUT)]))
    m = pool.bind(refs[len(MID_IN) + len(MID_OUT) :])
    early = Early(MID_EARLY, out, m)
    late = Late(MID_LATE, i, m)
    b, z, c = here()
    greet([(b, z, 1 - c)] + [(j, z, c) for j in others(b, nb)] + [(b, j, c) for j in others(z, nz)])
    own, D = i["tok_own"].shape
    cap = i["ids"].shape[0]
    fl = i["le"].shape[2] // nb
    fh = i["re"].shape[2]
    gain = i["vecs"][1:2]

    pick, pick_t = m["pick"], m["pick_t"]
    hot = hot_rows(i["ids"][...] - b * own, own)
    pick[...] = hot
    pick_t[...] = hot.T
    owned = jnp.sum(pick_t[...].astype(F32), axis=1, keepdims=True) > 0.5
    mid_o, mid_r = m["mid_o"], m["mid_r"]
    mid_o[...] = i["tok_own"][...].astype(F32) + jnp.where(
        owned, mm(pick_t[...], i["mixed"][...], 1, 0), i["attn_l"][...]
    )
    mid_r[...] = i["tok_r"][...].astype(F32) + i["mixed"][...].astype(F32)
    n_o, n_r = m["n_o"], m["n_r"]
    n_o[...] = normed(mid_o[...], gain)
    n_r[...] = normed(mid_r[...], gain)
    gate = i["gate"][...]
    seed_r = m["seed_r"]
    seed_r[...] = (gate * i["cot_r"][...].astype(F32)).astype(BF16)

    def both_ways(n, seed, expand, narrow, row0, tile, count, hid, du, dv, ff, dn):
        def one(t, carry):
            lanes = band(t * tile, tile)
            wd = narrow[band(row0 + t * tile, tile)]
            u = mm(n[...], expand[0, :, lanes], 1, 0)
            v = mm(n[...], expand[1, :, lanes], 1, 0)
            g, dg = gelu_parts(u)
            low = (g * v).astype(BF16)
            hid[:, lanes] = low
            dh = mm(seed[...], wd, 1, 1)
            du[:, lanes] = (dh * v * dg).astype(BF16)
            dv[:, lanes] = (dh * g).astype(BF16)
            one_ff = mm(low, wd, 1, 0)
            one_dn = mm(du[:, lanes], expand[0, :, lanes], 1, 1) + mm(dv[:, lanes], expand[1, :, lanes], 1, 1)
            ff[...] = jnp.where(t == 0, one_ff, ff[...] + one_ff)
            dn[...] = jnp.where(t == 0, one_dn, dn[...] + one_dn)
            return carry

        lax.fori_loop(0, count, one, 0)

    ff_r, dn_r, ff_o, dn_o = m["ff_r"], m["dn_r"], m["ff_o"], m["dn_o"]
    late.need("re", "rr")
    both_ways(
        n_r, seed_r, i["re"], i["rr"], c * fh, fl, fh // fl, m["hid_r"], m["du_r"], m["dv_r"], ff_r, dn_r
    )
    n_t = m["n_t"]
    n_t[...] = n_r[...].T
    g_gate = m["g_gate"]
    for k, x in enumerate(lane_blocks(mm(n_t[...], m["du_r"][...], 1, 0))):
        g_gate[pl.ds(k * D, D)] = x.astype(BF16)
    chain = BlockSum(nz, g_gate, out["f_gate"], m, "zg")
    chain.start()
    late.need()
    both_ways(
        n_o, i["cot_own"], i["le"], i["lr"], 0, fl, nb, m["hid_o"], m["du_o"], m["dv_o"], ff_o, dn_o,
    )
    out["gate_feed"][...] = jnp.sum(i["cot_r"][...].astype(F32) * ff_r[...], axis=-1, keepdims=True)
    part = m["part"]
    out["ff"][...] = ff_r[...].astype(BF16)
    out["base"][...] = mid_o[...] + ff_o[...]
    early.put("ff", "base")
    part[...] = (dn_r[...] + mm(pick[...], dn_o[...].astype(BF16), 1, 0)).astype(BF16)

    def weights_heavy():
        gx = out["g_rx"]
        for k, x in enumerate(lane_blocks(mm(n_t[...], m["dv_r"][...], 1, 0))):
            gx[k] = x.astype(BF16)
        pack_down(gx, fh // 128, mm(m["hid_r"][...], seed_r[...], 0, 0))
        early.put("g_rx")
        chain.spread()

    def weights_light():
        n_t[...] = n_o[...].T
        g = out["g_feed"]

        def one(t, carry):
            lanes = band(t * fl, fl)
            gate_part = mm(n_t[...], m["du_o"][:, lanes], 1, 0)
            up_part = mm(n_t[...], m["dv_o"][:, lanes], 1, 0)
            down = mm(m["hid_o"][:, lanes], i["cot_own"][...], 0, 0)
            pack_rows(g.at[t], 0, lane_blocks(gate_part) + lane_blocks(up_part) + lane_blocks(down))
            return carry

        lax.fori_loop(0, nb, one, 0)
        early.put("g_feed")

    sums = m["sums"]
    group_sum_steps(nb, part, sums, m, [weights_heavy, weights_light])
    dn_sum = sums[...]
    dn_own = jnp.where(owned, mm(pick_t[...], dn_sum, 1, 0), dn_o[...])
    r, xh = norm_parts(mid_o[...])
    out["gm_own"][...] = i["cot_own"][...].astype(F32) + norm_back(dn_own, xh, r, gain)
    out["gain_part"][...] = jnp.sum(dn_own * xh, axis=0, keepdims=True)
    r, xh = norm_parts(mid_r[...])
    out["gm_r"][...] = i["cot_r"][...].astype(F32) + norm_back(dn_sum.astype(F32), xh, r, gain)
    chain.forward()
    chain.end()
    early.end()


def middle(nb, nz, given):
    own, D = given["tok_own"].shape
    cap = given["ids"].shape[0]
    wide = given["le"].shape[2]
    fl = wide // nb
    fh = given["re"].shape[2]
    shape = lambda *dims: jax.ShapeDtypeStruct(dims, BF16)
    shape32 = lambda *dims: jax.ShapeDtypeStruct(dims, F32)
    packed = (2 * D * fl + fl * D) // 2 // 128
    outs = dict(
        base=shape32(own, D), ff=shape(cap, D), gm_own=shape32(own, D), gm_r=shape32(cap, D), gate_feed=shape32(cap, 1),
        gain_part=shape32(1, D), g_feed=shape(nb, 2, packed, 128), g_rx=shape(2 * fh // 128, D, 128), f_gate=shape(2, D * fh // 128, 128),
    )
    pool = Pool()
    Early.scratch(pool, MID_EARLY, outs)
    Late.scratch(pool, MID_LATE, given)
    pool.vmem("pick", (cap, own))
    pool.vmem("pick_t", (own, cap))
    for name, count in (("o", own), ("r", cap)):
        pool.vmem(f"mid_{name}", (count, D), F32)
        pool.vmem(f"n_{name}", (count, D))
        pool.vmem(f"ff_{name}", (count, D), F32)
        pool.vmem(f"dn_{name}", (count, D), F32)
        for kind in ("hid", "du", "dv"):
            pool.vmem(f"{kind}_{name}", (count, wide if name == "o" else fh))
    pool.vmem("seed_r", (cap, D))
    pool.vmem("n_t", (D, own))
    pool.vmem("part", (cap, D))
    pool.vmem("sums", (cap, D))
    pool.vmem("g_gate", (D * fh // 128, 128))
    group_sum_scratch(pool, nb, cap, D)
    BlockSum.scratch(pool, nz, D * fh // 128, "zg")
    got = pl.pallas_call(
        functools.partial(mid_kernel, nb, nz, pool),
        out_shape=tuple(outs[name] for name in MID_OUT),
        in_specs=[HB if name in MID_LATE else VM for name in MID_IN],
        out_specs=tuple(HB if name in ("f_gate",) + MID_EARLY else VM for name in MID_OUT),
        scratch_shapes=pool.shapes,
        compiler_params=pltpu.CompilerParams(
            collective_id=2, has_side_effects=True, vmem_limit_bytes=60 << 20
        ),
    )(*(given[name] for name in MID_IN))
    return dict(zip(MID_OUT, got))


BACK_OUT = ("gf_r", "gf_l", "g_att", "g_heavy", "router", "lay", "h_feed", "f_rx")
BACK_IN = (
    "gm_own", "gm_r", "gate", "gate_feed", "ids", "q", "k", "v", "lm", "lh", "first_w", "ctx_l",
    "qr", "kv", "rmerge", "rheads", "first_r", "ctx_r", "attn_r", "vecs",
    "base", "ff", "g_feed", "g_rx",
)


BACK_EARLY = ("h_feed", "gf_l", "g_att", "g_heavy")
BACK_LATE = (
    "base", "gm_own", "q", "k", "v", "lm", "lh", "first_w", "ctx_l", "rheads", "first_r", "attn_r",
)


def back_names(inner):
    return BACK_IN if inner else BACK_IN + ("trio",)


def heavy_back(i, m, seed, x):
    kv, qr = i["kv"], i["qr"]
    half, rw = qr.shape
    keys, values, keys_t, dk, dv, dq_t, do = (
        m[n] for n in ("keys", "values", "keys_t", "dk", "dv", "dq_t", "do")
    )
    keys[...] = kv[:, :rw]
    values[...] = kv[:, rw:]
    keys_t[...] = keys[...].T
    do[...] = mm(seed, i["rmerge"][...], 1, 1).astype(BF16)
    dk[...] = jnp.zeros_like(dk)
    dv[...] = jnp.zeros_like(dv)
    dq_t[...] = jnp.zeros_like(dq_t)
    some = 128

    def heavy(n):
        at = band(n * some, some)
        for h in range(rw // DH):
            qh, doh = only_head(qr[at], h), only_head(do[at], h)
            s = mm(keys[...], qh, 1, 1) * SCALE
            w = jnp.exp(s - jnp.max(s, axis=0, keepdims=True))
            p = w * (1.0 / jnp.sum(w, axis=0, keepdims=True))
            dp = mm(values[...], doh, 1, 1)
            ds = (p * (dp - jnp.sum(p * dp, axis=0, keepdims=True))).astype(BF16)
            dk[...] += mm(ds, qh, 1, 0)
            dv[...] += mm(p.astype(BF16), doh, 1, 0)
            got = mm(keys_t[...], ds, 1, 0)
            dq_t[:, at] += jnp.where(head_lanes(got.shape, h, 0), got, 0.0)

    def end():
        x[:, :rw] = (dk[...] * SCALE).astype(BF16)
        x[:, rw:] = dv[...].astype(BF16)

    return [functools.partial(heavy, n) for n in range(half // some)] + [end]


def heavy_back_plain(i):
    half, rw = i["qr"].shape
    split = lambda y: y.reshape(y.shape[0], -1, DH)
    at = lax.axis_index("core") * half
    seed = (i["gate"] * i["gm_r"]).astype(BF16)
    seed = lax.dynamic_slice(seed, (at, 0), (half, seed.shape[1]))
    do = split(mm(seed, i["rmerge"], 1, 1).astype(BF16))
    q, k, v = split(i["qr"]), split(i["kv"][:, :rw]), split(i["kv"][:, rw:])
    p = jax.nn.softmax(jnp.einsum("qhe,khe->hqk", q, k, preferred_element_type=F32) * SCALE, axis=-1)
    dp = jnp.einsum("qhe,khe->hqk", do, v, preferred_element_type=F32)
    ds = (p * (dp - jnp.sum(p * dp, -1, keepdims=True))).astype(BF16)
    dq = jnp.einsum("hqk,khe->qhe", ds, k, preferred_element_type=F32) * SCALE
    dk = jnp.einsum("hqk,qhe->khe", ds, q, preferred_element_type=F32) * SCALE
    dv = jnp.einsum("hqk,qhe->khe", p.astype(BF16), do, preferred_element_type=F32)
    both = jnp.concatenate([dk.reshape(-1, rw), dv.reshape(-1, rw)], 1).astype(BF16)
    both = lax.psum_scatter(both, DP, scatter_dimension=0, tiled=True)
    return jnp.stack([dq.reshape(half, rw).astype(BF16), both[:, :rw], both[:, rw:]], 0)


def back_kernel(nb, nz, pool, inner, *refs):
    names = back_names(inner)
    i = dict(zip(names, refs[: len(names)]))
    out = dict(zip(BACK_OUT, refs[len(names) : len(names) + len(BACK_OUT)]))
    m = pool.bind(refs[len(names) + len(BACK_OUT) :])
    late = Late(BACK_LATE, i, m)
    early = Early(BACK_EARLY, out, m)
    b, z, c = here()
    twin = (b, z, 1 - c)
    bpeers, zpeers = others(b, nb), others(z, nz)
    own, D = i["gm_own"].shape
    rows = own * nb
    cap = i["ids"].shape[0]
    half = cap // 2
    rw = i["rmerge"].shape[0]
    wl = i["q"].shape[1]
    last, first = b == nb - 1, b == 0
    after = (
        jnp.where(last, 0, b + 1), jnp.where(last, lax.rem(z + c, nz), z), jnp.where(last, 1 - c, c),
    )
    before = (
        jnp.where(first, nb - 1, b - 1),
        jnp.where(first, lax.rem(z + nz - 1 + c, nz), z),
        jnp.where(first, 1 - c, c),
    )
    greet([twin, after, before] + [(j, z, c) for j in bpeers] + [(b, j, c) for j in zpeers])
    mine_at, other_at = band(c * half, half), band((1 - c) * half, half)
    sends = []
    layer = Gather(m["layer"], out["lay"], m, "ly")
    shard = ShardSum(i["g_feed"], out["h_feed"], m, "gf")
    chain = BlockSum(nz, i["g_rx"], out["f_rx"], m, "zx")
    chain.start()
    shard.start()

    def go(copy):
        copy.start()
        sends.append(copy)

    gm_half = i["gm_r"][mine_at]
    gate_half = i["gate"][mine_at]
    seed = (gate_half * gm_half).astype(BF16)
    pack_rows(out["g_heavy"], 3 * rw // 2 * (D // 128), lane_blocks(mm(i["ctx_r"][...], seed, 0, 0)))
    trio = m["trio"] if inner else i["trio"]

    def spot(core, j):
        return band((2 * j + core) * half, half)

    def to_twin(j):
        return remote(x.at[spot(1 - c, j)], sib.at[j], m["bs_sib_s"].at[j], m["bs_sib_r"].at[j], twin)

    shard.spread()
    if inner:
        x, sib, came = m["dkv"], m["bs_sib"], m["bs_came"]
        pieces = heavy_back(i, m, seed, x)
        pieces[-1:] = [functools.partial(lambda f: (f(), [go(to_twin(j)) for j in zpeers + [z]]), pieces[-1])]
    else:
        pieces = []
    group_sum_steps(nb, i["ff"], m["ff_sum"], m, pieces, "fs")
    late.need()
    pick_t = hot_rows(i["ids"][...] - b * own, own).T
    scaled = (i["gate"][...] * m["ff_sum"][...].astype(F32)).astype(BF16)
    m["layer"][...] = (i["base"][...] + mm(pick_t, scaled, 1, 0)).astype(BF16)
    shard.relay()
    layer.start()

    low, do_l = m["low"], m["do_l"]
    low[...] = i["gm_own"][...].astype(BF16)
    do_l[...] = mm(low[...], i["lm"][...], 1, 1).astype(BF16)
    for j in zpeers if inner else []:
        to_twin(j).wait_recv()
        sib[j] = (x[spot(c, j)].astype(F32) + sib[j].astype(F32)).astype(BF16)
        go(remote(sib.at[j], came.at[z], m["bs_rs_s"].at[j], m["bs_rs_r"].at[z], (b, j, c)))

    q, k, v = i["q"], i["k"], i["v"]
    lk_t, dkl, dvl, dql = m["lk_t"], m["dkl"], m["dvl"], m["dql"]
    lk_t[...] = k[...].T
    dkl[...] = jnp.zeros_like(dkl)
    dvl[...] = jnp.zeros_like(dvl)
    blocks = own // WIN
    first_key = (2 * z + c) * rows + b * own - WIN
    total = 2 * nz * rows

    def light(n_, carry):
        g, n = n_ // blocks, lax.rem(n_, blocks)
        lanes = band(g * 2 * DH, 2 * DH)
        at = band(n * WIN, WIN)
        near = pl.ds(pl.multiple_of(n * WIN, WIN), 3 * WIN)
        q2, do2, k2, v2, kt2 = q[at, lanes], do_l[at, lanes], k[near, lanes], v[near, lanes], lk_t[lanes, near]
        allowed = near_keys((3 * WIN, WIN), 0, first_key + n * WIN, total)
        got_k = got_v = None
        got_q = []
        for h in range(2):
            qh, doh = only_head(q2, h), only_head(do2, h)
            s = jnp.where(allowed, mm(k2, qh, 1, 1) * SCALE, NEGATIVE)
            w = jnp.exp(s - jnp.max(s, axis=0, keepdims=True))
            p = w * (1.0 / jnp.sum(w, axis=0, keepdims=True))
            dp = mm(v2, doh, 1, 1)
            ds = (p * (dp - jnp.sum(p * dp, axis=0, keepdims=True))).astype(BF16)
            one_k, one_v = mm(ds, qh, 1, 0), mm(p.astype(BF16), doh, 1, 0)
            got_k = one_k if got_k is None else got_k + one_k
            got_v = one_v if got_v is None else got_v + one_v
            got_q.append(mm(kt2, ds, 1, 0))
        dkl[near, lanes] += got_k
        dvl[near, lanes] += got_v
        both = jnp.where(head_lanes((2 * DH, WIN), 0, 0), got_q[0], got_q[1])
        dql[at, lanes] = (both.T * SCALE).astype(BF16)
        return carry

    lax.fori_loop(0, blocks * (wl // (2 * DH)), light, 0)
    layer.relay()
    shard.collect()
    early.put("h_feed")
    rim, came_rim = m["rim"], m["came_rim"]
    for n, start in ((0, WIN + own), (1, 0)):
        rim[n, :, :wl] = (dkl[pl.ds(start, WIN)] * SCALE).astype(BF16)
        rim[n, :, wl:] = dvl[pl.ds(start, WIN)].astype(BF16)
    go(remote(rim.at[0], came_rim.at[0], m["rim_s"].at[0], m["rim_r"].at[0], after))
    go(remote(rim.at[1], came_rim.at[1], m["rim_s"].at[1], m["rim_r"].at[1], before))

    if inner:
        to_twin(z).wait_recv()
        mine = x[spot(c, z)].astype(F32) + sib[z].astype(F32)
        for j in zpeers:
            remote(sib.at[j], came.at[j], m["bs_rs_s"].at[j], m["bs_rs_r"].at[j], (b, j, c)).wait_recv()
            mine = mine + came[j].astype(F32)
        trio[0] = (m["dq_t"][...].T * SCALE).astype(BF16)
        trio[1] = mine[:, :rw].astype(BF16)
        trio[2] = mine[:, rw:].astype(BF16)
    chain.spread()
    rheads = i["rheads"]
    picked = mm(trio[0], rheads[0], 1, 0) + mm(trio[1], rheads[1], 1, 0) + mm(trio[2], rheads[2], 1, 0)

    for n, device in ((0, before), (1, after)):
        remote(rim.at[n], came_rim.at[n], m["rim_s"].at[n], m["rim_r"].at[n], device).wait_recv()
    dkl[pl.ds(WIN, WIN)] += came_rim[0, :, :wl].astype(F32) * (1.0 / SCALE)
    dvl[pl.ds(WIN, WIN)] += came_rim[0, :, wl:].astype(F32)
    dkl[pl.ds(own, WIN)] += came_rim[1, :, :wl].astype(F32) * (1.0 / SCALE)
    dvl[pl.ds(own, WIN)] += came_rim[1, :, wl:].astype(F32)
    dk_own, dv_own = m["dk_own"], m["dv_own"]
    dk_own[...] = (dkl[pl.ds(WIN, own)] * SCALE).astype(BF16)
    dv_own[...] = dvl[pl.ds(WIN, own)].astype(BF16)
    lh = i["lh"]
    gf_l = out["gf_l"]
    gf_l[...] = mm(dql[...], lh[0], 1, 1) + mm(dk_own[...], lh[1], 1, 1) + mm(dv_own[...], lh[2], 1, 1)

    early.put("gf_l")
    gate, first_r = i["gate"], i["first_r"]
    gate_attn = jnp.sum(gm_half * i["attn_r"][...], axis=-1, keepdims=True)
    total_part = m["part"]
    low_gf = gf_l[...].astype(BF16)
    router_sum = None
    for at, extra, more in ((other_at, None, None), (mine_at, gate_attn, picked)):
        g = gate[at]
        d_gate = i["gate_feed"][at] if extra is None else i["gate_feed"][at] + extra
        d_logit = d_gate * g * (1.0 - g)
        one = jnp.sum(d_logit * first_r[at].astype(F32), axis=0, keepdims=True)
        router_sum = one if router_sum is None else router_sum + one
        sum_ = mm(hot_rows(i["ids"][at] - b * own, own), low_gf, 1, 0) + d_logit * i["vecs"][2:3]
        if more is not None:
            sum_ = sum_ + more
        total_part[at] = sum_.astype(BF16)
    out["router"][...] = router_sum

    first_t, g_att = m["first_t"], out["g_att"]
    hl = wl // nb

    def weights_light():
        first_t[...] = i["first_w"][pl.ds(WIN, own)].T

        def one(t, carry):
            lanes = band(t * 2 * hl, 2 * hl)
            for n, x in enumerate((dql, dk_own, dv_own)):
                both = mm(first_t[...], x[:, lanes], 1, 0)
                for k in range(2):
                    pack_rows(g_att.at[2 * t + k], n * D // 2, [both[:, k * hl : (k + 1) * hl]])
            return carry

        lax.fori_loop(0, nb // 2, one, 0)

    def weights_rest():
        def one(t, carry):
            both = mm(i["ctx_l"][:, band(t * 2 * hl, 2 * hl)], low[...], 0, 0)
            for k in range(2):
                pack_rows(g_att.at[2 * t + k], 3 * D // 2, lane_blocks(both[k * hl : (k + 1) * hl]))
            return carry

        lax.fori_loop(0, nb // 2, one, 0)
        first_half = first_r[mine_at]
        for n in range(3):
            pack_rows(out["g_heavy"], n * rw // 2 * (D // 128), lane_blocks(mm(trio[n], first_half, 0, 0)))
        early.put("g_att", "g_heavy")

    group_sum_steps(nb, total_part, out["gf_r"], m, [weights_light, weights_rest])
    chain.forward()
    chain.end()
    shard.end()
    layer.wait()
    early.end()
    finish(sends)


def back(nb, nz, given):
    own, D = given["gm_own"].shape
    cap = given["ids"].shape[0]
    half = cap // 2
    rw = given["rmerge"].shape[0]
    wl = given["q"].shape[1]
    deep = 2 * nz * half
    feed_rows, rx_rows = given["g_feed"].shape[2], given["g_rx"].shape[0]
    shape = lambda *dims: jax.ShapeDtypeStruct(dims, BF16)
    outs = dict(
        gf_r=shape(cap, D), gf_l=jax.ShapeDtypeStruct((own, D), F32),
        g_att=shape(nb, 2, 2 * D * wl // nb // 128, 128), g_heavy=shape(2, 2 * D * rw // 128, 128),
        router=jax.ShapeDtypeStruct((1, D), F32),
        lay=shape(nb, own, D), h_feed=shape(feed_rows, 128), f_rx=shape(2, rx_rows, 128),
    )
    pool = Pool()
    inner = deep <= 4096
    if inner:
        pool.vmem("keys", (deep, rw))
        pool.vmem("values", (deep, rw))
        pool.vmem("keys_t", (rw, deep))
        pool.vmem("dk", (deep, rw), F32)
        pool.vmem("dv", (deep, rw), F32)
        pool.vmem("dq_t", (rw, half), F32)
        pool.vmem("do", (half, rw))
        pool.vmem("trio", (3, half, rw))
        pool.vmem("dkv", (deep, 2 * rw))
        for name in ("bs_sib", "bs_came"):
            pool.vmem(name, (nz, half, 2 * rw))
    pool.vmem("low", (own, D))
    pool.vmem("do_l", (own, wl))
    pool.vmem("lk_t", (wl, own + 2 * WIN))
    pool.vmem("dkl", (own + 2 * WIN, wl), F32)
    pool.vmem("dvl", (own + 2 * WIN, wl), F32)
    pool.vmem("dql", (own, wl))
    pool.vmem("dk_own", (own, wl))
    pool.vmem("dv_own", (own, wl))
    pool.vmem("rim", (2, WIN, 2 * wl))
    pool.vmem("came_rim", (2, WIN, 2 * wl))
    pool.vmem("first_t", (D, own))
    pool.vmem("part", (cap, D))
    group_sum_scratch(pool, nb, cap, D)
    for name in ("bs_sib", "bs_rs") if inner else ():
        pool.dma(f"{name}_s", nz)
        pool.dma(f"{name}_r", nz)
    if not inner:
        given = dict(given, trio=heavy_back_plain(given))
    Late.scratch(pool, BACK_LATE, given)
    Early.scratch(pool, BACK_EARLY, outs)
    pool.vmem("layer", (own, D))
    pool.vmem("ff_sum", (cap, D))
    group_sum_scratch(pool, nb, cap, D, "fs")
    ShardSum.scratch(pool, feed_rows, "gf")
    BlockSum.scratch(pool, nz, rx_rows, "zx")
    Gather.scratch(pool, "ly")
    pool.dma("rim_s", 2)
    pool.dma("rim_r", 2)
    got = pl.pallas_call(
        functools.partial(back_kernel, nb, nz, pool, inner),
        out_shape=tuple(outs[name] for name in BACK_OUT),
        in_specs=[HB if name in ("g_feed",) + BACK_LATE else VM for name in back_names(inner)],
        out_specs=tuple(HB if name in ("lay", "f_rx") + BACK_EARLY else VM for name in BACK_OUT),
        scratch_shapes=pool.shapes,
        compiler_params=pltpu.CompilerParams(
            collective_id=3, has_side_effects=True, vmem_limit_bytes=62 << 20
        ),
    )(*(given[name] for name in back_names(inner)))
    return dict(zip(BACK_OUT, got))


FIN_OUT = ("layer", "delta", "re", "rr", "lh", "lm", "rh", "rm", "le", "lr")


def finish_kernel(lay, dlt, gate, rx, att, both, *outs):
    o = dict(zip(FIN_OUT, outs))
    o["layer"][...] = lay[...].astype(F32)
    o["delta"][...] = dlt[...].astype(F32)
    size = rx.shape[2]
    blocks = gate.shape[1]
    for core in range(2):
        for part in range(2):
            for k in range(blocks):
                at = 2 * (core * blocks + k) + part
                o["re"][pl.ds(at, size, 4 * blocks), :] = (rx if part else gate)[core, k].astype(F32)
        for block, at, row, k in down_pieces(blocks * 128, size * 8):
            if row < blocks * 16:
                o["rr"][core, pl.ds(row, 32), k * 128 : (k + 1) * 128] = rx[core, blocks + block, pl.ds(at, 32)].astype(F32)

    @pl.when(pl.program_id(0) == 0)
    def _():
        for core in range(2):
            D, hl = o["lh"].shape[1:]
            start = 0
            for n in range(3):
                size = D // 2
                o["lh"][n, pl.ds(core * size, size)] = att[core, pl.ds(start, size)].astype(F32)
                start += size
            for k in range(D // 128):
                size = hl // 2
                o["lm"][pl.ds(core * size, size), k * 128 : (k + 1) * 128] = att[core, pl.ds(start, size)].astype(F32)
                start += size
            start = D * 3 * o["lr"].shape[0] // 256
            size = o["rm"].shape[0] // 2
            for n in range(4):
                dst = o["rm"] if n == 3 else o["rh"].at[n]
                for k in range(D // 128):
                    dst[pl.ds(core * size, size), k * 128 : (k + 1) * 128] = both[core, pl.ds(start, size)].astype(F32)
                    start += size
            start = 0
            fl = o["lr"].shape[0]
            lanes = fl // 128
            size = D // 2
            for part in range(2):
                for k in range(lanes):
                    o["le"][pl.ds(core * size * 2 * lanes + 2 * k + part, size, 2 * lanes), :] = both[
                        core, pl.ds(start, size)
                    ].astype(F32)
                    start += size
            size = fl // 2
            for k in range(D // 128):
                o["lr"][pl.ds(core * size, size), k * 128 : (k + 1) * 128] = both[core, pl.ds(start, size)].astype(F32)
                start += size


def finish_all(lay, dlt, gate, rx, att, both, hl, fl, rw):
    steps = 8
    rows, D = lay.shape
    fh = gate.shape[1] * 128
    shape = lambda *dims: jax.ShapeDtypeStruct(dims, F32)
    whole = lambda *dims: pl.BlockSpec(dims, lambda n: (0,) * len(dims))
    tall = lambda count, width: pl.BlockSpec((count // steps, width), lambda n: (n, 0))
    return dict(
        zip(
            FIN_OUT,
            pl.pallas_call(
                finish_kernel,
                grid=(steps,),
                out_shape=(
                    shape(rows, D), shape(rows, D), shape(D * 4 * fh // 128, 128), shape(2, fh, D),
                    shape(3, D, hl), shape(hl, D), shape(3, rw, D), shape(rw, D),
                    shape(D * 2 * fl // 128, 128), shape(fl, D),
                ),
                in_specs=[
                    tall(rows, D), tall(rows, D),
                    pl.BlockSpec((2, fh // 128, D // steps, 128), lambda n: (0, 0, n, 0)),
                    pl.BlockSpec((2, 2 * fh // 128, D // steps, 128), lambda n: (0, 0, n, 0)),
                    whole(*att.shape), whole(*both.shape),
                ],
                out_specs=(
                    tall(rows, D), tall(rows, D), tall(D * 4 * fh // 128, 128),
                    pl.BlockSpec((2, fh // steps, D), lambda n: (0, n, 0)),
                    whole(3, D, hl), whole(hl, D), whole(3, rw, D), whole(rw, D),
                    whole(D * 2 * fl // 128, 128), whole(fl, D),
                ),
                compiler_params=pltpu.CompilerParams(vmem_limit_bytes=50 << 20),
            )(lay, dlt, gate, rx, att, both),
        )
    )


def woven(x, width):
    blocks = width // 128
    return x.reshape(-1, blocks, 2, 128).transpose(0, 2, 1, 3).reshape(-1, 2, width)


def per_device(
    tokens,
    cotangent,
    gain_before,
    gain_middle,
    router_vector,
    local_heads,
    local_merge,
    routed_heads,
    routed_merge,
    local_expand,
    local_reduce,
    routed_expand,
    routed_reduce,
    routed_slots,
    routed_counts,
):
    nb = lax.axis_size("branch")
    nz = lax.axis_size("zz")
    core = lax.axis_index("core")
    rows, D = tokens.shape
    fh = routed_expand.shape[2] // 2
    vecs = jnp.stack([gain_before, gain_middle, router_vector])
    rheads = routed_heads.transpose(1, 2, 0)
    f = front(
        nb, nz, tokens, cotangent, routed_slots[None], routed_counts, vecs, rheads, routed_merge,
        local_heads.transpose(1, 0, 2), local_merge, local_expand.transpose(1, 0, 2), local_reduce,
    )
    re_half = lax.dynamic_slice(routed_expand, (0, 0, core * fh), (D, 2, fh)).transpose(1, 0, 2)
    f = dict(f, vecs=vecs, re=re_half, rr=routed_reduce, rmerge=routed_merge, rheads=rheads)
    f = dict(f, **middle(nb, nz, f))
    f["g_rx"] = f["g_rx"].reshape(-1, 128)
    f = dict(f, **back(nb, nz, f))
    f = dict(f, **tail(nb, nz, f))
    g = finish_all(
        f["lay"].reshape(rows, D), f["delta"].reshape(rows, D), f["f_gate"].reshape(2, -1, D, 128),
        f["f_rx"].reshape(2, -1, D, 128), f["f_att"], f["f_both"], hl=local_merge.shape[0], fl=local_reduce.shape[0],
        rw=routed_merge.shape[0],
    )
    return (
        g["layer"],
        g["delta"],
        f["vectors"][0],
        f["vectors"][1],
        f["vectors"][2],
        g["lh"].transpose(1, 0, 2),
        g["lm"],
        g["rh"].transpose(2, 0, 1),
        g["rm"],
        woven(g["le"], local_reduce.shape[0]),
        g["lr"],
        woven(g["re"], 2 * fh),
        g["rr"].reshape(2 * fh, D),
    )


def solution(mesh):
    nb = mesh.shape["branch"]
    fine = Mesh(mesh.devices.reshape(nb, -1, 2), ("branch", "zz", "core"))
    rows = P(DP, None)
    cols = P(None, None, "branch")
    deep = P("branch", None)
    return jax.shard_map(
        per_device,
        mesh=fine,
        in_specs=(
            rows, rows, P(), P(), P(), cols, deep, cols, deep, cols, deep, cols, deep, P(DP), P(),
        ),
        out_specs=(
            rows, rows, P(), P(), P(), cols, deep, cols, deep, cols, deep, cols, deep,
        ),
        check_vma=False,
    )
```

```python
import functools

import jax
import jax.numpy as jnp
from jax import lax
from jax.experimental import pallas as pl
from jax.experimental.pallas import tpu as pltpu
from jax.sharding import Mesh
from jax.sharding import PartitionSpec as P

DH = 64
WIN = 128
EPSILON = 1e-06
NEGATIVE = -1e30
HIGHEST = lax.Precision.HIGHEST
F32 = jnp.float32
BF16 = jnp.bfloat16
SCALE = DH ** (-0.5)
DP = ("zz", "core")


def mm(a, b, ca, cb):
    return lax.dot_general(a, b, (((ca,), (cb,)), ((), ())), preferred_element_type=F32)


def norm_parts(values):
    r = lax.rsqrt(jnp.mean(values * values, axis=-1, keepdims=True) + EPSILON)
    return r, values * r


def norm_back(dn, xh, r, gain):
    g = dn * gain
    return r * (g - xh * jnp.mean(g * xh, axis=-1, keepdims=True))


def gelu_parts(u):
    c = 0.7978845608028654
    t = jnp.tanh(c * (u + 0.044715 * u * u * u))
    g = 0.5 * u * (1.0 + t)
    dg = 0.5 * (1.0 + t) + 0.5 * u * (1.0 - t * t) * c * (1.0 + 3 * 0.044715 * u * u)
    return g, dg


def feed(n, seed, w_gate, w_up, w_down):
    u = mm(n, w_gate, 1, 0)
    v = mm(n, w_up, 1, 0)
    g, dg = gelu_parts(u)
    hidden = (g * v).astype(BF16)
    out = mm(hidden, w_down, 1, 0)
    dh = mm(seed, w_down, 1, 1)
    du = (dh * v * dg).astype(BF16)
    dv = (dh * g).astype(BF16)
    dn = mm(du, w_gate, 1, 1) + mm(dv, w_up, 1, 1)
    dwg = mm(n, du, 0, 0)
    dwu = mm(n, dv, 0, 0)
    dwd = mm(hidden, seed, 0, 0)
    return out, dn, dwg, dwu, dwd


MESH = pl.DeviceIdType.MESH


def remote(src, dst, send, recv, device):
    return pltpu.make_async_remote_copy(
        src_ref=src, dst_ref=dst, send_sem=send, recv_sem=recv, device_id=device, device_id_type=MESH
    )


def greet(devices):
    barrier = pltpu.get_barrier_semaphore()
    for device in devices:
        pl.semaphore_signal(barrier, inc=1, device_id=device, device_id_type=MESH)
    pl.semaphore_wait(barrier, len(devices))


def here():
    return lax.axis_index("branch"), lax.axis_index("zz"), lax.axis_index("core")


def others(me, count):
    return [lax.rem(me + k, count) for k in range(1, count)]


def band(start, size):
    return pl.ds(pl.multiple_of(start, size), size)


def finish(copies):
    for copy in copies:
        if copy.is_remote:
            copy.wait_send()
        else:
            copy.wait()


class Pool:
    def __init__(self):
        self.names = []
        self.shapes = []

    def add(self, name, shape):
        self.names.append(name)
        self.shapes.append(shape)

    def vmem(self, name, shape, dtype=BF16):
        self.add(name, pltpu.VMEM(shape, dtype))

    def dma(self, name, *shape):
        self.add(name, pltpu.SemaphoreType.DMA(shape))

    def bind(self, refs):
        return dict(zip(self.names, refs, strict=True))


class Early:
    def __init__(self, names, out, m):
        self.names, self.out, self.m = names, dict(out), m
        self.copies = []
        for name in names:
            out[name] = m[f"out_{name}"]

    def put(self, *names):
        for name in names:
            sem = self.m["out_s"].at[self.names.index(name)]
            copy = pltpu.make_async_copy(self.m[f"out_{name}"], self.out[name], sem)
            copy.start()
            self.copies.append(copy)

    def end(self):
        assert len(self.copies) == len(self.names)
        finish(self.copies)

    @staticmethod
    def scratch(pool, names, shapes):
        for name in names:
            pool.vmem(f"out_{name}", shapes[name].shape, shapes[name].dtype)
        pool.dma("out_s", len(names))


class Late:
    def __init__(self, names, given, m):
        self.copies = {}
        for k, name in enumerate(names):
            copy = pltpu.make_async_copy(given[name], m[f"in_{name}"], m["in_s"].at[k])
            copy.start()
            self.copies[name] = copy
            given[name] = m[f"in_{name}"]

    def need(self, *names):
        for name in names or tuple(self.copies):
            self.copies.pop(name).wait()

    @staticmethod
    def scratch(pool, names, given):
        for name in names:
            pool.vmem(f"in_{name}", given[name].shape, given[name].dtype)
        pool.dma("in_s", len(names))


def group_sum_scratch(pool, nb, rows, width, tag="gs"):
    for name in ("sib", "part", "came"):
        pool.vmem(f"{tag}_{name}", (nb, rows // 2 // nb, width))
    for name in ("sib", "rs", "ag", "fw"):
        pool.dma(f"{tag}_{name}_s", nb)
        pool.dma(f"{tag}_{name}_r", nb)


def group_sum_steps(nb, x, o, m, meanwhile=(), tag="gs"):
    m = {name[len(tag) + 1 :]: ref for name, ref in m.items() if name.startswith(tag + "_")}
    b, z, c = here()
    half = x.shape[0] // 2
    ch = half // nb
    twin = (b, z, 1 - c)
    peers = others(b, nb)
    sib, part, came = m["sib"], m["part"], m["came"]
    work = list(meanwhile)

    def aside():
        if work:
            work.pop(0)()

    def rows(core, j):
        return band(core * half + j * ch, ch)

    order = peers + [b]
    to_twin = [
        remote(x.at[rows(1 - c, j)], sib.at[j], m["sib_s"].at[j], m["sib_r"].at[j], twin)
        for j in order
    ]
    for copy in to_twin:
        copy.start()
    sends = []
    for j, copy in zip(peers, to_twin):
        copy.wait_recv()
        part[j] = (x[rows(c, j)].astype(F32) + sib[j].astype(F32)).astype(BF16)
        send = remote(part.at[j], came.at[b], m["rs_s"].at[j], m["rs_r"].at[b], (j, z, c))
        send.start()
        sends.append(send)
    aside()
    to_twin[-1].wait_recv()
    total = x[rows(c, b)].astype(F32) + sib[b].astype(F32)
    for j in peers:
        remote(part.at[j], came.at[j], m["rs_s"].at[j], m["rs_r"].at[j], (j, z, c)).wait_recv()
        total = total + came[j].astype(F32)
    mine = o.at[rows(c, b)]
    mine[...] = total.astype(BF16)
    for j in peers:
        send = remote(mine, mine, m["ag_s"].at[j], m["ag_r"].at[b], (j, z, c))
        send.start()
        sends.append(send)
    send = remote(mine, mine, m["fw_s"].at[b], m["fw_r"].at[b], twin)
    send.start()
    sends.append(send)
    aside()
    for j in peers:
        piece = o.at[rows(c, j)]
        remote(piece, piece, m["ag_s"].at[j], m["ag_r"].at[j], (j, z, c)).wait_recv()
        send = remote(piece, piece, m["fw_s"].at[j], m["fw_r"].at[j], twin)
        send.start()
        sends.append(send)
    while work:
        aside()
    for j in order:
        piece = o.at[rows(1 - c, j)]
        remote(piece, piece, m["fw_s"].at[j], m["fw_r"].at[j], twin).wait_recv()
    finish(to_twin + sends)


VM = pl.BlockSpec(memory_space=pltpu.VMEM)
HB = pl.BlockSpec(memory_space=pl.ANY)


def normed(x, gain):
    x = x.astype(F32)
    r = lax.rsqrt(jnp.mean(x * x, axis=-1, keepdims=True) + EPSILON)
    return (x * r * gain).astype(BF16)


def head_lanes(shape, h, dim):
    place = lax.broadcasted_iota(jnp.int32, shape, dim)
    return (place >= h * DH) & (place < (h + 1) * DH)


def only_head(x, h):
    return jnp.where(head_lanes(x.shape, h, 1), x, jnp.zeros_like(x))


def near_keys(shape, key_dim, first, total):
    key = lax.broadcasted_iota(jnp.int32, shape, key_dim)
    query = lax.broadcasted_iota(jnp.int32, shape, 1 - key_dim)
    gap = key - query
    return (gap >= 0) & (gap <= 2 * WIN) & (key + first >= 0) & (key + first < total)


def hot_rows(ids, count):
    spot = lax.broadcasted_iota(jnp.int32, (ids.shape[0], count), 1)
    return jnp.where(ids == spot, 1.0, 0.0).astype(BF16)


FRONT_OUT = (
    "tok_r", "cot_r", "first_r", "gate", "qr", "kv", "lh", "lm", "le", "lr", "first_w",
    "q", "k", "v", "ctx_l", "attn_l", "ctx_r", "attn_r", "mixed", "ids", "tok_own", "cot_own",
)


FRONT_EARLY = (
    "kv", "lh", "lm", "q", "k", "v", "first_w", "tok_r", "cot_r", "first_r", "ctx_l", "attn_l",
)


def front_kernel(nb, nz, pool, *refs):
    tokens, cotangent, slots, counts, vecs, rheads, rmerge, s_lh, s_lm, s_le, s_lr = refs[:11]
    out = dict(zip(FRONT_OUT, refs[11 : 11 + len(FRONT_OUT)]))
    m = pool.bind(refs[11 + len(FRONT_OUT) :])
    early = Early(FRONT_EARLY, out, m)
    ids = out["ids"]
    gain, router = vecs[0:1], vecs[2:3]
    b, z, c = here()
    twin = (b, z, 1 - c)
    bpeers, zpeers = others(b, nb), others(z, nz)
    rows, D = tokens.shape
    own = rows // nb
    cap = slots.shape[1]
    half = cap // 2
    rw = rmerge.shape[0]
    after = (b, lax.rem(z + c, nz), 1 - c)
    before = (b, lax.rem(z + nz - 1 + c, nz), 1 - c)
    far = (b, lax.rem(z + nz - 1 + 2 * c, nz), 1 - c)
    greet([twin, far] + [(j, z, c) for j in bpeers] + [(b, j, c) for j in zpeers])
    sends = []

    def go(copy):
        copy.start()
        sends.append(copy)

    pairs = [(s_lh, out["lh"]), (s_lm, out["lm"]), (s_le, out["le"]), (s_lr, out["lr"])]

    def place(i, j):
        src, dst = pairs[i]
        if i in (0, 2):
            return dst.at[:, :, band(j * src.shape[2], src.shape[2])]
        return dst.at[band(j * src.shape[0], src.shape[0])]

    def cut(i, ref, core):
        if i in (0, 2):
            size = ref.shape[1] // 2
            return ref.at[:, band(core * size, size)]
        size = ref.shape[0] // 2
        return ref.at[band(core * size, size)]

    def send_weights(i):
        for j in bpeers:
            go(remote(cut(i, pairs[i][0], c), cut(i, place(i, b), c), m["w_s"].at[i, j], m["w_r"].at[i, b], (j, z, c)))

    send_weights(0)
    send_weights(1)
    for i in range(4):
        pltpu.make_async_copy(pairs[i][0], place(i, b), m["own_s"].at[i]).start()
    halo = m["halo"]
    go(remote(tokens.at[pl.ds(rows - WIN, WIN)], halo.at[0], m["halo_s"].at[0], m["halo_r"].at[0], after))
    go(remote(tokens.at[pl.ds(0, WIN)], halo.at[1], m["halo_s"].at[1], m["halo_r"].at[1], before))

    n_own = counts[2 * z + c]
    offset = jnp.where(c == 0, 0, cap - n_own)
    rank = lax.broadcasted_iota(jnp.int32, (cap, cap), 0)
    slot = lax.broadcasted_iota(jnp.int32, (cap, cap), 1)
    shift = jnp.where((rank == slot + offset) & (slot < n_own), 1.0, 0.0).astype(BF16)
    line = lax.broadcasted_iota(jnp.int32, (16, cap), 0)
    high, rest = slots[...] // 64, slots[...] % 64
    digits = jnp.where(line == 0, high, jnp.where(line == 1, rest, jnp.where(line == 2, 1, 0)))
    found = mm(shift, digits.astype(F32).astype(BF16), 1, 1)
    ids[...] = jnp.where(found[:, 2:3] > 0.5, found[:, 0:1] * 64.0 + found[:, 1:2], -1.0).astype(jnp.int32)
    for n, (name, source) in enumerate((("tok_own", tokens), ("cot_own", cotangent))):
        go(pltpu.make_async_copy(source.at[band(b * own, own)], out[name], m["rows_s"].at[n]))
    picks, sib = m["picks"], m["sib"]
    step = cap // 4
    for k in range(4):
        at = pl.ds(k * step, step)
        hot = hot_rows(ids[at], rows)
        picks[at, :D] = mm(hot, tokens[...], 1, 0).astype(BF16)
        picks[at, D:] = mm(hot, cotangent[...], 1, 0).astype(BF16)
        go(remote(picks.at[at], sib.at[at], m["pick_s"].at[k], m["pick_r"].at[k], twin))
    for k in range(4):
        at = pl.ds(k * step, step)
        remote(picks.at[at], sib.at[at], m["pick_s"].at[k], m["pick_r"].at[k], twin).wait_recv()
        tok = picks[at, :D].astype(F32) + sib[at, :D].astype(F32)
        out["tok_r"][at] = tok.astype(BF16)
        out["cot_r"][at] = (picks[at, D:].astype(F32) + sib[at, D:].astype(F32)).astype(BF16)
        first = normed(tok, gain)
        out["first_r"][at] = first
        logit = jnp.sum(first.astype(F32) * router, axis=-1, keepdims=True)
        out["gate"][at] = 1.0 / (1.0 + jnp.exp(-logit))

    early.put("tok_r", "cot_r", "first_r")
    own_rows = out["first_r"][band(c * half, half)]
    out["qr"][...] = mm(own_rows, rheads[0], 1, 1).astype(BF16)
    kv = out["kv"]
    mine = kv.at[band((2 * z + c) * half, half)]
    mine[:, :rw] = mm(own_rows, rheads[1], 1, 1).astype(BF16)
    mine[:, rw:] = mm(own_rows, rheads[2], 1, 1).astype(BF16)
    for j in zpeers:
        go(remote(mine, mine, m["kv_s"].at[j], m["kv_r"].at[z], (b, j, c)))
    go(remote(mine, mine, m["kf_s"].at[z], m["kf_r"].at[z], twin))

    first_w = out["first_w"]
    first_w[pl.ds(WIN, own)] = normed(tokens[band(b * own, own)], gain)
    for i in range(2):
        remote(halo.at[i], halo.at[i], m["halo_s"].at[i], m["halo_r"].at[i], twin).wait_recv()
    lead = tokens[band(jnp.maximum(b * own - WIN, 0), WIN)]
    trail = tokens[band(jnp.minimum((b + 1) * own, rows - WIN), WIN)]
    first_w[pl.ds(0, WIN)] = normed(jnp.where(b > 0, lead, halo[0]), gain)
    first_w[pl.ds(WIN + own, WIN)] = normed(jnp.where(b < nb - 1, trail, halo[1]), gain)

    def pass_weights(i):
        for j in bpeers:
            dst = cut(i, place(i, j), c)
            remote(dst, dst, m["w_s"].at[i, j], m["w_r"].at[i, j], (j, z, c)).wait_recv()
            go(remote(dst, dst, m["wf_s"].at[i, j], m["wf_r"].at[i, j], twin))

    def take_weights(i):
        for j in bpeers:
            dst = cut(i, place(i, j), 1 - c)
            remote(dst, dst, m["wf_s"].at[i, j], m["wf_r"].at[i, j], twin).wait_recv()

    pass_weights(0)
    for j in zpeers:
        piece = kv.at[band((2 * j + c) * half, half)]
        remote(piece, piece, m["kv_s"].at[j], m["kv_r"].at[j], (b, j, c)).wait_recv()
        go(remote(piece, piece, m["kf_s"].at[j], m["kf_r"].at[j], twin))
    take_weights(0)
    send_weights(2)
    send_weights(3)
    pltpu.make_async_copy(pairs[0][0], place(0, b), m["own_s"].at[0]).wait()
    lh, q, k, v = out["lh"], out["q"], out["k"], out["v"]
    q[...] = mm(first_w[pl.ds(WIN, own)], lh[0], 1, 0).astype(BF16)
    k[...] = mm(first_w[...], lh[1], 1, 0).astype(BF16)
    v[...] = mm(first_w[...], lh[2], 1, 0).astype(BF16)
    early.put("lh", "q", "k", "v", "first_w")
    pass_weights(1)

    blocks = own // WIN
    ctx = out["ctx_l"]
    first_key = (2 * z + c) * rows + b * own - WIN
    total = 2 * nz * rows

    def light(i, carry):
        g, n = i // blocks, lax.rem(i, blocks)
        lanes = band(g * 2 * DH, 2 * DH)
        at = band(n * WIN, WIN)
        keys = pl.ds(pl.multiple_of(n * WIN, WIN), 3 * WIN)
        q2, k2, v2 = q[at, lanes], k[keys, lanes], v[keys, lanes]
        allowed = near_keys((WIN, 3 * WIN), 1, first_key + n * WIN, total)
        parts = []
        for h in range(2):
            s = jnp.where(allowed, mm(only_head(q2, h), k2, 1, 1) * SCALE, NEGATIVE)
            w = jnp.exp(s - jnp.max(s, axis=-1, keepdims=True))
            p = (w / jnp.sum(w, axis=-1, keepdims=True)).astype(BF16)
            parts.append(mm(p, v2, 1, 0))
        ctx[at, lanes] = jnp.where(head_lanes((WIN, 2 * DH), 0, 1), parts[0], parts[1]).astype(BF16)
        return carry

    lax.fori_loop(0, blocks * (q.shape[1] // (2 * DH)), light, 0, unroll=2)
    take_weights(1)
    pltpu.make_async_copy(pairs[1][0], place(1, b), m["own_s"].at[1]).wait()
    attn_l = out["attn_l"]
    attn_l[...] = mm(ctx[...], out["lm"][...], 1, 0)
    early.put("lm", "ctx_l", "attn_l")

    for j in zpeers + [z]:
        piece = kv.at[band((2 * j + 1 - c) * half, half)]
        remote(piece, piece, m["kf_s"].at[j], m["kf_r"].at[j], twin).wait_recv()
    keys, values, qr, ctx_r = m["keys"], m["values"], out["qr"], out["ctx_r"]
    early.put("kv")
    keys[...] = kv[:, :rw]
    values[...] = kv[:, rw:]
    some = 128

    def heavy(i, carry):
        at = band(i * some, some)
        got = jnp.zeros((some, rw), F32)
        for h in range(rw // DH):
            s = mm(only_head(qr[at], h), keys[...], 1, 1) * SCALE
            w = jnp.exp(s - jnp.max(s, axis=-1, keepdims=True))
            p = (w / jnp.sum(w, axis=-1, keepdims=True)).astype(BF16)
            got = jnp.where(head_lanes((some, rw), h, 1), mm(p, values[...], 1, 0), got)
        ctx_r[at] = got.astype(BF16)
        return carry

    lax.fori_loop(0, half // some, heavy, 0)
    pass_weights(2)
    attn_r = out["attn_r"]
    attn_r[...] = mm(ctx_r[...], rmerge[...], 1, 0)

    part = m["part"]
    mine_at, other_at = band(c * half, half), band((1 - c) * half, half)
    low = attn_l[...].astype(BF16)
    part[other_at] = mm(hot_rows(ids[other_at] - b * own, own), low, 1, 0).astype(BF16)
    part[mine_at] = (
        mm(hot_rows(ids[mine_at] - b * own, own), low, 1, 0) + out["gate"][mine_at] * attn_r[...]
    ).astype(BF16)
    group_sum_steps(nb, part, out["mixed"], m, [lambda: pass_weights(3)])
    take_weights(2)
    take_weights(3)
    early.end()
    finish(sends)
    for i in (2, 3):
        pltpu.make_async_copy(pairs[i][0], place(i, b), m["own_s"].at[i]).wait()


def front(nb, nz, tokens, cotangent, slots, counts, vecs, rheads, rmerge, s_lh, s_lm, s_le, s_lr):
    rows, D = tokens.shape
    own = rows // nb
    cap = slots.shape[1]
    half = cap // 2
    rw = rmerge.shape[0]
    wl = nb * s_lm.shape[0]
    shape = lambda *dims: jax.ShapeDtypeStruct(dims, BF16)
    shape32 = lambda *dims: jax.ShapeDtypeStruct(dims, F32)
    outs = dict(
        tok_r=shape(cap, D), cot_r=shape(cap, D), first_r=shape(cap, D), gate=shape32(cap, 1),
        qr=shape(half, rw), kv=shape(2 * nz * half, 2 * rw),
        lh=shape(3, D, wl), lm=shape(wl, D),
        le=shape(2, D, nb * s_le.shape[2]), lr=shape(nb * s_lr.shape[0], D),
        first_w=shape(own + 2 * WIN, D), q=shape(own, wl), k=shape(own + 2 * WIN, wl),
        v=shape(own + 2 * WIN, wl), ctx_l=shape(own, wl), attn_l=shape32(own, D),
        ctx_r=shape(half, rw), attn_r=shape32(half, D), mixed=shape(cap, D),
        ids=jax.ShapeDtypeStruct((cap, 1), jnp.int32), tok_own=shape(own, D), cot_own=shape(own, D),
    )
    pool = Pool()
    pool.vmem("picks", (cap, 2 * D))
    pool.vmem("sib", (cap, 2 * D))
    pool.vmem("halo", (2, WIN, D))
    pool.vmem("keys", (2 * nz * half, rw))
    pool.vmem("values", (2 * nz * half, rw))
    pool.vmem("part", (cap, D))
    group_sum_scratch(pool, nb, cap, D)
    pool.dma("own_s", 4)
    pool.dma("rows_s", 2)
    Early.scratch(pool, FRONT_EARLY, outs)
    pool.dma("halo_s", 2)
    pool.dma("halo_r", 2)
    pool.dma("pick_s", 4)
    pool.dma("pick_r", 4)
    for name in ("w", "wf"):
        pool.dma(f"{name}_s", 4, nb)
        pool.dma(f"{name}_r", 4, nb)
    for name in ("kv", "kf"):
        pool.dma(f"{name}_s", nz)
        pool.dma(f"{name}_r", nz)
    got = pl.pallas_call(
        functools.partial(front_kernel, nb, nz, pool),
        out_shape=tuple(outs[name] for name in FRONT_OUT),
        in_specs=[VM] * 3 + [pl.BlockSpec(memory_space=pltpu.SMEM)] + [VM] * 3 + [HB] * 4,
        out_specs=tuple(
            HB if name in ("le", "lr", "tok_own", "cot_own") + FRONT_EARLY else VM for name in FRONT_OUT
        ),
        scratch_shapes=pool.shapes,
        compiler_params=pltpu.CompilerParams(
            collective_id=0, has_side_effects=True, vmem_limit_bytes=56 << 20
        ),
    )(tokens, cotangent, slots, counts, vecs, rheads, rmerge, s_lh, s_lm, s_le, s_lr)
    return dict(zip(FRONT_OUT, got))


def neighbours(b):
    return b + 1 - 2 * lax.rem(b, 2), lax.rem(b + 2, 4), 3 - b


class Gather:
    def __init__(self, src, dst, m, name):
        b, z, c = here()
        self.src, self.dst, self.m, self.name, self.b = src, dst, m, name, b
        self.bx, self.by, self.bd = neighbours(b)
        self.dx, self.dy = (self.bx, z, c), (self.by, z, c)
        self.sends = []

    def half(self, ref, k):
        size = self.src.shape[0] // 2
        return ref.at[pl.ds(k * size, size)]

    def go(self, copy):
        copy.start()
        self.sends.append(copy)

    def copy(self, way, k, src, slot, device):
        m, n = self.m, self.name
        return remote(
            self.half(src, k), self.half(self.dst.at[slot], k), m[f"{n}_{way}_s"].at[k], m[f"{n}_{way}_r"].at[k], device
        )

    def start(self):
        own = pltpu.make_async_copy(self.src, self.dst.at[self.b], self.m[f"{self.name}_own"].at[0])
        self.go(own)
        for first, second in ((0, 1), (1, 0)):
            self.go(self.copy("x", second, self.src, self.b, self.dx))
            self.go(self.copy("y", first, self.src, self.b, self.dy))

    def relay(self):
        came = self.dst.at[self.bx]
        self.copy("x", 1, came, self.bx, self.dx).wait_recv()
        self.go(self.copy("f", 1, came, self.bx, self.dy))
        came = self.dst.at[self.by]
        self.copy("y", 0, came, self.by, self.dy).wait_recv()
        self.go(self.copy("f", 0, came, self.by, self.dx))

    def wait(self):
        self.copy("x", 0, self.dst.at[self.bx], self.bx, self.dx).wait_recv()
        self.copy("y", 1, self.dst.at[self.by], self.by, self.dy).wait_recv()
        far = self.dst.at[self.bd]
        self.copy("f", 0, far, self.bd, self.dx).wait_recv()
        self.copy("f", 1, far, self.bd, self.dy).wait_recv()
        finish(self.sends)

    @staticmethod
    def scratch(pool, name):
        pool.dma(f"{name}_own", 1)
        for way in ("x", "y", "f"):
            pool.dma(f"{name}_{way}_s", 2)
            pool.dma(f"{name}_{way}_r", 2)


class ShardSum:
    def __init__(self, g, h, m, name):
        self.b, self.z, self.c = here()
        self.bx, self.by, self.bd = neighbours(self.b)
        self.g, self.h, self.m, self.name = g, h, m, name
        self.sib = m[f"{name}_sib"]
        size = g.shape[2] // 2
        self.parts = (pl.ds(0, size), pl.ds(size, size))
        self.sends = []

    def go(self, copy):
        copy.start()
        self.sends.append(copy)

    def pair(self, j):
        m, n = self.m, self.name
        return remote(
            self.g.at[j, 1 - self.c], self.sib.at[j], m[f"{n}_a_s"].at[j], m[f"{n}_a_r"].at[j],
            (self.b, self.z, 1 - self.c),
        )

    def kept(self, j):
        return pltpu.make_async_copy(
            self.g.at[j, self.c], self.m[f"{self.name}_kept"].at[j], self.m[f"{self.name}_kept_s"].at[j]
        )

    def start(self):
        for j in (self.bd, self.bx, self.by, self.b):
            self.go(self.pair(j))
            self.kept(j).start()

    def step(self, n, src, k):
        m = self.m
        device = (self.bx if n in (0, 1, 5) else self.by, self.z, self.c)
        return remote(
            src.at[self.parts[k]], m[f"{self.name}_came"].at[n], m[f"{self.name}_b_s"].at[n], m[f"{self.name}_b_r"].at[n],
            device,
        )

    def add(self, j):
        self.kept(j).wait()
        self.pair(j).wait_recv()
        self.sib[j] = (self.m[f"{self.name}_kept"][j].astype(F32) + self.sib[j].astype(F32)).astype(BF16)

    def spread(self):
        self.add(self.bd)
        self.go(self.step(1, self.sib.at[self.bd], 0))
        self.go(self.step(3, self.sib.at[self.bd], 1))
        self.add(self.bx)
        self.go(self.step(0, self.sib.at[self.bx], 0))
        self.add(self.by)
        self.go(self.step(2, self.sib.at[self.by], 1))
        self.add(self.b)

    def relay(self):
        came = self.m[f"{self.name}_came"]
        for n, j, k, then in ((1, self.by, 0, 4), (3, self.bx, 1, 5)):
            self.step(n, self.sib.at[j], k).wait_recv()
            at = self.parts[k]
            self.sib[j, at] = (self.sib[j, at].astype(F32) + came[n].astype(F32)).astype(BF16)
            self.go(self.step(then, self.sib.at[j], k))

    def collect(self):
        came = self.m[f"{self.name}_came"]
        for k, one, two in ((0, 0, 4), (1, 2, 5)):
            at = self.parts[k]
            self.step(one, self.sib.at[self.b], k).wait_recv()
            self.step(two, self.sib.at[self.b], k).wait_recv()
            total = self.sib[self.b, at].astype(F32) + came[one].astype(F32) + came[two].astype(F32)
            self.h[at] = total.astype(BF16)

    def end(self):
        finish(self.sends)

    @staticmethod
    def scratch(pool, rows, name):
        pool.vmem(f"{name}_sib", (4, rows, 128))
        pool.vmem(f"{name}_kept", (4, rows, 128))
        pool.dma(f"{name}_kept_s", 4)
        pool.vmem(f"{name}_came", (6, rows // 2, 128))
        pool.dma(f"{name}_a_s", 4)
        pool.dma(f"{name}_a_r", 4)
        pool.dma(f"{name}_b_s", 6)
        pool.dma(f"{name}_b_r", 6)


class BlockSum:
    def __init__(self, nz, h, f, m, name):
        self.b, self.z, self.c = here()
        self.peers = others(self.z, nz)
        self.h, self.f, self.m, self.name = h, f, m, name
        self.ch = h.shape[0] // nz
        self.sends = []

    def go(self, copy):
        copy.start()
        self.sends.append(copy)

    def rows(self, j):
        return band(j * self.ch, self.ch)

    def sem(self, kind, j):
        return self.m[f"{self.name}_{kind}_s"].at[j], self.m[f"{self.name}_{kind}_r"].at[j]

    def start(self):
        for j in self.peers:
            self.go(
                remote(
                    self.h.at[self.rows(j)], self.m[f"{self.name}_came"].at[self.z], self.sem("a", j)[0],
                    self.sem("a", self.z)[1], (self.b, j, self.c),
                )
            )

    def spread(self):
        came, z, c = self.m[f"{self.name}_came"], self.z, self.c
        total = self.h[self.rows(z)].astype(F32)
        for j in self.peers:
            remote(self.h.at[self.rows(j)], came.at[j], *self.sem("a", j), (self.b, j, c)).wait_recv()
            total = total + came[j].astype(F32)
        stage = came.at[z]
        stage[...] = total.astype(BF16)
        piece = self.f.at[c, self.rows(z)]
        for j in self.peers:
            self.go(remote(stage, piece, self.sem("b", j)[0], self.sem("b", z)[1], (self.b, j, c)))
        self.go(remote(stage, piece, *self.sem("c", z), (self.b, z, 1 - c)))
        self.go(pltpu.make_async_copy(stage, piece, self.m[f"{self.name}_own"].at[0]))

    def forward(self):
        c = self.c
        for j in self.peers:
            piece = self.f.at[c, self.rows(j)]
            remote(piece, piece, *self.sem("b", j), (self.b, j, c)).wait_recv()
            self.go(remote(piece, piece, *self.sem("c", j), (self.b, self.z, 1 - c)))

    def end(self):
        for j in self.peers + [self.z]:
            piece = self.f.at[1 - self.c, self.rows(j)]
            remote(piece, piece, *self.sem("c", j), (self.b, self.z, 1 - self.c)).wait_recv()
        finish(self.sends)

    @staticmethod
    def scratch(pool, nz, rows, name):
        pool.vmem(f"{name}_came", (nz, rows // nz, 128))
        pool.dma(f"{name}_own", 1)
        for step in ("a", "b", "c"):
            pool.dma(f"{name}_{step}_s", nz)
            pool.dma(f"{name}_{step}_r", nz)


class ChainSum:
    def __init__(self, nz, pieces, slack, h, f, m, name):
        self.b, self.z, self.c = here()
        self.nz, self.pieces, self.h, self.f, self.m, self.name = nz, pieces, h, f, m, name
        self.ch = h.shape[0] // 2 // pieces
        self.slack = slack
        self.steps = pieces + 2 * slack * (nz - 1)
        self.next = 0

    def rows(self, side, p):
        return band(side * self.pieces * self.ch + p * self.ch, self.ch)

    def copies(self, side, p):
        m, n = self.m, self.name
        came = m[f"{n}_came"].at[side, p]
        piece = self.f.at[self.c, self.rows(side, p)]
        step = 1 - 2 * side
        on = (self.b, lax.rem(self.z + step + self.nz, self.nz), self.c)
        back = (self.b, lax.rem(self.z - step + self.nz, self.nz), self.c)
        over = (self.b, self.z, 1 - self.c)
        sem = lambda kind: m[f"{n}_{kind}"].at[side, p]
        return (
            lambda src: remote(src, came, sem("a_s"), sem("a_r"), on),
            lambda src: remote(src, piece, sem("b_s"), sem("b_r"), back),
            lambda src: remote(src, piece, sem("c_s"), sem("c_r"), over),
            piece,
        )

    def pump(self, s):
        last = self.nz - 1
        for side in range(2):
            pos = self.z if side == 0 else last - self.z
            p = s - self.slack * pos

            @pl.when((p >= 0) & (p < self.pieces))
            def _():
                on, back, over, piece = self.copies(side, p)
                own = self.h.at[self.rows(side, p)]
                came = self.m[f"{self.name}_came"].at[side, p]

                @pl.when(pos == 0)
                def _():
                    on(own).start()

                @pl.when(pos > 0)
                def _():
                    on(came).wait_recv()
                    came[...] = (own[...].astype(F32) + came[...].astype(F32)).astype(BF16)

                @pl.when((pos > 0) & (pos < last))
                def _():
                    on(came).start()

                @pl.when(pos == last)
                def _():
                    pltpu.make_async_copy(came, piece, self.m[f"{self.name}_own"].at[side, p]).start()
                    back(came).start()
                    over(came).start()

            q = s - self.slack * (last + last - pos)

            @pl.when((q >= 0) & (q < self.pieces) & (pos < last))
            def _():
                on, back, over, piece = self.copies(side, q)
                back(piece).wait_recv()
                over(piece).start()

                @pl.when(pos > 0)
                def _():
                    back(piece).start()

    def go(self, count=None):
        upto = self.steps if count is None else min(self.steps, self.next + count)
        if upto - self.next > 4:
            lax.fori_loop(self.next, upto, lambda s, carry: (self.pump(s), carry)[1], 0)
        else:
            for s in range(self.next, upto):
                self.pump(s)
        self.next = upto

    def end(self):
        self.go()
        last = self.nz - 1

        def one(p, carry):
            for side in range(2):
                pos = self.z if side == 0 else last - self.z
                on, back, over, piece = self.copies(side, p)
                other = self.f.at[1 - self.c, self.rows(side, p)]
                came = self.m[f"{self.name}_came"].at[side, p]
                sem = lambda kind: self.m[f"{self.name}_{kind}"].at[side, p]
                remote(other, other, sem("c_s"), sem("c_r"), (self.b, self.z, 1 - self.c)).wait_recv()
                over(piece).wait_send()

                @pl.when(pos < last)
                def _():
                    on(came).wait_send()

                @pl.when(pos > 0)
                def _():
                    back(piece).wait_send()

                @pl.when(pos == last)
                def _():
                    pltpu.make_async_copy(came, piece, self.m[f"{self.name}_own"].at[side, p]).wait()

            return carry

        lax.fori_loop(0, self.pieces, one, 0)

    @staticmethod
    def scratch(pool, rows, pieces, name):
        pool.vmem(f"{name}_came", (2, pieces, rows // 2 // pieces, 128))
        for kind in ("a_s", "a_r", "b_s", "b_r", "c_s", "c_r", "own"):
            pool.dma(f"{name}_{kind}", 2, pieces)


TAIL_IN = ("g_att", "g_heavy", "h_feed", "gm_own", "gf_l", "gf_r", "ids", "tok_own", "vecs", "gain_part", "router")
TAIL_LATE = ("gf_r", "gf_l", "tok_own", "gm_own")
TAIL_OUT = ("delta", "f_att", "f_both", "vectors")


def tail_kernel(nb, nz, pool, *refs):
    i = dict(zip(TAIL_IN, refs[: len(TAIL_IN)]))
    out = dict(zip(TAIL_OUT, refs[len(TAIL_IN) : len(TAIL_IN) + len(TAIL_OUT)]))
    m = pool.bind(refs[len(TAIL_IN) + len(TAIL_OUT) :])
    late = Late(TAIL_LATE, i, m)
    b, z, c = here()
    twin = (b, z, 1 - c)
    bpeers, zpeers = others(b, nb), others(z, nz)
    own, D = i["gm_own"].shape
    greet([twin] + [(j, z, c) for j in bpeers] + [(b, j, c) for j in zpeers])
    gh, sib_h, both_h = i["g_heavy"], m["sib_h"], m["both_h"]
    rf, rh = i["h_feed"].shape[0], sib_h.shape[0]
    to_twin = remote(gh.at[1 - c], sib_h, m["sib_h_s"].at[0], m["sib_h_r"].at[0], twin)
    to_twin.start()
    shard = ShardSum(i["g_att"], m["h_att"], m, "ga")
    shard.start()
    both = ChainSum(nz, 6, 2, both_h, out["f_both"], m, "zb")
    att = BlockSum(nz, m["h_att"], out["f_att"], m, "za")
    both_h[pl.ds(0, rf)] = i["h_feed"][...]
    to_twin.wait_recv()
    both_h[pl.ds(rf, rh)] = (gh[c].astype(F32) + sib_h[...].astype(F32)).astype(BF16)
    both.go(1)
    shard.spread()
    both.go(2)

    late.need()
    hot_t = hot_rows(i["ids"][...] - b * own, own).T
    owned = jnp.sum(hot_t.astype(F32), axis=1, keepdims=True) > 0.5
    gf = jnp.where(owned, mm(hot_t, i["gf_r"][...], 1, 0), i["gf_l"][...])
    r, xh = norm_parts(i["tok_own"][...].astype(F32))
    gain_part = jnp.sum(gf * xh, axis=0, keepdims=True)
    low = m["low"]
    low[...] = (i["gm_own"][...] + norm_back(gf, xh, r, i["vecs"][0:1])).astype(BF16)
    rows = Gather(low, out["delta"], m, "td")
    both.go(2)
    shard.relay()
    rows.start()
    both.go(3)

    vec = m["vec_mine"]
    vec[...] = jnp.zeros_like(vec)
    vec[pl.ds(0, 1)] = gain_part
    vec[pl.ds(1, 1)] = i["gain_part"][...]
    vec[pl.ds(2, 1)] = i["router"][...]
    sends = [to_twin]

    def vec_step(name, me, peers, device):
        got = m[f"{name}_got"]
        got[me] = vec[...]
        for j in peers:
            copy = remote(vec, got.at[me], m[f"{name}_s"].at[j], m[f"{name}_r"].at[me], device(j))
            copy.start()
            sends.append(copy)

    def vec_end(name, peers, device):
        got = m[f"{name}_got"]
        for j in peers:
            remote(got.at[j], got.at[j], m[f"{name}_s"].at[j], m[f"{name}_r"].at[j], device(j)).wait_recv()
        return functools.reduce(lambda x, y: x + y, [got[j] for j in range(got.shape[0])])

    by_core, by_branch, by_block = (lambda j: (b, z, j)), (lambda j: (j, z, c)), (lambda j: (b, j, c))
    vec_step("vc", c, [1 - c], by_core)
    both.go(1)
    shard.collect()
    att.start()
    total = vec_end("vc", [1 - c], by_core)
    vec2 = m["vec_pair"]
    vec2[...] = total
    vec = vec2
    vec_step("vb", b, bpeers, by_branch)
    both.go(3)
    total = vec_end("vb", bpeers, by_branch)
    vec3 = m["vec_group"]
    vec3[...] = total
    vec = vec3
    vec_step("vz", z, zpeers, by_block)
    both.go(2)
    att.spread()
    rows.relay()
    both.go(4)
    out["vectors"][...] = vec_end("vz", zpeers, by_block)
    both.go()
    att.forward()
    both.end()
    att.end()
    shard.end()
    rows.wait()
    finish(sends)


def tail(nb, nz, given):
    own, D = given["gm_own"].shape
    ra, rh, rf = given["g_att"].shape[2], given["g_heavy"].shape[1], given["h_feed"].shape[0]
    shape = lambda *dims: jax.ShapeDtypeStruct(dims, BF16)
    outs = dict(
        delta=shape(nb, own, D), f_att=shape(2, ra, 128), f_both=shape(2, rf + rh, 128),
        vectors=jax.ShapeDtypeStruct((8, D), F32),
    )
    pool = Pool()
    Late.scratch(pool, TAIL_LATE, given)
    pool.vmem("sib_h", (rh, 128))
    pool.vmem("both_h", (rf + rh, 128))
    pool.vmem("h_att", (ra, 128))
    pool.vmem("low", (own, D))
    pool.dma("sib_h_s", 1)
    pool.dma("sib_h_r", 1)
    ShardSum.scratch(pool, ra, "ga")
    BlockSum.scratch(pool, nz, ra, "za")
    ChainSum.scratch(pool, rf + rh, 6, "zb")
    Gather.scratch(pool, "td")
    for name in ("vec_mine", "vec_pair", "vec_group"):
        pool.vmem(name, (8, D), F32)
    for name, count in (("vc", 2), ("vb", nb), ("vz", nz)):
        pool.vmem(f"{name}_got", (count, 8, D), F32)
        pool.dma(f"{name}_s", count)
        pool.dma(f"{name}_r", count)
    got = pl.pallas_call(
        functools.partial(tail_kernel, nb, nz, pool),
        out_shape=tuple(outs[name] for name in TAIL_OUT),
        in_specs=[HB if name in ("g_att",) + TAIL_LATE else VM for name in TAIL_IN],
        out_specs=(HB,) * 3 + (VM,),
        scratch_shapes=pool.shapes,
        compiler_params=pltpu.CompilerParams(
            collective_id=4, has_side_effects=True, vmem_limit_bytes=56 << 20
        ),
    )(*(given[name] for name in TAIL_IN))
    return dict(zip(TAIL_OUT, got))


MID_IN = (
    "tok_own", "cot_own", "ids", "vecs", "tok_r", "cot_r", "gate", "mixed", "attn_l",
    "le", "lr", "re", "rr",
)
MID_OUT = ("base", "ff", "gm_own", "gm_r", "gate_feed", "gain_part", "g_feed", "g_rx", "f_gate")


MID_EARLY = ("base", "ff", "g_rx", "g_feed")
MID_LATE = ("re", "rr", "cot_own", "le", "lr")


def lane_blocks(x):
    return [x[:, n * 128 : (n + 1) * 128] for n in range(x.shape[1] // 128)]


def pack_rows(g, start, parts):
    for part in parts:
        size = part.shape[0] // 2
        for core in range(2):
            g[core, pl.ds(start, size)] = part[core * size : (core + 1) * size].astype(BF16)
        start += size
    return start


def down_pieces(rows, D):
    steps = 8
    per, step = D // steps // 32, rows // steps
    pieces = []
    for n in range(steps):
        spots = [(r, k) for k in range(D // 128) for r in range(0, step, 32)]
        pieces += [(p // per, n * (D // steps) + p % per * 32, n * step + r, k) for p, (r, k) in enumerate(spots)]
    return pieces


def pack_down(g, start, x):
    for block, at, row, k in down_pieces(*x.shape):
        g[start + block, pl.ds(at, 32)] = x[row : row + 32, k * 128 : (k + 1) * 128].astype(BF16)


def mid_kernel(nb, nz, pool, *refs):
    i = dict(zip(MID_IN, refs[: len(MID_IN)]))
    out = dict(zip(MID_OUT, refs[len(MID_IN) : len(MID_IN) + len(MID_OUT)]))
    m = pool.bind(refs[len(MID_IN) + len(MID_OUT) :])
    early = Early(MID_EARLY, out, m)
    late = Late(MID_LATE, i, m)
    b, z, c = here()
    greet([(b, z, 1 - c)] + [(j, z, c) for j in others(b, nb)] + [(b, j, c) for j in others(z, nz)])
    own, D = i["tok_own"].shape
    cap = i["ids"].shape[0]
    fl = i["le"].shape[2] // nb
    fh = i["re"].shape[2]
    gain = i["vecs"][1:2]

    pick, pick_t = m["pick"], m["pick_t"]
    hot = hot_rows(i["ids"][...] - b * own, own)
    pick[...] = hot
    pick_t[...] = hot.T
    owned = jnp.sum(pick_t[...].astype(F32), axis=1, keepdims=True) > 0.5
    mid_o, mid_r = m["mid_o"], m["mid_r"]
    mid_o[...] = i["tok_own"][...].astype(F32) + jnp.where(
        owned, mm(pick_t[...], i["mixed"][...], 1, 0), i["attn_l"][...]
    )
    mid_r[...] = i["tok_r"][...].astype(F32) + i["mixed"][...].astype(F32)
    n_o, n_r = m["n_o"], m["n_r"]
    n_o[...] = normed(mid_o[...], gain)
    n_r[...] = normed(mid_r[...], gain)
    gate = i["gate"][...]
    seed_r = m["seed_r"]
    seed_r[...] = (gate * i["cot_r"][...].astype(F32)).astype(BF16)

    def both_ways(n, seed, expand, narrow, row0, tile, count, hid, du, dv, ff, dn):
        def one(t, carry):
            lanes = band(t * tile, tile)
            wd = narrow[band(row0 + t * tile, tile)]
            u = mm(n[...], expand[0, :, lanes], 1, 0)
            v = mm(n[...], expand[1, :, lanes], 1, 0)
            g, dg = gelu_parts(u)
            low = (g * v).astype(BF16)
            hid[:, lanes] = low
            dh = mm(seed[...], wd, 1, 1)
            du[:, lanes] = (dh * v * dg).astype(BF16)
            dv[:, lanes] = (dh * g).astype(BF16)
            one_ff = mm(low, wd, 1, 0)
            one_dn = mm(du[:, lanes], expand[0, :, lanes], 1, 1) + mm(dv[:, lanes], expand[1, :, lanes], 1, 1)
            ff[...] = jnp.where(t == 0, one_ff, ff[...] + one_ff)
            dn[...] = jnp.where(t == 0, one_dn, dn[...] + one_dn)
            return carry

        lax.fori_loop(0, count, one, 0)

    ff_r, dn_r, ff_o, dn_o = m["ff_r"], m["dn_r"], m["ff_o"], m["dn_o"]
    late.need("re", "rr")
    both_ways(
        n_r, seed_r, i["re"], i["rr"], c * fh, fl, fh // fl, m["hid_r"], m["du_r"], m["dv_r"], ff_r, dn_r
    )
    n_t = m["n_t"]
    n_t[...] = n_r[...].T
    g_gate = m["g_gate"]
    for k, x in enumerate(lane_blocks(mm(n_t[...], m["du_r"][...], 1, 0))):
        g_gate[pl.ds(k * D, D)] = x.astype(BF16)
    chain = BlockSum(nz, g_gate, out["f_gate"], m, "zg")
    chain.start()
    late.need()
    both_ways(
        n_o, i["cot_own"], i["le"], i["lr"], 0, fl, nb, m["hid_o"], m["du_o"], m["dv_o"], ff_o, dn_o,
    )
    out["gate_feed"][...] = jnp.sum(i["cot_r"][...].astype(F32) * ff_r[...], axis=-1, keepdims=True)
    part = m["part"]
    out["ff"][...] = ff_r[...].astype(BF16)
    out["base"][...] = mid_o[...] + ff_o[...]
    early.put("ff", "base")
    part[...] = (dn_r[...] + mm(pick[...], dn_o[...].astype(BF16), 1, 0)).astype(BF16)

    def weights_heavy():
        gx = out["g_rx"]
        for k, x in enumerate(lane_blocks(mm(n_t[...], m["dv_r"][...], 1, 0))):
            gx[k] = x.astype(BF16)
        pack_down(gx, fh // 128, mm(m["hid_r"][...], seed_r[...], 0, 0))
        early.put("g_rx")
        chain.spread()

    def weights_light():
        n_t[...] = n_o[...].T
        g = out["g_feed"]

        def one(t, carry):
            lanes = band(t * fl, fl)
            gate_part = mm(n_t[...], m["du_o"][:, lanes], 1, 0)
            up_part = mm(n_t[...], m["dv_o"][:, lanes], 1, 0)
            down = mm(m["hid_o"][:, lanes], i["cot_own"][...], 0, 0)
            pack_rows(g.at[t], 0, lane_blocks(gate_part) + lane_blocks(up_part) + lane_blocks(down))
            return carry

        lax.fori_loop(0, nb, one, 0)
        early.put("g_feed")

    sums = m["sums"]
    group_sum_steps(nb, part, sums, m, [weights_heavy, weights_light])
    dn_sum = sums[...]
    dn_own = jnp.where(owned, mm(pick_t[...], dn_sum, 1, 0), dn_o[...])
    r, xh = norm_parts(mid_o[...])
    out["gm_own"][...] = i["cot_own"][...].astype(F32) + norm_back(dn_own, xh, r, gain)
    out["gain_part"][...] = jnp.sum(dn_own * xh, axis=0, keepdims=True)
    r, xh = norm_parts(mid_r[...])
    out["gm_r"][...] = i["cot_r"][...].astype(F32) + norm_back(dn_sum.astype(F32), xh, r, gain)
    chain.forward()
    chain.end()
    early.end()


def middle(nb, nz, given):
    own, D = given["tok_own"].shape
    cap = given["ids"].shape[0]
    wide = given["le"].shape[2]
    fl = wide // nb
    fh = given["re"].shape[2]
    shape = lambda *dims: jax.ShapeDtypeStruct(dims, BF16)
    shape32 = lambda *dims: jax.ShapeDtypeStruct(dims, F32)
    packed = (2 * D * fl + fl * D) // 2 // 128
    outs = dict(
        base=shape32(own, D), ff=shape(cap, D), gm_own=shape32(own, D), gm_r=shape32(cap, D), gate_feed=shape32(cap, 1),
        gain_part=shape32(1, D), g_feed=shape(nb, 2, packed, 128), g_rx=shape(2 * fh // 128, D, 128), f_gate=shape(2, D * fh // 128, 128),
    )
    pool = Pool()
    Early.scratch(pool, MID_EARLY, outs)
    Late.scratch(pool, MID_LATE, given)
    pool.vmem("pick", (cap, own))
    pool.vmem("pick_t", (own, cap))
    for name, count in (("o", own), ("r", cap)):
        pool.vmem(f"mid_{name}", (count, D), F32)
        pool.vmem(f"n_{name}", (count, D))
        pool.vmem(f"ff_{name}", (count, D), F32)
        pool.vmem(f"dn_{name}", (count, D), F32)
        for kind in ("hid", "du", "dv"):
            pool.vmem(f"{kind}_{name}", (count, wide if name == "o" else fh))
    pool.vmem("seed_r", (cap, D))
    pool.vmem("n_t", (D, own))
    pool.vmem("part", (cap, D))
    pool.vmem("sums", (cap, D))
    pool.vmem("g_gate", (D * fh // 128, 128))
    group_sum_scratch(pool, nb, cap, D)
    BlockSum.scratch(pool, nz, D * fh // 128, "zg")
    got = pl.pallas_call(
        functools.partial(mid_kernel, nb, nz, pool),
        out_shape=tuple(outs[name] for name in MID_OUT),
        in_specs=[HB if name in MID_LATE else VM for name in MID_IN],
        out_specs=tuple(HB if name in ("f_gate",) + MID_EARLY else VM for name in MID_OUT),
        scratch_shapes=pool.shapes,
        compiler_params=pltpu.CompilerParams(
            collective_id=2, has_side_effects=True, vmem_limit_bytes=60 << 20
        ),
    )(*(given[name] for name in MID_IN))
    return dict(zip(MID_OUT, got))


BACK_OUT = ("gf_r", "gf_l", "g_att", "g_heavy", "router", "lay", "h_feed", "f_rx")
BACK_IN = (
    "gm_own", "gm_r", "gate", "gate_feed", "ids", "q", "k", "v", "lm", "lh", "first_w", "ctx_l",
    "qr", "kv", "rmerge", "rheads", "first_r", "ctx_r", "attn_r", "vecs",
    "base", "ff", "g_feed", "g_rx",
)


BACK_EARLY = ("h_feed", "gf_l", "g_att", "g_heavy")
BACK_LATE = (
    "base", "gm_own", "q", "k", "v", "lm", "lh", "first_w", "ctx_l", "rheads", "first_r", "attn_r",
)


def back_names(inner):
    return BACK_IN if inner else BACK_IN + ("trio",)


def heavy_back(i, m, seed, x):
    kv, qr = i["kv"], i["qr"]
    half, rw = qr.shape
    keys, values, keys_t, dk, dv, dq_t, do = (
        m[n] for n in ("keys", "values", "keys_t", "dk", "dv", "dq_t", "do")
    )
    keys[...] = kv[:, :rw]
    values[...] = kv[:, rw:]
    keys_t[...] = keys[...].T
    do[...] = mm(seed, i["rmerge"][...], 1, 1).astype(BF16)
    dk[...] = jnp.zeros_like(dk)
    dv[...] = jnp.zeros_like(dv)
    dq_t[...] = jnp.zeros_like(dq_t)
    some = 128

    def heavy(n):
        at = band(n * some, some)
        for h in range(rw // DH):
            qh, doh = only_head(qr[at], h), only_head(do[at], h)
            s = mm(keys[...], qh, 1, 1) * SCALE
            w = jnp.exp(s - jnp.max(s, axis=0, keepdims=True))
            p = w * (1.0 / jnp.sum(w, axis=0, keepdims=True))
            dp = mm(values[...], doh, 1, 1)
            ds = (p * (dp - jnp.sum(p * dp, axis=0, keepdims=True))).astype(BF16)
            dk[...] += mm(ds, qh, 1, 0)
            dv[...] += mm(p.astype(BF16), doh, 1, 0)
            got = mm(keys_t[...], ds, 1, 0)
            dq_t[:, at] += jnp.where(head_lanes(got.shape, h, 0), got, 0.0)

    def end():
        x[:, :rw] = (dk[...] * SCALE).astype(BF16)
        x[:, rw:] = dv[...].astype(BF16)

    return [functools.partial(heavy, n) for n in range(half // some)] + [end]


def heavy_back_plain(i):
    half, rw = i["qr"].shape
    split = lambda y: y.reshape(y.shape[0], -1, DH)
    at = lax.axis_index("core") * half
    seed = (i["gate"] * i["gm_r"]).astype(BF16)
    seed = lax.dynamic_slice(seed, (at, 0), (half, seed.shape[1]))
    do = split(mm(seed, i["rmerge"], 1, 1).astype(BF16))
    q, k, v = split(i["qr"]), split(i["kv"][:, :rw]), split(i["kv"][:, rw:])
    p = jax.nn.softmax(jnp.einsum("qhe,khe->hqk", q, k, preferred_element_type=F32) * SCALE, axis=-1)
    dp = jnp.einsum("qhe,khe->hqk", do, v, preferred_element_type=F32)
    ds = (p * (dp - jnp.sum(p * dp, -1, keepdims=True))).astype(BF16)
    dq = jnp.einsum("hqk,khe->qhe", ds, k, preferred_element_type=F32) * SCALE
    dk = jnp.einsum("hqk,qhe->khe", ds, q, preferred_element_type=F32) * SCALE
    dv = jnp.einsum("hqk,qhe->khe", p.astype(BF16), do, preferred_element_type=F32)
    both = jnp.concatenate([dk.reshape(-1, rw), dv.reshape(-1, rw)], 1).astype(BF16)
    both = lax.psum_scatter(both, DP, scatter_dimension=0, tiled=True)
    return jnp.stack([dq.reshape(half, rw).astype(BF16), both[:, :rw], both[:, rw:]], 0)


def back_kernel(nb, nz, pool, inner, *refs):
    names = back_names(inner)
    i = dict(zip(names, refs[: len(names)]))
    out = dict(zip(BACK_OUT, refs[len(names) : len(names) + len(BACK_OUT)]))
    m = pool.bind(refs[len(names) + len(BACK_OUT) :])
    late = Late(BACK_LATE, i, m)
    early = Early(BACK_EARLY, out, m)
    b, z, c = here()
    twin = (b, z, 1 - c)
    bpeers, zpeers = others(b, nb), others(z, nz)
    own, D = i["gm_own"].shape
    rows = own * nb
    cap = i["ids"].shape[0]
    half = cap // 2
    rw = i["rmerge"].shape[0]
    wl = i["q"].shape[1]
    last, first = b == nb - 1, b == 0
    after = (
        jnp.where(last, 0, b + 1), jnp.where(last, lax.rem(z + c, nz), z), jnp.where(last, 1 - c, c),
    )
    before = (
        jnp.where(first, nb - 1, b - 1),
        jnp.where(first, lax.rem(z + nz - 1 + c, nz), z),
        jnp.where(first, 1 - c, c),
    )
    greet([twin, after, before] + [(j, z, c) for j in bpeers] + [(b, j, c) for j in zpeers])
    mine_at, other_at = band(c * half, half), band((1 - c) * half, half)
    sends = []
    layer = Gather(m["layer"], out["lay"], m, "ly")
    shard = ShardSum(i["g_feed"], out["h_feed"], m, "gf")
    chain = BlockSum(nz, i["g_rx"], out["f_rx"], m, "zx")
    chain.start()
    shard.start()

    def go(copy):
        copy.start()
        sends.append(copy)

    gm_half = i["gm_r"][mine_at]
    gate_half = i["gate"][mine_at]
    seed = (gate_half * gm_half).astype(BF16)
    pack_rows(out["g_heavy"], 3 * rw // 2 * (D // 128), lane_blocks(mm(i["ctx_r"][...], seed, 0, 0)))
    trio = m["trio"] if inner else i["trio"]

    def spot(core, j):
        return band((2 * j + core) * half, half)

    def to_twin(j):
        return remote(x.at[spot(1 - c, j)], sib.at[j], m["bs_sib_s"].at[j], m["bs_sib_r"].at[j], twin)

    shard.spread()
    if inner:
        x, sib, came = m["dkv"], m["bs_sib"], m["bs_came"]
        pieces = heavy_back(i, m, seed, x)
        pieces[-1:] = [functools.partial(lambda f: (f(), [go(to_twin(j)) for j in zpeers + [z]]), pieces[-1])]
    else:
        pieces = []
    group_sum_steps(nb, i["ff"], m["ff_sum"], m, pieces, "fs")
    late.need()
    pick_t = hot_rows(i["ids"][...] - b * own, own).T
    scaled = (i["gate"][...] * m["ff_sum"][...].astype(F32)).astype(BF16)
    m["layer"][...] = (i["base"][...] + mm(pick_t, scaled, 1, 0)).astype(BF16)
    shard.relay()
    layer.start()

    low, do_l = m["low"], m["do_l"]
    low[...] = i["gm_own"][...].astype(BF16)
    do_l[...] = mm(low[...], i["lm"][...], 1, 1).astype(BF16)
    for j in zpeers if inner else []:
        to_twin(j).wait_recv()
        sib[j] = (x[spot(c, j)].astype(F32) + sib[j].astype(F32)).astype(BF16)
        go(remote(sib.at[j], came.at[z], m["bs_rs_s"].at[j], m["bs_rs_r"].at[z], (b, j, c)))

    q, k, v = i["q"], i["k"], i["v"]
    lk_t, dkl, dvl, dql = m["lk_t"], m["dkl"], m["dvl"], m["dql"]
    lk_t[...] = k[...].T
    dkl[...] = jnp.zeros_like(dkl)
    dvl[...] = jnp.zeros_like(dvl)
    blocks = own // WIN
    first_key = (2 * z + c) * rows + b * own - WIN
    total = 2 * nz * rows

    def light(n_, carry):
        g, n = n_ // blocks, lax.rem(n_, blocks)
        lanes = band(g * 2 * DH, 2 * DH)
        at = band(n * WIN, WIN)
        near = pl.ds(pl.multiple_of(n * WIN, WIN), 3 * WIN)
        q2, do2, k2, v2, kt2 = q[at, lanes], do_l[at, lanes], k[near, lanes], v[near, lanes], lk_t[lanes, near]
        allowed = near_keys((3 * WIN, WIN), 0, first_key + n * WIN, total)
        got_k = got_v = None
        got_q = []
        for h in range(2):
            qh, doh = only_head(q2, h), only_head(do2, h)
            s = jnp.where(allowed, mm(k2, qh, 1, 1) * SCALE, NEGATIVE)
            w = jnp.exp(s - jnp.max(s, axis=0, keepdims=True))
            p = w * (1.0 / jnp.sum(w, axis=0, keepdims=True))
            dp = mm(v2, doh, 1, 1)
            ds = (p * (dp - jnp.sum(p * dp, axis=0, keepdims=True))).astype(BF16)
            one_k, one_v = mm(ds, qh, 1, 0), mm(p.astype(BF16), doh, 1, 0)
            got_k = one_k if got_k is None else got_k + one_k
            got_v = one_v if got_v is None else got_v + one_v
            got_q.append(mm(kt2, ds, 1, 0))
        dkl[near, lanes] += got_k
        dvl[near, lanes] += got_v
        both = jnp.where(head_lanes((2 * DH, WIN), 0, 0), got_q[0], got_q[1])
        dql[at, lanes] = (both.T * SCALE).astype(BF16)
        return carry

    lax.fori_loop(0, blocks * (wl // (2 * DH)), light, 0, unroll=2)
    layer.relay()
    shard.collect()
    early.put("h_feed")
    rim, came_rim = m["rim"], m["came_rim"]
    for n, start in ((0, WIN + own), (1, 0)):
        rim[n, :, :wl] = (dkl[pl.ds(start, WIN)] * SCALE).astype(BF16)
        rim[n, :, wl:] = dvl[pl.ds(start, WIN)].astype(BF16)
    go(remote(rim.at[0], came_rim.at[0], m["rim_s"].at[0], m["rim_r"].at[0], after))
    go(remote(rim.at[1], came_rim.at[1], m["rim_s"].at[1], m["rim_r"].at[1], before))

    if inner:
        to_twin(z).wait_recv()
        mine = x[spot(c, z)].astype(F32) + sib[z].astype(F32)
        for j in zpeers:
            remote(sib.at[j], came.at[j], m["bs_rs_s"].at[j], m["bs_rs_r"].at[j], (b, j, c)).wait_recv()
            mine = mine + came[j].astype(F32)
        trio[0] = (m["dq_t"][...].T * SCALE).astype(BF16)
        trio[1] = mine[:, :rw].astype(BF16)
        trio[2] = mine[:, rw:].astype(BF16)
    chain.spread()
    rheads = i["rheads"]
    picked = mm(trio[0], rheads[0], 1, 0) + mm(trio[1], rheads[1], 1, 0) + mm(trio[2], rheads[2], 1, 0)

    for n, device in ((0, before), (1, after)):
        remote(rim.at[n], came_rim.at[n], m["rim_s"].at[n], m["rim_r"].at[n], device).wait_recv()
    dkl[pl.ds(WIN, WIN)] += came_rim[0, :, :wl].astype(F32) * (1.0 / SCALE)
    dvl[pl.ds(WIN, WIN)] += came_rim[0, :, wl:].astype(F32)
    dkl[pl.ds(own, WIN)] += came_rim[1, :, :wl].astype(F32) * (1.0 / SCALE)
    dvl[pl.ds(own, WIN)] += came_rim[1, :, wl:].astype(F32)
    dk_own, dv_own = m["dk_own"], m["dv_own"]
    dk_own[...] = (dkl[pl.ds(WIN, own)] * SCALE).astype(BF16)
    dv_own[...] = dvl[pl.ds(WIN, own)].astype(BF16)
    lh = i["lh"]
    gf_l = out["gf_l"]
    gf_l[...] = mm(dql[...], lh[0], 1, 1) + mm(dk_own[...], lh[1], 1, 1) + mm(dv_own[...], lh[2], 1, 1)

    early.put("gf_l")
    gate, first_r = i["gate"], i["first_r"]
    gate_attn = jnp.sum(gm_half * i["attn_r"][...], axis=-1, keepdims=True)
    total_part = m["part"]
    low_gf = gf_l[...].astype(BF16)
    router_sum = None
    for at, extra, more in ((other_at, None, None), (mine_at, gate_attn, picked)):
        g = gate[at]
        d_gate = i["gate_feed"][at] if extra is None else i["gate_feed"][at] + extra
        d_logit = d_gate * g * (1.0 - g)
        one = jnp.sum(d_logit * first_r[at].astype(F32), axis=0, keepdims=True)
        router_sum = one if router_sum is None else router_sum + one
        sum_ = mm(hot_rows(i["ids"][at] - b * own, own), low_gf, 1, 0) + d_logit * i["vecs"][2:3]
        if more is not None:
            sum_ = sum_ + more
        total_part[at] = sum_.astype(BF16)
    out["router"][...] = router_sum

    first_t, g_att = m["first_t"], out["g_att"]
    hl = wl // nb

    def weights_light():
        first_t[...] = i["first_w"][pl.ds(WIN, own)].T

        def one(t, carry):
            lanes = band(t * 2 * hl, 2 * hl)
            for n, x in enumerate((dql, dk_own, dv_own)):
                both = mm(first_t[...], x[:, lanes], 1, 0)
                for k in range(2):
                    pack_rows(g_att.at[2 * t + k], n * D // 2, [both[:, k * hl : (k + 1) * hl]])
            return carry

        lax.fori_loop(0, nb // 2, one, 0)

    def weights_rest():
        def one(t, carry):
            both = mm(i["ctx_l"][:, band(t * 2 * hl, 2 * hl)], low[...], 0, 0)
            for k in range(2):
                pack_rows(g_att.at[2 * t + k], 3 * D // 2, lane_blocks(both[k * hl : (k + 1) * hl]))
            return carry

        lax.fori_loop(0, nb // 2, one, 0)
        first_half = first_r[mine_at]
        for n in range(3):
            pack_rows(out["g_heavy"], n * rw // 2 * (D // 128), lane_blocks(mm(trio[n], first_half, 0, 0)))
        early.put("g_att", "g_heavy")

    group_sum_steps(nb, total_part, out["gf_r"], m, [weights_light, weights_rest])
    chain.forward()
    chain.end()
    shard.end()
    layer.wait()
    early.end()
    finish(sends)


def back(nb, nz, given):
    own, D = given["gm_own"].shape
    cap = given["ids"].shape[0]
    half = cap // 2
    rw = given["rmerge"].shape[0]
    wl = given["q"].shape[1]
    deep = 2 * nz * half
    feed_rows, rx_rows = given["g_feed"].shape[2], given["g_rx"].shape[0]
    shape = lambda *dims: jax.ShapeDtypeStruct(dims, BF16)
    outs = dict(
        gf_r=shape(cap, D), gf_l=jax.ShapeDtypeStruct((own, D), F32),
        g_att=shape(nb, 2, 2 * D * wl // nb // 128, 128), g_heavy=shape(2, 2 * D * rw // 128, 128),
        router=jax.ShapeDtypeStruct((1, D), F32),
        lay=shape(nb, own, D), h_feed=shape(feed_rows, 128), f_rx=shape(2, rx_rows, 128),
    )
    pool = Pool()
    inner = deep <= 4096
    if inner:
        pool.vmem("keys", (deep, rw))
        pool.vmem("values", (deep, rw))
        pool.vmem("keys_t", (rw, deep))
        pool.vmem("dk", (deep, rw), F32)
        pool.vmem("dv", (deep, rw), F32)
        pool.vmem("dq_t", (rw, half), F32)
        pool.vmem("do", (half, rw))
        pool.vmem("trio", (3, half, rw))
        pool.vmem("dkv", (deep, 2 * rw))
        for name in ("bs_sib", "bs_came"):
            pool.vmem(name, (nz, half, 2 * rw))
    pool.vmem("low", (own, D))
    pool.vmem("do_l", (own, wl))
    pool.vmem("lk_t", (wl, own + 2 * WIN))
    pool.vmem("dkl", (own + 2 * WIN, wl), F32)
    pool.vmem("dvl", (own + 2 * WIN, wl), F32)
    pool.vmem("dql", (own, wl))
    pool.vmem("dk_own", (own, wl))
    pool.vmem("dv_own", (own, wl))
    pool.vmem("rim", (2, WIN, 2 * wl))
    pool.vmem("came_rim", (2, WIN, 2 * wl))
    pool.vmem("first_t", (D, own))
    pool.vmem("part", (cap, D))
    group_sum_scratch(pool, nb, cap, D)
    for name in ("bs_sib", "bs_rs") if inner else ():
        pool.dma(f"{name}_s", nz)
        pool.dma(f"{name}_r", nz)
    if not inner:
        given = dict(given, trio=heavy_back_plain(given))
    Late.scratch(pool, BACK_LATE, given)
    Early.scratch(pool, BACK_EARLY, outs)
    pool.vmem("layer", (own, D))
    pool.vmem("ff_sum", (cap, D))
    group_sum_scratch(pool, nb, cap, D, "fs")
    ShardSum.scratch(pool, feed_rows, "gf")
    BlockSum.scratch(pool, nz, rx_rows, "zx")
    Gather.scratch(pool, "ly")
    pool.dma("rim_s", 2)
    pool.dma("rim_r", 2)
    got = pl.pallas_call(
        functools.partial(back_kernel, nb, nz, pool, inner),
        out_shape=tuple(outs[name] for name in BACK_OUT),
        in_specs=[HB if name in ("g_feed",) + BACK_LATE else VM for name in back_names(inner)],
        out_specs=tuple(HB if name in ("lay", "f_rx") + BACK_EARLY else VM for name in BACK_OUT),
        scratch_shapes=pool.shapes,
        compiler_params=pltpu.CompilerParams(
            collective_id=3, has_side_effects=True, vmem_limit_bytes=62 << 20
        ),
    )(*(given[name] for name in back_names(inner)))
    return dict(zip(BACK_OUT, got))


FIN_OUT = ("layer", "delta", "re", "rr", "lh", "lm", "rh", "rm", "le", "lr")


def finish_kernel(lay, dlt, gate, rx, att, both, *outs):
    o = dict(zip(FIN_OUT, outs))
    o["layer"][...] = lay[...].astype(F32)
    o["delta"][...] = dlt[...].astype(F32)
    size = rx.shape[2]
    blocks = gate.shape[1]
    for core in range(2):
        for part in range(2):
            for k in range(blocks):
                at = 2 * (core * blocks + k) + part
                o["re"][pl.ds(at, size, 4 * blocks), :] = (rx if part else gate)[core, k].astype(F32)
        for block, at, row, k in down_pieces(blocks * 128, size * 8):
            if row < blocks * 16:
                o["rr"][core, pl.ds(row, 32), k * 128 : (k + 1) * 128] = rx[core, blocks + block, pl.ds(at, 32)].astype(F32)

    @pl.when(pl.program_id(0) == 0)
    def _():
        for core in range(2):
            D, hl = o["lh"].shape[1:]
            start = 0
            for n in range(3):
                size = D // 2
                o["lh"][n, pl.ds(core * size, size)] = att[core, pl.ds(start, size)].astype(F32)
                start += size
            for k in range(D // 128):
                size = hl // 2
                o["lm"][pl.ds(core * size, size), k * 128 : (k + 1) * 128] = att[core, pl.ds(start, size)].astype(F32)
                start += size
            start = D * 3 * o["lr"].shape[0] // 256
            size = o["rm"].shape[0] // 2
            for n in range(4):
                dst = o["rm"] if n == 3 else o["rh"].at[n]
                for k in range(D // 128):
                    dst[pl.ds(core * size, size), k * 128 : (k + 1) * 128] = both[core, pl.ds(start, size)].astype(F32)
                    start += size
            start = 0
            fl = o["lr"].shape[0]
            lanes = fl // 128
            size = D // 2
            for part in range(2):
                for k in range(lanes):
                    o["le"][pl.ds(core * size * 2 * lanes + 2 * k + part, size, 2 * lanes), :] = both[
                        core, pl.ds(start, size)
                    ].astype(F32)
                    start += size
            size = fl // 2
            for k in range(D // 128):
                o["lr"][pl.ds(core * size, size), k * 128 : (k + 1) * 128] = both[core, pl.ds(start, size)].astype(F32)
                start += size


def finish_all(lay, dlt, gate, rx, att, both, hl, fl, rw):
    steps = 8
    rows, D = lay.shape
    fh = gate.shape[1] * 128
    shape = lambda *dims: jax.ShapeDtypeStruct(dims, F32)
    whole = lambda *dims: pl.BlockSpec(dims, lambda n: (0,) * len(dims))
    tall = lambda count, width: pl.BlockSpec((count // steps, width), lambda n: (n, 0))
    return dict(
        zip(
            FIN_OUT,
            pl.pallas_call(
                finish_kernel,
                grid=(steps,),
                out_shape=(
                    shape(rows, D), shape(rows, D), shape(D * 4 * fh // 128, 128), shape(2, fh, D),
                    shape(3, D, hl), shape(hl, D), shape(3, rw, D), shape(rw, D),
                    shape(D * 2 * fl // 128, 128), shape(fl, D),
                ),
                in_specs=[
                    tall(rows, D), tall(rows, D),
                    pl.BlockSpec((2, fh // 128, D // steps, 128), lambda n: (0, 0, n, 0)),
                    pl.BlockSpec((2, 2 * fh // 128, D // steps, 128), lambda n: (0, 0, n, 0)),
                    whole(*att.shape), whole(*both.shape),
                ],
                out_specs=(
                    tall(rows, D), tall(rows, D), tall(D * 4 * fh // 128, 128),
                    pl.BlockSpec((2, fh // steps, D), lambda n: (0, n, 0)),
                    whole(3, D, hl), whole(hl, D), whole(3, rw, D), whole(rw, D),
                    whole(D * 2 * fl // 128, 128), whole(fl, D),
                ),
                compiler_params=pltpu.CompilerParams(vmem_limit_bytes=50 << 20),
            )(lay, dlt, gate, rx, att, both),
        )
    )


def woven(x, width):
    blocks = width // 128
    return x.reshape(-1, blocks, 2, 128).transpose(0, 2, 1, 3).reshape(-1, 2, width)


def per_device(
    tokens,
    cotangent,
    gain_before,
    gain_middle,
    router_vector,
    local_heads,
    local_merge,
    routed_heads,
    routed_merge,
    local_expand,
    local_reduce,
    routed_expand,
    routed_reduce,
    routed_slots,
    routed_counts,
):
    nb = lax.axis_size("branch")
    nz = lax.axis_size("zz")
    core = lax.axis_index("core")
    rows, D = tokens.shape
    fh = routed_expand.shape[2] // 2
    vecs = jnp.stack([gain_before, gain_middle, router_vector])
    rheads = routed_heads.transpose(1, 2, 0)
    f = front(
        nb, nz, tokens, cotangent, routed_slots[None], routed_counts, vecs, rheads, routed_merge,
        local_heads.transpose(1, 0, 2), local_merge, local_expand.transpose(1, 0, 2), local_reduce,
    )
    re_half = lax.dynamic_slice(routed_expand, (0, 0, core * fh), (D, 2, fh)).transpose(1, 0, 2)
    f = dict(f, vecs=vecs, re=re_half, rr=routed_reduce, rmerge=routed_merge, rheads=rheads)
    f = dict(f, **middle(nb, nz, f))
    f["g_rx"] = f["g_rx"].reshape(-1, 128)
    f = dict(f, **back(nb, nz, f))
    f = dict(f, **tail(nb, nz, f))
    g = finish_all(
        f["lay"].reshape(rows, D), f["delta"].reshape(rows, D), f["f_gate"].reshape(2, -1, D, 128),
        f["f_rx"].reshape(2, -1, D, 128), f["f_att"], f["f_both"], hl=local_merge.shape[0], fl=local_reduce.shape[0],
        rw=routed_merge.shape[0],
    )
    return (
        g["layer"],
        g["delta"],
        f["vectors"][0],
        f["vectors"][1],
        f["vectors"][2],
        g["lh"].transpose(1, 0, 2),
        g["lm"],
        g["rh"].transpose(2, 0, 1),
        g["rm"],
        woven(g["le"], local_reduce.shape[0]),
        g["lr"],
        woven(g["re"], 2 * fh),
        g["rr"].reshape(2 * fh, D),
    )


def solution(mesh):
    nb = mesh.shape["branch"]
    fine = Mesh(mesh.devices.reshape(nb, -1, 2), ("branch", "zz", "core"))
    rows = P(DP, None)
    cols = P(None, None, "branch")
    deep = P("branch", None)
    return jax.shard_map(
        per_device,
        mesh=fine,
        in_specs=(
            rows, rows, P(), P(), P(), cols, deep, cols, deep, cols, deep, cols, deep, P(DP), P(),
        ),
        out_specs=(
            rows, rows, P(), P(), P(), cols, deep, cols, deep, cols, deep, cols, deep,
        ),
        check_vma=False,
    )
```
